32 devices in a mesh: seq: 8 (over y, x, core), fsdp: 4 (over z).
Axes of the slice: x: 2, y: 2, z: 4, core: 2. Of those that a mesh axis runs over, the one named last changes fastest.
Arguments:
- inputs: bfloat16 [4, 1024, 1152], P('fsdp', 'seq'), may hold values from -6 to 6
- segments: int32 [4, 1024], P('fsdp', 'seq'), may hold values from 0 to 1023, as said below
- cotangent: bfloat16 [4, 1024, 1152], P('fsdp', 'seq'), may hold values from -6 to 6
- gain_attn_in: bfloat16 [1152], P('fsdp'), may hold values from 0.099609375 to 1.8984375
- w_query: bfloat16 [1152, 1024], P('fsdp'), may hold values from -0.1875 to 0.1875
- w_key: bfloat16 [1152, 256], P('fsdp'), may hold values from -0.1875 to 0.1875
- w_value: bfloat16 [1152, 256], P('fsdp'), may hold values from -0.1875 to 0.1875
- gain_query: bfloat16 [256], P('fsdp'), may hold values from 0.099609375 to 1.8984375
- gain_key: bfloat16 [256], P('fsdp'), may hold values from 0.099609375 to 1.8984375
- w_output: bfloat16 [1024, 1152], P('fsdp'), may hold values from -0.1875 to 0.1875
- gain_attn_out: bfloat16 [1152], P('fsdp'), may hold values from 0.099609375 to 1.8984375
- gain_ffn_in: bfloat16 [1152], P('fsdp'), may hold values from 0.099609375 to 1.8984375
- w_gate: bfloat16 [1152, 6912], P('fsdp'), may hold values from -0.1875 to 0.1875
- w_up: bfloat16 [1152, 6912], P('fsdp'), may hold values from -0.1875 to 0.1875
- w_down: bfloat16 [6912, 1152], P('fsdp'), may hold values from -0.078125 to 0.078125
- gain_ffn_out: bfloat16 [1152], P('fsdp'), may hold values from 0.099609375 to 1.8984375
Outputs:
- outputs: bfloat16 [4, 1024, 1152], P('fsdp', 'seq')
- d_inputs: float32 [4, 1024, 1152], P('fsdp', 'seq')
- grad_gain_attn_in: float32 [1152], P('fsdp')
- grad_w_query: float32 [1152, 1024], P('fsdp')
- grad_w_key: float32 [1152, 256], P('fsdp')
- grad_w_value: float32 [1152, 256], P('fsdp')
- grad_gain_query: float32 [256], P('fsdp')
- grad_gain_key: float32 [256], P('fsdp')
- grad_w_output: float32 [1024, 1152], P('fsdp')
- grad_gain_attn_out: float32 [1152], P('fsdp')
- grad_gain_ffn_in: float32 [1152], P('fsdp')
- grad_w_gate: float32 [1152, 6912], P('fsdp')
- grad_w_up: float32 [1152, 6912], P('fsdp')
- grad_w_down: float32 [6912, 1152], P('fsdp')
- grad_gain_ffn_out: float32 [1152], P('fsdp')
The draws below stay inside these ranges and needn't reach their ends.
Inputs may be any that keep to these rules, and one draw needn't show every extreme that they name: `segments`: each token's number is the position within its sequence of its document's first token, so numbers never fall along a sequence and the first is 0. In every sequence one document begins within the first 64 positions and ends within the last 64 positions; the other documents are short, and the last position is a document of one token.
All inputs are finite; a program needn't handle non-finite values.
Results may differ from the reference program's by a relative error of at most 0.022.
Values may be sent and summed in bfloat16 or wider, within the bound.
A program may use at most 448 MiB of HBM per device.

```python
import jax
import jax.numpy as jnp
from jax import lax

D = 1152
HEADS = 4
HEAD = 256
FF = 6912
WINDOW = 512
TOK_DEV = 128
LEN = 1024
SEQS = 4


def draw_segments(key, part):
    key = jax.random.fold_in(key, 11)
    key_start, key_end, key_coin = jax.random.split(key, 3)
    positions = jnp.arange(LEN, dtype=jnp.int32)[None, :]
    start_at = jax.random.randint(key_start, (SEQS, 1), 1, TOK_DEV // 2)
    end_at = LEN - jax.random.randint(key_end, (SEQS, 1), 2, TOK_DEV // 2)
    coin_flip = jax.random.randint(key_coin, (SEQS, LEN), 0, 12) == 0
    outside = (positions < start_at) | (positions > end_at)
    begins = (positions == 0) | (positions == start_at) | (positions == end_at) | (positions == LEN - 1) | outside & coin_flip
    start_marks = jnp.where(begins, positions, 0).astype(jnp.int32)
    return lax.cummax(start_marks, axis=1).astype(jnp.int32)


def steps_of(key, shape, cuts, least, largest):
    loudness, own = 1.0, jax.random.fold_in(key, 6)
    for position, shards_of in cuts:
        heights = jnp.exp(jax.random.uniform(jax.random.fold_in(own, position), (shards_of,), jnp.float32, least / len(cuts), largest / len(cuts)))
        loudness = loudness * jnp.repeat(heights, shape[position] // shards_of).reshape([-1 if axis == position else 1 for axis in range(len(shape))])
    return loudness


def noise(rng, shape, scale, most, shards=(), kind=jnp.bfloat16):
    array = scale * jax.random.normal(rng, shape, jnp.float32)
    if shards:
        array = array * steps_of(rng, shape, shards, -0.22, 0.18)
    return jnp.clip(array, -most, most).astype(kind)


def setup_inputs(seed: int = 0) -> dict:
    streams_of = jax.random.split(jax.random.key(seed), 17)
    return {
        "inputs": noise(streams_of[0], (SEQS, LEN, D), 1.0, 6.0, ((0, 4), (1, 8))),
        "segments": draw_segments(jax.random.fold_in(streams_of[16], 71), 0),
        "cotangent": noise(streams_of[2], (SEQS, LEN, D), 1.0, 6.0, ((0, 4), (1, 8))),
        "gain_attn_in": jnp.clip(1.0 + 0.18 * jax.random.normal(streams_of[3], (D,), jnp.float32), 0.099609375, 1.8984375).astype(jnp.bfloat16),
        "w_query": noise(streams_of[4], (D, HEADS * HEAD), D ** -0.5, 0.1875, ((0, 4),)),
        "w_key": noise(streams_of[5], (D, HEAD), D ** -0.5, 0.1875, ((0, 4),)),
        "w_value": noise(streams_of[6], (D, HEAD), D ** -0.5, 0.1875, ((0, 4),)),
        "gain_query": jnp.clip(1.0 + 0.18 * jax.random.normal(streams_of[7], (HEAD,), jnp.float32), 0.099609375, 1.8984375).astype(jnp.bfloat16),
        "gain_key": jnp.clip(1.0 + 0.18 * jax.random.normal(streams_of[8], (HEAD,), jnp.float32), 0.099609375, 1.8984375).astype(jnp.bfloat16),
        "w_output": noise(streams_of[9], (HEADS * HEAD, D), (HEADS * HEAD) ** -0.5, 0.1875, ((0, 4),)),
        "gain_attn_out": jnp.clip(1.0 + 0.18 * jax.random.normal(streams_of[10], (D,), jnp.float32), 0.099609375, 1.8984375).astype(jnp.bfloat16),
        "gain_ffn_in": jnp.clip(1.0 + 0.18 * jax.random.normal(streams_of[11], (D,), jnp.float32), 0.099609375, 1.8984375).astype(jnp.bfloat16),
        "w_gate": noise(streams_of[12], (D, FF), D ** -0.5, 0.1875, ((0, 4),)),
        "w_up": noise(streams_of[13], (D, FF), D ** -0.5, 0.1875, ((0, 4),)),
        "w_down": noise(streams_of[14], (FF, D), FF ** -0.5, 0.078125, ((0, 4),)),
        "gain_ffn_out": jnp.clip(1.0 + 0.18 * jax.random.normal(streams_of[15], (D,), jnp.float32), 0.099609375, 1.8984375).astype(jnp.bfloat16),
    }


epsilon = 1e-06
highest = lax.Precision.HIGHEST
masked_value = -1e+30

@jax.custom_vjp
def low(v):
    return lax.optimization_barrier(v.astype(jnp.bfloat16)).astype(jnp.float32)

@jax.custom_vjp
def low_back(v):
    return v

def low_keep(v):
    return (low(v), None)

def low_pass(kept, grad):
    return (grad,)

def back_keep(v):
    return (v, None)

def back_low(kept, grad):
    return (low(grad),)
low.defvjp(low_keep, low_pass)
low_back.defvjp(back_keep, back_low)

def norm_rows(rows_in, gain_vec):
    return rows_in * lax.rsqrt(lax.optimization_barrier(jnp.mean(rows_in * rows_in, axis=-1, keepdims=True)) + epsilon) * gain_vec

def angles(positions, head_width):
    inv_rates = 10000.0 ** (-(jnp.arange(head_width // 2, dtype=jnp.float32) * 2.0) / head_width)
    return positions.astype(jnp.float32)[:, None] * inv_rates[None, :]

def rotate(rows_in, angles_at):
    half_width = rows_in.shape[-1] // 2
    lower_half = rows_in[..., :half_width]
    upper_half = rows_in[..., half_width:]
    cosine = jnp.cos(angles_at)
    sine_part = jnp.sin(angles_at)
    return jnp.concatenate([lower_half * cosine - upper_half * sine_part, upper_half * cosine + lower_half * sine_part], axis=-1)

def geglu_act(gate_proj, up_proj):
    return jax.nn.gelu(gate_proj, approximate=True) * up_proj

def attend(q_low, k_low, v_low, seg_ids):
    length = q_low.shape[0]
    block_rows = min(512, length)
    score_scale = HEAD ** (-0.5)
    key_pad = jnp.concatenate([jnp.zeros((WINDOW, HEAD), jnp.float32), k_low], axis=0)
    value_pad = jnp.concatenate([jnp.zeros((WINDOW, HEAD), jnp.float32), v_low], axis=0)
    seg_pad = jnp.concatenate([jnp.full((WINDOW,), -1, jnp.int32), seg_ids.astype(jnp.int32)], axis=0)

    def one_block(offset_at):
        offset_at = offset_at.astype(jnp.int32)
        q_rows = lax.dynamic_slice_in_dim(q_low, offset_at, block_rows, 0)
        k_rows = lax.dynamic_slice_in_dim(key_pad, offset_at, block_rows + WINDOW, 0)
        v_rows = lax.dynamic_slice_in_dim(value_pad, offset_at, block_rows + WINDOW, 0)
        q_segs = lax.dynamic_slice_in_dim(seg_ids.astype(jnp.int32), offset_at, block_rows, 0)
        k_segs = lax.dynamic_slice_in_dim(seg_pad, offset_at, block_rows + WINDOW, 0)
        q_place = offset_at + jnp.arange(block_rows, dtype=jnp.int32)
        k_place = offset_at - WINDOW + jnp.arange(block_rows + WINDOW, dtype=jnp.int32)
        distance = q_place[:, None] - k_place[None, :]
        allowed = (distance >= 0) & (distance < WINDOW) & (k_place[None, :] >= 0) & (q_segs[:, None] == k_segs[None, :])
        scores = low_back(jnp.einsum('qhd,kd->qhk', q_rows, k_rows, precision=highest) * score_scale)
        masked = jnp.where(allowed[:, None, :], scores, masked_value)
        attn_probs = low(jax.nn.softmax(masked, axis=-1))
        return jnp.einsum('qhk,kd->qhd', attn_probs, v_rows, precision=highest).reshape(block_rows, HEADS * HEAD)
    starts = jnp.arange(length // block_rows, dtype=jnp.int32) * block_rows
    result = lax.map(jax.checkpoint(one_block), starts)
    return result.reshape(length, HEADS * HEAD)

def decoder_layer(rows_in, seg_ids, gain_attn_in, w_query, w_key, w_value, gain_query, gain_key, w_output, gain_attn_out, gain_ffn_in, w_gate, w_up, w_down, gain_ffn_out):
    length = rows_in.shape[0]
    positions = jnp.arange(length, dtype=jnp.int32) - seg_ids.astype(jnp.int32)
    angles_at = angles(positions, HEAD)
    h_one = low(norm_rows(rows_in, gain_attn_in))
    q_raw = low_back(jnp.dot(h_one, w_query, precision=highest))
    k_raw = low_back(jnp.dot(h_one, w_key, precision=highest))
    v_low = low(low_back(jnp.dot(h_one, w_value, precision=highest)))
    q_low = low(rotate(norm_rows(q_raw.reshape(length, HEADS, HEAD), gain_query), angles_at[:, None, :]))
    k_low = low(rotate(norm_rows(k_raw, gain_key), angles_at))
    attended = low(low_back(attend(q_low, k_low, v_low, seg_ids)))
    o_raw = low_back(jnp.dot(attended, w_output, precision=highest))
    middle = rows_in + norm_rows(o_raw, gain_attn_out)
    h_two = low(norm_rows(middle, gain_ffn_in))
    gate_proj = low_back(jnp.dot(h_two, w_gate, precision=highest))
    up_proj = low_back(jnp.dot(h_two, w_up, precision=highest))
    act_low = low(geglu_act(gate_proj, up_proj))
    f_raw = low_back(jnp.dot(act_low, w_down, precision=highest))
    return middle + norm_rows(f_raw, gain_ffn_out)

def reference(inputs, segments, cotangent, gain_attn_in, w_query, w_key, w_value, gain_query, gain_key, w_output, gain_attn_out, gain_ffn_in, w_gate, w_up, w_down, gain_ffn_out):
    weights_in = tuple((weight_arr.astype(jnp.float32) for weight_arr in (gain_attn_in, w_query, w_key, w_value, gain_query, gain_key, w_output, gain_attn_out, gain_ffn_in, w_gate, w_up, w_down, gain_ffn_out)))

    def per_sequence(running, seq_item):
        rows_in, seg_ids, grad_out = seq_item

        def forward(tokens_in, *params_in):
            return decoder_layer(tokens_in, seg_ids, *params_in)
        result, pull_back = jax.vjp(forward, rows_in.astype(jnp.float32), *weights_in)
        gradients = pull_back(grad_out.astype(jnp.float32))
        running = tuple((acc_sum + new_grad for acc_sum, new_grad in zip(running, gradients[1:])))
        return (running, (result.astype(jnp.bfloat16), gradients[0]))
    zero_grads = tuple((jnp.zeros_like(weight_arr) for weight_arr in weights_in))
    running, (outputs, d_inputs) = lax.scan(per_sequence, zero_grads, (inputs, segments, cotangent))
    return (outputs, d_inputs, running[0], running[1], running[2], running[3], running[4], running[5], running[6], running[7], running[8], running[9], running[10], running[11], running[12])
```

```python
import functools

import jax
import jax.numpy as jnp
from jax import lax
from jax.experimental import pallas as pl
from jax.experimental.pallas import tpu as pltpu
from jax.sharding import PartitionSpec as P

WINDOW = 512


epsilon = 1e-06
masked_value = -1e30


def from_behind(block, axis, distance):
    devices = range(lax.axis_size(axis))
    route = [(i - distance, i) for i in devices if i - distance in devices]
    return lax.ppermute(block, axis, route)


def norm_rows(rows_in, gain_vec):
    return (
        rows_in
        * lax.rsqrt(jnp.mean(rows_in * rows_in, axis=-1, keepdims=True) + epsilon)
        * gain_vec
    )


def angles(positions, head_width):
    inv_rates = 10000.0 ** (-(jnp.arange(head_width // 2, dtype=jnp.float32) * 2.0) / head_width)
    return positions.astype(jnp.float32)[:, None] * inv_rates[None, :]


def rotate(rows_in, angles_at):
    half_width = rows_in.shape[-1] // 2
    lower_half = rows_in[..., :half_width]
    upper_half = rows_in[..., half_width:]
    cosine = jnp.cos(angles_at)
    sine_part = jnp.sin(angles_at)
    return jnp.concatenate(
        [
            lower_half * cosine - upper_half * sine_part,
            upper_half * cosine + lower_half * sine_part,
        ],
        axis=-1,
    )


def geglu_act(gate_proj, up_proj):
    return jax.nn.gelu(gate_proj, approximate=True) * up_proj


def inner_rows(left, right):
    return lax.dot_general(
        left, right, (((0,), (0,)), ((), ())), preferred_element_type=jnp.float32
    )


def outer_cols(left, right):
    return lax.dot_general(
        left, right, (((1,), (1,)), ((), ())), preferred_element_type=jnp.float32
    )


def shards_plain(
    inputs,
    segments,
    cotangent,
    gain_attn_in,
    w_query,
    w_key,
    w_value,
    gain_query,
    gain_key,
    w_output,
    gain_attn_out,
    gain_ffn_in,
    w_gate,
    w_up,
    w_down,
    gain_ffn_out,
):
    rows_here = inputs.shape[1]
    head_width = w_key.shape[1]
    head_count = w_query.shape[1] // head_width
    reach_devs = (WINDOW - 2 + rows_here) // rows_here
    score_scale = head_width ** (-0.5)
    first_row = lax.axis_index("seq") * rows_here
    tokens = inputs[0].astype(jnp.float32)
    seg_here = segments[0]
    positions = first_row + jnp.arange(rows_here, dtype=jnp.int32)
    angles_at = angles(positions - seg_here, head_width)
    wq_all, wk_all, wv_all, wo_all, g_attn_in, g_query, g_key, g_attn_out, g_ffn_in, g_ffn_out = (
        lax.all_gather(w_query, "fsdp", axis=0, tiled=True),
        lax.all_gather(w_key, "fsdp", axis=0, tiled=True),
        lax.all_gather(w_value, "fsdp", axis=0, tiled=True),
        lax.all_gather(w_output, "fsdp", axis=0, tiled=True),
        lax.all_gather(gain_attn_in, "fsdp", axis=0, tiled=True),
        lax.all_gather(gain_query, "fsdp", axis=0, tiled=True),
        lax.all_gather(gain_key, "fsdp", axis=0, tiled=True),
        lax.all_gather(gain_attn_out, "fsdp", axis=0, tiled=True),
        lax.all_gather(gain_ffn_in, "fsdp", axis=0, tiled=True),
        lax.all_gather(gain_ffn_out, "fsdp", axis=0, tiled=True),
    )
    g_attn_in = g_attn_in.astype(jnp.float32)
    g_query = g_query.astype(jnp.float32)
    g_key = g_key.astype(jnp.float32)
    g_attn_out = g_attn_out.astype(jnp.float32)
    g_ffn_in = g_ffn_in.astype(jnp.float32)
    g_ffn_out = g_ffn_out.astype(jnp.float32)
    normed_one, pull_one = jax.vjp(norm_rows, tokens, g_attn_in)
    h_one = normed_one.astype(jnp.bfloat16)
    q_raw = jnp.dot(h_one, wq_all, preferred_element_type=jnp.float32)
    k_raw = jnp.dot(h_one, wk_all, preferred_element_type=jnp.float32)
    v_raw = jnp.dot(h_one, wv_all, preferred_element_type=jnp.float32)

    def prepare(q_in, k_in, gq_in, gk_in):
        q_rows = q_in.reshape(q_in.shape[0], head_count, head_width)
        q_fin = rotate(norm_rows(q_rows, gq_in), angles_at[:, None, :])
        k_fin = rotate(norm_rows(k_in, gk_in), angles_at)
        return (q_fin, k_fin)

    (q_fin, k_fin), pull_prep = jax.vjp(prepare, q_raw, k_raw, g_query, g_key)
    q_low = q_fin.astype(jnp.bfloat16).reshape(rows_here * head_count, head_width)
    k_low = k_fin.astype(jnp.bfloat16)
    v_low = v_raw.astype(jnp.bfloat16)
    key_parts = []
    value_parts = []
    seg_parts = []
    for offset in range(reach_devs, 0, -1):
        k_came, v_came, s_came = from_behind((k_low, v_low, seg_here), "seq", offset)
        key_parts.append(k_came)
        value_parts.append(v_came)
        seg_parts.append(s_came)
    key_rows = jnp.concatenate(key_parts + [k_low], axis=0)
    value_rows = jnp.concatenate(value_parts + [v_low], axis=0)
    key_segs = jnp.concatenate(seg_parts + [seg_here], axis=0)
    key_place = (
        first_row
        - reach_devs * rows_here
        + jnp.arange((reach_devs + 1) * rows_here, dtype=jnp.int32)
    )
    distance = positions[:, None] - key_place[None, :]
    allowed = (
        (distance >= 0)
        & (distance < WINDOW)
        & (key_place[None, :] >= 0)
        & (seg_here[:, None] == key_segs[None, :])
    )
    scores = (outer_cols(q_low, key_rows) * score_scale).reshape(rows_here, head_count, -1)
    masked = jnp.where(allowed[:, None, :], scores, masked_value)
    attn_probs = jax.nn.softmax(masked, axis=-1).reshape(rows_here * head_count, -1)
    probs_low = attn_probs.astype(jnp.bfloat16)
    attended = jnp.dot(probs_low, value_rows, preferred_element_type=jnp.float32)
    att_low = attended.reshape(rows_here, head_count * head_width).astype(jnp.bfloat16)
    o_raw = jnp.dot(att_low, wo_all, preferred_element_type=jnp.float32)
    branch_att, pull_att = jax.vjp(norm_rows, o_raw, g_attn_out)
    middle = tokens + branch_att
    normed_two, pull_mid = jax.vjp(norm_rows, middle, g_ffn_in)
    h_two = normed_two.astype(jnp.bfloat16)
    gate_all, up_all, down_all = (
        lax.all_gather(w_gate, "fsdp", axis=0, tiled=True),
        lax.all_gather(w_up, "fsdp", axis=0, tiled=True),
        lax.all_gather(w_down, "fsdp", axis=0, tiled=True),
    )
    gate_proj = jnp.dot(h_two, gate_all, preferred_element_type=jnp.float32)
    up_proj = jnp.dot(h_two, up_all, preferred_element_type=jnp.float32)
    act_full, pull_act = jax.vjp(geglu_act, gate_proj, up_proj)
    act_low = act_full.astype(jnp.bfloat16)
    f_raw = jnp.dot(act_low, down_all, preferred_element_type=jnp.float32)
    branch_ffn, pull_out = jax.vjp(norm_rows, f_raw, g_ffn_out)
    outputs = (middle + branch_ffn).astype(jnp.bfloat16)
    upstream = cotangent[0].astype(jnp.float32)
    d_fraw, d_gffn_out = pull_out(upstream)
    d_flow = d_fraw.astype(jnp.bfloat16)
    gate_shard, up_shard, down_shard, d_flow = lax.optimization_barrier(
        (w_gate, w_up, w_down, d_flow)
    )
    gate_back, up_back, down_back = (
        lax.all_gather(gate_shard, "fsdp", axis=0, tiled=True),
        lax.all_gather(up_shard, "fsdp", axis=0, tiled=True),
        lax.all_gather(down_shard, "fsdp", axis=0, tiled=True),
    )
    d_act = outer_cols(d_flow, down_back)
    d_gate, d_up = pull_act(d_act)
    dg_low = d_gate.astype(jnp.bfloat16)
    du_low = d_up.astype(jnp.bfloat16)
    d_htwo = outer_cols(dg_low, gate_back) + outer_cols(du_low, up_back)
    grad_down_part = lax.psum_scatter(
        inner_rows(act_low, d_flow).astype(jnp.bfloat16), "fsdp", scatter_dimension=0, tiled=True
    )
    grad_in_part = lax.psum_scatter(
        jnp.concatenate([inner_rows(h_two, dg_low), inner_rows(h_two, du_low)], axis=1).astype(
            jnp.bfloat16
        ),
        "fsdp",
        scatter_dimension=0,
        tiled=True,
    ).astype(jnp.float32)
    hidden_width = w_gate.shape[1]
    grad_gate_part = grad_in_part[:, :hidden_width]
    grad_up_part = grad_in_part[:, hidden_width:]
    d_mid_norm, d_gffn_in = pull_mid(d_htwo)
    d_middle = upstream + d_mid_norm
    d_oraw, d_gattn_out = pull_att(d_middle)
    d_olow = d_oraw.astype(jnp.bfloat16)
    grad_wo = inner_rows(att_low, d_olow)
    d_att_low = (
        outer_cols(d_olow, wo_all).astype(jnp.bfloat16).reshape(rows_here * head_count, head_width)
    )
    d_probs = outer_cols(d_att_low, value_rows)
    d_scores = attn_probs * (d_probs - jnp.sum(attn_probs * d_probs, axis=-1, keepdims=True))
    ds_low = d_scores.astype(jnp.bfloat16)
    d_qfin = jnp.dot(ds_low, key_rows, preferred_element_type=jnp.float32) * score_scale
    d_keys = inner_rows(ds_low, q_low) * score_scale
    d_values = inner_rows(probs_low, d_att_low)
    d_kfin = d_keys[reach_devs * rows_here :]
    d_vsum = d_values[reach_devs * rows_here :]
    for offset in range(1, reach_devs + 1):
        slot_index = reach_devs - offset
        k_back, v_back = (
            from_behind(
                d_keys[slot_index * rows_here : (slot_index + 1) * rows_here].astype(jnp.bfloat16),
                "seq",
                -offset,
            ).astype(jnp.float32),
            from_behind(
                d_values[slot_index * rows_here : (slot_index + 1) * rows_here].astype(
                    jnp.bfloat16
                ),
                "seq",
                -offset,
            ).astype(jnp.float32),
        )
        d_kfin = d_kfin + k_back
        d_vsum = d_vsum + v_back
    d_qraw, d_kraw, d_gquery, d_gkey = pull_prep(
        (d_qfin.reshape(rows_here, head_count, head_width), d_kfin)
    )
    dq_low = d_qraw.astype(jnp.bfloat16)
    dk_low = d_kraw.astype(jnp.bfloat16)
    dv_low = d_vsum.astype(jnp.bfloat16)
    d_hone = outer_cols(dq_low, wq_all) + outer_cols(dk_low, wk_all) + outer_cols(dv_low, wv_all)
    grad_wq = inner_rows(h_one, dq_low)
    grad_wk = inner_rows(h_one, dk_low)
    grad_wv = inner_rows(h_one, dv_low)
    d_tok_norm, d_gattn_in = pull_one(d_hone)
    d_inputs = d_middle + d_tok_norm
    part_wq, part_wk, part_wv, part_wo, part_gai, part_gq, part_gk, part_gao, part_gfi, part_gfo = (
        lax.psum_scatter(
            grad_wq.astype(jnp.bfloat16), "fsdp", scatter_dimension=0, tiled=True
        ).astype(jnp.float32),
        lax.psum_scatter(
            grad_wk.astype(jnp.bfloat16), "fsdp", scatter_dimension=0, tiled=True
        ).astype(jnp.float32),
        lax.psum_scatter(
            grad_wv.astype(jnp.bfloat16), "fsdp", scatter_dimension=0, tiled=True
        ).astype(jnp.float32),
        lax.psum_scatter(
            grad_wo.astype(jnp.bfloat16), "fsdp", scatter_dimension=0, tiled=True
        ).astype(jnp.float32),
        lax.psum_scatter(
            d_gattn_in.astype(jnp.bfloat16), "fsdp", scatter_dimension=0, tiled=True
        ).astype(jnp.float32),
        lax.psum_scatter(
            d_gquery.astype(jnp.bfloat16), "fsdp", scatter_dimension=0, tiled=True
        ).astype(jnp.float32),
        lax.psum_scatter(
            d_gkey.astype(jnp.bfloat16), "fsdp", scatter_dimension=0, tiled=True
        ).astype(jnp.float32),
        lax.psum_scatter(
            d_gattn_out.astype(jnp.bfloat16), "fsdp", scatter_dimension=0, tiled=True
        ).astype(jnp.float32),
        lax.psum_scatter(
            d_gffn_in.astype(jnp.bfloat16), "fsdp", scatter_dimension=0, tiled=True
        ).astype(jnp.float32),
        lax.psum_scatter(
            d_gffn_out.astype(jnp.bfloat16), "fsdp", scatter_dimension=0, tiled=True
        ).astype(jnp.float32),
    )
    cols_wq, cols_wk, cols_wv, cols_wo, cols_gate, cols_up, cols_down = (
        lax.psum_scatter(
            part_wq.astype(jnp.bfloat16), "seq", scatter_dimension=1, tiled=True
        ).astype(jnp.float32),
        lax.psum_scatter(
            part_wk.astype(jnp.bfloat16), "seq", scatter_dimension=1, tiled=True
        ).astype(jnp.float32),
        lax.psum_scatter(
            part_wv.astype(jnp.bfloat16), "seq", scatter_dimension=1, tiled=True
        ).astype(jnp.float32),
        lax.psum_scatter(
            part_wo.astype(jnp.bfloat16), "seq", scatter_dimension=1, tiled=True
        ).astype(jnp.float32),
        lax.psum_scatter(
            grad_gate_part.astype(jnp.bfloat16), "seq", scatter_dimension=1, tiled=True
        ).astype(jnp.float32),
        lax.psum_scatter(
            grad_up_part.astype(jnp.bfloat16), "seq", scatter_dimension=1, tiled=True
        ).astype(jnp.float32),
        lax.psum_scatter(grad_down_part, "seq", scatter_dimension=1, tiled=True).astype(
            jnp.float32
        ),
    )
    sum_wq, sum_wk, sum_wv, sum_wo, sum_gate, sum_up, sum_down = (
        lax.all_gather(cols_wq.astype(jnp.bfloat16), "seq", axis=1, tiled=True).astype(
            cols_wq.dtype
        ),
        lax.all_gather(cols_wk.astype(jnp.bfloat16), "seq", axis=1, tiled=True).astype(
            cols_wk.dtype
        ),
        lax.all_gather(cols_wv.astype(jnp.bfloat16), "seq", axis=1, tiled=True).astype(
            cols_wv.dtype
        ),
        lax.all_gather(cols_wo.astype(jnp.bfloat16), "seq", axis=1, tiled=True).astype(
            cols_wo.dtype
        ),
        lax.all_gather(cols_gate.astype(jnp.bfloat16), "seq", axis=1, tiled=True).astype(
            cols_gate.dtype
        ),
        lax.all_gather(cols_up.astype(jnp.bfloat16), "seq", axis=1, tiled=True).astype(
            cols_up.dtype
        ),
        lax.all_gather(cols_down.astype(jnp.bfloat16), "seq", axis=1, tiled=True).astype(
            cols_down.dtype
        ),
    )
    sum_gai, sum_gq, sum_gk, sum_gao, sum_gfi, sum_gfo = lax.psum(
        (part_gai, part_gq, part_gk, part_gao, part_gfi, part_gfo), "seq"
    )
    return (
        outputs[None],
        d_inputs[None],
        sum_gai,
        sum_wq,
        sum_wk,
        sum_wv,
        sum_gq,
        sum_gk,
        sum_wo,
        sum_gao,
        sum_gfi,
        sum_gate,
        sum_up,
        sum_down,
        sum_gfo,
    )


MESH = pl.DeviceIdType.MESH
BF16 = jnp.bfloat16
F32 = jnp.float32
GELU_RATE = 0.7978845608028654
GELU_CUBE = 0.044715
HID_TILE = 256


def bit_of(value, mask):
    return lax.rem(lax.div(value, mask), 2)


def flip(value, masks, bits):
    for b in range(bits):
        if (masks >> b) & 1:
            value = value + (1 << b) * (1 - 2 * bit_of(value, 1 << b))
    return value


def greet(devices):
    barrier = pltpu.get_barrier_semaphore()
    for device in devices:
        pl.semaphore_signal(barrier, inc=1, device_id=device, device_id_type=MESH)
    pl.semaphore_wait(barrier, len(devices))


def remote(src, dst, send, recv, device):
    return pltpu.make_async_remote_copy(
        src_ref=src, dst_ref=dst, send_sem=send, recv_sem=recv,
        device_id=device, device_id_type=MESH,
    )


def many(offset, size):
    return pl.ds(pl.multiple_of(offset, size if size % 128 == 0 else 16), size)


def lanes(offset, size):
    return pl.ds(pl.multiple_of(offset, 128), size)


class Place:
    def __init__(self, n_seq, n_fsdp):
        self.n_seq, self.n_fsdp = n_seq, n_fsdp
        self.s = lax.axis_index("seq")
        self.z = lax.axis_index("fsdp")
        self.c = bit_of(self.s, 1)
        self.x = bit_of(self.s, 2)
        self.y = bit_of(self.s, 4)

    def plane(self, masks):
        return (flip(self.s, masks, 3), self.z)

    def line(self, masks):
        return (self.s, flip(self.z, masks, 2))

    def halves(self, first_x):
        if first_x:
            return self.x, self.y, 2, 4
        return self.y, self.x, 4, 2


def spread_kernel(
    n_seq, n_fsdp,
    gu_ref, qkv_ref, wo_ref, pack_ref, seg_ref,
    gu_all, qkv_all, wo_all, pack_all, seg_all,
    send, recv, own_sem, small_send, small_recv, seg_send, seg_recv,
):
    at = Place(n_seq, n_fsdp)
    z, c = at.z, at.c
    depth, heads_width = qkv_ref.shape
    rows_o, width = wo_ref.shape
    hidden = gu_ref.shape[3]
    greet([at.plane(k) for k in range(1, n_seq)] + [at.line(m) for m in range(1, n_fsdp)])

    own = [
        pltpu.make_async_copy(gu_ref.at[i, z], gu_all.at[i, many(z * depth, depth)], own_sem.at[i])
        for i in range(2)
    ]
    own.append(pltpu.make_async_copy(qkv_ref, qkv_all.at[many(z * depth, depth)], own_sem.at[2]))
    own.append(pltpu.make_async_copy(wo_ref, wo_all.at[many(z * rows_o, rows_o)], own_sem.at[3]))
    own.append(pltpu.make_async_copy(pack_ref, pack_all.at[z], own_sem.at[4]))
    own.append(pltpu.make_async_copy(seg_ref, seg_all.at[at.s], own_sem.at[5]))

    small = [
        remote(pack_ref, pack_all.at[z], small_send.at[m], small_recv.at[m], at.line(m))
        for m in range(1, n_fsdp)
    ] + [
        remote(seg_ref, seg_all.at[at.s], seg_send.at[k], seg_recv.at[k], at.plane(k))
        for k in range(1, n_seq)
    ]

    def region(kind, whose, hi, lo, level):
        base = whose * depth
        if kind == "qkv":
            cols = {
                0: lanes(hi * (heads_width // 2) + lo * (heads_width // 4), heads_width // 4),
                1: lanes(hi * (heads_width // 2), heads_width // 2),
                2: slice(None),
            }[level]
            return qkv_all.at[many(base + c * (depth // 2), depth // 2), cols]
        if kind == "wo":
            start = whose * rows_o + c * (rows_o // 2)
            if level < 2:
                start = start + hi * (rows_o // 4)
            if level < 1:
                start = start + lo * (rows_o // 8)
            return wo_all.at[many(start, rows_o // (8, 4, 2)[level])]
        if level == 2:
            return gu_all.at[c, many(base, depth)]
        rows = many(base + hi * (depth // 2), depth // 2)
        if level == 1:
            return gu_all.at[c, rows]
        return gu_all.at[c, rows, lanes(lo * (hidden // 2), hidden // 2)]

    def source(kind, to, hi, lo):
        if kind == "qkv":
            cols = lanes(hi * (heads_width // 2) + lo * (heads_width // 4), heads_width // 4)
            return qkv_ref.at[many(c * (depth // 2), depth // 2), cols]
        if kind == "wo":
            start = c * (rows_o // 2) + hi * (rows_o // 4) + lo * (rows_o // 8)
            return wo_ref.at[many(start, rows_o // 8)]
        rows = many(hi * (depth // 2), depth // 2)
        return gu_ref.at[c, to, rows, lanes(lo * (hidden // 2), hidden // 2)]

    items = []
    for kind in ("qkv", "wo", "gu"):
        for m in range(1, n_fsdp):
            items.append((kind, m, (m % 2 == 1) != (kind == "wo")))
    steps = []
    for i, (kind, m, first_x) in enumerate(items):
        hi, lo, mask_hi, mask_lo = at.halves(first_x)
        there = flip(z, m, 2)
        steps.append((
            remote(source(kind, there, hi, lo), region(kind, z, hi, lo, 0),
                   send.at[i, 0], recv.at[i, 0], at.line(m)),
            remote(region(kind, there, hi, lo, 0), region(kind, there, hi, lo, 0),
                   send.at[i, 1], recv.at[i, 1], at.plane(mask_lo)),
            remote(region(kind, there, hi, lo, 1), region(kind, there, hi, lo, 1),
                   send.at[i, 2], recv.at[i, 2], at.plane(mask_hi)),
            remote(region(kind, there, hi, lo, 2), region(kind, there, hi, lo, 2),
                   send.at[i, 3], recv.at[i, 3], at.plane(1)),
        ))
    for i in range(len(items)):
        steps[i][0].start()
    for copy in small:
        copy.start()
    for copy in own:
        copy.start()
    for t in range(len(items) + 2):
        for stage in (3, 2, 1):
            i = t - (stage - 1)
            if 0 <= i < len(items):
                steps[i][stage - 1].wait_recv()
                steps[i][stage].start()
    for i in range(len(items)):
        steps[i][3].wait_recv()
        for stage in range(4):
            steps[i][stage].wait_send()
    for copy in small:
        copy.wait()
    for copy in own:
        copy.wait()


def spread(n_seq, n_fsdp, gu_blocks, qkv, wo, pack, segs):
    depth, heads_width = qkv.shape
    rows_o, width = wo.shape
    hidden = gu_blocks.shape[3]
    n_items = 3 * (n_fsdp - 1)
    anywhere = pl.BlockSpec(memory_space=pl.ANY)
    return pl.pallas_call(
        functools.partial(spread_kernel, n_seq, n_fsdp),
        out_shape=[
            jax.ShapeDtypeStruct((2, n_fsdp * depth, hidden), BF16),
            jax.ShapeDtypeStruct((n_fsdp * depth, heads_width), BF16),
            jax.ShapeDtypeStruct((n_fsdp * rows_o, width), BF16),
            jax.ShapeDtypeStruct((n_fsdp,) + pack.shape, BF16),
            jax.ShapeDtypeStruct((n_seq,) + segs.shape, jnp.int32),
        ],
        in_specs=[anywhere] * 5,
        out_specs=[anywhere] * 5,
        scratch_shapes=[
            pltpu.SemaphoreType.DMA((n_items, 4)),
            pltpu.SemaphoreType.DMA((n_items, 4)),
            pltpu.SemaphoreType.DMA((6,)),
            pltpu.SemaphoreType.DMA((n_fsdp,)),
            pltpu.SemaphoreType.DMA((n_fsdp,)),
            pltpu.SemaphoreType.DMA((n_seq,)),
            pltpu.SemaphoreType.DMA((n_seq,)),
        ],
        compiler_params=pltpu.CompilerParams(collective_id=0, has_side_effects=True),
        name="spread_weights",
    )(gu_blocks, qkv, wo, pack, segs)


def behind_kernel(n_seq, reach, kv_ref, came_ref, send, recv):
    s, z = lax.axis_index("seq"), lax.axis_index("fsdp")
    greet([(lax.rem(s + n_seq - o, n_seq), z) for o in range(1, reach + 1)])
    copies = [
        remote(kv_ref, came_ref.at[reach - o], send.at[o - 1], recv.at[o - 1],
               (lax.rem(s + o, n_seq), z))
        for o in range(1, reach + 1)
    ]
    for copy in copies:
        copy.start()
    came_ref[reach] = kv_ref[...]
    for copy in copies:
        copy.wait()


def from_blocks_behind(n_seq, reach, keys_values):
    return pl.pallas_call(
        functools.partial(behind_kernel, n_seq, reach),
        out_shape=jax.ShapeDtypeStruct((reach + 1,) + keys_values.shape, keys_values.dtype),
        in_specs=[pl.BlockSpec(memory_space=pltpu.VMEM)],
        out_specs=pl.BlockSpec(memory_space=pltpu.VMEM),
        scratch_shapes=[pltpu.SemaphoreType.DMA((reach,)), pltpu.SemaphoreType.DMA((reach,))],
        compiler_params=pltpu.CompilerParams(collective_id=1, has_side_effects=True),
        name="keys_values_behind",
    )(keys_values)


def return_kernel(n_seq, reach, parts_ref, own_ref, sum_ref, came, send, recv):
    s, z = lax.axis_index("seq"), lax.axis_index("fsdp")
    greet([(lax.rem(s + o, n_seq), z) for o in range(1, reach + 1)])
    copies = [
        remote(parts_ref.at[reach - o], came.at[o - 1], send.at[o - 1], recv.at[o - 1],
               (lax.rem(s + n_seq - o, n_seq), z))
        for o in range(1, reach + 1)
    ]
    for copy in copies:
        copy.start()
    for copy in copies:
        copy.wait()
    total = own_ref[...]
    for o in range(reach):
        total = total + came[o].astype(F32)
    sum_ref[...] = total


def return_to_blocks(n_seq, reach, parts, own):
    in_vmem = pl.BlockSpec(memory_space=pltpu.VMEM)
    return pl.pallas_call(
        functools.partial(return_kernel, n_seq, reach),
        out_shape=jax.ShapeDtypeStruct(own.shape, F32),
        in_specs=[in_vmem] * 2,
        out_specs=in_vmem,
        scratch_shapes=[
            pltpu.VMEM(parts.shape, BF16),
            pltpu.SemaphoreType.DMA((reach,)),
            pltpu.SemaphoreType.DMA((reach,)),
        ],
        compiler_params=pltpu.CompilerParams(collective_id=2, has_side_effects=True),
        name="keys_values_return",
    )(parts, own)


def dot_nt(left, right):
    return lax.dot_general(left, right, (((1,), (1,)), ((), ())), preferred_element_type=F32)


def dot_nn(left, right):
    return jnp.dot(left, right, preferred_element_type=F32)


def ffn_kernel(
    n_seq, n_fsdp,
    h_ref, mid_ref, cot_ref, gains_ref, gu_ref, wd_ref,
    out_ref, dmid_ref, ggu_ref, gd_ref, dgain_ref,
    w_in, w_down, h_all, df_all, gelu_s, slope_s, act, dgate, dup, h_turn,
    part_out, part_in, total, stage, w_sem, ex_send, ex_recv, stage_sem,
):
    at = Place(n_seq, n_fsdp)
    rows, width = h_ref.shape
    hidden = w_in.shape[2]
    hidden_used = wd_ref.shape[0]
    n_hid = hidden // HID_TILE
    out_tile = width // 3
    loads = [
        pltpu.make_async_copy(gu_ref.at[0], w_in.at[0], w_sem.at[0]),
        pltpu.make_async_copy(gu_ref.at[1], w_in.at[1], w_sem.at[1]),
        pltpu.make_async_copy(wd_ref, w_down.at[pl.ds(0, hidden_used)], w_sem.at[2]),
    ]
    for load in loads:
        load.start()
    h_all[0] = h_ref[...]
    greet([at.line(m) for m in range(1, n_fsdp)])

    def exchange(phase, src, dst):
        copies = {}
        for m in range(1, n_fsdp):
            copies[m] = remote(
                src(m), dst(m), ex_send.at[phase, m], ex_recv.at[phase, m], at.line(m)
            )
        return copies

    send_h = exchange(0, lambda m: h_all.at[0], lambda m: h_all.at[m])
    send_f = exchange(1, lambda m: part_out.at[0, m], lambda m: part_in.at[0, m])
    send_df = exchange(2, lambda m: df_all.at[0], lambda m: df_all.at[m])
    send_dh = exchange(3, lambda m: part_out.at[1, m], lambda m: part_in.at[1, m])
    for m in range(1, n_fsdp):
        send_h[m].start()
    if hidden > hidden_used:
        w_down[pl.ds(hidden_used, hidden - hidden_used)] = jnp.zeros(
            (hidden - hidden_used, width), BF16
        )
    for load in loads:
        load.wait()

    def hid(n):
        return pl.ds(pl.multiple_of(n * HID_TILE, HID_TILE), HID_TILE)

    def outs(n):
        return pl.ds(pl.multiple_of(n * out_tile, 128), out_tile)

    for m in range(n_fsdp):
        if m:
            send_h[m].wait_recv()

        @pl.loop(0, n_hid)
        def _(n):
            rows_h = h_all[m]
            gate = dot_nn(rows_h, w_in[0, :, hid(n)])
            up = dot_nn(rows_h, w_in[1, :, hid(n)])
            squared = gate * gate
            bent = jnp.tanh(GELU_RATE * (gate + GELU_CUBE * squared * gate))
            gelu = 0.5 * gate * (1.0 + bent)
            slope = 0.5 * (1.0 + bent) + 0.5 * gate * (1.0 - bent * bent) * (
                GELU_RATE * (1.0 + 3.0 * GELU_CUBE * squared)
            )
            gelu_s[m, :, hid(n)] = gelu
            slope_s[m, :, hid(n)] = slope * up
            act[m, :, hid(n)] = (gelu * up).astype(BF16)

        @pl.loop(0, 3)
        def _(n):
            part = dot_nn(act[m], w_down[:, outs(n)])
            if m:
                part_out[0, m, :, outs(n)] = part.astype(BF16)
            else:
                total[:, outs(n)] = part

        if m:
            send_f[m].start()

    for m in range(n_fsdp):
        h_turn[:, pl.ds(m * rows, rows)] = h_all[m].T

    for m in range(1, n_fsdp):
        send_f[m].wait_recv()
    f_raw = total[...]
    for m in range(1, n_fsdp):
        f_raw = f_raw + part_in[0, m].astype(F32)
    cot = cot_ref[...].astype(F32)
    gain = gains_ref[0:1, :]
    scale = lax.rsqrt(jnp.mean(f_raw * f_raw, axis=-1, keepdims=True) + epsilon)
    out_ref[...] = (mid_ref[...] + f_raw * scale * gain).astype(BF16)
    pulled = cot * gain
    inner = jnp.mean(pulled * f_raw, axis=-1, keepdims=True)
    df_all[0] = (scale * pulled - f_raw * (scale * scale * scale * inner)).astype(BF16)
    for m in range(1, n_fsdp):
        send_df[m].start()
    dgain_ref[...] = jnp.zeros(dgain_ref.shape, F32)
    dgain_ref[0:1, :] = jnp.sum(cot * f_raw * scale, axis=0, keepdims=True)

    for m in range(n_fsdp):
        if m:
            send_df[m].wait_recv()

        @pl.loop(0, n_hid)
        def _(n):
            dact = dot_nt(df_all[m], w_down[hid(n), :])
            dgate[m, :, hid(n)] = (dact * slope_s[m, :, hid(n)]).astype(BF16)
            dup[m, :, hid(n)] = (dact * gelu_s[m, :, hid(n)]).astype(BF16)

        @pl.loop(0, 3)
        def _(n):
            part = dot_nt(dgate[m], w_in[0, outs(n), :]) + dot_nt(dup[m], w_in[1, outs(n), :])
            if m:
                part_out[1, m, :, outs(n)] = part.astype(BF16)
            else:
                total[:, outs(n)] = part

        if m:
            send_dh[m].start()

    tokens = n_fsdp * rows
    df_rows = df_all[...].reshape(tokens, width)

    def leave(slot, dst):
        return pltpu.make_async_copy(stage.at[slot], dst, stage_sem.at[slot])

    def leave_down(n):
        return pltpu.make_async_copy(
            stage.at[2, pl.ds(0, HID_TILE), :], gd_ref.at[hid(n), :], stage_sem.at[2]
        )

    @pl.loop(0, n_hid)
    def _(n):
        @pl.when(n > 0)
        def _():
            leave_down(n - 1).wait()

        left = act[:, :, hid(n)].reshape(tokens, HID_TILE)
        stage[2, pl.ds(0, HID_TILE), :] = inner_rows(left, df_rows).astype(BF16)
        leave_down(n).start()

    leave_down(n_hid - 1).wait()

    def leave_in(i, n):
        return pltpu.make_async_copy(
            stage_in(i), ggu_ref.at[i, :, hid(n)], stage_sem.at[i]
        )

    def stage_in(i):
        return stage.at[i, :, pl.ds(0, HID_TILE)]

    for i, grads in enumerate((dgate, dup)):

        @pl.loop(0, n_hid)
        def _(n):
            @pl.when(n > 0)
            def _():
                leave_in(i, n - 1).wait()

            right = grads[:, :, hid(n)].reshape(tokens, HID_TILE)
            stage[i, :, pl.ds(0, HID_TILE)] = dot_nn(h_turn[...], right).astype(BF16)
            leave_in(i, n).start()

        leave_in(i, n_hid - 1).wait()

    for m in range(1, n_fsdp):
        send_dh[m].wait_recv()
    dh = total[...]
    for m in range(1, n_fsdp):
        dh = dh + part_in[1, m].astype(F32)
    mid = mid_ref[...]
    gain = gains_ref[1:2, :]
    scale = lax.rsqrt(jnp.mean(mid * mid, axis=-1, keepdims=True) + epsilon)
    pulled = dh * gain
    inner = jnp.mean(pulled * mid, axis=-1, keepdims=True)
    dmid_ref[...] = (
        cot_ref[...].astype(F32) + scale * pulled - mid * (scale * scale * scale * inner)
    )
    dgain_ref[1:2, :] = jnp.sum(dh * mid * scale, axis=0, keepdims=True)
    for copies in (send_h, send_f, send_df, send_dh):
        for m in range(1, n_fsdp):
            copies[m].wait_send()


def feed_forward(n_seq, n_fsdp, h_two, middle, cot, gains, gu_all, w_down):
    rows, width = h_two.shape
    hidden = gu_all.shape[2]
    in_vmem = pl.BlockSpec(memory_space=pltpu.VMEM)
    anywhere = pl.BlockSpec(memory_space=pl.ANY)
    return pl.pallas_call(
        functools.partial(ffn_kernel, n_seq, n_fsdp),
        out_shape=[
            jax.ShapeDtypeStruct((rows, width), BF16),
            jax.ShapeDtypeStruct((rows, width), F32),
            jax.ShapeDtypeStruct((2, width, hidden), BF16),
            jax.ShapeDtypeStruct((hidden, width), BF16),
            jax.ShapeDtypeStruct((8, width), F32),
        ],
        in_specs=[in_vmem] * 4 + [anywhere] * 2,
        out_specs=[in_vmem, in_vmem, anywhere, anywhere, in_vmem],
        scratch_shapes=[
            pltpu.VMEM((2, width, hidden), BF16),
            pltpu.VMEM((hidden, width), BF16),
            pltpu.VMEM((n_fsdp, rows, width), BF16),
            pltpu.VMEM((n_fsdp, rows, width), BF16),
            pltpu.VMEM((n_fsdp, rows, hidden), F32),
            pltpu.VMEM((n_fsdp, rows, hidden), F32),
            pltpu.VMEM((n_fsdp, rows, hidden), BF16),
            pltpu.VMEM((n_fsdp, rows, hidden), BF16),
            pltpu.VMEM((n_fsdp, rows, hidden), BF16),
            pltpu.VMEM((width, n_fsdp * rows), BF16),
            pltpu.VMEM((2, n_fsdp, rows, width), BF16),
            pltpu.VMEM((2, n_fsdp, rows, width), BF16),
            pltpu.VMEM((rows, width), F32),
            pltpu.VMEM((3, width, width), BF16),
            pltpu.SemaphoreType.DMA((3,)),
            pltpu.SemaphoreType.DMA((4, n_fsdp)),
            pltpu.SemaphoreType.DMA((4, n_fsdp)),
            pltpu.SemaphoreType.DMA((3,)),
        ],
        compiler_params=pltpu.CompilerParams(
            collective_id=3, has_side_effects=True, vmem_limit_bytes=60 << 20
        ),
        name="feed_forward",
    )(h_two, middle, cot, gains, gu_all, w_down)


def grads_kernel(
    n_seq, n_fsdp,
    gu_ref, gd_ref, qkv_ref, wo_ref, gains_ref,
    fin_gu, fin_d, fin_qkv, fin_wo, gains_out,
    own_d, own_g, own_q, own_o, c_d, c_g, c_q, c_o,
    hi_d, hi_g, hi_q, hi_o, lo_d, lo_g, lo_q, lo_o, z_q, z_o, gain_in, gain_line,
    load_sem, c_send, c_recv, hi_send, hi_recv, lo_send, lo_recv, z_send, z_recv,
    put_sem, ag_send, ag_recv, gain_send, gain_recv,
):
    at = Place(n_seq, n_fsdp)
    z, c = at.z, at.c
    hidden = gd_ref.shape[0]
    width = gd_ref.shape[1]
    depth = width // n_fsdp
    heads_width = qkv_ref.shape[1]
    rows_o = wo_ref.shape[0] // n_fsdp
    greet([at.plane(k) for k in range(1, n_seq)] + [at.line(m) for m in range(1, n_fsdp)])

    chunks = [("d", i, i == 0) for i in range(2)]
    chunks += [("g", m, m % 2 == 0) for m in range(n_fsdp)]
    chunks += [("q", m, True) for m in range(n_fsdp)]
    chunks += [("o", m, False) for m in range(n_fsdp)]
    own = {"d": own_d, "g": own_g, "q": own_q, "o": own_o}
    from_core = {"d": c_d, "g": c_g, "q": c_q, "o": c_o}
    from_hi = {"d": hi_d, "g": hi_g, "q": hi_q, "o": hi_o}
    from_lo = {"d": lo_d, "g": lo_g, "q": lo_q, "o": lo_o}

    def core_part(kind, i, core):
        if kind == "d":
            size = hidden // 4
            return gd_ref.at[many(core * (hidden // 2) + i * size, size)]
        to = flip(z, i, 2)
        if kind == "g":
            return gu_ref.at[core, many(to * depth, depth)]
        if kind == "q":
            return qkv_ref.at[many(to * depth + core * (depth // 2), depth // 2)]
        return wo_ref.at[many(to * rows_o + core * (rows_o // 2), rows_o // 2)]

    def hi_part(kind, hi):
        if kind == "d":
            return many(hi * (hidden // 8), hidden // 8), slice(None)
        if kind == "g":
            return many(hi * (depth // 2), depth // 2), slice(None)
        if kind == "q":
            return slice(None), lanes(hi * (heads_width // 2), heads_width // 2)
        return many(hi * (rows_o // 4), rows_o // 4), slice(None)

    def lo_part(kind, hi, lo):
        if kind == "d":
            return many(hi * (hidden // 8) + lo * (hidden // 16), hidden // 16), slice(None)
        if kind == "g":
            return (
                many(hi * (depth // 2), depth // 2),
                lanes(lo * (hidden // 2), hidden // 2),
            )
        if kind == "q":
            start = hi * (heads_width // 2) + lo * (heads_width // 4)
            return slice(None), lanes(start, heads_width // 4)
        return many(hi * (rows_o // 4) + lo * (rows_o // 8), rows_o // 8), slice(None)

    def fin_part(kind, i, where, core):
        rows_at, cols_at = where
        if kind == "g":
            return fin_gu.at[core, i, rows_at, cols_at]
        ref, base, size = {
            "d": (fin_d, core * (hidden // 2) + i * (hidden // 4), hidden // 4),
            "q": (fin_qkv, core * (depth // 2), depth // 2),
            "o": (fin_wo, core * (rows_o // 2), rows_o // 2),
        }[kind]
        if isinstance(rows_at, slice):
            rows_at = many(base, size)
        else:
            rows_at = many(base + rows_at.start, rows_at.size)
        return ref.at[rows_at, cols_at]

    def add(ref, where, other):
        rows_at, cols_at = where
        start = 0 if isinstance(rows_at, slice) else rows_at.start
        n_rows = other.shape[0]
        slab = 16

        @pl.loop(0, n_rows // slab)
        def _(n):
            here = pl.ds(pl.multiple_of(start + n * slab, slab), slab)
            there = pl.ds(pl.multiple_of(n * slab, slab), slab)
            ref[here, cols_at] = (
                ref[here, cols_at].astype(F32) + other[there, :].astype(F32)
            ).astype(BF16)

    whole = (slice(None), slice(None))
    loads, cores, his, los, lines = [], [], [], [], []
    for j, (kind, i, first_x) in enumerate(chunks):
        hi, lo, mask_hi, mask_lo = at.halves(first_x)
        mine = own[kind].at[i]
        loads.append(pltpu.make_async_copy(core_part(kind, i, c), mine, load_sem.at[j]))
        cores.append(remote(core_part(kind, i, 1 - c), from_core[kind].at[i],
                            c_send.at[j], c_recv.at[j], at.plane(1)))
        his.append(remote(mine.at[hi_part(kind, 1 - hi)], from_hi[kind].at[i],
                          hi_send.at[j], hi_recv.at[j], at.plane(mask_hi)))
        los.append(remote(mine.at[lo_part(kind, hi, 1 - lo)], from_lo[kind].at[i],
                          lo_send.at[j], lo_recv.at[j], at.plane(mask_lo)))
        piece = mine.at[lo_part(kind, hi, lo)]
        line = None
        if kind == "g" and i:
            line = remote(piece, fin_part(kind, z, lo_part(kind, hi, lo), c),
                          z_send.at[j], z_recv.at[j], at.line(i))
        elif kind in "qo" and i:
            line = remote(piece, {"q": z_q, "o": z_o}[kind].at[i],
                          z_send.at[j], z_recv.at[j], at.line(i))
        lines.append(line)

    rounds = [("d", 0, 0), ("d", 1, 1)] + [("g", m, 2 + m) for m in range(n_fsdp)]
    rounds += [("q", 0, 2 + n_fsdp), ("o", 0, 2 + 2 * n_fsdp)]
    puts, hands = [], []
    for r, (kind, i, j) in enumerate(rounds):
        hi, lo, mask_hi, mask_lo = at.halves(chunks[j][2])
        which = flip(z, i, 2) if kind == "g" else i
        piece = fin_part(kind, which, lo_part(kind, hi, lo), c)
        half = fin_part(kind, which, hi_part(kind, hi), c)
        full = fin_part(kind, which, whole, c)
        put = None
        if not (kind == "g" and i):
            put = pltpu.make_async_copy(
                own[kind].at[i].at[lo_part(kind, hi, lo)], piece, put_sem.at[r]
            )
        puts.append(put)
        hands.append([
            remote(part, part, ag_send.at[r, k], ag_recv.at[r, k], at.plane(mask))
            for k, (part, mask) in enumerate(((piece, mask_lo), (half, mask_hi), (full, 1)))
        ])

    gain_copies = [
        remote(gains_ref, gain_in.at[k], gain_send.at[k], gain_recv.at[k], at.plane(k))
        for k in range(1, n_seq)
    ]
    gain_lines = [
        remote(gain_line.at[0], gain_line.at[m], gain_send.at[n_seq + m], gain_recv.at[n_seq + m],
               at.line(m))
        for m in range(1, n_fsdp)
    ]

    n = len(chunks)
    for j in range(n):
        loads[j].start()
        cores[j].start()
    for copy in gain_copies:
        copy.start()

    def take_core(j):
        kind, i, _ = chunks[j]
        loads[j].wait()
        cores[j].wait_recv()
        add(own[kind].at[i], whole, from_core[kind].at[i])
        his[j].start()

    def take_hi(j):
        kind, i, first_x = chunks[j]
        hi, lo, _, _ = at.halves(first_x)
        his[j].wait_recv()
        add(own[kind].at[i], hi_part(kind, hi), from_hi[kind].at[i])
        los[j].start()

    def take_lo(j):
        kind, i, first_x = chunks[j]
        hi, lo, _, _ = at.halves(first_x)
        los[j].wait_recv()
        add(own[kind].at[i], lo_part(kind, hi, lo), from_lo[kind].at[i])
        if lines[j] is not None:
            lines[j].start()

    def begin_hand(r):
        kind, i, j = rounds[r]
        hi, lo, _, _ = at.halves(chunks[j][2])
        if kind == "g" and i:
            lines[j].wait_recv()
        if kind in "qo":
            for m in range(1, n_fsdp):
                lines[j + m].wait_recv()
                add(own[kind].at[0], lo_part(kind, hi, lo), {"q": z_q, "o": z_o}[kind].at[m])
        if puts[r] is not None:
            puts[r].start()
            puts[r].wait()
        hands[r][0].start()

    def pass_on(r, k):
        hands[r][k - 1].wait_recv()
        hands[r][k].start()

    first = [6, 7, 8, 10, 11, 12] + [15, 19]
    for t in range(26):
        for r, when in enumerate(first):
            if t == when + 4:
                pass_on(r, 2)
            if t == when + 2:
                pass_on(r, 1)
            if t == when:
                begin_hand(r)
        if 0 <= t - 4 < n:
            take_lo(t - 4)
        if 0 <= t - 2 < n:
            take_hi(t - 2)
        if t < n:
            take_core(t)
        if t == 6:
            total = gains_ref[...]
            for k, copy in enumerate(gain_copies):
                copy.wait_recv()
                total = total + gain_in[k + 1]
            gain_line[0] = total
            for copy in gain_lines:
                copy.start()
    total = gain_line[0]
    for m, copy in enumerate(gain_lines):
        copy.wait_recv()
        total = total + gain_line[m + 1]
    gains_out[...] = total
    for r in range(len(rounds)):
        hands[r][2].wait_recv()
        for k in range(3):
            hands[r][k].wait_send()
    for j in range(n):
        cores[j].wait_send()
        his[j].wait_send()
        los[j].wait_send()
        if lines[j] is not None:
            lines[j].wait_send()
    for copy in gain_copies + gain_lines:
        copy.wait_send()


def sum_grads(n_seq, n_fsdp, ggu, gd, gqkv, gwo, gains):
    _, width, hidden = ggu.shape
    depth = width // n_fsdp
    heads_width = gqkv.shape[1]
    rows_o = gwo.shape[0] // n_fsdp
    in_vmem = pl.BlockSpec(memory_space=pltpu.VMEM)
    anywhere = pl.BlockSpec(memory_space=pl.ANY)
    n_chunks = 2 + 3 * n_fsdp
    n_rounds = 4 + n_fsdp

    def blocks(d, g, q, o):
        return [
            pltpu.VMEM((2,) + d, BF16),
            pltpu.VMEM((n_fsdp,) + g, BF16),
            pltpu.VMEM((n_fsdp,) + q, BF16),
            pltpu.VMEM((n_fsdp,) + o, BF16),
        ]

    core_size = blocks(
        (hidden // 4, width), (depth, hidden), (depth // 2, heads_width), (rows_o // 2, width)
    )
    hi_size = blocks(
        (hidden // 8, width),
        (depth // 2, hidden),
        (depth // 2, heads_width // 2),
        (rows_o // 4, width),
    )
    lo_size = blocks(
        (hidden // 16, width),
        (depth // 2, hidden // 2),
        (depth // 2, heads_width // 4),
        (rows_o // 8, width),
    )
    chunk_sems = pltpu.SemaphoreType.DMA((n_chunks,))
    return pl.pallas_call(
        functools.partial(grads_kernel, n_seq, n_fsdp),
        out_shape=[
            jax.ShapeDtypeStruct((2, n_fsdp, depth, hidden), BF16),
            jax.ShapeDtypeStruct((hidden, width), BF16),
            jax.ShapeDtypeStruct((depth, heads_width), BF16),
            jax.ShapeDtypeStruct((rows_o, width), BF16),
            jax.ShapeDtypeStruct(gains.shape, F32),
        ],
        in_specs=[anywhere] * 4 + [in_vmem],
        out_specs=[anywhere] * 4 + [in_vmem],
        scratch_shapes=core_size
        + core_size
        + hi_size
        + lo_size
        + lo_size[2:]
        + [
            pltpu.VMEM((n_seq,) + gains.shape, F32),
            pltpu.VMEM((n_fsdp,) + gains.shape, F32),
        ]
        + [chunk_sems] * 9
        + [
            pltpu.SemaphoreType.DMA((n_rounds,)),
            pltpu.SemaphoreType.DMA((n_rounds, 3)),
            pltpu.SemaphoreType.DMA((n_rounds, 3)),
            pltpu.SemaphoreType.DMA((n_seq + n_fsdp,)),
            pltpu.SemaphoreType.DMA((n_seq + n_fsdp,)),
        ],
        compiler_params=pltpu.CompilerParams(
            collective_id=4, has_side_effects=True, vmem_limit_bytes=60 << 20
        ),
        name="sum_weight_grads",
    )(ggu, gd, gqkv, gwo, gains)


def shards(n_seq, n_fsdp, *args):
    w_query, w_key, w_output, w_gate = args[4], args[5], args[9], args[12]
    depth, hidden = w_gate.shape
    rows_here = args[0].shape[1]
    heads_width = w_query.shape[1] + 2 * w_key.shape[1]
    fits = (
        n_seq == 8
        and n_fsdp == 4
        and args[0].shape[0] == 1
        and depth % 32 == 0
        and rows_here % 16 == 0
        and w_output.shape[0] % 128 == 0
        and heads_width % 512 == 0
        and w_output.shape[1] % 384 == 0
        and hidden % n_fsdp == 0
        and (hidden // n_fsdp) % 16 == 0
    )
    return (shards_fused if fits else shards_plain)(*((n_seq, n_fsdp) if fits else ()), *args)


def shards_fused(
    n_seq,
    n_fsdp,
    inputs,
    segments,
    cotangent,
    gain_attn_in,
    w_query,
    w_key,
    w_value,
    gain_query,
    gain_key,
    w_output,
    gain_attn_out,
    gain_ffn_in,
    w_gate,
    w_up,
    w_down,
    gain_ffn_out,
):
    rows_here, width = inputs.shape[1:]
    head_width = w_key.shape[1]
    query_width = w_query.shape[1]
    head_count = query_width // head_width
    depth, ffn_width = w_gate.shape
    share = ffn_width // n_fsdp
    padded = -(-share // HID_TILE) * HID_TILE
    reach = (WINDOW - 2 + rows_here) // rows_here
    score_scale = head_width ** (-0.5)
    place = lax.axis_index("seq")
    line = lax.axis_index("fsdp")
    first_row = place * rows_here
    tokens = inputs[0].astype(F32)
    seg_here = segments[0]

    def blocked(weight):
        by_share = weight.reshape(depth, n_fsdp, share).transpose(1, 0, 2)
        return jnp.pad(by_share, ((0, 0), (0, 0), (0, padded - share)))

    gu_blocks = jnp.stack([blocked(w_gate), blocked(w_up)])
    qkv_shard = jnp.concatenate([w_query, w_key, w_value], axis=1)
    pack_width = -(-depth // 128) * 128
    gains = (gain_attn_in, gain_attn_out, gain_ffn_in, gain_ffn_out, gain_query, gain_key)
    pack = jnp.stack([jnp.pad(g, (0, pack_width - g.shape[0])) for g in gains])
    pack = jnp.pad(pack, ((0, 16 - len(gains)), (0, 0)))
    segs = jnp.broadcast_to(segments, (8, rows_here))
    gu_all, qkv_all, wo_all, pack_all, seg_all = spread(
        n_seq, n_fsdp, gu_blocks, qkv_shard, w_output, pack, segs
    )
    g_attn_in, g_attn_out, g_ffn_in, g_ffn_out, g_query, g_key = (
        pack_all[:, i, : g.shape[0]].reshape(-1).astype(F32) for i, g in enumerate(gains)
    )

    positions = first_row + jnp.arange(rows_here, dtype=jnp.int32)
    angles_at = angles(positions - seg_here, head_width)
    normed_one, pull_one = jax.vjp(norm_rows, tokens, g_attn_in)
    h_one = normed_one.astype(BF16)
    qkv_raw = dot_nn(h_one, qkv_all)
    q_raw = qkv_raw[:, :query_width]
    k_raw = qkv_raw[:, query_width : query_width + head_width]
    v_low = qkv_raw[:, query_width + head_width :].astype(BF16)

    def prepare(q_in, k_in, gq_in, gk_in):
        q_rows = q_in.reshape(q_in.shape[0], head_count, head_width)
        q_fin = rotate(norm_rows(q_rows, gq_in), angles_at[:, None, :])
        k_fin = rotate(norm_rows(k_in, gk_in), angles_at)
        return (q_fin, k_fin)

    (q_fin, k_fin), pull_prep = jax.vjp(prepare, q_raw, k_raw, g_query, g_key)
    q_low = q_fin.astype(BF16).reshape(rows_here * head_count, head_width)
    kv_low = jnp.concatenate([k_fin.astype(BF16), v_low], axis=1)
    kv_rows = from_blocks_behind(n_seq, reach, kv_low).reshape(-1, 2 * head_width)
    key_rows, value_rows = kv_rows[:, :head_width], kv_rows[:, head_width:]
    seg_twice = jnp.concatenate([seg_all[:, 0], seg_all[:, 0]], axis=0)
    key_segs = lax.dynamic_slice(
        seg_twice, (place + n_seq - reach, jnp.int32(0)), (reach + 1, rows_here)
    ).reshape(-1)
    key_place = (
        first_row - reach * rows_here + jnp.arange((reach + 1) * rows_here, dtype=jnp.int32)
    )
    distance = positions[:, None] - key_place[None, :]
    allowed = (
        (distance >= 0)
        & (distance < WINDOW)
        & (key_place[None, :] >= 0)
        & (seg_here[:, None] == key_segs[None, :])
    )
    scores = (outer_cols(q_low, key_rows) * score_scale).reshape(rows_here, head_count, -1)
    masked = jnp.where(allowed[:, None, :], scores, masked_value)
    attn_probs = jax.nn.softmax(masked, axis=-1).reshape(rows_here * head_count, -1)
    probs_low = attn_probs.astype(BF16)
    attended = dot_nn(probs_low, value_rows)
    att_low = attended.reshape(rows_here, query_width).astype(BF16)
    o_raw = dot_nn(att_low, wo_all)
    branch_att, pull_att = jax.vjp(norm_rows, o_raw, g_attn_out)
    middle = tokens + branch_att
    h_two = norm_rows(middle, g_ffn_in).astype(BF16)

    ffn_gains = jnp.pad(jnp.stack([g_ffn_out, g_ffn_in]), ((0, 6), (0, 0)))
    outputs, d_middle, ggu, gd, d_ffn_gains = feed_forward(
        n_seq, n_fsdp, h_two, middle, cotangent[0], ffn_gains, gu_all, w_down
    )

    d_oraw, d_gattn_out = pull_att(d_middle)
    d_olow = d_oraw.astype(BF16)
    grad_wo = inner_rows(att_low, d_olow)
    d_att_low = outer_cols(d_olow, wo_all).astype(BF16)
    d_att_low = d_att_low.reshape(rows_here * head_count, head_width)
    d_probs = outer_cols(d_att_low, value_rows)
    d_scores = attn_probs * (d_probs - jnp.sum(attn_probs * d_probs, axis=-1, keepdims=True))
    ds_low = d_scores.astype(BF16)
    d_qfin = dot_nn(ds_low, key_rows) * score_scale
    d_kv = jnp.concatenate(
        [inner_rows(ds_low, q_low) * score_scale, inner_rows(probs_low, d_att_low)], axis=1
    ).reshape(reach + 1, rows_here, 2 * head_width)
    d_kv_sum = return_to_blocks(n_seq, reach, d_kv[:reach].astype(BF16), d_kv[reach])
    d_kfin, d_vsum = d_kv_sum[:, :head_width], d_kv_sum[:, head_width:]
    d_qraw, d_kraw, d_gquery, d_gkey = pull_prep(
        (d_qfin.reshape(rows_here, head_count, head_width), d_kfin)
    )
    d_qkv = jnp.concatenate([d_qraw, d_kraw, d_vsum], axis=1).astype(BF16)
    d_hone = outer_cols(d_qkv, qkv_all)
    grad_qkv = inner_rows(h_one, d_qkv)
    d_tok_norm, d_gattn_in = pull_one(d_hone)
    d_inputs = d_middle + d_tok_norm

    def wide(vector):
        return jnp.pad(vector, (0, width - vector.shape[0]))

    gain_rows = jnp.stack(
        [d_gattn_in, d_gattn_out, d_ffn_gains[1], d_ffn_gains[0], wide(d_gquery), wide(d_gkey)]
    )
    gain_rows = jnp.pad(gain_rows, ((0, 2), (0, 0)))
    fin_gu, fin_d, fin_qkv, fin_wo, gain_sums = sum_grads(
        n_seq, n_fsdp, ggu, gd, grad_qkv.astype(BF16), grad_wo.astype(BF16), gain_rows
    )

    def unblocked(blocks):
        return blocks[:, :, :share].transpose(1, 0, 2).reshape(depth, ffn_width).astype(F32)

    def mine(row, gain):
        size = gain.shape[0]
        return lax.dynamic_slice(gain_sums[row], (line * size,), (size,))

    fin_qkv = fin_qkv.astype(F32)
    return (
        outputs[None],
        d_inputs[None],
        mine(0, gain_attn_in),
        fin_qkv[:, :query_width],
        fin_qkv[:, query_width : query_width + head_width],
        fin_qkv[:, query_width + head_width :],
        mine(4, gain_query),
        mine(5, gain_key),
        fin_wo.astype(F32),
        mine(1, gain_attn_out),
        mine(2, gain_ffn_in),
        unblocked(fin_gu[0]),
        unblocked(fin_gu[1]),
        fin_d[:share].astype(F32),
        mine(3, gain_ffn_out),
    )


def solution(mesh):
    placed = (
        P("fsdp", "seq", None),
        P("fsdp", "seq"),
        P("fsdp", "seq", None),
        P("fsdp"),
        P("fsdp", None),
        P("fsdp", None),
        P("fsdp", None),
        P("fsdp"),
        P("fsdp"),
        P("fsdp", None),
        P("fsdp"),
        P("fsdp"),
        P("fsdp", None),
        P("fsdp", None),
        P("fsdp", None),
        P("fsdp"),
    )
    return jax.shard_map(
        functools.partial(shards, mesh.shape["seq"], mesh.shape["fsdp"]),
        mesh=mesh,
        in_specs=placed,
        out_specs=(
            P("fsdp", "seq", None),
            P("fsdp", "seq", None),
            P("fsdp"),
            P("fsdp", None),
            P("fsdp", None),
            P("fsdp", None),
            P("fsdp"),
            P("fsdp"),
            P("fsdp", None),
            P("fsdp"),
            P("fsdp"),
            P("fsdp", None),
            P("fsdp", None),
            P("fsdp", None),
            P("fsdp"),
        ),
        check_vma=False,
    )
```

```python
import functools

import jax
import jax.numpy as jnp
from jax import lax
from jax.experimental import pallas as pl
from jax.experimental.pallas import tpu as pltpu
from jax.sharding import PartitionSpec as P

WINDOW = 512


epsilon = 1e-06
masked_value = -1e30


def from_behind(block, axis, distance):
    devices = range(lax.axis_size(axis))
    route = [(i - distance, i) for i in devices if i - distance in devices]
    return lax.ppermute(block, axis, route)


def norm_rows(rows_in, gain_vec):
    return (
        rows_in
        * lax.rsqrt(jnp.mean(rows_in * rows_in, axis=-1, keepdims=True) + epsilon)
        * gain_vec
    )


def angles(positions, head_width):
    inv_rates = 10000.0 ** (-(jnp.arange(head_width // 2, dtype=jnp.float32) * 2.0) / head_width)
    return positions.astype(jnp.float32)[:, None] * inv_rates[None, :]


def rotate(rows_in, angles_at):
    half_width = rows_in.shape[-1] // 2
    lower_half = rows_in[..., :half_width]
    upper_half = rows_in[..., half_width:]
    cosine = jnp.cos(angles_at)
    sine_part = jnp.sin(angles_at)
    return jnp.concatenate(
        [
            lower_half * cosine - upper_half * sine_part,
            upper_half * cosine + lower_half * sine_part,
        ],
        axis=-1,
    )


def geglu_act(gate_proj, up_proj):
    return jax.nn.gelu(gate_proj, approximate=True) * up_proj


def inner_rows(left, right):
    return lax.dot_general(
        left, right, (((0,), (0,)), ((), ())), preferred_element_type=jnp.float32
    )


def outer_cols(left, right):
    return lax.dot_general(
        left, right, (((1,), (1,)), ((), ())), preferred_element_type=jnp.float32
    )


def shards_plain(
    inputs,
    segments,
    cotangent,
    gain_attn_in,
    w_query,
    w_key,
    w_value,
    gain_query,
    gain_key,
    w_output,
    gain_attn_out,
    gain_ffn_in,
    w_gate,
    w_up,
    w_down,
    gain_ffn_out,
):
    rows_here = inputs.shape[1]
    head_width = w_key.shape[1]
    head_count = w_query.shape[1] // head_width
    reach_devs = (WINDOW - 2 + rows_here) // rows_here
    score_scale = head_width ** (-0.5)
    first_row = lax.axis_index("seq") * rows_here
    tokens = inputs[0].astype(jnp.float32)
    seg_here = segments[0]
    positions = first_row + jnp.arange(rows_here, dtype=jnp.int32)
    angles_at = angles(positions - seg_here, head_width)
    wq_all, wk_all, wv_all, wo_all, g_attn_in, g_query, g_key, g_attn_out, g_ffn_in, g_ffn_out = (
        lax.all_gather(w_query, "fsdp", axis=0, tiled=True),
        lax.all_gather(w_key, "fsdp", axis=0, tiled=True),
        lax.all_gather(w_value, "fsdp", axis=0, tiled=True),
        lax.all_gather(w_output, "fsdp", axis=0, tiled=True),
        lax.all_gather(gain_attn_in, "fsdp", axis=0, tiled=True),
        lax.all_gather(gain_query, "fsdp", axis=0, tiled=True),
        lax.all_gather(gain_key, "fsdp", axis=0, tiled=True),
        lax.all_gather(gain_attn_out, "fsdp", axis=0, tiled=True),
        lax.all_gather(gain_ffn_in, "fsdp", axis=0, tiled=True),
        lax.all_gather(gain_ffn_out, "fsdp", axis=0, tiled=True),
    )
    g_attn_in = g_attn_in.astype(jnp.float32)
    g_query = g_query.astype(jnp.float32)
    g_key = g_key.astype(jnp.float32)
    g_attn_out = g_attn_out.astype(jnp.float32)
    g_ffn_in = g_ffn_in.astype(jnp.float32)
    g_ffn_out = g_ffn_out.astype(jnp.float32)
    normed_one, pull_one = jax.vjp(norm_rows, tokens, g_attn_in)
    h_one = normed_one.astype(jnp.bfloat16)
    q_raw = jnp.dot(h_one, wq_all, preferred_element_type=jnp.float32)
    k_raw = jnp.dot(h_one, wk_all, preferred_element_type=jnp.float32)
    v_raw = jnp.dot(h_one, wv_all, preferred_element_type=jnp.float32)

    def prepare(q_in, k_in, gq_in, gk_in):
        q_rows = q_in.reshape(q_in.shape[0], head_count, head_width)
        q_fin = rotate(norm_rows(q_rows, gq_in), angles_at[:, None, :])
        k_fin = rotate(norm_rows(k_in, gk_in), angles_at)
        return (q_fin, k_fin)

    (q_fin, k_fin), pull_prep = jax.vjp(prepare, q_raw, k_raw, g_query, g_key)
    q_low = q_fin.astype(jnp.bfloat16).reshape(rows_here * head_count, head_width)
    k_low = k_fin.astype(jnp.bfloat16)
    v_low = v_raw.astype(jnp.bfloat16)
    key_parts = []
    value_parts = []
    seg_parts = []
    for offset in range(reach_devs, 0, -1):
        k_came, v_came, s_came = from_behind((k_low, v_low, seg_here), "seq", offset)
        key_parts.append(k_came)
        value_parts.append(v_came)
        seg_parts.append(s_came)
    key_rows = jnp.concatenate(key_parts + [k_low], axis=0)
    value_rows = jnp.concatenate(value_parts + [v_low], axis=0)
    key_segs = jnp.concatenate(seg_parts + [seg_here], axis=0)
    key_place = (
        first_row
        - reach_devs * rows_here
        + jnp.arange((reach_devs + 1) * rows_here, dtype=jnp.int32)
    )
    distance = positions[:, None] - key_place[None, :]
    allowed = (
        (distance >= 0)
        & (distance < WINDOW)
        & (key_place[None, :] >= 0)
        & (seg_here[:, None] == key_segs[None, :])
    )
    scores = (outer_cols(q_low, key_rows) * score_scale).reshape(rows_here, head_count, -1)
    masked = jnp.where(allowed[:, None, :], scores, masked_value)
    attn_probs = jax.nn.softmax(masked, axis=-1).reshape(rows_here * head_count, -1)
    probs_low = attn_probs.astype(jnp.bfloat16)
    attended = jnp.dot(probs_low, value_rows, preferred_element_type=jnp.float32)
    att_low = attended.reshape(rows_here, head_count * head_width).astype(jnp.bfloat16)
    o_raw = jnp.dot(att_low, wo_all, preferred_element_type=jnp.float32)
    branch_att, pull_att = jax.vjp(norm_rows, o_raw, g_attn_out)
    middle = tokens + branch_att
    normed_two, pull_mid = jax.vjp(norm_rows, middle, g_ffn_in)
    h_two = normed_two.astype(jnp.bfloat16)
    gate_all, up_all, down_all = (
        lax.all_gather(w_gate, "fsdp", axis=0, tiled=True),
        lax.all_gather(w_up, "fsdp", axis=0, tiled=True),
        lax.all_gather(w_down, "fsdp", axis=0, tiled=True),
    )
    gate_proj = jnp.dot(h_two, gate_all, preferred_element_type=jnp.float32)
    up_proj = jnp.dot(h_two, up_all, preferred_element_type=jnp.float32)
    act_full, pull_act = jax.vjp(geglu_act, gate_proj, up_proj)
    act_low = act_full.astype(jnp.bfloat16)
    f_raw = jnp.dot(act_low, down_all, preferred_element_type=jnp.float32)
    branch_ffn, pull_out = jax.vjp(norm_rows, f_raw, g_ffn_out)
    outputs = (middle + branch_ffn).astype(jnp.bfloat16)
    upstream = cotangent[0].astype(jnp.float32)
    d_fraw, d_gffn_out = pull_out(upstream)
    d_flow = d_fraw.astype(jnp.bfloat16)
    gate_shard, up_shard, down_shard, d_flow = lax.optimization_barrier(
        (w_gate, w_up, w_down, d_flow)
    )
    gate_back, up_back, down_back = (
        lax.all_gather(gate_shard, "fsdp", axis=0, tiled=True),
        lax.all_gather(up_shard, "fsdp", axis=0, tiled=True),
        lax.all_gather(down_shard, "fsdp", axis=0, tiled=True),
    )
    d_act = outer_cols(d_flow, down_back)
    d_gate, d_up = pull_act(d_act)
    dg_low = d_gate.astype(jnp.bfloat16)
    du_low = d_up.astype(jnp.bfloat16)
    d_htwo = outer_cols(dg_low, gate_back) + outer_cols(du_low, up_back)
    grad_down_part = lax.psum_scatter(
        inner_rows(act_low, d_flow).astype(jnp.bfloat16), "fsdp", scatter_dimension=0, tiled=True
    )
    grad_in_part = lax.psum_scatter(
        jnp.concatenate([inner_rows(h_two, dg_low), inner_rows(h_two, du_low)], axis=1).astype(
            jnp.bfloat16
        ),
        "fsdp",
        scatter_dimension=0,
        tiled=True,
    ).astype(jnp.float32)
    hidden_width = w_gate.shape[1]
    grad_gate_part = grad_in_part[:, :hidden_width]
    grad_up_part = grad_in_part[:, hidden_width:]
    d_mid_norm, d_gffn_in = pull_mid(d_htwo)
    d_middle = upstream + d_mid_norm
    d_oraw, d_gattn_out = pull_att(d_middle)
    d_olow = d_oraw.astype(jnp.bfloat16)
    grad_wo = inner_rows(att_low, d_olow)
    d_att_low = (
        outer_cols(d_olow, wo_all).astype(jnp.bfloat16).reshape(rows_here * head_count, head_width)
    )
    d_probs = outer_cols(d_att_low, value_rows)
    d_scores = attn_probs * (d_probs - jnp.sum(attn_probs * d_probs, axis=-1, keepdims=True))
    ds_low = d_scores.astype(jnp.bfloat16)
    d_qfin = jnp.dot(ds_low, key_rows, preferred_element_type=jnp.float32) * score_scale
    d_keys = inner_rows(ds_low, q_low) * score_scale
    d_values = inner_rows(probs_low, d_att_low)
    d_kfin = d_keys[reach_devs * rows_here :]
    d_vsum = d_values[reach_devs * rows_here :]
    for offset in range(1, reach_devs + 1):
        slot_index = reach_devs - offset
        k_back, v_back = (
            from_behind(
                d_keys[slot_index * rows_here : (slot_index + 1) * rows_here].astype(jnp.bfloat16),
                "seq",
                -offset,
            ).astype(jnp.float32),
            from_behind(
                d_values[slot_index * rows_here : (slot_index + 1) * rows_here].astype(
                    jnp.bfloat16
                ),
                "seq",
                -offset,
            ).astype(jnp.float32),
        )
        d_kfin = d_kfin + k_back
        d_vsum = d_vsum + v_back
    d_qraw, d_kraw, d_gquery, d_gkey = pull_prep(
        (d_qfin.reshape(rows_here, head_count, head_width), d_kfin)
    )
    dq_low = d_qraw.astype(jnp.bfloat16)
    dk_low = d_kraw.astype(jnp.bfloat16)
    dv_low = d_vsum.astype(jnp.bfloat16)
    d_hone = outer_cols(dq_low, wq_all) + outer_cols(dk_low, wk_all) + outer_cols(dv_low, wv_all)
    grad_wq = inner_rows(h_one, dq_low)
    grad_wk = inner_rows(h_one, dk_low)
    grad_wv = inner_rows(h_one, dv_low)
    d_tok_norm, d_gattn_in = pull_one(d_hone)
    d_inputs = d_middle + d_tok_norm
    part_wq, part_wk, part_wv, part_wo, part_gai, part_gq, part_gk, part_gao, part_gfi, part_gfo = (
        lax.psum_scatter(
            grad_wq.astype(jnp.bfloat16), "fsdp", scatter_dimension=0, tiled=True
        ).astype(jnp.float32),
        lax.psum_scatter(
            grad_wk.astype(jnp.bfloat16), "fsdp", scatter_dimension=0, tiled=True
        ).astype(jnp.float32),
        lax.psum_scatter(
            grad_wv.astype(jnp.bfloat16), "fsdp", scatter_dimension=0, tiled=True
        ).astype(jnp.float32),
        lax.psum_scatter(
            grad_wo.astype(jnp.bfloat16), "fsdp", scatter_dimension=0, tiled=True
        ).astype(jnp.float32),
        lax.psum_scatter(
            d_gattn_in.astype(jnp.bfloat16), "fsdp", scatter_dimension=0, tiled=True
        ).astype(jnp.float32),
        lax.psum_scatter(
            d_gquery.astype(jnp.bfloat16), "fsdp", scatter_dimension=0, tiled=True
        ).astype(jnp.float32),
        lax.psum_scatter(
            d_gkey.astype(jnp.bfloat16), "fsdp", scatter_dimension=0, tiled=True
        ).astype(jnp.float32),
        lax.psum_scatter(
            d_gattn_out.astype(jnp.bfloat16), "fsdp", scatter_dimension=0, tiled=True
        ).astype(jnp.float32),
        lax.psum_scatter(
            d_gffn_in.astype(jnp.bfloat16), "fsdp", scatter_dimension=0, tiled=True
        ).astype(jnp.float32),
        lax.psum_scatter(
            d_gffn_out.astype(jnp.bfloat16), "fsdp", scatter_dimension=0, tiled=True
        ).astype(jnp.float32),
    )
    cols_wq, cols_wk, cols_wv, cols_wo, cols_gate, cols_up, cols_down = (
        lax.psum_scatter(
            part_wq.astype(jnp.bfloat16), "seq", scatter_dimension=1, tiled=True
        ).astype(jnp.float32),
        lax.psum_scatter(
            part_wk.astype(jnp.bfloat16), "seq", scatter_dimension=1, tiled=True
        ).astype(jnp.float32),
        lax.psum_scatter(
            part_wv.astype(jnp.bfloat16), "seq", scatter_dimension=1, tiled=True
        ).astype(jnp.float32),
        lax.psum_scatter(
            part_wo.astype(jnp.bfloat16), "seq", scatter_dimension=1, tiled=True
        ).astype(jnp.float32),
        lax.psum_scatter(
            grad_gate_part.astype(jnp.bfloat16), "seq", scatter_dimension=1, tiled=True
        ).astype(jnp.float32),
        lax.psum_scatter(
            grad_up_part.astype(jnp.bfloat16), "seq", scatter_dimension=1, tiled=True
        ).astype(jnp.float32),
        lax.psum_scatter(grad_down_part, "seq", scatter_dimension=1, tiled=True).astype(
            jnp.float32
        ),
    )
    sum_wq, sum_wk, sum_wv, sum_wo, sum_gate, sum_up, sum_down = (
        lax.all_gather(cols_wq.astype(jnp.bfloat16), "seq", axis=1, tiled=True).astype(
            cols_wq.dtype
        ),
        lax.all_gather(cols_wk.astype(jnp.bfloat16), "seq", axis=1, tiled=True).astype(
            cols_wk.dtype
        ),
        lax.all_gather(cols_wv.astype(jnp.bfloat16), "seq", axis=1, tiled=True).astype(
            cols_wv.dtype
        ),
        lax.all_gather(cols_wo.astype(jnp.bfloat16), "seq", axis=1, tiled=True).astype(
            cols_wo.dtype
        ),
        lax.all_gather(cols_gate.astype(jnp.bfloat16), "seq", axis=1, tiled=True).astype(
            cols_gate.dtype
        ),
        lax.all_gather(cols_up.astype(jnp.bfloat16), "seq", axis=1, tiled=True).astype(
            cols_up.dtype
        ),
        lax.all_gather(cols_down.astype(jnp.bfloat16), "seq", axis=1, tiled=True).astype(
            cols_down.dtype
        ),
    )
    sum_gai, sum_gq, sum_gk, sum_gao, sum_gfi, sum_gfo = lax.psum(
        (part_gai, part_gq, part_gk, part_gao, part_gfi, part_gfo), "seq"
    )
    return (
        outputs[None],
        d_inputs[None],
        sum_gai,
        sum_wq,
        sum_wk,
        sum_wv,
        sum_gq,
        sum_gk,
        sum_wo,
        sum_gao,
        sum_gfi,
        sum_gate,
        sum_up,
        sum_down,
        sum_gfo,
    )


MESH = pl.DeviceIdType.MESH
BF16 = jnp.bfloat16
F32 = jnp.float32
GELU_RATE = 0.7978845608028654
GELU_CUBE = 0.044715
HID_TILE = 256
ATT_IN, ATT_OUT, FFN_IN, FFN_OUT, QUERY, KEY = range(6)


def bit_of(value, mask):
    return lax.rem(lax.div(value, mask), 2)


def flip(value, masks, bits):
    for b in range(bits):
        if (masks >> b) & 1:
            value = value + (1 << b) * (1 - 2 * bit_of(value, 1 << b))
    return value


def greet(devices):
    barrier = pltpu.get_barrier_semaphore()
    for device in devices:
        pl.semaphore_signal(barrier, inc=1, device_id=device, device_id_type=MESH)
    pl.semaphore_wait(barrier, len(devices))


def remote(src, dst, send, recv, device):
    return pltpu.make_async_remote_copy(
        src_ref=src, dst_ref=dst, send_sem=send, recv_sem=recv,
        device_id=device, device_id_type=MESH,
    )


def many(offset, size):
    return pl.ds(pl.multiple_of(offset, size if size % 128 == 0 else 16), size)


def lanes(offset, size):
    return pl.ds(pl.multiple_of(offset, 128), size)


def window_start(z, share):
    if isinstance(z, int):
        return z * share // 128 * 128
    return lax.div(z * share, 128) * 128


def window_width(share, n_fsdp):
    widest = max((z + 1) * share - window_start(z, share) for z in range(n_fsdp))
    return -(-widest // HID_TILE) * HID_TILE


def dot_nt(left, right):
    return lax.dot_general(left, right, (((1,), (1,)), ((), ())), preferred_element_type=F32)


def dot_nn(left, right):
    return jnp.dot(left, right, preferred_element_type=F32)


def norm_scale(rows_in):
    return lax.rsqrt(jnp.mean(rows_in * rows_in, axis=-1, keepdims=True) + epsilon)


def norm_back(rows_in, gain, scale, upstream):
    pulled = upstream * gain
    inner = jnp.mean(pulled * rows_in, axis=-1, keepdims=True)
    d_rows = scale * pulled - rows_in * (scale * scale * scale * inner)
    return d_rows, jnp.sum(upstream * rows_in * scale, axis=0, keepdims=True)


def turn(rows_in, cosine, sine_part):
    half = rows_in.shape[-1] // 2
    lower, upper = rows_in[:, :half], rows_in[:, half:]
    return jnp.concatenate(
        [lower * cosine - upper * sine_part, upper * cosine + lower * sine_part], axis=-1
    )


class Place:
    def __init__(self):
        self.s = lax.axis_index("seq")
        self.z = lax.axis_index("fsdp")
        self.c = bit_of(self.s, 1)
        self.x = bit_of(self.s, 2)
        self.y = bit_of(self.s, 4)

    def plane(self, masks):
        return (flip(self.s, masks, 3), self.z)

    def line(self, masks):
        return (self.s, flip(self.z, masks, 2))

    def halves(self, first_x):
        if first_x:
            return self.x, self.y, 2, 4
        return self.y, self.x, 4, 2


def layer_kernel(
    n_seq, n_fsdp, share, reach, head_count,
    x_ref, cot_ref, rates_ref, pack_ref, seg_ref,
    gate_ref, up_ref, wq_ref, wk_ref, wv_ref, wo_ref, wd_ref,
    out_ref, dx_out, gains_out, fin_gu, fin_d, fin_qkv, fin_wo,
    qkv_s, wo_s, w_in, w_down, pack_all, seg_all, gains, allowed, turns,
    h1_s, raw_s, q_s, kv_own, kv_s, p_s, att_s, o_s, mid_s,
    h_all, df_all, bent_s, act, d_in, h_turn, part_out, part_in, relay_in, total,
    own_d, own_g, own_o, own_q, hi_d, hi_g, hi_o, hi_q, lo_d, lo_g, lo_o, lo_q, line_o, line_q,
    do_s, datt_s, dkv_s, dkv_send, dkv_came, dqkv_s, dgains, gain_in, gain_line,
    w_send, w_recv, own_sem, pack_send, pack_recv, seg_send, seg_recv, kv_send, kv_recv,
    ex_send, ex_recv, relay_sem, dkv_ssem, dkv_rsem,
    c_send, c_recv, hi_send, hi_recv, lo_send, lo_recv, z_send, z_recv, oq_send, oq_recv,
    put_sem, ag_send, ag_recv, gain_send, gain_recv,
):
    at = Place()
    s, z, c = at.s, at.z, at.c
    rows, width = x_ref.shape
    depth = width // n_fsdp
    hidden = w_in.shape[2]
    head_width = wk_ref.shape[1]
    query_width = head_count * head_width
    heads_width = query_width + 2 * head_width
    rows_o = wo_ref.shape[0]
    n_hid = hidden // HID_TILE
    third = width // 3
    middle_z = (z > 0) & (z < n_fsdp - 1)
    tokens = n_fsdp * rows

    def hid(n):
        return lanes(n * HID_TILE, HID_TILE)

    def outs(n):
        return lanes(n * third, third)

    skipped = z * share - window_start(z, share)
    spare = hidden - share
    if spare:
        w_down[pl.ds(0, spare)] = jnp.zeros((spare, width), BF16)
        w_down[pl.ds(share, spare)] = jnp.zeros((spare, width), BF16)
    here_z = many(z * depth, depth)
    own_copies = [
        pltpu.make_async_copy(src, dst, own_sem.at[i])
        for i, (src, dst) in enumerate((
            (wq_ref, qkv_s.at[here_z, pl.ds(0, query_width)]),
            (wk_ref, qkv_s.at[here_z, pl.ds(query_width, head_width)]),
            (wv_ref, qkv_s.at[here_z, pl.ds(query_width + head_width, head_width)]),
            (wo_ref, wo_s.at[many(z * rows_o, rows_o)]),
            (wd_ref, w_down.at[many(skipped, share)]),
            (gate_ref.at[:, lanes(window_start(z, share), hidden)], w_in.at[0, here_z]),
            (up_ref.at[:, lanes(window_start(z, share), hidden)], w_in.at[1, here_z]),
        ))
    ]
    seg_all[s] = jnp.broadcast_to(seg_ref[...], seg_all.shape[1:])
    pack_all[z] = jnp.broadcast_to(pack_ref[...], pack_all.shape[1:])
    greet([at.plane(k) for k in range(1, n_seq)] + [at.line(m) for m in range(1, n_fsdp)])

    packs = [
        remote(pack_all.at[z], pack_all.at[z], pack_send.at[m], pack_recv.at[m], at.line(m))
        for m in range(1, n_fsdp)
    ]
    seg_copies = [
        remote(seg_all.at[s], seg_all.at[s], seg_send.at[k], seg_recv.at[k], at.plane(k))
        for k in range(1, n_seq)
    ]
    kv_copies = [
        remote(kv_own, kv_s.at[reach - o], kv_send.at[o - 1], kv_recv.at[o - 1],
               (lax.rem(s + o, n_seq), z))
        for o in range(1, reach + 1)
    ]

    def w_region(kind, whose, hi, lo, level):
        base = whose * depth
        if kind == "q":
            cols = (
                lanes(hi * (query_width // 2) + lo * (query_width // 4), query_width // 4),
                lanes(hi * (query_width // 2), query_width // 2),
                pl.ds(0, query_width),
            )[level]
            return qkv_s.at[many(base + c * (depth // 2), depth // 2), cols]
        if kind == "kv":
            start = query_width + c * head_width
            if level == 0:
                start = start + lo * (head_width // 2)
            cols = lanes(start, head_width if level else head_width // 2)
            if level == 2:
                return qkv_s.at[many(base, depth), cols]
            return qkv_s.at[many(base + hi * (depth // 2), depth // 2), cols]
        if kind == "wo":
            start = whose * rows_o + c * (rows_o // 2)
            if level < 2:
                start = start + hi * (rows_o // 4)
            if level < 1:
                start = start + lo * (rows_o // 8)
            return wo_s.at[many(start, rows_o // (8, 4, 2)[level])]
        if level == 2:
            return w_in.at[c, many(base, depth)]
        here = many(base + hi * (depth // 2), depth // 2)
        if level == 1:
            return w_in.at[c, here]
        return w_in.at[c, here, lanes(lo * (hidden // 2), hidden // 2)]

    def w_sources(kind, to, hi, lo):
        if kind == "q":
            cols = lanes(hi * (query_width // 2) + lo * (query_width // 4), query_width // 4)
            return [wq_ref.at[many(c * (depth // 2), depth // 2), cols]]
        if kind == "wo":
            start = c * (rows_o // 2) + hi * (rows_o // 4) + lo * (rows_o // 8)
            return [wo_ref.at[many(start, rows_o // 8)]]
        here = many(hi * (depth // 2), depth // 2)
        if kind == "kv":
            cols = lanes(lo * (head_width // 2), head_width // 2)
            return [ref.at[here, cols] for ref in (wk_ref, wv_ref)]
        cols = lanes(window_start(to, share) + lo * (hidden // 2), hidden // 2)
        return [ref.at[here, cols] for ref in (gate_ref, up_ref)]

    items = []
    for k, kind in enumerate(("q", "kv", "wo", "gu")):
        for m in range(1, n_fsdp):
            items.append((kind, m, (m % 2 == 1) != (kind in ("kv", "wo"))))
    steps, starts = [], []
    for i, (kind, m, first_x) in enumerate(items):
        hi, lo, mask_hi, mask_lo = at.halves(first_x)
        there = flip(z, m, 2)
        firsts = [
            remote(src, w_region(kind, z, hi, lo, 0), w_send.at[i, 0], w_recv.at[i, 0], at.line(m))
            for src in w_sources(kind, there, hi, lo)
        ]
        starts.append(firsts)
        steps.append([firsts[0]] + [
            remote(w_region(kind, there, hi, lo, k), w_region(kind, there, hi, lo, k),
                   w_send.at[i, k + 1], w_recv.at[i, k + 1], at.plane(mask))
            for k, mask in enumerate((mask_lo, mask_hi, 1))
        ])

    def begin_weight(i):
        if len(starts[i]) == 1:
            starts[i][0].start()
        else:
            for core, first in enumerate(starts[i]):
                pl.when(c == core)(first.start)

    def move_weight(i, stage):
        steps[i][stage - 1].wait_recv()
        steps[i][stage].start()

    n_items = len(items)
    n_att = n_items - (n_fsdp - 1)
    n_qkv = 2 * (n_fsdp - 1)
    for copy in packs + seg_copies:
        copy.start()
    for i in range(n_att):
        begin_weight(i)
    for copy in own_copies:
        copy.start()

    for copy in seg_copies:
        copy.wait_recv()
    across = lax.broadcasted_iota(jnp.int32, (rows, rows), 0)
    along = lax.broadcasted_iota(jnp.int32, (rows, rows), 1)
    seg_here = jnp.broadcast_to(seg_ref[...].astype(F32), (rows, rows)).T
    for o in range(reach, -1, -1):
        key_seg = seg_all[lax.rem(s + n_seq - o, n_seq), 0:1, :].astype(F32)
        apart = across - along + o * rows
        fine = (apart >= 0) & (apart < WINDOW) & (seg_here == key_seg) & (s >= o)
        allowed[:, pl.ds((reach - o) * rows, rows)] = jnp.where(fine, 1.0, 0.0)
    angle = ((s * rows + across).astype(F32) - seg_here) * rates_ref[...]
    turns[0] = jnp.cos(angle)
    turns[1] = jnp.sin(angle)
    for copy in packs:
        copy.wait_recv()
    gains[...] = jnp.zeros(gains.shape, F32)
    start = 0
    for row in range(6):
        size = (depth if row < QUERY else head_width // n_fsdp)
        for block in range(n_fsdp):
            gains[row : row + 1, block * size : (block + 1) * size] = pack_all[
                block, 0:1, start : start + size
            ]
        start += size

    def gain(row):
        return gains[row : row + 1, : (width if row < QUERY else head_width)]

    x = x_ref[...].astype(F32)
    h1_s[...] = (x * norm_scale(x) * gain(ATT_IN)).astype(BF16)

    for t in range(n_att + 2):
        for stage in (3, 2, 1):
            i = t - (stage - 1)
            if 0 <= i < n_att:
                move_weight(i, stage)
        if t == n_att - 1:
            for i in range(n_att, n_items):
                begin_weight(i)
    for i in range(n_qkv):
        steps[i][3].wait_recv()
    for copy in own_copies[:3]:
        copy.wait()

    gu_moves = []
    for t in range(n_fsdp + 1):
        gu_moves.append(
            [(n_att + t - (k - 1), k) for k in (3, 2, 1) if 0 <= t - (k - 1) < n_fsdp - 1]
        )

    def move_gu(t):
        for i, stage in gu_moves[t]:
            move_weight(i, stage)

    tile = heads_width // 3

    @pl.loop(0, 3)
    def _(n):
        cols = lanes(n * tile, tile)
        raw_s[:, cols] = dot_nn(h1_s[...], qkv_s[:, cols])

    k_raw = raw_s[:, query_width : query_width + head_width]
    kv_own[:, :head_width] = turn(
        k_raw * norm_scale(k_raw) * gain(KEY), turns[0], turns[1]
    ).astype(BF16)
    kv_own[:, head_width:] = raw_s[:, query_width + head_width :].astype(BF16)
    for copy in kv_copies:
        copy.start()
    kv_s[reach] = kv_own[...]
    for h in range(head_count):
        q_raw = raw_s[:, h * head_width : (h + 1) * head_width]
        q_fin = q_raw * norm_scale(q_raw) * gain(QUERY)
        q_s[h] = turn(q_fin, turns[0], turns[1]).astype(BF16)
    for i in range(n_qkv, n_att):
        steps[i][3].wait_recv()
    own_copies[3].wait()
    move_gu(0)
    for copy in kv_copies:
        copy.wait_recv()

    def keys():
        return kv_s[:, :, :head_width].reshape((reach + 1) * rows, head_width)

    def values():
        return kv_s[:, :, head_width:].reshape((reach + 1) * rows, head_width)

    for h in range(head_count):
        scores = dot_nt(q_s[h], keys()) * (head_width**-0.5)
        masked = jnp.where(allowed[...] > 0.5, scores, masked_value)
        grown = jnp.exp(masked - jnp.max(masked, axis=-1, keepdims=True))
        probs = grown / jnp.sum(grown, axis=-1, keepdims=True)
        p_s[h] = probs
        att_s[:, h * head_width : (h + 1) * head_width] = dot_nn(
            probs.astype(BF16), values()
        ).astype(BF16)
        if h == 1:
            move_gu(1)
        if h == 3:
            move_gu(2)

    @pl.loop(0, 3)
    def _(n):
        o_s[:, outs(n)] = dot_nn(att_s[...], wo_s[:, outs(n)])

    o_raw = o_s[...]
    middle = x_ref[...].astype(F32) + o_raw * norm_scale(o_raw) * gain(ATT_OUT)
    mid_s[...] = middle
    h_all[0] = (middle * norm_scale(middle) * gain(FFN_IN)).astype(BF16)

    def exchange(phase, src, dst):
        return {
            m: remote(src(m), dst(m), ex_send.at[phase, m], ex_recv.at[phase, m], at.line(m))
            for m in range(1, n_fsdp)
        }

    last = n_fsdp - 1
    send_h = exchange(0, lambda m: h_all.at[0], lambda m: h_all.at[m])
    send_f = exchange(1, lambda m: part_out.at[m - 1], lambda m: part_in.at[0, m - 1])
    send_df = exchange(2, lambda m: df_all.at[0], lambda m: df_all.at[m])
    send_dh = exchange(3, lambda m: part_out.at[m - 1], lambda m: part_in.at[1, m - 1])
    onward = {
        phase: remote(rows_all.at[2], rows_all.at[last],
                      relay_sem.at[phase], ex_recv.at[phase, last], at.line(1))
        for phase, rows_all in ((0, h_all), (2, df_all))
    }
    by_way = {
        phase: remote(part_out.at[last - 1], relay_in.at[phase // 2],
                      relay_sem.at[phase], relay_sem.at[phase + 3], at.line(1))
        for phase in (1, 3)
    }

    def send_rows(copies):
        copies[1].start()
        copies[2].start()
        pl.when(middle_z)(copies[last].start)

    def take_rows(copies, phase, m):
        copies[m].wait_recv()
        if m == 2:
            pl.when(middle_z)(onward[phase].start)

    def send_part(copies, phase, m):
        if m == 1:
            copies[1].start()
        elif m == 2:
            pl.when(~middle_z)(copies[2].start)
        elif m == last:
            pl.when(~middle_z)(by_way[phase].start)

            @pl.when(middle_z)
            def _():
                copies[last].start()
                by_way[phase].wait_recv()
                part_out[1] = (
                    part_out[1].astype(F32) + relay_in[phase // 2].astype(F32)
                ).astype(BF16)
                copies[2].start()

    def take_parts(copies):
        copies[1].wait_recv()
        copies[2].wait_recv()
        pl.when(middle_z)(copies[last].wait_recv)

    def rows_sent(copies, phase):
        copies[1].wait_send()
        copies[2].wait_send()

        @pl.when(middle_z)
        def _():
            copies[last].wait_send()
            onward[phase].wait_send()

    def parts_sent(copies, phase):
        copies[1].wait_send()
        copies[2].wait_send()
        pl.when(middle_z)(copies[last].wait_send)
        pl.when(~middle_z)(by_way[phase].wait_send)

    send_rows(send_h)

    @pl.when(~middle_z)
    def _():
        part_in[0, last - 1] = jnp.zeros((rows, width), BF16)
        part_in[1, last - 1] = jnp.zeros((rows, width), BF16)

    move_gu(3)
    move_gu(4)
    for i in range(n_att, n_items):
        steps[i][3].wait_recv()
    for copy in own_copies[4:]:
        copy.wait()

    for m in range(n_fsdp):
        if m:
            take_rows(send_h, 0, m)

        @pl.loop(0, n_hid)
        def _(n):
            rows_h = h_all[m]
            gate = dot_nn(rows_h, w_in[0, :, hid(n)])
            up = dot_nn(rows_h, w_in[1, :, hid(n)])
            squared = gate * gate
            bent = jnp.tanh(GELU_RATE * (gate + GELU_CUBE * squared * gate))
            gelu = 0.5 * gate * (1.0 + bent)
            slope = 0.5 * (1.0 + bent) + 0.5 * gate * (1.0 - bent * bent) * (
                GELU_RATE * (1.0 + 3.0 * GELU_CUBE * squared)
            )
            bent_s[pl.ds(m * rows, rows), hid(n)] = gelu.astype(BF16)
            bent_s[pl.ds(tokens + m * rows, rows), hid(n)] = (slope * up).astype(BF16)
            act[m, :, hid(n)] = (gelu * up).astype(BF16)

        @pl.loop(0, 3)
        def _(n):
            part = dot_nn(act[m], w_down[:, outs(n)])
            if m:
                part_out[m - 1, :, outs(n)] = part.astype(BF16)
            else:
                total[:, outs(n)] = part

        if m:
            send_part(send_f, 1, m)

    for m in range(n_fsdp):
        h_turn[:, pl.ds(m * rows, rows)] = h_all[m].T
    for i in range(n_att, n_items):
        for k in range(4):
            steps[i][k].wait_send()

    take_parts(send_f)
    f_raw = total[...]
    for m in range(1, n_fsdp):
        f_raw = f_raw + part_in[0, m - 1].astype(F32)
    cot = cot_ref[...].astype(F32)
    scale = norm_scale(f_raw)
    d_f, d_gain = norm_back(f_raw, gain(FFN_OUT), scale, cot)
    df_all[0] = d_f.astype(BF16)
    send_rows(send_df)
    out_ref[...] = (mid_s[...] + f_raw * scale * gain(FFN_OUT)).astype(BF16)
    dgains[...] = jnp.zeros(dgains.shape, F32)
    dgains[FFN_OUT : FFN_OUT + 1, :] = d_gain
    parts_sent(send_f, 1)

    for m in range(n_fsdp):
        if m:
            take_rows(send_df, 2, m)

        @pl.loop(0, n_hid)
        def _(n):
            d_act = dot_nt(df_all[m], w_down[hid(n), :])
            gelu = bent_s[pl.ds(m * rows, rows), hid(n)].astype(F32)
            slope = bent_s[pl.ds(tokens + m * rows, rows), hid(n)].astype(F32)
            d_in[0, m, :, hid(n)] = (d_act * slope).astype(BF16)
            d_in[1, m, :, hid(n)] = (d_act * gelu).astype(BF16)

        @pl.loop(0, 3)
        def _(n):
            part = dot_nt(d_in[0, m], w_in[0, outs(n), :]) + dot_nt(
                d_in[1, m], w_in[1, outs(n), :]
            )
            if m:
                part_out[m - 1, :, outs(n)] = part.astype(BF16)
            else:
                total[:, outs(n)] = part

        if m:
            send_part(send_dh, 3, m)

    chunks = [("d", 0, True), ("d", 1, False)]
    chunks += [("g", m, m % 2 == 0) for m in range(n_fsdp)]
    chunks += [("o", 0, False), ("q", 0, True)]
    n_ffn = 2 + n_fsdp
    half_d = hidden // 4

    def mine_of(kind, i):
        if kind == "d":
            return own_d.at[pl.ds(i * half_d, half_d)]
        return {"g": own_g, "o": own_o, "q": own_q}[kind].at[i]

    def hi_part(kind, hi):
        if kind == "d":
            return many(hi * (half_d // 2), half_d // 2), slice(None)
        if kind == "g":
            return many(hi * (depth // 2), depth // 2), slice(None)
        if kind == "q":
            return slice(None), lanes(hi * (heads_width // 2), heads_width // 2)
        return many(hi * (rows_o // 4), rows_o // 4), slice(None)

    def lo_part(kind, hi, lo):
        if kind == "d":
            return many(hi * (half_d // 2) + lo * (half_d // 4), half_d // 4), slice(None)
        if kind == "g":
            return (
                many(hi * (depth // 2), depth // 2),
                lanes(lo * (hidden // 2), hidden // 2),
            )
        if kind == "q":
            start = hi * (heads_width // 2) + lo * (heads_width // 4)
            return slice(None), lanes(start, heads_width // 4)
        return many(hi * (rows_o // 4) + lo * (rows_o // 8), rows_o // 8), slice(None)

    def fin_part(kind, i, where, core):
        rows_at, cols_at = where
        if kind == "g":
            return fin_gu.at[core, i, rows_at, cols_at]
        ref, base, size = {
            "d": (fin_d, core * (hidden // 2) + i * half_d, half_d),
            "q": (fin_qkv, core * (depth // 2), depth // 2),
            "o": (fin_wo, core * (rows_o // 2), rows_o // 2),
        }[kind]
        if isinstance(rows_at, slice):
            rows_at = many(base, size)
        else:
            rows_at = many(base + rows_at.start, rows_at.size)
        return ref.at[rows_at, cols_at]

    def add(ref, where, other):
        rows_at, cols_at = where
        start = 0 if isinstance(rows_at, slice) else rows_at.start
        slab = 16

        @pl.loop(0, other.shape[0] // slab)
        def _(n):
            here = pl.ds(pl.multiple_of(start + n * slab, slab), slab)
            there = pl.ds(pl.multiple_of(n * slab, slab), slab)
            ref[here, cols_at] = (
                ref[here, cols_at].astype(F32) + other[there, :].astype(F32)
            ).astype(BF16)

    whole = (slice(None), slice(None))
    from_hi = {"d": hi_d, "g": hi_g, "o": hi_o, "q": hi_q}
    from_lo = {"d": lo_d, "g": lo_g, "o": lo_o, "q": lo_q}
    his, los, lines = [], [], []
    for j, (kind, i, first_x) in enumerate(chunks):
        hi, lo, mask_hi, mask_lo = at.halves(first_x)
        mine = mine_of(kind, i)
        his.append(remote(mine.at[hi_part(kind, 1 - hi)], from_hi[kind].at[i],
                          hi_send.at[j], hi_recv.at[j], at.plane(mask_hi)))
        los.append(remote(mine.at[lo_part(kind, hi, 1 - lo)], from_lo[kind].at[i],
                          lo_send.at[j], lo_recv.at[j], at.plane(mask_lo)))
        line = None
        if kind == "g" and i:
            line = remote(mine.at[lo_part(kind, hi, lo)],
                          fin_part(kind, z, lo_part(kind, hi, lo), c),
                          z_send.at[j], z_recv.at[j], at.line(i))
        lines.append(line)
    stage = {
        "d": lambda i: w_down.at[pl.ds(i * half_d, half_d)],
        "g": lambda i: bent_s.at[pl.ds(i * depth, depth)],
        "q": lambda i: w_in.at[0, pl.ds(i * (depth // 2), depth // 2), pl.ds(0, heads_width)],
        "o": lambda i: w_in.at[1, pl.ds(i * (rows_o // 2), rows_o // 2), pl.ds(0, width)],
    }
    to_core = [("d", 0), ("d", 1)]
    to_core += [(kind, m) for kind in "goq" for m in range(n_fsdp)]
    cores = {
        key: remote(stage[key[0]](key[1]), mine_of(*key), c_send.at[k], c_recv.at[k], at.plane(1))
        for k, key in enumerate(to_core)
    }
    line_sums = {}
    for k, (kind, ref) in enumerate((("o", line_o), ("q", line_q))):
        for m in range(1, n_fsdp):
            line_sums[kind, m] = remote(mine_of(kind, m), ref.at[m - 1],
                                        oq_send.at[k, m], oq_recv.at[k, m], at.line(m))

    puts, hands = [], []
    for j, (kind, i, first_x) in enumerate(chunks):
        hi, lo, mask_hi, mask_lo = at.halves(first_x)
        which = flip(z, i, 2) if kind == "g" else i
        piece = fin_part(kind, which, lo_part(kind, hi, lo), c)
        half = fin_part(kind, which, hi_part(kind, hi), c)
        full = fin_part(kind, which, whole, c)
        put = None
        if lines[j] is None:
            put = pltpu.make_async_copy(
                mine_of(kind, i).at[lo_part(kind, hi, lo)], piece, put_sem.at[j]
            )
        puts.append(put)
        hands.append([
            remote(part, part, ag_send.at[j, k], ag_recv.at[j, k], at.plane(mask))
            for k, (part, mask) in enumerate(((piece, mask_lo), (half, mask_hi), (full, 1)))
        ])

    def take_hi(j):
        kind, i, first_x = chunks[j]
        hi, lo, _, _ = at.halves(first_x)
        his[j].wait_recv()
        add(mine_of(kind, i), hi_part(kind, hi), from_hi[kind].at[i])
        los[j].start()

    def take_lo(j):
        kind, i, first_x = chunks[j]
        hi, lo, _, _ = at.halves(first_x)
        los[j].wait_recv()
        add(mine_of(kind, i), lo_part(kind, hi, lo), from_lo[kind].at[i])
        if lines[j] is not None:
            lines[j].start()
        else:
            puts[j].start()

    def begin_hand(j):
        if lines[j] is not None:
            lines[j].wait_recv()
        else:
            puts[j].wait()
        hands[j][0].start()

    def hand_on(j, k):
        hands[j][k - 1].wait_recv()
        hands[j][k].start()

    def down_grads(core, dst, adds):
        @pl.loop(0, hidden // 256)
        def _(n):
            left = act[:, :, lanes(core * (hidden // 2) + n * 128, 128)].reshape(tokens, 128).T
            here = pl.ds(pl.multiple_of(n * 128, 128), 128)
            for k in range(3):
                right = df_all[:, :, k * third : (k + 1) * third].reshape(tokens, third)
                grads = dot_nn(left, right)
                if adds:
                    grads = grads + dst[here, k * third : (k + 1) * third].astype(F32)
                dst[here, k * third : (k + 1) * third] = grads.astype(BF16)

    def in_grads(core, m, dst, adds):
        left_at = many(flip(z, m, 2) * depth, depth)

        @pl.loop(0, n_hid)
        def _(n):
            right = d_in[core, :, :, hid(n)].reshape(tokens, HID_TILE)
            grads = dot_nn(h_turn[left_at, :], right)
            if adds:
                grads = grads + dst[:, hid(n)].astype(F32)
            dst[:, hid(n)] = grads.astype(BF16)

    down_grads(1 - c, w_down, False)
    cores["d", 0].start()
    cores["d", 1].start()
    for m in range(n_fsdp):
        in_grads(1 - c, m, stage["g"](m), False)
        cores["g", m].start()
    cores["d", 0].wait_recv()
    cores["d", 1].wait_recv()
    down_grads(c, own_d, True)
    his[0].start()
    his[1].start()
    for m in range(n_fsdp):
        cores["g", m].wait_recv()
        in_grads(c, m, own_g.at[m], True)
        his[2 + m].start()

    dkv_copies = [
        remote(dkv_send.at[reach - o], dkv_came.at[o - 1], dkv_ssem.at[o - 1], dkv_rsem.at[o - 1],
               (lax.rem(s + n_seq - o, n_seq), z))
        for o in range(1, reach + 1)
    ]
    gain_copies = [
        remote(dgains, gain_in.at[k], gain_send.at[k], gain_recv.at[k], at.plane(k))
        for k in range(1, n_seq)
    ]
    gain_lines = [
        remote(gain_line.at[0], gain_line.at[m], gain_send.at[n_seq + m], gain_recv.at[n_seq + m],
               at.line(m))
        for m in range(1, n_fsdp)
    ]

    def to_middle():
        take_parts(send_dh)
        dh = total[...]
        for m in range(1, n_fsdp):
            dh = dh + part_in[1, m - 1].astype(F32)
        mid = mid_s[...]
        d_mid, d_gain = norm_back(mid, gain(FFN_IN), norm_scale(mid), dh)
        d_mid = d_mid + cot_ref[...].astype(F32)
        mid_s[...] = d_mid
        dgains[FFN_IN : FFN_IN + 1, :] = d_gain
        o_raw = o_s[...]
        d_o, d_gain = norm_back(o_raw, gain(ATT_OUT), norm_scale(o_raw), d_mid)
        dgains[ATT_OUT : ATT_OUT + 1, :] = d_gain
        do_s[...] = d_o.astype(BF16)
        for h in range(head_count):
            here = pl.ds(h * head_width, head_width)
            datt_s[h] = dot_nt(do_s[...], wo_s[here, :]).astype(BF16)

    def unturn(rows_in):
        return turn(rows_in, turns[0], -turns[1])

    def through_head(h):
        probs = p_s[h]
        d_att = datt_s[h]
        d_probs = dot_nt(d_att, values())
        d_scores = probs * (d_probs - jnp.sum(probs * d_probs, axis=-1, keepdims=True))
        ds_low = d_scores.astype(BF16)
        scale = head_width**-0.5
        d_keys = inner_rows(ds_low, q_s[h]) * scale
        d_values = inner_rows(probs.astype(BF16), d_att)
        if h:
            d_keys = d_keys + dkv_s[:, :head_width]
            d_values = d_values + dkv_s[:, head_width:]
        dkv_s[:, :head_width] = d_keys
        dkv_s[:, head_width:] = d_values
        cols = slice(h * head_width, (h + 1) * head_width)
        q_raw = raw_s[:, cols]
        d_q, d_gain = norm_back(
            q_raw, gain(QUERY), norm_scale(q_raw), unturn(dot_nn(ds_low, keys()) * scale)
        )
        dqkv_s[:, cols] = d_q.astype(BF16)
        dgains[QUERY : QUERY + 1, :head_width] += d_gain

    def return_keys():
        for b in range(reach):
            dkv_send[b] = dkv_s[pl.ds(b * rows, rows), :].astype(BF16)
        for copy in dkv_copies:
            copy.start()

    def grad_tiles(left_at, turned, right, n_cols, dst, adds):
        tile = n_cols // 3
        for k in range(3):
            grads = dot_nn(turned[left_at, :], right[:, k * tile : (k + 1) * tile])
            if adds:
                grads = grads + dst[:, k * tile : (k + 1) * tile].astype(F32)
            dst[:, k * tile : (k + 1) * tile] = grads.astype(BF16)

    def core_grads(kind, turned, right, span, n_cols):
        for m in range(n_fsdp):
            start = flip(z, m, 2) * span + (1 - c) * (span // 2)
            grad_tiles(many(start, span // 2), turned, right, n_cols, stage[kind](m), False)
            cores[kind, m].start()
        for m in list(range(1, n_fsdp)) + [0]:
            start = flip(z, m, 2) * span + c * (span // 2)
            cores[kind, m].wait_recv()
            grad_tiles(many(start, span // 2), turned, right, n_cols, mine_of(kind, m), True)
            if m:
                line_sums[kind, m].start()

    def output_grads():
        h_turn[pl.ds(0, query_width), pl.ds(0, rows)] = att_s[...].T
        core_grads("o", h_turn.at[:, pl.ds(0, rows)], do_s, rows_o, width)

    def key_grads():
        h_turn[:, pl.ds(rows, rows)] = h1_s[...].T
        d_kv = dkv_s[pl.ds(reach * rows, rows), :]
        for o in range(reach):
            dkv_copies[o].wait_recv()
            d_kv = d_kv + dkv_came[o].astype(F32)
        k_raw = raw_s[:, query_width : query_width + head_width]
        d_k, d_gain = norm_back(
            k_raw, gain(KEY), norm_scale(k_raw), unturn(d_kv[:, :head_width])
        )
        dqkv_s[:, query_width : query_width + head_width] = d_k.astype(BF16)
        dqkv_s[:, query_width + head_width :] = d_kv[:, head_width:].astype(BF16)
        dgains[KEY : KEY + 1, :head_width] = d_gain
        core_grads("q", h_turn.at[:, pl.ds(rows, rows)], dqkv_s, depth, heads_width)

    def sum_line(j):
        kind = chunks[j][0]
        for m in range(1, n_fsdp):
            line_sums[kind, m].wait_recv()
            add(mine_of(kind, 0), whole, {"o": line_o, "q": line_q}[kind].at[m - 1])
        his[j].start()

    def to_input():
        x = x_ref[...].astype(F32)
        d_h = dot_nt(dqkv_s[...], qkv_s[...])
        d_x, d_gain = norm_back(x, gain(ATT_IN), norm_scale(x), d_h)
        dx_out[...] = mid_s[...] + d_x
        dgains[ATT_IN : ATT_IN + 1, :] = d_gain
        for copy in gain_copies:
            copy.start()

    def sum_gains():
        sums = dgains[...]
        for k, copy in enumerate(gain_copies):
            copy.wait_recv()
            sums = sums + gain_in[k + 1]
        gain_line[0] = sums
        for copy in gain_lines:
            copy.start()

    take_hi(0)
    take_hi(1)
    to_middle()
    through_head(0)
    through_head(1)
    take_hi(2)
    take_hi(3)
    take_lo(0)
    take_lo(1)
    through_head(2)
    through_head(3)
    return_keys()
    output_grads()
    begin_hand(0)
    begin_hand(1)
    take_hi(4)
    take_hi(5)
    take_lo(2)
    take_lo(3)
    key_grads()
    hand_on(0, 1)
    hand_on(1, 1)
    begin_hand(2)
    begin_hand(3)
    take_lo(4)
    take_lo(5)
    to_input()
    sum_line(6)
    hand_on(0, 2)
    hand_on(1, 2)
    begin_hand(4)
    begin_hand(5)
    hand_on(2, 1)
    hand_on(3, 1)
    sum_line(7)
    take_hi(6)
    hand_on(2, 2)
    hand_on(3, 2)
    take_hi(7)
    take_lo(6)
    hand_on(4, 1)
    hand_on(5, 1)
    begin_hand(6)
    take_lo(7)
    sum_gains()
    begin_hand(7)
    hand_on(4, 2)
    hand_on(5, 2)
    hand_on(6, 1)
    hand_on(7, 1)
    hand_on(6, 2)
    hand_on(7, 2)
    sums = gain_line[0]
    for m, copy in enumerate(gain_lines):
        copy.wait_recv()
        sums = sums + gain_line[m + 1]
    gains_out[...] = sums

    for j in range(len(chunks)):
        hands[j][2].wait_recv()
        for k in range(3):
            hands[j][k].wait_send()
        his[j].wait_send()
        los[j].wait_send()
        if lines[j] is not None:
            lines[j].wait_send()
    for copy in list(cores.values()) + list(line_sums.values()):
        copy.wait_send()
    for copy in gain_copies + gain_lines + dkv_copies + kv_copies + packs + seg_copies:
        copy.wait_send()
    for i in range(n_att):
        for k in range(4):
            steps[i][k].wait_send()
    rows_sent(send_h, 0)
    rows_sent(send_df, 2)
    parts_sent(send_dh, 3)


def layer(n_seq, n_fsdp, share, hidden, reach, head_count, x, cot, rates, pack, segs,
          w_gate, w_up, w_query, w_key, w_value, w_output, w_down):
    rows, width = x.shape
    depth = width // n_fsdp
    head_width = w_key.shape[1]
    query_width = w_query.shape[1]
    heads_width = query_width + 2 * head_width
    rows_o = w_output.shape[0]
    n_items = 4 * (n_fsdp - 1)
    anywhere = pl.BlockSpec(memory_space=pl.ANY)
    in_vmem = pl.BlockSpec(memory_space=pltpu.VMEM)
    shape = jax.ShapeDtypeStruct
    sems = pltpu.SemaphoreType.DMA

    def low(*size):
        return pltpu.VMEM(size, BF16)

    def full(*size):
        return pltpu.VMEM(size, F32)

    return pl.pallas_call(
        functools.partial(layer_kernel, n_seq, n_fsdp, share, reach, head_count),
        out_shape=[
            shape((rows, width), BF16),
            shape((rows, width), F32),
            shape((8, width), F32),
            shape((2, n_fsdp, depth, hidden), BF16),
            shape((hidden, width), BF16),
            shape((depth, heads_width), BF16),
            shape((rows_o, width), BF16),
        ],
        in_specs=[in_vmem] * 5 + [anywhere] * 7,
        out_specs=[in_vmem] * 3 + [anywhere] * 4,
        scratch_shapes=[
            low(width, heads_width),
            low(n_fsdp * rows_o, width),
            low(2, width, hidden),
            low(hidden, width),
            full(n_fsdp, 8, pack.shape[1]),
            pltpu.VMEM((n_seq, 8, rows), jnp.int32),
            full(8, width),
            full(rows, (reach + 1) * rows),
            full(2, rows, head_width // 2),
            low(rows, width),
            full(rows, heads_width),
            low(head_count, rows, head_width),
            low(rows, 2 * head_width),
            low(reach + 1, rows, 2 * head_width),
            full(head_count, rows, (reach + 1) * rows),
            low(rows, query_width),
            full(rows, width),
            full(rows, width),
            low(n_fsdp, rows, width),
            low(n_fsdp, rows, width),
            low(max(width, 2 * n_fsdp * rows), hidden),
            low(n_fsdp, rows, hidden),
            low(2, n_fsdp, rows, hidden),
            low(width, n_fsdp * rows),
            low(n_fsdp - 1, rows, width),
            low(2, n_fsdp - 1, rows, width),
            low(2, rows, width),
            full(rows, width),
            low(hidden // 2, width),
            low(n_fsdp, depth, hidden),
            low(n_fsdp, rows_o // 2, width),
            low(n_fsdp, depth // 2, heads_width),
            low(2, hidden // 8, width),
            low(n_fsdp, depth // 2, hidden),
            low(1, rows_o // 4, width),
            low(1, depth // 2, heads_width // 2),
            low(2, hidden // 16, width),
            low(n_fsdp, depth // 2, hidden // 2),
            low(1, rows_o // 8, width),
            low(1, depth // 2, heads_width // 4),
            low(n_fsdp - 1, rows_o // 2, width),
            low(n_fsdp - 1, depth // 2, heads_width),
            low(rows, width),
            low(head_count, rows, head_width),
            full((reach + 1) * rows, 2 * head_width),
            low(reach, rows, 2 * head_width),
            low(reach, rows, 2 * head_width),
            low(rows, heads_width),
            full(8, width),
            full(n_seq, 8, width),
            full(n_fsdp, 8, width),
            sems((n_items, 4)),
            sems((n_items, 4)),
            sems((7,)),
            sems((n_fsdp,)),
            sems((n_fsdp,)),
            sems((n_seq,)),
            sems((n_seq,)),
            sems((reach,)),
            sems((reach,)),
            sems((4, n_fsdp)),
            sems((4, n_fsdp)),
            sems((7,)),
            sems((reach,)),
            sems((reach,)),
            sems((2 + 3 * n_fsdp,)),
            sems((2 + 3 * n_fsdp,)),
            sems((4 + n_fsdp,)),
            sems((4 + n_fsdp,)),
            sems((4 + n_fsdp,)),
            sems((4 + n_fsdp,)),
            sems((4 + n_fsdp,)),
            sems((4 + n_fsdp,)),
            sems((2, n_fsdp)),
            sems((2, n_fsdp)),
            sems((4 + n_fsdp,)),
            sems((4 + n_fsdp, 3)),
            sems((4 + n_fsdp, 3)),
            sems((n_seq + n_fsdp,)),
            sems((n_seq + n_fsdp,)),
        ],
        compiler_params=pltpu.CompilerParams(
            collective_id=0, has_side_effects=True, vmem_limit_bytes=62 << 20
        ),
        name="decoder_layer",
    )(x, cot, rates, pack, segs, w_gate, w_up, w_query, w_key, w_value, w_output, w_down)


def join_kernel(share, wins_ref, gate_ref, up_ref):
    n_win, hidden = wins_ref.shape[1], wins_ref.shape[3]
    starts = [window_start(i, share) for i in range(n_win)]
    for i, ref in enumerate((gate_ref, up_ref)):
        for w in range(n_win):
            first = starts[w]
            last = starts[w + 1] if w + 1 < n_win else first + hidden
            shared = starts[w - 1] + hidden - first if w else 0
            if shared:
                ref[:, first : first + shared] = wins_ref[i, w, :, :shared].astype(F32) + wins_ref[
                    i, w - 1, :, hidden - shared :
                ].astype(F32)
            ref[:, first + shared : last] = wins_ref[i, w, :, shared : last - first].astype(F32)


def joined(share, windows):
    _, n_win, rows, hidden = windows.shape
    slab = 32
    wide = pl.BlockSpec((slab, n_win * share), lambda i: (i, 0))
    return pl.pallas_call(
        functools.partial(join_kernel, share),
        grid=(rows // slab,),
        out_shape=[jax.ShapeDtypeStruct((rows, n_win * share), F32)] * 2,
        in_specs=[pl.BlockSpec((2, n_win, slab, hidden), lambda i: (0, 0, i, 0))],
        out_specs=[wide, wide],
        compiler_params=pltpu.CompilerParams(vmem_limit_bytes=32 << 20),
        name="join_windows",
    )(windows)


def shards(n_seq, n_fsdp, *args):
    w_query, w_key, w_output, w_gate = args[4], args[5], args[9], args[12]
    depth, ffn_width = w_gate.shape
    rows_here = args[0].shape[1]
    share = ffn_width // n_fsdp
    reach = (WINDOW - 2 + rows_here) // rows_here
    fits = (
        n_seq == 8
        and n_fsdp == 4
        and args[0].shape[0] == 1
        and reach < n_seq
        and rows_here % 128 == 0
        and depth % 32 == 0
        and w_output.shape[0] % 128 == 0
        and w_key.shape[1] % 256 == 0
        and w_query.shape[1] % 512 == 0
        and w_output.shape[1] % 384 == 0
        and ffn_width % n_fsdp == 0
        and share % 16 == 0
        and window_start(n_fsdp - 1, share) + window_width(share, n_fsdp) == ffn_width
    )
    if fits:
        return shards_fused(n_seq, n_fsdp, *args)
    return shards_plain(*args)


def shards_fused(
    n_seq,
    n_fsdp,
    inputs,
    segments,
    cotangent,
    gain_attn_in,
    w_query,
    w_key,
    w_value,
    gain_query,
    gain_key,
    w_output,
    gain_attn_out,
    gain_ffn_in,
    w_gate,
    w_up,
    w_down,
    gain_ffn_out,
):
    rows_here, width = inputs.shape[1:]
    head_width = w_key.shape[1]
    query_width = w_query.shape[1]
    head_count = query_width // head_width
    share = w_gate.shape[1] // n_fsdp
    hidden = window_width(share, n_fsdp)
    reach = (WINDOW - 2 + rows_here) // rows_here
    line = lax.axis_index("fsdp")
    gains = (gain_attn_in, gain_attn_out, gain_ffn_in, gain_ffn_out, gain_query, gain_key)
    pack = jnp.concatenate(gains).astype(F32)[None]
    rates = 10000.0 ** (-(jnp.arange(head_width // 2, dtype=F32) * 2.0) / head_width)
    outputs, d_inputs, gain_sums, fin_gu, fin_d, fin_qkv, fin_wo = layer(
        n_seq, n_fsdp, share, hidden, reach, head_count,
        inputs[0], cotangent[0], rates[None], pack, segments,
        w_gate, w_up, w_query, w_key, w_value, w_output, w_down,
    )
    grad_gate, grad_up = joined(share, fin_gu)
    skipped = line * share - window_start(line, share)
    grad_down = lax.dynamic_slice(fin_d, (skipped, jnp.int32(0)), (share, width)).astype(F32)

    def part(row, gain):
        size = gain.shape[0]
        return lax.dynamic_slice(gain_sums[row], (line * size,), (size,))

    fin_qkv = fin_qkv.astype(F32)
    return (
        outputs[None],
        d_inputs[None],
        part(ATT_IN, gain_attn_in),
        fin_qkv[:, :query_width],
        fin_qkv[:, query_width : query_width + head_width],
        fin_qkv[:, query_width + head_width :],
        part(QUERY, gain_query),
        part(KEY, gain_key),
        fin_wo.astype(F32),
        part(ATT_OUT, gain_attn_out),
        part(FFN_IN, gain_ffn_in),
        grad_gate,
        grad_up,
        grad_down,
        part(FFN_OUT, gain_ffn_out),
    )


def solution(mesh):
    placed = (
        P("fsdp", "seq", None),
        P("fsdp", "seq"),
        P("fsdp", "seq", None),
        P("fsdp"),
        P("fsdp", None),
        P("fsdp", None),
        P("fsdp", None),
        P("fsdp"),
        P("fsdp"),
        P("fsdp", None),
        P("fsdp"),
        P("fsdp"),
        P("fsdp", None),
        P("fsdp", None),
        P("fsdp", None),
        P("fsdp"),
    )
    return jax.shard_map(
        functools.partial(shards, mesh.shape["seq"], mesh.shape["fsdp"]),
        mesh=mesh,
        in_specs=placed,
        out_specs=(
            P("fsdp", "seq", None),
            P("fsdp", "seq", None),
            P("fsdp"),
            P("fsdp", None),
            P("fsdp", None),
            P("fsdp", None),
            P("fsdp"),
            P("fsdp"),
            P("fsdp", None),
            P("fsdp"),
            P("fsdp"),
            P("fsdp", None),
            P("fsdp", None),
            P("fsdp", None),
            P("fsdp"),
        ),
        check_vma=False,
    )
```

```python
import functools

import jax
import jax.numpy as jnp
from jax import lax
from jax.experimental import pallas as pl
from jax.experimental.pallas import tpu as pltpu
from jax.sharding import PartitionSpec as P

WINDOW = 512


epsilon = 1e-06
masked_value = -1e30


def from_behind(block, axis, distance):
    devices = range(lax.axis_size(axis))
    route = [(i - distance, i) for i in devices if i - distance in devices]
    return lax.ppermute(block, axis, route)


def norm_rows(rows_in, gain_vec):
    return (
        rows_in
        * lax.rsqrt(jnp.mean(rows_in * rows_in, axis=-1, keepdims=True) + epsilon)
        * gain_vec
    )


def angles(positions, head_width):
    inv_rates = 10000.0 ** (-(jnp.arange(head_width // 2, dtype=jnp.float32) * 2.0) / head_width)
    return positions.astype(jnp.float32)[:, None] * inv_rates[None, :]


def rotate(rows_in, angles_at):
    half_width = rows_in.shape[-1] // 2
    lower_half = rows_in[..., :half_width]
    upper_half = rows_in[..., half_width:]
    cosine = jnp.cos(angles_at)
    sine_part = jnp.sin(angles_at)
    return jnp.concatenate(
        [
            lower_half * cosine - upper_half * sine_part,
            upper_half * cosine + lower_half * sine_part,
        ],
        axis=-1,
    )


def geglu_act(gate_proj, up_proj):
    return jax.nn.gelu(gate_proj, approximate=True) * up_proj


def inner_rows(left, right):
    return lax.dot_general(
        left, right, (((0,), (0,)), ((), ())), preferred_element_type=jnp.float32
    )


def outer_cols(left, right):
    return lax.dot_general(
        left, right, (((1,), (1,)), ((), ())), preferred_element_type=jnp.float32
    )


def shards_plain(
    inputs,
    segments,
    cotangent,
    gain_attn_in,
    w_query,
    w_key,
    w_value,
    gain_query,
    gain_key,
    w_output,
    gain_attn_out,
    gain_ffn_in,
    w_gate,
    w_up,
    w_down,
    gain_ffn_out,
):
    rows_here = inputs.shape[1]
    head_width = w_key.shape[1]
    head_count = w_query.shape[1] // head_width
    reach_devs = (WINDOW - 2 + rows_here) // rows_here
    score_scale = head_width ** (-0.5)
    first_row = lax.axis_index("seq") * rows_here
    tokens = inputs[0].astype(jnp.float32)
    seg_here = segments[0]
    positions = first_row + jnp.arange(rows_here, dtype=jnp.int32)
    angles_at = angles(positions - seg_here, head_width)
    wq_all, wk_all, wv_all, wo_all, g_attn_in, g_query, g_key, g_attn_out, g_ffn_in, g_ffn_out = (
        lax.all_gather(w_query, "fsdp", axis=0, tiled=True),
        lax.all_gather(w_key, "fsdp", axis=0, tiled=True),
        lax.all_gather(w_value, "fsdp", axis=0, tiled=True),
        lax.all_gather(w_output, "fsdp", axis=0, tiled=True),
        lax.all_gather(gain_attn_in, "fsdp", axis=0, tiled=True),
        lax.all_gather(gain_query, "fsdp", axis=0, tiled=True),
        lax.all_gather(gain_key, "fsdp", axis=0, tiled=True),
        lax.all_gather(gain_attn_out, "fsdp", axis=0, tiled=True),
        lax.all_gather(gain_ffn_in, "fsdp", axis=0, tiled=True),
        lax.all_gather(gain_ffn_out, "fsdp", axis=0, tiled=True),
    )
    g_attn_in = g_attn_in.astype(jnp.float32)
    g_query = g_query.astype(jnp.float32)
    g_key = g_key.astype(jnp.float32)
    g_attn_out = g_attn_out.astype(jnp.float32)
    g_ffn_in = g_ffn_in.astype(jnp.float32)
    g_ffn_out = g_ffn_out.astype(jnp.float32)
    normed_one, pull_one = jax.vjp(norm_rows, tokens, g_attn_in)
    h_one = normed_one.astype(jnp.bfloat16)
    q_raw = jnp.dot(h_one, wq_all, preferred_element_type=jnp.float32)
    k_raw = jnp.dot(h_one, wk_all, preferred_element_type=jnp.float32)
    v_raw = jnp.dot(h_one, wv_all, preferred_element_type=jnp.float32)

    def prepare(q_in, k_in, gq_in, gk_in):
        q_rows = q_in.reshape(q_in.shape[0], head_count, head_width)
        q_fin = rotate(norm_rows(q_rows, gq_in), angles_at[:, None, :])
        k_fin = rotate(norm_rows(k_in, gk_in), angles_at)
        return (q_fin, k_fin)

    (q_fin, k_fin), pull_prep = jax.vjp(prepare, q_raw, k_raw, g_query, g_key)
    q_low = q_fin.astype(jnp.bfloat16).reshape(rows_here * head_count, head_width)
    k_low = k_fin.astype(jnp.bfloat16)
    v_low = v_raw.astype(jnp.bfloat16)
    key_parts = []
    value_parts = []
    seg_parts = []
    for offset in range(reach_devs, 0, -1):
        k_came, v_came, s_came = from_behind((k_low, v_low, seg_here), "seq", offset)
        key_parts.append(k_came)
        value_parts.append(v_came)
        seg_parts.append(s_came)
    key_rows = jnp.concatenate(key_parts + [k_low], axis=0)
    value_rows = jnp.concatenate(value_parts + [v_low], axis=0)
    key_segs = jnp.concatenate(seg_parts + [seg_here], axis=0)
    key_place = (
        first_row
        - reach_devs * rows_here
        + jnp.arange((reach_devs + 1) * rows_here, dtype=jnp.int32)
    )
    distance = positions[:, None] - key_place[None, :]
    allowed = (
        (distance >= 0)
        & (distance < WINDOW)
        & (key_place[None, :] >= 0)
        & (seg_here[:, None] == key_segs[None, :])
    )
    scores = (outer_cols(q_low, key_rows) * score_scale).reshape(rows_here, head_count, -1)
    masked = jnp.where(allowed[:, None, :], scores, masked_value)
    attn_probs = jax.nn.softmax(masked, axis=-1).reshape(rows_here * head_count, -1)
    probs_low = attn_probs.astype(jnp.bfloat16)
    attended = jnp.dot(probs_low, value_rows, preferred_element_type=jnp.float32)
    att_low = attended.reshape(rows_here, head_count * head_width).astype(jnp.bfloat16)
    o_raw = jnp.dot(att_low, wo_all, preferred_element_type=jnp.float32)
    branch_att, pull_att = jax.vjp(norm_rows, o_raw, g_attn_out)
    middle = tokens + branch_att
    normed_two, pull_mid = jax.vjp(norm_rows, middle, g_ffn_in)
    h_two = normed_two.astype(jnp.bfloat16)
    gate_all, up_all, down_all = (
        lax.all_gather(w_gate, "fsdp", axis=0, tiled=True),
        lax.all_gather(w_up, "fsdp", axis=0, tiled=True),
        lax.all_gather(w_down, "fsdp", axis=0, tiled=True),
    )
    gate_proj = jnp.dot(h_two, gate_all, preferred_element_type=jnp.float32)
    up_proj = jnp.dot(h_two, up_all, preferred_element_type=jnp.float32)
    act_full, pull_act = jax.vjp(geglu_act, gate_proj, up_proj)
    act_low = act_full.astype(jnp.bfloat16)
    f_raw = jnp.dot(act_low, down_all, preferred_element_type=jnp.float32)
    branch_ffn, pull_out = jax.vjp(norm_rows, f_raw, g_ffn_out)
    outputs = (middle + branch_ffn).astype(jnp.bfloat16)
    upstream = cotangent[0].astype(jnp.float32)
    d_fraw, d_gffn_out = pull_out(upstream)
    d_flow = d_fraw.astype(jnp.bfloat16)
    gate_shard, up_shard, down_shard, d_flow = lax.optimization_barrier(
        (w_gate, w_up, w_down, d_flow)
    )
    gate_back, up_back, down_back = (
        lax.all_gather(gate_shard, "fsdp", axis=0, tiled=True),
        lax.all_gather(up_shard, "fsdp", axis=0, tiled=True),
        lax.all_gather(down_shard, "fsdp", axis=0, tiled=True),
    )
    d_act = outer_cols(d_flow, down_back)
    d_gate, d_up = pull_act(d_act)
    dg_low = d_gate.astype(jnp.bfloat16)
    du_low = d_up.astype(jnp.bfloat16)
    d_htwo = outer_cols(dg_low, gate_back) + outer_cols(du_low, up_back)
    grad_down_part = lax.psum_scatter(
        inner_rows(act_low, d_flow).astype(jnp.bfloat16), "fsdp", scatter_dimension=0, tiled=True
    )
    grad_in_part = lax.psum_scatter(
        jnp.concatenate([inner_rows(h_two, dg_low), inner_rows(h_two, du_low)], axis=1).astype(
            jnp.bfloat16
        ),
        "fsdp",
        scatter_dimension=0,
        tiled=True,
    ).astype(jnp.float32)
    hidden_width = w_gate.shape[1]
    grad_gate_part = grad_in_part[:, :hidden_width]
    grad_up_part = grad_in_part[:, hidden_width:]
    d_mid_norm, d_gffn_in = pull_mid(d_htwo)
    d_middle = upstream + d_mid_norm
    d_oraw, d_gattn_out = pull_att(d_middle)
    d_olow = d_oraw.astype(jnp.bfloat16)
    grad_wo = inner_rows(att_low, d_olow)
    d_att_low = (
        outer_cols(d_olow, wo_all).astype(jnp.bfloat16).reshape(rows_here * head_count, head_width)
    )
    d_probs = outer_cols(d_att_low, value_rows)
    d_scores = attn_probs * (d_probs - jnp.sum(attn_probs * d_probs, axis=-1, keepdims=True))
    ds_low = d_scores.astype(jnp.bfloat16)
    d_qfin = jnp.dot(ds_low, key_rows, preferred_element_type=jnp.float32) * score_scale
    d_keys = inner_rows(ds_low, q_low) * score_scale
    d_values = inner_rows(probs_low, d_att_low)
    d_kfin = d_keys[reach_devs * rows_here :]
    d_vsum = d_values[reach_devs * rows_here :]
    for offset in range(1, reach_devs + 1):
        slot_index = reach_devs - offset
        k_back, v_back = (
            from_behind(
                d_keys[slot_index * rows_here : (slot_index + 1) * rows_here].astype(jnp.bfloat16),
                "seq",
                -offset,
            ).astype(jnp.float32),
            from_behind(
                d_values[slot_index * rows_here : (slot_index + 1) * rows_here].astype(
                    jnp.bfloat16
                ),
                "seq",
                -offset,
            ).astype(jnp.float32),
        )
        d_kfin = d_kfin + k_back
        d_vsum = d_vsum + v_back
    d_qraw, d_kraw, d_gquery, d_gkey = pull_prep(
        (d_qfin.reshape(rows_here, head_count, head_width), d_kfin)
    )
    dq_low = d_qraw.astype(jnp.bfloat16)
    dk_low = d_kraw.astype(jnp.bfloat16)
    dv_low = d_vsum.astype(jnp.bfloat16)
    d_hone = outer_cols(dq_low, wq_all) + outer_cols(dk_low, wk_all) + outer_cols(dv_low, wv_all)
    grad_wq = inner_rows(h_one, dq_low)
    grad_wk = inner_rows(h_one, dk_low)
    grad_wv = inner_rows(h_one, dv_low)
    d_tok_norm, d_gattn_in = pull_one(d_hone)
    d_inputs = d_middle + d_tok_norm
    part_wq, part_wk, part_wv, part_wo, part_gai, part_gq, part_gk, part_gao, part_gfi, part_gfo = (
        lax.psum_scatter(
            grad_wq.astype(jnp.bfloat16), "fsdp", scatter_dimension=0, tiled=True
        ).astype(jnp.float32),
        lax.psum_scatter(
            grad_wk.astype(jnp.bfloat16), "fsdp", scatter_dimension=0, tiled=True
        ).astype(jnp.float32),
        lax.psum_scatter(
            grad_wv.astype(jnp.bfloat16), "fsdp", scatter_dimension=0, tiled=True
        ).astype(jnp.float32),
        lax.psum_scatter(
            grad_wo.astype(jnp.bfloat16), "fsdp", scatter_dimension=0, tiled=True
        ).astype(jnp.float32),
        lax.psum_scatter(
            d_gattn_in.astype(jnp.bfloat16), "fsdp", scatter_dimension=0, tiled=True
        ).astype(jnp.float32),
        lax.psum_scatter(
            d_gquery.astype(jnp.bfloat16), "fsdp", scatter_dimension=0, tiled=True
        ).astype(jnp.float32),
        lax.psum_scatter(
            d_gkey.astype(jnp.bfloat16), "fsdp", scatter_dimension=0, tiled=True
        ).astype(jnp.float32),
        lax.psum_scatter(
            d_gattn_out.astype(jnp.bfloat16), "fsdp", scatter_dimension=0, tiled=True
        ).astype(jnp.float32),
        lax.psum_scatter(
            d_gffn_in.astype(jnp.bfloat16), "fsdp", scatter_dimension=0, tiled=True
        ).astype(jnp.float32),
        lax.psum_scatter(
            d_gffn_out.astype(jnp.bfloat16), "fsdp", scatter_dimension=0, tiled=True
        ).astype(jnp.float32),
    )
    cols_wq, cols_wk, cols_wv, cols_wo, cols_gate, cols_up, cols_down = (
        lax.psum_scatter(
            part_wq.astype(jnp.bfloat16), "seq", scatter_dimension=1, tiled=True
        ).astype(jnp.float32),
        lax.psum_scatter(
            part_wk.astype(jnp.bfloat16), "seq", scatter_dimension=1, tiled=True
        ).astype(jnp.float32),
        lax.psum_scatter(
            part_wv.astype(jnp.bfloat16), "seq", scatter_dimension=1, tiled=True
        ).astype(jnp.float32),
        lax.psum_scatter(
            part_wo.astype(jnp.bfloat16), "seq", scatter_dimension=1, tiled=True
        ).astype(jnp.float32),
        lax.psum_scatter(
            grad_gate_part.astype(jnp.bfloat16), "seq", scatter_dimension=1, tiled=True
        ).astype(jnp.float32),
        lax.psum_scatter(
            grad_up_part.astype(jnp.bfloat16), "seq", scatter_dimension=1, tiled=True
        ).astype(jnp.float32),
        lax.psum_scatter(grad_down_part, "seq", scatter_dimension=1, tiled=True).astype(
            jnp.float32
        ),
    )
    sum_wq, sum_wk, sum_wv, sum_wo, sum_gate, sum_up, sum_down = (
        lax.all_gather(cols_wq.astype(jnp.bfloat16), "seq", axis=1, tiled=True).astype(
            cols_wq.dtype
        ),
        lax.all_gather(cols_wk.astype(jnp.bfloat16), "seq", axis=1, tiled=True).astype(
            cols_wk.dtype
        ),
        lax.all_gather(cols_wv.astype(jnp.bfloat16), "seq", axis=1, tiled=True).astype(
            cols_wv.dtype
        ),
        lax.all_gather(cols_wo.astype(jnp.bfloat16), "seq", axis=1, tiled=True).astype(
            cols_wo.dtype
        ),
        lax.all_gather(cols_gate.astype(jnp.bfloat16), "seq", axis=1, tiled=True).astype(
            cols_gate.dtype
        ),
        lax.all_gather(cols_up.astype(jnp.bfloat16), "seq", axis=1, tiled=True).astype(
            cols_up.dtype
        ),
        lax.all_gather(cols_down.astype(jnp.bfloat16), "seq", axis=1, tiled=True).astype(
            cols_down.dtype
        ),
    )
    sum_gai, sum_gq, sum_gk, sum_gao, sum_gfi, sum_gfo = lax.psum(
        (part_gai, part_gq, part_gk, part_gao, part_gfi, part_gfo), "seq"
    )
    return (
        outputs[None],
        d_inputs[None],
        sum_gai,
        sum_wq,
        sum_wk,
        sum_wv,
        sum_gq,
        sum_gk,
        sum_wo,
        sum_gao,
        sum_gfi,
        sum_gate,
        sum_up,
        sum_down,
        sum_gfo,
    )


MESH = pl.DeviceIdType.MESH
BF16 = jnp.bfloat16
F32 = jnp.float32
GELU_RATE = 0.7978845608028654
GELU_CUBE = 0.044715
HID_TILE = 256
ATT_IN, ATT_OUT, FFN_IN, FFN_OUT, QUERY, KEY = range(6)


def bit_of(value, mask):
    return lax.rem(lax.div(value, mask), 2)


def flip(value, masks, bits):
    for b in range(bits):
        if (masks >> b) & 1:
            value = value + (1 << b) * (1 - 2 * bit_of(value, 1 << b))
    return value


def greet(devices):
    barrier = pltpu.get_barrier_semaphore()
    for device in devices:
        pl.semaphore_signal(barrier, inc=1, device_id=device, device_id_type=MESH)
    pl.semaphore_wait(barrier, len(devices))


def remote(src, dst, send, recv, device):
    return pltpu.make_async_remote_copy(
        src_ref=src, dst_ref=dst, send_sem=send, recv_sem=recv,
        device_id=device, device_id_type=MESH,
    )


def many(offset, size):
    return pl.ds(pl.multiple_of(offset, size if size % 128 == 0 else 16), size)


def lanes(offset, size):
    return pl.ds(pl.multiple_of(offset, 128), size)


def window_start(z, share):
    if isinstance(z, int):
        return z * share // 128 * 128
    return lax.div(z * share, 128) * 128


def window_width(share, n_fsdp):
    widest = max((z + 1) * share - window_start(z, share) for z in range(n_fsdp))
    return -(-widest // HID_TILE) * HID_TILE


def dot_nt(left, right):
    return lax.dot_general(left, right, (((1,), (1,)), ((), ())), preferred_element_type=F32)


def dot_nn(left, right):
    return jnp.dot(left, right, preferred_element_type=F32)


def norm_scale(rows_in):
    return lax.rsqrt(jnp.mean(rows_in * rows_in, axis=-1, keepdims=True) + epsilon)


def norm_back(rows_in, gain, scale, upstream):
    pulled = upstream * gain
    inner = jnp.mean(pulled * rows_in, axis=-1, keepdims=True)
    d_rows = scale * pulled - rows_in * (scale * scale * scale * inner)
    return d_rows, jnp.sum(upstream * rows_in * scale, axis=0, keepdims=True)


def turn(rows_in, cosine, sine_part):
    half = rows_in.shape[-1] // 2
    lower, upper = rows_in[:, :half], rows_in[:, half:]
    return jnp.concatenate(
        [lower * cosine - upper * sine_part, upper * cosine + lower * sine_part], axis=-1
    )


class Place:
    def __init__(self):
        self.s = lax.axis_index("seq")
        self.z = lax.axis_index("fsdp")
        self.c = bit_of(self.s, 1)
        self.x = bit_of(self.s, 2)
        self.y = bit_of(self.s, 4)

    def plane(self, masks):
        return (flip(self.s, masks, 3), self.z)

    def line(self, masks):
        return (self.s, flip(self.z, masks, 2))

    def halves(self, first_x):
        if first_x:
            return self.x, self.y, 2, 4
        return self.y, self.x, 4, 2


def layer_kernel(
    n_seq, n_fsdp, share, reach, head_count,
    x_ref, cot_ref, rates_ref, pack_ref, seg_ref,
    gate_ref, up_ref, wq_ref, wk_ref, wv_ref, wo_ref, wd_ref,
    out_ref, dx_out, gains_out, fin_gu, fin_d, fin_qkv, fin_wo,
    qkv_s, wo_s, w_in, w_down, pack_all, seg_all, gains, allowed, turns,
    h1_s, raw_s, q_s, kv_own, kv_s, p_s, att_s, o_s, mid_s,
    h_all, df_all, bent_s, act, d_in, h_turn, part_out, part_in, relay_in, total,
    own_d, own_g, own_o, own_q, hi_d, hi_g, hi_o, hi_q, lo_d, lo_g, lo_o, lo_q, line_o, line_q,
    do_s, datt_s, ds_s, dkv_s, dkv_send, dkv_came, dqkv_s, dgains, gain_in, gain_line,
    w_send, w_recv, own_sem, pack_send, pack_recv, seg_send, seg_recv, kv_send, kv_recv,
    ex_send, ex_recv, relay_sem, dkv_ssem, dkv_rsem,
    c_send, c_recv, hi_send, hi_recv, lo_send, lo_recv, z_send, z_recv, oq_send, oq_recv,
    put_sem, ag_send, ag_recv, gain_send, gain_recv,
):
    at = Place()
    s, z, c = at.s, at.z, at.c
    rows, width = x_ref.shape
    depth = width // n_fsdp
    hidden = w_in.shape[2]
    head_width = wk_ref.shape[1]
    query_width = head_count * head_width
    heads_width = query_width + 2 * head_width
    rows_o = wo_ref.shape[0]
    n_hid = hidden // HID_TILE
    third = width // 3
    middle_z = (z > 0) & (z < n_fsdp - 1)
    tokens = n_fsdp * rows

    def hid(n):
        return lanes(n * HID_TILE, HID_TILE)

    def outs(n):
        return lanes(n * third, third)

    skipped = z * share - window_start(z, share)
    spare = hidden - share
    if spare:
        w_down[pl.ds(0, spare)] = jnp.zeros((spare, width), BF16)
        w_down[pl.ds(share, spare)] = jnp.zeros((spare, width), BF16)
    here_z = many(z * depth, depth)
    own_copies = [
        pltpu.make_async_copy(src, dst, own_sem.at[i])
        for i, (src, dst) in enumerate((
            (wq_ref, qkv_s.at[here_z, pl.ds(0, query_width)]),
            (wk_ref, qkv_s.at[here_z, pl.ds(query_width, head_width)]),
            (wv_ref, qkv_s.at[here_z, pl.ds(query_width + head_width, head_width)]),
            (wo_ref, wo_s.at[many(z * rows_o, rows_o)]),
            (wd_ref, w_down.at[many(skipped, share)]),
            (gate_ref.at[:, lanes(window_start(z, share), hidden)], w_in.at[0, here_z]),
            (up_ref.at[:, lanes(window_start(z, share), hidden)], w_in.at[1, here_z]),
        ))
    ]
    seg_all[s] = jnp.broadcast_to(seg_ref[...], seg_all.shape[1:])
    pack_all[z] = jnp.broadcast_to(pack_ref[...], pack_all.shape[1:])
    greet([at.plane(k) for k in range(1, n_seq)] + [at.line(m) for m in range(1, n_fsdp)])

    packs = [
        remote(pack_all.at[z], pack_all.at[z], pack_send.at[m], pack_recv.at[m], at.line(m))
        for m in range(1, n_fsdp)
    ]
    seg_copies = [
        remote(seg_all.at[s], seg_all.at[s], seg_send.at[k], seg_recv.at[k], at.plane(k))
        for k in range(1, n_seq)
    ]
    kv_copies = [
        remote(kv_own, kv_s.at[reach - o], kv_send.at[o - 1], kv_recv.at[o - 1],
               (lax.rem(s + o, n_seq), z))
        for o in range(1, reach + 1)
    ]

    def w_region(kind, whose, hi, lo, level):
        base = whose * depth
        if kind == "q":
            cols = (
                lanes(hi * (query_width // 2) + lo * (query_width // 4), query_width // 4),
                lanes(hi * (query_width // 2), query_width // 2),
                pl.ds(0, query_width),
            )[level]
            return qkv_s.at[many(base + c * (depth // 2), depth // 2), cols]
        if kind == "kv":
            start = query_width + c * head_width
            if level == 0:
                start = start + lo * (head_width // 2)
            cols = lanes(start, head_width if level else head_width // 2)
            if level == 2:
                return qkv_s.at[many(base, depth), cols]
            return qkv_s.at[many(base + hi * (depth // 2), depth // 2), cols]
        if kind == "wo":
            start = whose * rows_o + c * (rows_o // 2)
            if level < 2:
                start = start + hi * (rows_o // 4)
            if level < 1:
                start = start + lo * (rows_o // 8)
            return wo_s.at[many(start, rows_o // (8, 4, 2)[level])]
        if level == 2:
            return w_in.at[c, many(base, depth)]
        here = many(base + hi * (depth // 2), depth // 2)
        if level == 1:
            return w_in.at[c, here]
        return w_in.at[c, here, lanes(lo * (hidden // 2), hidden // 2)]

    def w_sources(kind, to, hi, lo):
        if kind == "q":
            cols = lanes(hi * (query_width // 2) + lo * (query_width // 4), query_width // 4)
            return [wq_ref.at[many(c * (depth // 2), depth // 2), cols]]
        if kind == "wo":
            start = c * (rows_o // 2) + hi * (rows_o // 4) + lo * (rows_o // 8)
            return [wo_ref.at[many(start, rows_o // 8)]]
        here = many(hi * (depth // 2), depth // 2)
        if kind == "kv":
            cols = lanes(lo * (head_width // 2), head_width // 2)
            return [ref.at[here, cols] for ref in (wk_ref, wv_ref)]
        cols = lanes(window_start(to, share) + lo * (hidden // 2), hidden // 2)
        return [ref.at[here, cols] for ref in (gate_ref, up_ref)]

    items = []
    for kinds in (("q", "kv"), ("wo",), ("gu",)):
        for m in range(1, n_fsdp):
            for kind in kinds:
                items.append((kind, m, (m % 2 == 1) != (kind in ("kv", "wo"))))
    steps, starts = [], []
    for i, (kind, m, first_x) in enumerate(items):
        hi, lo, mask_hi, mask_lo = at.halves(first_x)
        there = flip(z, m, 2)
        firsts = [
            remote(src, w_region(kind, z, hi, lo, 0), w_send.at[i, 0], w_recv.at[i, 0], at.line(m))
            for src in w_sources(kind, there, hi, lo)
        ]
        starts.append(firsts)
        steps.append([firsts[0]] + [
            remote(w_region(kind, there, hi, lo, k), w_region(kind, there, hi, lo, k),
                   w_send.at[i, k + 1], w_recv.at[i, k + 1], at.plane(mask))
            for k, mask in enumerate((mask_lo, mask_hi, 1))
        ])

    def begin_weight(i):
        if len(starts[i]) == 1:
            starts[i][0].start()
        else:
            for core, first in enumerate(starts[i]):
                pl.when(c == core)(first.start)

    def move_weight(i, stage):
        steps[i][stage - 1].wait_recv()
        steps[i][stage].start()

    n_items = len(items)
    n_att = n_items - (n_fsdp - 1)
    n_qkv = 2 * (n_fsdp - 1)
    ahead, lag = 6, 3
    for copy in packs + seg_copies:
        copy.start()
    for i in range(ahead):
        begin_weight(i)
    for copy in own_copies:
        copy.start()

    for copy in seg_copies:
        copy.wait_recv()
    across = lax.broadcasted_iota(jnp.int32, (rows, rows), 0)
    along = lax.broadcasted_iota(jnp.int32, (rows, rows), 1)
    seg_here = jnp.broadcast_to(seg_ref[...].astype(F32), (rows, rows)).T
    for o in range(reach, -1, -1):
        key_seg = seg_all[lax.rem(s + n_seq - o, n_seq), 0:1, :].astype(F32)
        apart = across - along + o * rows
        fine = (apart >= 0) & (apart < WINDOW) & (seg_here == key_seg) & (s >= o)
        allowed[:, pl.ds((reach - o) * rows, rows)] = jnp.where(fine, 1.0, 0.0).astype(BF16)
    angle = ((s * rows + across).astype(F32) - seg_here) * rates_ref[...]
    turns[0] = jnp.cos(angle)
    turns[1] = jnp.sin(angle)
    for copy in packs:
        copy.wait_recv()
    gains[...] = jnp.zeros(gains.shape, F32)
    start = 0
    for row in range(6):
        size = (depth if row < QUERY else head_width // n_fsdp)
        for block in range(n_fsdp):
            gains[row : row + 1, block * size : (block + 1) * size] = pack_all[
                block, 0:1, start : start + size
            ]
        start += size

    def gain(row):
        return gains[row : row + 1, : (width if row < QUERY else head_width)]

    x = x_ref[...].astype(F32)
    h1_s[...] = (x * norm_scale(x) * gain(ATT_IN)).astype(BF16)

    for t in range(n_att + 2 * lag):
        for stage in (3, 2, 1):
            i = t - lag * (stage - 1)
            if 0 <= i < n_att:
                move_weight(i, stage)
                if stage == 1 and i + ahead < n_items:
                    begin_weight(i + ahead)
    for i in range(n_qkv):
        steps[i][3].wait_recv()
    for copy in own_copies[:3]:
        copy.wait()

    def move_gu(*moves):
        for m, stage in moves:
            move_weight(n_att + m - 1, stage)

    move_gu((1, 1))
    tile = heads_width // 3

    @pl.loop(0, 3)
    def _(n):
        cols = lanes(n * tile, tile)
        raw_s[:, cols] = dot_nn(h1_s[...], qkv_s[:, cols])

    k_raw = raw_s[:, query_width : query_width + head_width]
    kv_own[:, :head_width] = turn(
        k_raw * norm_scale(k_raw) * gain(KEY), turns[0], turns[1]
    ).astype(BF16)
    kv_own[:, head_width:] = raw_s[:, query_width + head_width :].astype(BF16)
    for copy in kv_copies:
        copy.start()
    kv_s[reach] = kv_own[...]
    for h in range(head_count):
        q_raw = raw_s[:, h * head_width : (h + 1) * head_width]
        q_fin = q_raw * norm_scale(q_raw) * gain(QUERY)
        q_s[h] = turn(q_fin, turns[0], turns[1]).astype(BF16)
    for i in range(n_qkv, n_att):
        steps[i][3].wait_recv()
    own_copies[3].wait()
    move_gu((2, 1), (1, 2))
    for copy in kv_copies:
        copy.wait_recv()

    def keys():
        return kv_s[:, :, :head_width].reshape((reach + 1) * rows, head_width)

    def values():
        return kv_s[:, :, head_width:].reshape((reach + 1) * rows, head_width)

    for h in range(head_count):
        scores = dot_nt(q_s[h], keys()) * (head_width**-0.5)
        masked = jnp.where(allowed[...].astype(F32) > 0.5, scores, masked_value)
        grown = jnp.exp(masked - jnp.max(masked, axis=-1, keepdims=True))
        probs = grown / jnp.sum(grown, axis=-1, keepdims=True)
        p_s[h] = probs.astype(BF16)
        att_s[:, h * head_width : (h + 1) * head_width] = dot_nn(p_s[h], values()).astype(BF16)
        move_gu((((3, 1),), ((2, 2),), ((1, 3),), ((3, 2),))[h][0])

    @pl.loop(0, 3)
    def _(n):
        o_s[:, outs(n)] = dot_nn(att_s[...], wo_s[:, outs(n)])

    o_raw = o_s[...]
    middle = x_ref[...].astype(F32) + o_raw * norm_scale(o_raw) * gain(ATT_OUT)
    mid_s[...] = middle
    h_all[0] = (middle * norm_scale(middle) * gain(FFN_IN)).astype(BF16)

    def exchange(phase, src, dst):
        return {
            m: remote(src(m), dst(m), ex_send.at[phase, m], ex_recv.at[phase, m], at.line(m))
            for m in range(1, n_fsdp)
        }

    last = n_fsdp - 1
    send_h = exchange(0, lambda m: h_all.at[0], lambda m: h_all.at[m])
    send_f = exchange(1, lambda m: part_out.at[m - 1], lambda m: part_in.at[0, m - 1])
    send_df = exchange(2, lambda m: df_all.at[0], lambda m: df_all.at[m])
    send_dh = exchange(3, lambda m: part_out.at[m - 1], lambda m: part_in.at[1, m - 1])
    onward = {
        phase: remote(rows_all.at[2], rows_all.at[last],
                      relay_sem.at[phase], ex_recv.at[phase, last], at.line(1))
        for phase, rows_all in ((0, h_all), (2, df_all))
    }
    by_way = {
        phase: remote(part_out.at[last - 1], relay_in.at[phase // 2],
                      relay_sem.at[phase], relay_sem.at[phase + 3], at.line(1))
        for phase in (1, 3)
    }

    def send_rows(copies):
        copies[1].start()
        copies[2].start()
        pl.when(middle_z)(copies[last].start)

    def relay_rows(copies, phase):
        copies[2].wait_recv()
        pl.when(middle_z)(onward[phase].start)

    def send_part(copies, phase, m):
        if m == 1:
            copies[1].start()
        elif m == 2:
            pl.when(~middle_z)(copies[2].start)
        else:
            pl.when(~middle_z)(by_way[phase].start)
            pl.when(middle_z)(copies[last].start)

    def send_joint_part(copies, phase):
        @pl.when(middle_z)
        def _():
            by_way[phase].wait_recv()
            part_out[1] = (
                part_out[1].astype(F32) + relay_in[phase // 2].astype(F32)
            ).astype(BF16)
            copies[2].start()

    def take_parts(copies):
        copies[1].wait_recv()
        copies[2].wait_recv()
        pl.when(middle_z)(copies[last].wait_recv)

    def rows_sent(copies, phase):
        copies[1].wait_send()
        copies[2].wait_send()

        @pl.when(middle_z)
        def _():
            copies[last].wait_send()
            onward[phase].wait_send()

    def parts_sent(copies, phase):
        copies[1].wait_send()
        copies[2].wait_send()
        pl.when(middle_z)(copies[last].wait_send)
        pl.when(~middle_z)(by_way[phase].wait_send)

    send_rows(send_h)

    @pl.when(~middle_z)
    def _():
        part_in[0, last - 1] = jnp.zeros((rows, width), BF16)
        part_in[1, last - 1] = jnp.zeros((rows, width), BF16)

    move_gu((2, 3))
    relay_rows(send_h, 0)
    move_gu((3, 3))
    for i in range(n_att, n_items):
        steps[i][3].wait_recv()
    for copy in own_copies[4:]:
        copy.wait()
    half_h = hidden // 2

    for m in (*range(1, n_fsdp), 0):
        if m not in (0, 2):
            send_h[m].wait_recv()
        for n in range(2):
            cols = slice(n * half_h, (n + 1) * half_h)
            gate = dot_nn(h_all[m], w_in[0, :, cols])
            up = dot_nn(h_all[m], w_in[1, :, cols])
            squared = gate * gate
            bent = jnp.tanh(GELU_RATE * (gate + GELU_CUBE * squared * gate))
            gelu = 0.5 * gate * (1.0 + bent)
            slope = 0.5 * (1.0 + bent) + 0.5 * gate * (1.0 - bent * bent) * (
                GELU_RATE * (1.0 + 3.0 * GELU_CUBE * squared)
            )
            bent_s[pl.ds(m * rows, rows), cols] = gelu.astype(BF16)
            bent_s[pl.ds(tokens + m * rows, rows), cols] = (slope * up).astype(BF16)
            act[m, :, cols] = (gelu * up).astype(BF16)
        part = dot_nn(act[m], w_down[...])
        if m:
            part_out[m - 1] = part.astype(BF16)
            send_part(send_f, 1, m)
        else:
            total[...] = part

    send_joint_part(send_f, 1)
    for m in range(n_fsdp):
        h_turn[:, pl.ds(m * rows, rows)] = h_all[m].T
    for i in range(n_att, n_items):
        for k in range(4):
            steps[i][k].wait_send()

    take_parts(send_f)
    f_raw = total[...]
    for m in range(1, n_fsdp):
        f_raw = f_raw + part_in[0, m - 1].astype(F32)
    cot = cot_ref[...].astype(F32)
    scale = norm_scale(f_raw)
    d_f, d_gain = norm_back(f_raw, gain(FFN_OUT), scale, cot)
    df_all[0] = d_f.astype(BF16)
    send_rows(send_df)
    out_ref[...] = (mid_s[...] + f_raw * scale * gain(FFN_OUT)).astype(BF16)
    dgains[...] = jnp.zeros(dgains.shape, F32)
    dgains[FFN_OUT : FFN_OUT + 1, :] = d_gain
    parts_sent(send_f, 1)

    chunks = [("d", 0, False), ("d", 1, True)]
    chunks += [("g", m, m % 2 == 0) for m in range(n_fsdp)]
    chunks += [("o", 0, False), ("q", 0, True)]
    tiles_d = hidden // 256
    spans_d = (pl.ds(0, n_fsdp), pl.ds(n_fsdp, tiles_d - n_fsdp))

    def mine_of(kind, i):
        if kind == "d":
            return own_d.at[spans_d[i]]
        return {"g": own_g, "o": own_o, "q": own_q}[kind].at[i]

    def hi_part(kind, hi):
        if kind == "d":
            return slice(None), many(hi * 64, 64), slice(None)
        if kind == "g":
            return many(hi * (depth // 2), depth // 2), slice(None)
        if kind == "q":
            return slice(None), lanes(hi * (heads_width // 2), heads_width // 2)
        return many(hi * (rows_o // 4), rows_o // 4), slice(None)

    def lo_part(kind, hi, lo):
        if kind == "d":
            return slice(None), many(hi * 64 + lo * 32, 32), slice(None)
        if kind == "g":
            return (
                many(hi * (depth // 2), depth // 2),
                lanes(lo * (hidden // 2), hidden // 2),
            )
        if kind == "q":
            start = hi * (heads_width // 2) + lo * (heads_width // 4)
            return slice(None), lanes(start, heads_width // 4)
        return many(hi * (rows_o // 4) + lo * (rows_o // 8), rows_o // 8), slice(None)

    def fin_part(kind, i, where, core):
        if kind == "d":
            return fin_d.at[core, spans_d[i], where[-2], :]
        rows_at, cols_at = where
        if kind == "g":
            return fin_gu.at[core, i, rows_at, cols_at]
        ref, base, size = {
            "q": (fin_qkv, core * (depth // 2), depth // 2),
            "o": (fin_wo, core * (rows_o // 2), rows_o // 2),
        }[kind]
        if isinstance(rows_at, slice):
            rows_at = many(base, size)
        else:
            rows_at = many(base + rows_at.start, rows_at.size)
        return ref.at[rows_at, cols_at]

    def add(ref, where, other):
        rows_at, cols_at = where
        start = 0 if isinstance(rows_at, slice) else rows_at.start
        slab = 16

        @pl.loop(0, other.shape[0] // slab)
        def _(n):
            here = pl.ds(pl.multiple_of(start + n * slab, slab), slab)
            there = pl.ds(pl.multiple_of(n * slab, slab), slab)
            ref[here, cols_at] = (
                ref[here, cols_at].astype(F32) + other[there, :].astype(F32)
            ).astype(BF16)

    whole = (slice(None), slice(None))
    from_hi = {"d": hi_d, "g": hi_g, "o": hi_o, "q": hi_q}
    from_lo = {"d": lo_d, "g": lo_g, "o": lo_o, "q": lo_q}
    his, los, lines = [], [], []
    for j, (kind, i, first_x) in enumerate(chunks):
        hi, lo, mask_hi, mask_lo = at.halves(first_x)
        mine = mine_of(kind, i)
        if kind == "q":
            parts = (
                own_q.at[:, :, hi_part(kind, 1 - hi)[1]], hi_q,
                own_q.at[:, :, lo_part(kind, hi, 1 - lo)[1]], lo_q,
            )
        else:
            slot = spans_d[i] if kind == "d" else i
            parts = (
                mine.at[hi_part(kind, 1 - hi)], from_hi[kind].at[slot],
                mine.at[lo_part(kind, hi, 1 - lo)], from_lo[kind].at[slot],
            )
        his.append(
            remote(parts[0], parts[1], hi_send.at[j], hi_recv.at[j], at.plane(mask_hi))
        )
        los.append(
            remote(parts[2], parts[3], lo_send.at[j], lo_recv.at[j], at.plane(mask_lo))
        )
        line = None
        if kind == "g" and i:
            line = remote(mine.at[lo_part(kind, hi, lo)],
                          fin_part(kind, z, lo_part(kind, hi, lo), c),
                          z_send.at[j], z_recv.at[j], at.line(i))
        lines.append(line)
    stage = {
        "d": lambda i: part_in.at[0] if i else h_all,
        "g": lambda i: bent_s.at[pl.ds(i * depth, depth)],
        "q": lambda i: w_in.at[0, pl.ds(i * (depth // 2), depth // 2), pl.ds(0, heads_width)],
        "o": lambda i: w_in.at[1, pl.ds(i * (rows_o // 2), rows_o // 2), pl.ds(0, width)],
    }
    to_core = [("d", 0), ("d", 1)]
    to_core += [(kind, m) for kind in "goq" for m in range(n_fsdp)]
    cores = {
        key: remote(stage[key[0]](key[1]), mine_of(*key), c_send.at[k], c_recv.at[k], at.plane(1))
        for k, key in enumerate(to_core)
    }
    line_sums = {}
    for k, (kind, ref) in enumerate((("o", line_o), ("q", line_q))):
        for m in range(1, n_fsdp):
            part = mine_of(kind, m)
            if kind == "q":
                part = part.at[lo_part(kind, at.x, at.y)]
            line_sums[kind, m] = remote(
                part, ref.at[m - 1], oq_send.at[k, m], oq_recv.at[k, m], at.line(m)
            )

    puts, hands = [], []
    for j, (kind, i, first_x) in enumerate(chunks):
        hi, lo, mask_hi, mask_lo = at.halves(first_x)
        which = flip(z, i, 2) if kind == "g" else i
        piece = fin_part(kind, which, lo_part(kind, hi, lo), c)
        half = fin_part(kind, which, hi_part(kind, hi), c)
        full = fin_part(kind, which, whole, c)
        put = None
        if lines[j] is None:
            put = pltpu.make_async_copy(
                mine_of(kind, i).at[lo_part(kind, hi, lo)], piece, put_sem.at[j]
            )
        puts.append(put)
        hands.append([
            remote(part, part, ag_send.at[j, k], ag_recv.at[j, k], at.plane(mask))
            for k, (part, mask) in enumerate(((piece, mask_lo), (half, mask_hi), (full, 1)))
        ])

    def add_all(kind, i, where, came):
        if kind == "d":
            for n in range(spans_d[i].start, spans_d[i].start + spans_d[i].size):
                add(own_d.at[n], where[1:], came.at[n])
        elif kind == "q":
            for m in range(n_fsdp):
                add(own_q.at[m], where, came.at[m])
        else:
            add(mine_of(kind, i), where, came.at[i])

    def take_hi(j):
        kind, i, first_x = chunks[j]
        hi, lo, _, _ = at.halves(first_x)
        his[j].wait_recv()
        add_all(kind, i, hi_part(kind, hi), from_hi[kind])
        los[j].start()

    def take_lo(j):
        kind, i, first_x = chunks[j]
        hi, lo, _, _ = at.halves(first_x)
        los[j].wait_recv()
        add_all(kind, i, lo_part(kind, hi, lo), from_lo[kind])
        if lines[j] is not None:
            lines[j].start()
        elif kind == "q":
            for m in range(1, n_fsdp):
                line_sums[kind, m].start()
        else:
            puts[j].start()

    def begin_hand(j):
        if lines[j] is not None:
            lines[j].wait_recv()
        else:
            puts[j].wait()
        hands[j][0].start()

    def hand_on(j, k):
        hands[j][k - 1].wait_recv()
        hands[j][k].start()

    def down_stage(n):
        return h_all.at[n] if n < n_fsdp else part_in.at[0, n - n_fsdp]

    def down_grads(core, dst_of, adds):
        right = df_all[...].reshape(tokens, width)
        for n in range(tiles_d):
            left = act[:, :, lanes(core * (hidden // 2) + n * 128, 128)].reshape(tokens, 128).T
            grads = dot_nn(left, right)
            dst = dst_of[n] if adds else dst_of(n)
            if adds:
                grads = grads + dst[...].astype(F32)
            dst[...] = grads.astype(BF16)

    def in_grads(core, m, dst, adds):
        left_at = many(flip(z, m, 2) * depth, depth)

        for n in range(2):
            cols = slice(n * half_h, (n + 1) * half_h)
            grads = dot_nn(h_turn[left_at, :], d_in[core, :, :, cols].reshape(tokens, half_h))
            if adds:
                grads = grads + dst[:, cols].astype(F32)
            dst[:, cols] = grads.astype(BF16)

    rows_sent(send_h, 0)
    for m in range(n_fsdp):
        if m == 1:
            relay_rows(send_df, 2)
        if m not in (0, 2):
            send_df[m].wait_recv()
        if m == last:
            down_grads(1 - c, down_stage, False)
            cores["d", 0].start()
            cores["d", 1].start()
        for n in range(2):
            cols = slice(n * half_h, (n + 1) * half_h)
            d_act = dot_nt(df_all[m], w_down[cols, :])
            slope = bent_s[pl.ds(tokens + m * rows, rows), cols].astype(F32)
            d_in[0, m, :, cols] = (d_act * slope).astype(BF16)
            gelu = bent_s[pl.ds(m * rows, rows), cols].astype(F32)
            d_in[1, m, :, cols] = (d_act * gelu).astype(BF16)
        part = dot_nt(d_in[0, m], w_in[0]) + dot_nt(d_in[1, m], w_in[1])
        if m:
            part_out[m - 1] = part.astype(BF16)
            send_part(send_dh, 3, m)
        else:
            total[...] = part

    cores["d", 0].wait_recv()
    cores["d", 1].wait_recv()
    down_grads(c, own_d.at, True)
    his[0].start()
    his[1].start()
    send_joint_part(send_dh, 3)
    for m in range(n_fsdp):
        in_grads(1 - c, m, stage["g"](m), False)
        cores["g", m].start()
    for m in range(n_fsdp):
        cores["g", m].wait_recv()
        in_grads(c, m, own_g.at[m], True)
        his[2 + m].start()

    dkv_copies = [
        remote(dkv_send.at[reach - o], dkv_came.at[o - 1], dkv_ssem.at[o - 1], dkv_rsem.at[o - 1],
               (lax.rem(s + n_seq - o, n_seq), z))
        for o in range(1, reach + 1)
    ]
    gain_copies = [
        remote(dgains, gain_in.at[k], gain_send.at[k], gain_recv.at[k], at.plane(k))
        for k in range(1, n_seq)
    ]
    gain_lines = [
        remote(gain_line.at[0], gain_line.at[m], gain_send.at[n_seq + m], gain_recv.at[n_seq + m],
               at.line(m))
        for m in range(1, n_fsdp)
    ]

    def to_middle():
        take_parts(send_dh)
        dh = total[...]
        for m in range(1, n_fsdp):
            dh = dh + part_in[1, m - 1].astype(F32)
        mid = mid_s[...]
        d_mid, d_gain = norm_back(mid, gain(FFN_IN), norm_scale(mid), dh)
        d_mid = d_mid + cot_ref[...].astype(F32)
        mid_s[...] = d_mid
        dgains[FFN_IN : FFN_IN + 1, :] = d_gain
        o_raw = o_s[...]
        d_o, d_gain = norm_back(o_raw, gain(ATT_OUT), norm_scale(o_raw), d_mid)
        dgains[ATT_OUT : ATT_OUT + 1, :] = d_gain
        do_s[...] = d_o.astype(BF16)
        for h in range(head_count):
            here = pl.ds(h * head_width, head_width)
            datt_s[h] = dot_nt(do_s[...], wo_s[here, :]).astype(BF16)

    def unturn(rows_in):
        return turn(rows_in, turns[0], -turns[1])

    def through_head(h):
        probs = p_s[h].astype(F32)
        d_att = datt_s[h]
        d_probs = dot_nt(d_att, values())
        d_scores = probs * (d_probs - jnp.sum(probs * d_probs, axis=-1, keepdims=True))
        ds_low = d_scores.astype(BF16)
        scale = head_width**-0.5
        ds_s[h] = ds_low
        cols = slice(h * head_width, (h + 1) * head_width)
        q_raw = raw_s[:, cols]
        d_q, d_gain = norm_back(
            q_raw, gain(QUERY), norm_scale(q_raw), unturn(dot_nn(ds_low, keys()) * scale)
        )
        dqkv_s[:, cols] = d_q.astype(BF16)
        dgains[QUERY : QUERY + 1, :head_width] += d_gain

    def return_keys():
        for side, left, right, scale in (
            (0, ds_s, q_s, head_width**-0.5),
            (1, p_s, datt_s, 1.0),
        ):
            cols = slice(side * head_width, (side + 1) * head_width)
            d_side = scale * inner_rows(
                left[...].reshape(head_count * rows, (reach + 1) * rows),
                right[...].reshape(head_count * rows, head_width),
            )
            for b in range(reach):
                dkv_send[b, :, cols] = d_side[b * rows : (b + 1) * rows].astype(BF16)
            dkv_s[:, cols] = d_side[reach * rows :]
        for copy in dkv_copies:
            copy.start()

    def grad_tiles(left_at, turned, right, n_cols, dst, adds):
        tile = n_cols // 3
        for k in range(3):
            grads = dot_nn(turned[left_at, :], right[:, k * tile : (k + 1) * tile])
            if adds:
                grads = grads + dst[:, k * tile : (k + 1) * tile].astype(F32)
            dst[:, k * tile : (k + 1) * tile] = grads.astype(BF16)

    def core_grads(kind, turned, right, span, n_cols):
        for m in range(n_fsdp):
            start = flip(z, m, 2) * span + (1 - c) * (span // 2)
            grad_tiles(many(start, span // 2), turned, right, n_cols, stage[kind](m), False)
            cores[kind, m].start()
        for m in list(range(1, n_fsdp)) + [0]:
            start = flip(z, m, 2) * span + c * (span // 2)
            cores[kind, m].wait_recv()
            grad_tiles(many(start, span // 2), turned, right, n_cols, mine_of(kind, m), True)
            if m and kind == "o":
                line_sums[kind, m].start()
        if kind == "q":
            his[-1].start()

    def output_grads():
        h_turn[pl.ds(0, query_width), pl.ds(0, rows)] = att_s[...].T
        core_grads("o", h_turn.at[:, pl.ds(0, rows)], do_s, rows_o, width)

    def key_grads():
        h_turn[:, pl.ds(rows, rows)] = h1_s[...].T
        d_kv = dkv_s[...]
        for o in range(reach):
            dkv_copies[o].wait_recv()
            d_kv = d_kv + dkv_came[o].astype(F32)
        k_raw = raw_s[:, query_width : query_width + head_width]
        d_k, d_gain = norm_back(
            k_raw, gain(KEY), norm_scale(k_raw), unturn(d_kv[:, :head_width])
        )
        dqkv_s[:, query_width : query_width + head_width] = d_k.astype(BF16)
        dqkv_s[:, query_width + head_width :] = d_kv[:, head_width:].astype(BF16)
        dgains[KEY : KEY + 1, :head_width] = d_gain
        core_grads("q", h_turn.at[:, pl.ds(rows, rows)], dqkv_s, depth, heads_width)

    def sum_line(j):
        kind = chunks[j][0]
        where = lo_part(kind, at.x, at.y) if kind == "q" else whole
        for m in range(1, n_fsdp):
            line_sums[kind, m].wait_recv()
            add(mine_of(kind, 0), where, {"o": line_o, "q": line_q}[kind].at[m - 1])
        (puts if kind == "q" else his)[j].start()

    def to_input():
        x = x_ref[...].astype(F32)
        d_h = dot_nt(dqkv_s[...], qkv_s[...])
        d_x, d_gain = norm_back(x, gain(ATT_IN), norm_scale(x), d_h)
        dx_out[...] = mid_s[...] + d_x
        dgains[ATT_IN : ATT_IN + 1, :] = d_gain
        for copy in gain_copies:
            copy.start()

    def sum_gains():
        sums = dgains[...]
        for k, copy in enumerate(gain_copies):
            copy.wait_recv()
            sums = sums + gain_in[k + 1]
        gain_line[0] = sums
        for copy in gain_lines:
            copy.start()

    take_hi(0)
    take_hi(1)
    to_middle()
    through_head(0)
    through_head(1)
    take_hi(2)
    take_hi(3)
    take_lo(0)
    take_lo(1)
    begin_hand(0)
    begin_hand(1)
    through_head(2)
    through_head(3)
    return_keys()
    output_grads()
    take_hi(4)
    take_hi(5)
    take_lo(2)
    take_lo(3)
    key_grads()
    begin_hand(2)
    hand_on(0, 1)
    hand_on(1, 1)
    take_lo(4)
    take_lo(5)
    begin_hand(3)
    to_input()
    hand_on(0, 2)
    hand_on(1, 2)
    sum_line(6)
    hand_on(2, 1)
    begin_hand(4)
    begin_hand(5)
    take_hi(7)
    hand_on(3, 1)
    hand_on(2, 2)
    sum_gains()
    take_hi(6)
    take_lo(7)
    hand_on(4, 1)
    hand_on(5, 1)
    hand_on(3, 2)
    take_lo(6)
    begin_hand(6)
    sum_line(7)
    begin_hand(7)
    hand_on(6, 1)
    hand_on(4, 2)
    hand_on(5, 2)
    hand_on(7, 1)
    hand_on(6, 2)
    hand_on(7, 2)
    sums = gain_line[0]
    for m, copy in enumerate(gain_lines):
        copy.wait_recv()
        sums = sums + gain_line[m + 1]
    gains_out[...] = sums

    for j in range(len(chunks)):
        hands[j][2].wait_recv()
        for k in range(3):
            hands[j][k].wait_send()
        his[j].wait_send()
        los[j].wait_send()
        if lines[j] is not None:
            lines[j].wait_send()
    for copy in list(cores.values()) + list(line_sums.values()):
        copy.wait_send()
    for copy in gain_copies + gain_lines + dkv_copies + kv_copies + packs + seg_copies:
        copy.wait_send()
    for i in range(n_att):
        for k in range(4):
            steps[i][k].wait_send()
    rows_sent(send_df, 2)
    parts_sent(send_dh, 3)


def layer(n_seq, n_fsdp, share, hidden, reach, head_count, x, cot, rates, pack, segs,
          w_gate, w_up, w_query, w_key, w_value, w_output, w_down):
    rows, width = x.shape
    depth = width // n_fsdp
    head_width = w_key.shape[1]
    query_width = w_query.shape[1]
    heads_width = query_width + 2 * head_width
    rows_o = w_output.shape[0]
    n_items = 4 * (n_fsdp - 1)
    anywhere = pl.BlockSpec(memory_space=pl.ANY)
    in_vmem = pl.BlockSpec(memory_space=pltpu.VMEM)
    shape = jax.ShapeDtypeStruct
    sems = pltpu.SemaphoreType.DMA

    def low(*size):
        return pltpu.VMEM(size, BF16)

    def full(*size):
        return pltpu.VMEM(size, F32)

    return pl.pallas_call(
        functools.partial(layer_kernel, n_seq, n_fsdp, share, reach, head_count),
        out_shape=[
            shape((rows, width), BF16),
            shape((rows, width), F32),
            shape((8, width), F32),
            shape((2, n_fsdp, depth, hidden), BF16),
            shape((2, hidden // 256, 128, width), BF16),
            shape((depth, heads_width), BF16),
            shape((rows_o, width), BF16),
        ],
        in_specs=[in_vmem] * 5 + [anywhere] * 7,
        out_specs=[in_vmem] * 3 + [anywhere] * 4,
        scratch_shapes=[
            low(width, heads_width),
            low(n_fsdp * rows_o, width),
            low(2, width, hidden),
            low(hidden, width),
            full(n_fsdp, 8, pack.shape[1]),
            pltpu.VMEM((n_seq, 8, rows), jnp.int32),
            full(8, width),
            low(rows, (reach + 1) * rows),
            full(2, rows, head_width // 2),
            low(rows, width),
            full(rows, heads_width),
            low(head_count, rows, head_width),
            low(rows, 2 * head_width),
            low(reach + 1, rows, 2 * head_width),
            low(head_count, rows, (reach + 1) * rows),
            low(rows, query_width),
            full(rows, width),
            full(rows, width),
            low(n_fsdp, rows, width),
            low(n_fsdp, rows, width),
            low(max(width, 2 * n_fsdp * rows), hidden),
            low(n_fsdp, rows, hidden),
            low(2, n_fsdp, rows, hidden),
            low(width, n_fsdp * rows),
            low(n_fsdp - 1, rows, width),
            low(2, n_fsdp - 1, rows, width),
            low(2, rows, width),
            full(rows, width),
            low(hidden // 256, 128, width),
            low(n_fsdp, depth, hidden),
            low(n_fsdp, rows_o // 2, width),
            low(n_fsdp, depth // 2, heads_width),
            low(hidden // 256, 64, width),
            low(n_fsdp, depth // 2, hidden),
            low(1, rows_o // 4, width),
            low(n_fsdp, depth // 2, heads_width // 2),
            low(hidden // 256, 32, width),
            low(n_fsdp, depth // 2, hidden // 2),
            low(1, rows_o // 8, width),
            low(n_fsdp, depth // 2, heads_width // 4),
            low(n_fsdp - 1, rows_o // 2, width),
            low(n_fsdp - 1, depth // 2, heads_width // 4),
            low(rows, width),
            low(head_count, rows, head_width),
            low(head_count, rows, (reach + 1) * rows),
            full(rows, 2 * head_width),
            low(reach, rows, 2 * head_width),
            low(reach, rows, 2 * head_width),
            low(rows, heads_width),
            full(8, width),
            full(n_seq, 8, width),
            full(n_fsdp, 8, width),
            sems((n_items, 4)),
            sems((n_items, 4)),
            sems((7,)),
            sems((n_fsdp,)),
            sems((n_fsdp,)),
            sems((n_seq,)),
            sems((n_seq,)),
            sems((reach,)),
            sems((reach,)),
            sems((4, n_fsdp)),
            sems((4, n_fsdp)),
            sems((7,)),
            sems((reach,)),
            sems((reach,)),
            sems((2 + 3 * n_fsdp,)),
            sems((2 + 3 * n_fsdp,)),
            sems((4 + n_fsdp,)),
            sems((4 + n_fsdp,)),
            sems((4 + n_fsdp,)),
            sems((4 + n_fsdp,)),
            sems((4 + n_fsdp,)),
            sems((4 + n_fsdp,)),
            sems((2, n_fsdp)),
            sems((2, n_fsdp)),
            sems((4 + n_fsdp,)),
            sems((4 + n_fsdp, 3)),
            sems((4 + n_fsdp, 3)),
            sems((n_seq + n_fsdp,)),
            sems((n_seq + n_fsdp,)),
        ],
        compiler_params=pltpu.CompilerParams(
            collective_id=0, has_side_effects=True, vmem_limit_bytes=63 << 20
        ),
        name="decoder_layer",
    )(x, cot, rates, pack, segs, w_gate, w_up, w_query, w_key, w_value, w_output, w_down)


def join_kernel(share, wins_ref, gate_ref, up_ref):
    n_win, hidden = wins_ref.shape[1], wins_ref.shape[3]
    starts = [window_start(i, share) for i in range(n_win)]
    for i, ref in enumerate((gate_ref, up_ref)):
        for w in range(n_win):
            first = starts[w]
            last = starts[w + 1] if w + 1 < n_win else first + hidden
            shared = starts[w - 1] + hidden - first if w else 0
            if shared:
                ref[:, first : first + shared] = wins_ref[i, w, :, :shared].astype(F32) + wins_ref[
                    i, w - 1, :, hidden - shared :
                ].astype(F32)
            ref[:, first + shared : last] = wins_ref[i, w, :, shared : last - first].astype(F32)


def joined(share, windows):
    _, n_win, rows, hidden = windows.shape
    slab = 32
    wide = pl.BlockSpec((slab, n_win * share), lambda i: (i, 0))
    return pl.pallas_call(
        functools.partial(join_kernel, share),
        grid=(rows // slab,),
        out_shape=[jax.ShapeDtypeStruct((rows, n_win * share), F32)] * 2,
        in_specs=[pl.BlockSpec((2, n_win, slab, hidden), lambda i: (0, 0, i, 0))],
        out_specs=[wide, wide],
        compiler_params=pltpu.CompilerParams(vmem_limit_bytes=32 << 20),
        name="join_windows",
    )(windows)


def shards(n_seq, n_fsdp, *args):
    w_query, w_key, w_output, w_gate = args[4], args[5], args[9], args[12]
    depth, ffn_width = w_gate.shape
    rows_here = args[0].shape[1]
    share = ffn_width // n_fsdp
    reach = (WINDOW - 2 + rows_here) // rows_here
    fits = (
        n_seq == 8
        and n_fsdp == 4
        and args[0].shape[0] == 1
        and reach < n_seq
        and rows_here == 128
        and window_width(share, n_fsdp) == 256 * (2 * n_fsdp - 1)
        and depth % 32 == 0
        and w_output.shape[0] % 128 == 0
        and w_key.shape[1] % 256 == 0
        and w_query.shape[1] % 512 == 0
        and w_output.shape[1] % 384 == 0
        and ffn_width % n_fsdp == 0
        and share % 16 == 0
        and window_start(n_fsdp - 1, share) + window_width(share, n_fsdp) == ffn_width
    )
    if fits:
        return shards_fused(n_seq, n_fsdp, *args)
    return shards_plain(*args)


def shards_fused(
    n_seq,
    n_fsdp,
    inputs,
    segments,
    cotangent,
    gain_attn_in,
    w_query,
    w_key,
    w_value,
    gain_query,
    gain_key,
    w_output,
    gain_attn_out,
    gain_ffn_in,
    w_gate,
    w_up,
    w_down,
    gain_ffn_out,
):
    rows_here, width = inputs.shape[1:]
    head_width = w_key.shape[1]
    query_width = w_query.shape[1]
    head_count = query_width // head_width
    share = w_gate.shape[1] // n_fsdp
    hidden = window_width(share, n_fsdp)
    reach = (WINDOW - 2 + rows_here) // rows_here
    line = lax.axis_index("fsdp")
    gains = (gain_attn_in, gain_attn_out, gain_ffn_in, gain_ffn_out, gain_query, gain_key)
    pack = jnp.concatenate(gains).astype(F32)[None]
    rates = 10000.0 ** (-(jnp.arange(head_width // 2, dtype=F32) * 2.0) / head_width)
    outputs, d_inputs, gain_sums, fin_gu, fin_d, fin_qkv, fin_wo = layer(
        n_seq, n_fsdp, share, hidden, reach, head_count,
        inputs[0], cotangent[0], rates[None], pack, segments,
        w_gate, w_up, w_query, w_key, w_value, w_output, w_down,
    )
    grad_gate, grad_up = joined(share, fin_gu)
    skipped = line * share - window_start(line, share)
    grad_down = lax.dynamic_slice(fin_d.reshape(hidden, width), (skipped, jnp.int32(0)), (share, width)).astype(F32)

    def part(row, gain):
        size = gain.shape[0]
        return lax.dynamic_slice(gain_sums[row], (line * size,), (size,))

    fin_qkv = fin_qkv.astype(F32)
    return (
        outputs[None],
        d_inputs[None],
        part(ATT_IN, gain_attn_in),
        fin_qkv[:, :query_width],
        fin_qkv[:, query_width : query_width + head_width],
        fin_qkv[:, query_width + head_width :],
        part(QUERY, gain_query),
        part(KEY, gain_key),
        fin_wo.astype(F32),
        part(ATT_OUT, gain_attn_out),
        part(FFN_IN, gain_ffn_in),
        grad_gate,
        grad_up,
        grad_down,
        part(FFN_OUT, gain_ffn_out),
    )


def solution(mesh):
    placed = (
        P("fsdp", "seq", None),
        P("fsdp", "seq"),
        P("fsdp", "seq", None),
        P("fsdp"),
        P("fsdp", None),
        P("fsdp", None),
        P("fsdp", None),
        P("fsdp"),
        P("fsdp"),
        P("fsdp", None),
        P("fsdp"),
        P("fsdp"),
        P("fsdp", None),
        P("fsdp", None),
        P("fsdp", None),
        P("fsdp"),
    )
    return jax.shard_map(
        functools.partial(shards, mesh.shape["seq"], mesh.shape["fsdp"]),
        mesh=mesh,
        in_specs=placed,
        out_specs=(
            P("fsdp", "seq", None),
            P("fsdp", "seq", None),
            P("fsdp"),
            P("fsdp", None),
            P("fsdp", None),
            P("fsdp", None),
            P("fsdp"),
            P("fsdp"),
            P("fsdp", None),
            P("fsdp"),
            P("fsdp"),
            P("fsdp", None),
            P("fsdp", None),
            P("fsdp", None),
            P("fsdp"),
        ),
        check_vma=False,
    )
```

```python
import functools

import jax
import jax.numpy as jnp
import numpy as np
from jax import lax
from jax.experimental import pallas as pl
from jax.experimental.pallas import tpu as pltpu
from jax.sharding import PartitionSpec as P

WINDOW = 512


epsilon = 1e-06
masked_value = -1e30


def from_behind(block, axis, distance):
    devices = range(lax.axis_size(axis))
    route = [(i - distance, i) for i in devices if i - distance in devices]
    return lax.ppermute(block, axis, route)


def norm_rows(rows_in, gain_vec):
    return (
        rows_in
        * lax.rsqrt(jnp.mean(rows_in * rows_in, axis=-1, keepdims=True) + epsilon)
        * gain_vec
    )


def angles(positions, head_width):
    inv_rates = 10000.0 ** (-(jnp.arange(head_width // 2, dtype=jnp.float32) * 2.0) / head_width)
    return positions.astype(jnp.float32)[:, None] * inv_rates[None, :]


def rotate(rows_in, angles_at):
    half_width = rows_in.shape[-1] // 2
    lower_half = rows_in[..., :half_width]
    upper_half = rows_in[..., half_width:]
    cosine = jnp.cos(angles_at)
    sine_part = jnp.sin(angles_at)
    return jnp.concatenate(
        [
            lower_half * cosine - upper_half * sine_part,
            upper_half * cosine + lower_half * sine_part,
        ],
        axis=-1,
    )


def geglu_act(gate_proj, up_proj):
    return jax.nn.gelu(gate_proj, approximate=True) * up_proj


def inner_rows(left, right):
    return lax.dot_general(
        left, right, (((0,), (0,)), ((), ())), preferred_element_type=jnp.float32
    )


def outer_cols(left, right):
    return lax.dot_general(
        left, right, (((1,), (1,)), ((), ())), preferred_element_type=jnp.float32
    )


def shards_plain(
    inputs,
    segments,
    cotangent,
    gain_attn_in,
    w_query,
    w_key,
    w_value,
    gain_query,
    gain_key,
    w_output,
    gain_attn_out,
    gain_ffn_in,
    w_gate,
    w_up,
    w_down,
    gain_ffn_out,
):
    rows_here = inputs.shape[1]
    head_width = w_key.shape[1]
    head_count = w_query.shape[1] // head_width
    reach_devs = (WINDOW - 2 + rows_here) // rows_here
    score_scale = head_width ** (-0.5)
    first_row = lax.axis_index("seq") * rows_here
    tokens = inputs[0].astype(jnp.float32)
    seg_here = segments[0]
    positions = first_row + jnp.arange(rows_here, dtype=jnp.int32)
    angles_at = angles(positions - seg_here, head_width)
    wq_all, wk_all, wv_all, wo_all, g_attn_in, g_query, g_key, g_attn_out, g_ffn_in, g_ffn_out = (
        lax.all_gather(w_query, "fsdp", axis=0, tiled=True),
        lax.all_gather(w_key, "fsdp", axis=0, tiled=True),
        lax.all_gather(w_value, "fsdp", axis=0, tiled=True),
        lax.all_gather(w_output, "fsdp", axis=0, tiled=True),
        lax.all_gather(gain_attn_in, "fsdp", axis=0, tiled=True),
        lax.all_gather(gain_query, "fsdp", axis=0, tiled=True),
        lax.all_gather(gain_key, "fsdp", axis=0, tiled=True),
        lax.all_gather(gain_attn_out, "fsdp", axis=0, tiled=True),
        lax.all_gather(gain_ffn_in, "fsdp", axis=0, tiled=True),
        lax.all_gather(gain_ffn_out, "fsdp", axis=0, tiled=True),
    )
    g_attn_in = g_attn_in.astype(jnp.float32)
    g_query = g_query.astype(jnp.float32)
    g_key = g_key.astype(jnp.float32)
    g_attn_out = g_attn_out.astype(jnp.float32)
    g_ffn_in = g_ffn_in.astype(jnp.float32)
    g_ffn_out = g_ffn_out.astype(jnp.float32)
    normed_one, pull_one = jax.vjp(norm_rows, tokens, g_attn_in)
    h_one = normed_one.astype(jnp.bfloat16)
    q_raw = jnp.dot(h_one, wq_all, preferred_element_type=jnp.float32)
    k_raw = jnp.dot(h_one, wk_all, preferred_element_type=jnp.float32)
    v_raw = jnp.dot(h_one, wv_all, preferred_element_type=jnp.float32)

    def prepare(q_in, k_in, gq_in, gk_in):
        q_rows = q_in.reshape(q_in.shape[0], head_count, head_width)
        q_fin = rotate(norm_rows(q_rows, gq_in), angles_at[:, None, :])
        k_fin = rotate(norm_rows(k_in, gk_in), angles_at)
        return (q_fin, k_fin)

    (q_fin, k_fin), pull_prep = jax.vjp(prepare, q_raw, k_raw, g_query, g_key)
    q_low = q_fin.astype(jnp.bfloat16).reshape(rows_here * head_count, head_width)
    k_low = k_fin.astype(jnp.bfloat16)
    v_low = v_raw.astype(jnp.bfloat16)
    key_parts = []
    value_parts = []
    seg_parts = []
    for offset in range(reach_devs, 0, -1):
        k_came, v_came, s_came = from_behind((k_low, v_low, seg_here), "seq", offset)
        key_parts.append(k_came)
        value_parts.append(v_came)
        seg_parts.append(s_came)
    key_rows = jnp.concatenate(key_parts + [k_low], axis=0)
    value_rows = jnp.concatenate(value_parts + [v_low], axis=0)
    key_segs = jnp.concatenate(seg_parts + [seg_here], axis=0)
    key_place = (
        first_row
        - reach_devs * rows_here
        + jnp.arange((reach_devs + 1) * rows_here, dtype=jnp.int32)
    )
    distance = positions[:, None] - key_place[None, :]
    allowed = (
        (distance >= 0)
        & (distance < WINDOW)
        & (key_place[None, :] >= 0)
        & (seg_here[:, None] == key_segs[None, :])
    )
    scores = (outer_cols(q_low, key_rows) * score_scale).reshape(rows_here, head_count, -1)
    masked = jnp.where(allowed[:, None, :], scores, masked_value)
    attn_probs = jax.nn.softmax(masked, axis=-1).reshape(rows_here * head_count, -1)
    probs_low = attn_probs.astype(jnp.bfloat16)
    attended = jnp.dot(probs_low, value_rows, preferred_element_type=jnp.float32)
    att_low = attended.reshape(rows_here, head_count * head_width).astype(jnp.bfloat16)
    o_raw = jnp.dot(att_low, wo_all, preferred_element_type=jnp.float32)
    branch_att, pull_att = jax.vjp(norm_rows, o_raw, g_attn_out)
    middle = tokens + branch_att
    normed_two, pull_mid = jax.vjp(norm_rows, middle, g_ffn_in)
    h_two = normed_two.astype(jnp.bfloat16)
    gate_all, up_all, down_all = (
        lax.all_gather(w_gate, "fsdp", axis=0, tiled=True),
        lax.all_gather(w_up, "fsdp", axis=0, tiled=True),
        lax.all_gather(w_down, "fsdp", axis=0, tiled=True),
    )
    gate_proj = jnp.dot(h_two, gate_all, preferred_element_type=jnp.float32)
    up_proj = jnp.dot(h_two, up_all, preferred_element_type=jnp.float32)
    act_full, pull_act = jax.vjp(geglu_act, gate_proj, up_proj)
    act_low = act_full.astype(jnp.bfloat16)
    f_raw = jnp.dot(act_low, down_all, preferred_element_type=jnp.float32)
    branch_ffn, pull_out = jax.vjp(norm_rows, f_raw, g_ffn_out)
    outputs = (middle + branch_ffn).astype(jnp.bfloat16)
    upstream = cotangent[0].astype(jnp.float32)
    d_fraw, d_gffn_out = pull_out(upstream)
    d_flow = d_fraw.astype(jnp.bfloat16)
    gate_shard, up_shard, down_shard, d_flow = lax.optimization_barrier(
        (w_gate, w_up, w_down, d_flow)
    )
    gate_back, up_back, down_back = (
        lax.all_gather(gate_shard, "fsdp", axis=0, tiled=True),
        lax.all_gather(up_shard, "fsdp", axis=0, tiled=True),
        lax.all_gather(down_shard, "fsdp", axis=0, tiled=True),
    )
    d_act = outer_cols(d_flow, down_back)
    d_gate, d_up = pull_act(d_act)
    dg_low = d_gate.astype(jnp.bfloat16)
    du_low = d_up.astype(jnp.bfloat16)
    d_htwo = outer_cols(dg_low, gate_back) + outer_cols(du_low, up_back)
    grad_down_part = lax.psum_scatter(
        inner_rows(act_low, d_flow).astype(jnp.bfloat16), "fsdp", scatter_dimension=0, tiled=True
    )
    grad_in_part = lax.psum_scatter(
        jnp.concatenate([inner_rows(h_two, dg_low), inner_rows(h_two, du_low)], axis=1).astype(
            jnp.bfloat16
        ),
        "fsdp",
        scatter_dimension=0,
        tiled=True,
    ).astype(jnp.float32)
    hidden_width = w_gate.shape[1]
    grad_gate_part = grad_in_part[:, :hidden_width]
    grad_up_part = grad_in_part[:, hidden_width:]
    d_mid_norm, d_gffn_in = pull_mid(d_htwo)
    d_middle = upstream + d_mid_norm
    d_oraw, d_gattn_out = pull_att(d_middle)
    d_olow = d_oraw.astype(jnp.bfloat16)
    grad_wo = inner_rows(att_low, d_olow)
    d_att_low = (
        outer_cols(d_olow, wo_all).astype(jnp.bfloat16).reshape(rows_here * head_count, head_width)
    )
    d_probs = outer_cols(d_att_low, value_rows)
    d_scores = attn_probs * (d_probs - jnp.sum(attn_probs * d_probs, axis=-1, keepdims=True))
    ds_low = d_scores.astype(jnp.bfloat16)
    d_qfin = jnp.dot(ds_low, key_rows, preferred_element_type=jnp.float32) * score_scale
    d_keys = inner_rows(ds_low, q_low) * score_scale
    d_values = inner_rows(probs_low, d_att_low)
    d_kfin = d_keys[reach_devs * rows_here :]
    d_vsum = d_values[reach_devs * rows_here :]
    for offset in range(1, reach_devs + 1):
        slot_index = reach_devs - offset
        k_back, v_back = (
            from_behind(
                d_keys[slot_index * rows_here : (slot_index + 1) * rows_here].astype(jnp.bfloat16),
                "seq",
                -offset,
            ).astype(jnp.float32),
            from_behind(
                d_values[slot_index * rows_here : (slot_index + 1) * rows_here].astype(
                    jnp.bfloat16
                ),
                "seq",
                -offset,
            ).astype(jnp.float32),
        )
        d_kfin = d_kfin + k_back
        d_vsum = d_vsum + v_back
    d_qraw, d_kraw, d_gquery, d_gkey = pull_prep(
        (d_qfin.reshape(rows_here, head_count, head_width), d_kfin)
    )
    dq_low = d_qraw.astype(jnp.bfloat16)
    dk_low = d_kraw.astype(jnp.bfloat16)
    dv_low = d_vsum.astype(jnp.bfloat16)
    d_hone = outer_cols(dq_low, wq_all) + outer_cols(dk_low, wk_all) + outer_cols(dv_low, wv_all)
    grad_wq = inner_rows(h_one, dq_low)
    grad_wk = inner_rows(h_one, dk_low)
    grad_wv = inner_rows(h_one, dv_low)
    d_tok_norm, d_gattn_in = pull_one(d_hone)
    d_inputs = d_middle + d_tok_norm
    part_wq, part_wk, part_wv, part_wo, part_gai, part_gq, part_gk, part_gao, part_gfi, part_gfo = (
        lax.psum_scatter(
            grad_wq.astype(jnp.bfloat16), "fsdp", scatter_dimension=0, tiled=True
        ).astype(jnp.float32),
        lax.psum_scatter(
            grad_wk.astype(jnp.bfloat16), "fsdp", scatter_dimension=0, tiled=True
        ).astype(jnp.float32),
        lax.psum_scatter(
            grad_wv.astype(jnp.bfloat16), "fsdp", scatter_dimension=0, tiled=True
        ).astype(jnp.float32),
        lax.psum_scatter(
            grad_wo.astype(jnp.bfloat16), "fsdp", scatter_dimension=0, tiled=True
        ).astype(jnp.float32),
        lax.psum_scatter(
            d_gattn_in.astype(jnp.bfloat16), "fsdp", scatter_dimension=0, tiled=True
        ).astype(jnp.float32),
        lax.psum_scatter(
            d_gquery.astype(jnp.bfloat16), "fsdp", scatter_dimension=0, tiled=True
        ).astype(jnp.float32),
        lax.psum_scatter(
            d_gkey.astype(jnp.bfloat16), "fsdp", scatter_dimension=0, tiled=True
        ).astype(jnp.float32),
        lax.psum_scatter(
            d_gattn_out.astype(jnp.bfloat16), "fsdp", scatter_dimension=0, tiled=True
        ).astype(jnp.float32),
        lax.psum_scatter(
            d_gffn_in.astype(jnp.bfloat16), "fsdp", scatter_dimension=0, tiled=True
        ).astype(jnp.float32),
        lax.psum_scatter(
            d_gffn_out.astype(jnp.bfloat16), "fsdp", scatter_dimension=0, tiled=True
        ).astype(jnp.float32),
    )
    cols_wq, cols_wk, cols_wv, cols_wo, cols_gate, cols_up, cols_down = (
        lax.psum_scatter(
            part_wq.astype(jnp.bfloat16), "seq", scatter_dimension=1, tiled=True
        ).astype(jnp.float32),
        lax.psum_scatter(
            part_wk.astype(jnp.bfloat16), "seq", scatter_dimension=1, tiled=True
        ).astype(jnp.float32),
        lax.psum_scatter(
            part_wv.astype(jnp.bfloat16), "seq", scatter_dimension=1, tiled=True
        ).astype(jnp.float32),
        lax.psum_scatter(
            part_wo.astype(jnp.bfloat16), "seq", scatter_dimension=1, tiled=True
        ).astype(jnp.float32),
        lax.psum_scatter(
            grad_gate_part.astype(jnp.bfloat16), "seq", scatter_dimension=1, tiled=True
        ).astype(jnp.float32),
        lax.psum_scatter(
            grad_up_part.astype(jnp.bfloat16), "seq", scatter_dimension=1, tiled=True
        ).astype(jnp.float32),
        lax.psum_scatter(grad_down_part, "seq", scatter_dimension=1, tiled=True).astype(
            jnp.float32
        ),
    )
    sum_wq, sum_wk, sum_wv, sum_wo, sum_gate, sum_up, sum_down = (
        lax.all_gather(cols_wq.astype(jnp.bfloat16), "seq", axis=1, tiled=True).astype(
            cols_wq.dtype
        ),
        lax.all_gather(cols_wk.astype(jnp.bfloat16), "seq", axis=1, tiled=True).astype(
            cols_wk.dtype
        ),
        lax.all_gather(cols_wv.astype(jnp.bfloat16), "seq", axis=1, tiled=True).astype(
            cols_wv.dtype
        ),
        lax.all_gather(cols_wo.astype(jnp.bfloat16), "seq", axis=1, tiled=True).astype(
            cols_wo.dtype
        ),
        lax.all_gather(cols_gate.astype(jnp.bfloat16), "seq", axis=1, tiled=True).astype(
            cols_gate.dtype
        ),
        lax.all_gather(cols_up.astype(jnp.bfloat16), "seq", axis=1, tiled=True).astype(
            cols_up.dtype
        ),
        lax.all_gather(cols_down.astype(jnp.bfloat16), "seq", axis=1, tiled=True).astype(
            cols_down.dtype
        ),
    )
    sum_gai, sum_gq, sum_gk, sum_gao, sum_gfi, sum_gfo = lax.psum(
        (part_gai, part_gq, part_gk, part_gao, part_gfi, part_gfo), "seq"
    )
    return (
        outputs[None],
        d_inputs[None],
        sum_gai,
        sum_wq,
        sum_wk,
        sum_wv,
        sum_gq,
        sum_gk,
        sum_wo,
        sum_gao,
        sum_gfi,
        sum_gate,
        sum_up,
        sum_down,
        sum_gfo,
    )


MESH = pl.DeviceIdType.MESH
BF16 = jnp.bfloat16
F32 = jnp.float32
GELU_RATE = 0.7978845608028654
GELU_CUBE = 0.044715
HID_TILE = 256
ATT_IN, ATT_OUT, FFN_IN, FFN_OUT, QUERY, KEY = range(6)


def bit_of(value, mask):
    return lax.rem(lax.div(value, mask), 2)


def flip(value, masks, bits):
    for b in range(bits):
        if (masks >> b) & 1:
            value = value + (1 << b) * (1 - 2 * bit_of(value, 1 << b))
    return value


def greet(devices):
    barrier = pltpu.get_barrier_semaphore()
    for device in devices:
        pl.semaphore_signal(barrier, inc=1, device_id=device, device_id_type=MESH)
    pl.semaphore_wait(barrier, len(devices))


def remote(src, dst, send, recv, device):
    return pltpu.make_async_remote_copy(
        src_ref=src, dst_ref=dst, send_sem=send, recv_sem=recv,
        device_id=device, device_id_type=MESH,
    )


def many(offset, size):
    return pl.ds(pl.multiple_of(offset, size if size % 128 == 0 else 16), size)


def lanes(offset, size):
    return pl.ds(pl.multiple_of(offset, 128), size)


def window_start(z, share):
    if isinstance(z, int):
        return z * share // 128 * 128
    return lax.div(z * share, 128) * 128


def window_width(share, n_fsdp):
    widest = max((z + 1) * share - window_start(z, share) for z in range(n_fsdp))
    return -(-widest // HID_TILE) * HID_TILE


def dot_nt(left, right):
    return lax.dot_general(left, right, (((1,), (1,)), ((), ())), preferred_element_type=F32)


def dot_nn(left, right):
    return jnp.dot(left, right, preferred_element_type=F32)


def norm_scale(rows_in):
    return lax.rsqrt(jnp.mean(rows_in * rows_in, axis=-1, keepdims=True) + epsilon)


def norm_back(rows_in, gain, scale, upstream):
    pulled = upstream * gain
    inner = jnp.mean(pulled * rows_in, axis=-1, keepdims=True)
    d_rows = scale * pulled - rows_in * (scale * scale * scale * inner)
    return d_rows, jnp.sum(upstream * rows_in * scale, axis=0, keepdims=True)


def turn(rows_in, cosine, sine_part):
    half = rows_in.shape[-1] // 2
    lower, upper = rows_in[:, :half], rows_in[:, half:]
    return jnp.concatenate(
        [lower * cosine - upper * sine_part, upper * cosine + lower * sine_part], axis=-1
    )


class Place:
    def __init__(self):
        self.s = lax.axis_index("seq")
        self.z = lax.axis_index("fsdp")
        self.c = bit_of(self.s, 1)
        self.x = bit_of(self.s, 2)
        self.y = bit_of(self.s, 4)

    def plane(self, masks):
        return (flip(self.s, masks, 3), self.z)

    def line(self, masks):
        return (self.s, flip(self.z, masks, 2))

    def halves(self, first_x):
        if first_x:
            return self.x, self.y, 2, 4
        return self.y, self.x, 4, 2


def layer_kernel(
    n_seq, n_fsdp, share, reach, head_count,
    x_ref, cot_ref, rates_ref, seg_ref,
    gain_a, gain_b, gain_c, gain_d, gain_e, gain_f,
    gate_ref, up_ref, wq_ref, wk_ref, wv_ref, wo_ref, wd_ref,
    small_out, fin_gu, fin_d,
    qkv_s, wo_s, w_in, w_down, pack_all, seg_all, gains, allowed, turns,
    h1_s, raw_s, q_s, kv_own, kv_s, p_s, att_s, o_s, mid_s,
    h_all, df_all, bent_s, act, d_in, h_turn, part_out, part_in, relay_in, total,
    own_d, own_g, own_o, own_q, hi_d, hi_g, hi_o, hi_q, lo_d, lo_g, lo_o, lo_q, line_o, line_q,
    do_s, datt_s, ds_s, dkv_s, dkv_send, dkv_came, dqkv_s, dgains, gain_in, gain_line,
    w_send, w_recv, own_sem, pack_send, pack_recv, seg_send, seg_recv, kv_send, kv_recv,
    ex_send, ex_recv, relay_sem, dkv_ssem, dkv_rsem,
    c_send, c_recv, hi_send, hi_recv, lo_send, lo_recv, z_send, z_recv, oq_send, oq_recv,
    put_sem, ag_send, ag_recv, gain_send, gain_recv,
):
    at = Place()
    s, z, c = at.s, at.z, at.c
    rows, width = x_ref.shape
    depth = width // n_fsdp
    hidden = w_in.shape[2]
    head_width = wk_ref.shape[1]
    query_width = head_count * head_width
    heads_width = query_width + 2 * head_width
    rows_o = wo_ref.shape[0]
    n_hid = hidden // HID_TILE
    third = width // 3
    middle_z = (z > 0) & (z < n_fsdp - 1)
    tokens = n_fsdp * rows

    def hid(n):
        return lanes(n * HID_TILE, HID_TILE)

    def outs(n):
        return lanes(n * third, third)

    skipped = z * share - window_start(z, share)
    spare = hidden - share
    if spare:
        w_down[pl.ds(0, spare)] = jnp.zeros((spare, width), BF16)
        w_down[pl.ds(share, spare)] = jnp.zeros((spare, width), BF16)
    here_z = many(z * depth, depth)
    own_copies = [
        pltpu.make_async_copy(src, dst, own_sem.at[i])
        for i, (src, dst) in enumerate((
            (wq_ref, qkv_s.at[here_z, pl.ds(0, query_width)]),
            (wk_ref, qkv_s.at[here_z, pl.ds(query_width, head_width)]),
            (wv_ref, qkv_s.at[here_z, pl.ds(query_width + head_width, head_width)]),
            (wo_ref, wo_s.at[many(z * rows_o, rows_o)]),
            (wd_ref, w_down.at[many(skipped, share)]),
            (gate_ref.at[:, lanes(window_start(z, share), hidden)], w_in.at[0, here_z]),
            (up_ref.at[:, lanes(window_start(z, share), hidden)], w_in.at[1, here_z]),
        ))
    ]
    seg_all[s] = jnp.broadcast_to(seg_ref[...], seg_all.shape[1:])
    start = 0
    for ref in (gain_a, gain_b, gain_c, gain_d, gain_e, gain_f):
        size = ref.shape[0]
        pack_all[z, 0:1, start : start + size] = ref[...].astype(F32).reshape(1, size)
        start += size
    greet([at.plane(k) for k in range(1, n_seq)] + [at.line(m) for m in range(1, n_fsdp)])

    packs = [
        remote(pack_all.at[z], pack_all.at[z], pack_send.at[m], pack_recv.at[m], at.line(m))
        for m in range(1, n_fsdp)
    ]
    seg_copies = [
        remote(seg_all.at[s], seg_all.at[s], seg_send.at[k], seg_recv.at[k], at.plane(k))
        for k in range(1, n_seq)
    ]
    kv_copies = [
        remote(kv_own, kv_s.at[reach - o], kv_send.at[o - 1], kv_recv.at[o - 1],
               (lax.rem(s + o, n_seq), z))
        for o in range(1, reach + 1)
    ]

    def w_region(kind, sub, whose, hi, lo, level):
        base = whose * depth
        if kind == "q":
            cols = (
                lanes(hi * (query_width // 2) + lo * (query_width // 4), query_width // 4),
                lanes(hi * (query_width // 2), query_width // 2),
                pl.ds(0, query_width),
            )[level]
            return qkv_s.at[many(base + c * (depth // 2), depth // 2), cols]
        if kind == "kv":
            start = query_width + c * head_width
            if level == 0:
                start = start + lo * (head_width // 2)
            cols = lanes(start, head_width if level else head_width // 2)
            if level == 2:
                return qkv_s.at[many(base, depth), cols]
            return qkv_s.at[many(base + hi * (depth // 2), depth // 2), cols]
        if kind == "wo":
            start = whose * rows_o + c * (rows_o // 2)
            if level < 2:
                start = start + hi * (rows_o // 4)
            if level < 1:
                start = start + lo * (rows_o // 8)
            return wo_s.at[many(start, rows_o // (8, 4, 2)[level])]
        skip, size = sub
        if level == 2:
            return [
                w_in.at[c, many(base + half * (depth // 2) + skip, size)] for half in range(2)
            ]
        here = many(base + hi * (depth // 2) + skip, size)
        if level == 1:
            return w_in.at[c, here]
        return w_in.at[c, here, lanes(lo * (hidden // 2), hidden // 2)]

    def w_sources(kind, sub, to, hi, lo):
        if kind == "q":
            cols = lanes(hi * (query_width // 2) + lo * (query_width // 4), query_width // 4)
            return [wq_ref.at[many(c * (depth // 2), depth // 2), cols]]
        if kind == "wo":
            start = c * (rows_o // 2) + hi * (rows_o // 4) + lo * (rows_o // 8)
            return [wo_ref.at[many(start, rows_o // 8)]]
        if kind == "kv":
            here = many(hi * (depth // 2), depth // 2)
            cols = lanes(lo * (head_width // 2), head_width // 2)
            return [ref.at[here, cols] for ref in (wk_ref, wv_ref)]
        skip, size = sub
        here = many(hi * (depth // 2) + skip, size)
        cols = lanes(window_start(to, share) + lo * (hidden // 2), hidden // 2)
        return [ref.at[here, cols] for ref in (gate_ref, up_ref)]

    items = []
    for kinds in (("q", "kv"), ("wo",)):
        for m in range(1, n_fsdp):
            for kind in kinds:
                items.append((kind, m, (m % 2 == 1) != (kind in ("kv", "wo")), None))
    n_att = len(items)
    for m in range(1, n_fsdp):
        items.append(("gu", m, m % 2 == 1, (0, depth // 2)))
    steps, starts = [], []
    for i, (kind, m, first_x, sub) in enumerate(items):
        hi, lo, mask_hi, mask_lo = at.halves(first_x)
        there = flip(z, m, 2)
        firsts = [
            remote(src, w_region(kind, sub, z, hi, lo, 0), w_send.at[i, 0], w_recv.at[i, 0],
                   at.line(m))
            for src in w_sources(kind, sub, there, hi, lo)
        ]
        starts.append(firsts)
        stages = [firsts[:1]]
        for k, mask in enumerate((mask_lo, mask_hi, 1)):
            parts = w_region(kind, sub, there, hi, lo, k)
            stages.append([
                remote(part, part, w_send.at[i, k + 1 + n], w_recv.at[i, k + 1 + n], at.plane(mask))
                for n, part in enumerate(parts if isinstance(parts, list) else [parts])
            ])
        steps.append(stages)

    def begin_weight(i):
        if len(starts[i]) == 1:
            starts[i][0].start()
        else:
            for core, first in enumerate(starts[i]):
                pl.when(c == core)(first.start)

    def weight_here(i, stage):
        for copy in steps[i][stage]:
            copy.wait_recv()

    def move_weight(i, stage):
        weight_here(i, stage - 1)
        for copy in steps[i][stage]:
            copy.start()

    def weight_sent(i):
        for copies in steps[i]:
            for copy in copies:
                copy.wait_send()

    n_items = len(items)
    n_qkv = 2 * (n_fsdp - 1)
    ahead, lag = 6, 3
    for copy in packs + seg_copies:
        copy.start()
    for i in range(ahead):
        begin_weight(i)
    for copy in own_copies:
        copy.start()

    def weight_steps(t):
        for stage in (3, 2, 1):
            i = t - lag * (stage - 1)
            if 0 <= i < n_att:
                move_weight(i, stage)
                if stage == 1 and i + ahead < n_items:
                    begin_weight(i + ahead)

    weight_steps(0)
    weight_steps(1)
    for copy in seg_copies:
        copy.wait_recv()
    across = lax.broadcasted_iota(jnp.int32, (rows, rows), 0)
    along = lax.broadcasted_iota(jnp.int32, (rows, rows), 1)
    seg_here = jnp.broadcast_to(seg_ref[...].astype(F32), (rows, rows)).T
    for o in range(reach, -1, -1):
        key_seg = seg_all[lax.rem(s + n_seq - o, n_seq), 0:1, :].astype(F32)
        apart = across - along + o * rows
        fine = (apart >= 0) & (apart < WINDOW) & (seg_here == key_seg) & (s >= o)
        allowed[:, pl.ds((reach - o) * rows, rows)] = jnp.where(fine, 1.0, 0.0).astype(BF16)
    angle = ((s * rows + across).astype(F32) - seg_here) * rates_ref[...]
    turns[0] = jnp.cos(angle)
    turns[1] = jnp.sin(angle)
    for copy in packs:
        copy.wait_recv()
    gains[...] = jnp.zeros(gains.shape, F32)
    start = 0
    for row in range(6):
        size = (depth if row < QUERY else head_width // n_fsdp)
        for block in range(n_fsdp):
            gains[row : row + 1, block * size : (block + 1) * size] = pack_all[
                block, 0:1, start : start + size
            ]
        start += size

    def gain(row):
        return gains[row : row + 1, : (width if row < QUERY else head_width)]

    x = x_ref[...].astype(F32)
    h1_s[...] = (x * norm_scale(x) * gain(ATT_IN)).astype(BF16)

    for t in range(2, n_att + 2 * lag):
        weight_steps(t)
    for i in range(n_qkv):
        weight_here(i, 3)
    for copy in own_copies[:3]:
        copy.wait()

    def move_gu(*moves):
        for k, stage in moves:
            move_weight(n_att + k - 1, stage)

    move_gu((1, 1))
    tile = heads_width // 3

    @pl.loop(0, 3)
    def _(n):
        cols = lanes(n * tile, tile)
        raw_s[:, cols] = dot_nn(h1_s[...], qkv_s[:, cols])

    k_raw = raw_s[:, query_width : query_width + head_width]
    kv_own[:, :head_width] = turn(
        k_raw * norm_scale(k_raw) * gain(KEY), turns[0], turns[1]
    ).astype(BF16)
    kv_own[:, head_width:] = raw_s[:, query_width + head_width :].astype(BF16)
    for copy in kv_copies:
        copy.start()
    kv_s[reach] = kv_own[...]
    for h in range(head_count):
        q_raw = raw_s[:, h * head_width : (h + 1) * head_width]
        q_fin = q_raw * norm_scale(q_raw) * gain(QUERY)
        q_s[h] = turn(q_fin, turns[0], turns[1]).astype(BF16)
    for i in range(n_qkv, n_att):
        weight_here(i, 3)
    own_copies[3].wait()
    move_gu((1, 2))
    for copy in kv_copies:
        copy.wait_recv()

    def keys():
        return kv_s[:, :, :head_width].reshape((reach + 1) * rows, head_width)

    def values():
        return kv_s[:, :, head_width:].reshape((reach + 1) * rows, head_width)

    for h in range(head_count):
        scores = dot_nt(q_s[h], keys()) * (head_width**-0.5)
        masked = jnp.where(allowed[...].astype(F32) > 0.5, scores, masked_value)
        grown = jnp.exp(masked - jnp.max(masked, axis=-1, keepdims=True))
        probs = grown / jnp.sum(grown, axis=-1, keepdims=True)
        p_s[h] = probs.astype(BF16)
        att_s[:, h * head_width : (h + 1) * head_width] = dot_nn(p_s[h], values()).astype(BF16)

    @pl.loop(0, 3)
    def _(n):
        o_s[:, outs(n)] = dot_nn(att_s[...], wo_s[:, outs(n)])

    o_raw = o_s[...]
    middle = x_ref[...].astype(F32) + o_raw * norm_scale(o_raw) * gain(ATT_OUT)
    mid_s[...] = middle
    h_all[0] = (middle * norm_scale(middle) * gain(FFN_IN)).astype(BF16)

    def exchange(phase, src, dst):
        return {
            m: remote(src(m), dst(m), ex_send.at[phase, m], ex_recv.at[phase, m], at.line(m))
            for m in range(1, n_fsdp)
        }

    last = n_fsdp - 1
    send_h = exchange(0, lambda m: h_all.at[0], lambda m: h_all.at[m])
    send_f = exchange(1, lambda m: part_out.at[m - 1], lambda m: part_in.at[0, m - 1])
    send_df = exchange(2, lambda m: df_all.at[0], lambda m: df_all.at[m])
    send_dh = exchange(3, lambda m: part_out.at[m - 1], lambda m: part_in.at[1, m - 1])
    onward = {
        phase: remote(rows_all.at[2], rows_all.at[last],
                      relay_sem.at[phase], ex_recv.at[phase, last], at.line(1))
        for phase, rows_all in ((0, h_all), (2, df_all))
    }
    by_way = {
        phase: remote(part_out.at[last - 1], relay_in.at[phase // 2],
                      relay_sem.at[phase], relay_sem.at[phase + 3], at.line(1))
        for phase in (1, 3)
    }

    def send_rows(copies):
        copies[2].start()
        pl.when(middle_z)(copies[last].start)
        copies[1].start()

    def relay_rows(copies, phase):
        @pl.when(middle_z)
        def _():
            copies[2].wait_recv()
            onward[phase].start()

    def take_rows(copies, m):
        if m == 2:
            pl.when(~middle_z)(copies[2].wait_recv)
        elif m:
            copies[m].wait_recv()

    def send_part(copies, phase, m):
        if m == 1:
            copies[1].start()
        elif m == 2:
            pl.when(~middle_z)(copies[2].start)
        else:
            pl.when(~middle_z)(by_way[phase].start)
            pl.when(middle_z)(copies[last].start)

    def send_joint_part(copies, phase):
        @pl.when(middle_z)
        def _():
            by_way[phase].wait_recv()
            part_out[1] = (
                part_out[1].astype(F32) + relay_in[phase // 2].astype(F32)
            ).astype(BF16)
            copies[2].start()

    def take_parts(copies):
        copies[1].wait_recv()
        copies[2].wait_recv()
        pl.when(middle_z)(copies[last].wait_recv)

    def rows_sent(copies, phase):
        copies[1].wait_send()
        copies[2].wait_send()

        @pl.when(middle_z)
        def _():
            copies[last].wait_send()
            onward[phase].wait_send()

    def parts_sent(copies, phase):
        copies[1].wait_send()
        copies[2].wait_send()
        pl.when(middle_z)(copies[last].wait_send)
        pl.when(~middle_z)(by_way[phase].wait_send)

    send_rows(send_h)

    @pl.when(~middle_z)
    def _():
        part_in[0, last - 1] = jnp.zeros((rows, width), BF16)
        part_in[1, last - 1] = jnp.zeros((rows, width), BF16)

    move_gu((2, 1))
    move_gu((3, 1))
    move_gu((2, 2))
    move_gu((1, 3))
    move_gu((3, 2))
    relay_rows(send_h, 0)
    move_gu((2, 3))
    move_gu((3, 3))
    for i in range(n_att, n_items):
        weight_here(i, 3)
    for copy in own_copies[4:]:
        copy.wait()
    half_h = hidden // 2

    for m in range(n_fsdp - 1, -1, -1):
        take_rows(send_h, m)
        for n in range(2):
            cols = slice(n * half_h, (n + 1) * half_h)
            gate = dot_nn(h_all[m], w_in[0, :, cols])
            up = dot_nn(h_all[m], w_in[1, :, cols])
            squared = gate * gate
            bent = jnp.tanh(GELU_RATE * (gate + GELU_CUBE * squared * gate))
            gelu = 0.5 * gate * (1.0 + bent)
            slope = 0.5 * (1.0 + bent) + 0.5 * gate * (1.0 - bent * bent) * (
                GELU_RATE * (1.0 + 3.0 * GELU_CUBE * squared)
            )
            bent_s[pl.ds(m * rows, rows), cols] = gelu.astype(BF16)
            bent_s[pl.ds(tokens + m * rows, rows), cols] = (slope * up).astype(BF16)
            act[m, :, cols] = (gelu * up).astype(BF16)
        part = dot_nn(act[m], w_down[...])
        if m:
            part_out[m - 1] = part.astype(BF16)
            send_part(send_f, 1, m)
        else:
            total[...] = part

    send_joint_part(send_f, 1)
    for m in range(n_fsdp):
        h_turn[:, pl.ds(m * rows, rows)] = h_all[m].T
    for i in range(n_att, n_items):
        weight_sent(i)

    take_parts(send_f)
    f_raw = total[...]
    for m in range(1, n_fsdp):
        f_raw = f_raw + part_in[0, m - 1].astype(F32)
    cot = cot_ref[...].astype(F32)
    scale = norm_scale(f_raw)
    d_f, d_gain = norm_back(f_raw, gain(FFN_OUT), scale, cot)
    df_all[0] = d_f.astype(BF16)
    send_rows(send_df)
    small_out[pl.ds(rows, rows), :] = mid_s[...] + f_raw * scale * gain(FFN_OUT)
    dgains[...] = jnp.zeros(dgains.shape, F32)
    dgains[FFN_OUT : FFN_OUT + 1, :] = d_gain
    parts_sent(send_f, 1)

    chunks = [("d", 0, False), ("d", 1, True)]
    chunks += [("g", m, m % 2 == 0) for m in range(n_fsdp)]
    chunks += [("o", 0, False), ("q", 0, True)]
    tiles_d = hidden // 256
    spans_d = (pl.ds(0, n_fsdp), pl.ds(n_fsdp, tiles_d - n_fsdp))

    def mine_of(kind, i):
        if kind == "d":
            return own_d.at[spans_d[i]]
        return {"g": own_g, "o": own_o, "q": own_q}[kind].at[i]

    def hi_part(kind, hi):
        if kind == "d":
            return slice(None), many(hi * 64, 64), slice(None)
        if kind == "g":
            return many(hi * (depth // 2), depth // 2), slice(None)
        if kind == "q":
            return slice(None), lanes(hi * (heads_width // 2), heads_width // 2)
        return many(hi * (rows_o // 4), rows_o // 4), slice(None)

    def lo_part(kind, hi, lo):
        if kind == "d":
            return slice(None), many(hi * 64 + lo * 32, 32), slice(None)
        if kind == "g":
            return (
                many(hi * (depth // 2), depth // 2),
                lanes(lo * (hidden // 2), hidden // 2),
            )
        if kind == "q":
            start = hi * (heads_width // 2) + lo * (heads_width // 4)
            return slice(None), lanes(start, heads_width // 4)
        return many(hi * (rows_o // 4) + lo * (rows_o // 8), rows_o // 8), slice(None)

    def fin_part(kind, i, where, core):
        if kind == "d":
            span = spans_d[i]
            tiles = pl.ds(core * tiles_d + span.start, span.size)
            return fin_d.at[tiles, where[-2], :]
        rows_at, cols_at = where
        if kind == "g":
            return fin_gu.at[core * n_fsdp + i, rows_at, cols_at]
        if kind == "o":
            return fin_d.at[2 * tiles_d + core, rows_at, :]
        base = core * (depth // 2)
        if isinstance(cols_at, slice):
            cols_at = pl.ds(0, heads_width)
        return fin_gu.at[2 * n_fsdp, many(base, depth // 2), cols_at]
    def add(ref, where, other):
        rows_at, cols_at = where
        start = 0 if isinstance(rows_at, slice) else rows_at.start
        slab = 16

        @pl.loop(0, other.shape[0] // slab)
        def _(n):
            here = pl.ds(pl.multiple_of(start + n * slab, slab), slab)
            there = pl.ds(pl.multiple_of(n * slab, slab), slab)
            ref[here, cols_at] = (
                ref[here, cols_at].astype(F32) + other[there, :].astype(F32)
            ).astype(BF16)

    whole = (slice(None), slice(None))
    from_hi = {"d": hi_d, "g": hi_g, "o": hi_o, "q": hi_q}
    from_lo = {"d": lo_d, "g": lo_g, "o": lo_o, "q": lo_q}
    his, los, lines = [], [], []
    for j, (kind, i, first_x) in enumerate(chunks):
        hi, lo, mask_hi, mask_lo = at.halves(first_x)
        mine = mine_of(kind, i)
        if kind == "q":
            parts = (
                own_q.at[:, :, hi_part(kind, 1 - hi)[1]], hi_q,
                own_q.at[:, :, lo_part(kind, hi, 1 - lo)[1]], lo_q,
            )
        else:
            slot = spans_d[i] if kind == "d" else i
            parts = (
                mine.at[hi_part(kind, 1 - hi)], from_hi[kind].at[slot],
                mine.at[lo_part(kind, hi, 1 - lo)], from_lo[kind].at[slot],
            )
        his.append(
            remote(parts[0], parts[1], hi_send.at[j], hi_recv.at[j], at.plane(mask_hi))
        )
        los.append(
            remote(parts[2], parts[3], lo_send.at[j], lo_recv.at[j], at.plane(mask_lo))
        )
        line = None
        if kind == "g" and i:
            line = remote(mine.at[lo_part(kind, hi, lo)],
                          fin_part(kind, z, lo_part(kind, hi, lo), c),
                          z_send.at[j], z_recv.at[j], at.line(i))
        lines.append(line)
    stage = {
        "d": lambda i: part_in.at[0] if i else h_all,
        "g": lambda i: bent_s.at[pl.ds(i * depth, depth)],
        "q": lambda i: w_in.at[0, pl.ds(i * (depth // 2), depth // 2), pl.ds(0, heads_width)],
        "o": lambda i: w_in.at[1, pl.ds(i * (rows_o // 2), rows_o // 2), pl.ds(0, width)],
    }
    to_core = [("d", 0), ("d", 1)]
    to_core += [(kind, m) for kind in "goq" for m in range(n_fsdp)]
    cores = {
        key: remote(stage[key[0]](key[1]), mine_of(*key), c_send.at[k], c_recv.at[k], at.plane(1))
        for k, key in enumerate(to_core)
    }
    line_sums = {}
    for k, (kind, ref) in enumerate((("o", line_o), ("q", line_q))):
        for m in range(1, n_fsdp):
            part = mine_of(kind, m)
            if kind == "q":
                part = part.at[lo_part(kind, at.x, at.y)]
            line_sums[kind, m] = remote(
                part, ref.at[m - 1], oq_send.at[k, m], oq_recv.at[k, m], at.line(m)
            )

    puts, hands = [], []
    for j, (kind, i, first_x) in enumerate(chunks):
        hi, lo, mask_hi, mask_lo = at.halves(first_x)
        which = flip(z, i, 2) if kind == "g" else i
        piece = fin_part(kind, which, lo_part(kind, hi, lo), c)
        half = fin_part(kind, which, hi_part(kind, hi), c)
        full = fin_part(kind, which, whole, c)
        put = None
        if lines[j] is None:
            put = pltpu.make_async_copy(
                mine_of(kind, i).at[lo_part(kind, hi, lo)], piece, put_sem.at[j]
            )
        puts.append(put)
        hands.append([
            remote(part, part, ag_send.at[j, k], ag_recv.at[j, k], at.plane(mask))
            for k, (part, mask) in enumerate(((piece, mask_lo), (half, mask_hi), (full, 1)))
        ])

    def add_all(kind, i, where, came):
        if kind == "d":
            for n in range(spans_d[i].start, spans_d[i].start + spans_d[i].size):
                add(own_d.at[n], where[1:], came.at[n])
        elif kind == "q":
            for m in range(n_fsdp):
                add(own_q.at[m], where, came.at[m])
        else:
            add(mine_of(kind, i), where, came.at[i])

    def take_hi(j):
        kind, i, first_x = chunks[j]
        hi, lo, _, _ = at.halves(first_x)
        his[j].wait_recv()
        add_all(kind, i, hi_part(kind, hi), from_hi[kind])
        los[j].start()

    def take_lo(j):
        kind, i, first_x = chunks[j]
        hi, lo, _, _ = at.halves(first_x)
        los[j].wait_recv()
        add_all(kind, i, lo_part(kind, hi, lo), from_lo[kind])
        if lines[j] is not None:
            lines[j].start()
        elif kind == "q":
            for m in range(1, n_fsdp):
                line_sums[kind, m].start()
        else:
            puts[j].start()

    def begin_hand(j):
        if lines[j] is not None:
            lines[j].wait_recv()
        else:
            puts[j].wait()
        hands[j][0].start()

    def hand_on(j, k):
        hands[j][k - 1].wait_recv()
        hands[j][k].start()

    def down_stage(n):
        return h_all.at[n] if n < n_fsdp else part_in.at[0, n - n_fsdp]

    def down_grads(core, dst_of, adds):
        right = df_all[...].reshape(tokens, width)
        for n in range(tiles_d):
            left = act[:, :, lanes(core * (hidden // 2) + n * 128, 128)].reshape(tokens, 128).T
            grads = dot_nn(left, right)
            dst = dst_of[n] if adds else dst_of(n)
            if adds:
                grads = grads + dst[...].astype(F32)
            dst[...] = grads.astype(BF16)

    def in_grads(core, m, dst, adds):
        left_at = many(flip(z, m, 2) * depth, depth)

        for n in range(2):
            cols = slice(n * half_h, (n + 1) * half_h)
            grads = dot_nn(h_turn[left_at, :], d_in[core, :, :, cols].reshape(tokens, half_h))
            if adds:
                grads = grads + dst[:, cols].astype(F32)
            dst[:, cols] = grads.astype(BF16)

    rows_sent(send_h, 0)
    for m in range(n_fsdp):
        if m == 1:
            relay_rows(send_df, 2)
        take_rows(send_df, m)
        if m == last:
            down_grads(1 - c, down_stage, False)
            cores["d", 0].start()
            cores["d", 1].start()
        for n in range(2):
            cols = slice(n * half_h, (n + 1) * half_h)
            d_act = dot_nt(df_all[m], w_down[cols, :])
            slope = bent_s[pl.ds(tokens + m * rows, rows), cols].astype(F32)
            d_in[0, m, :, cols] = (d_act * slope).astype(BF16)
            gelu = bent_s[pl.ds(m * rows, rows), cols].astype(F32)
            d_in[1, m, :, cols] = (d_act * gelu).astype(BF16)
        part = dot_nt(d_in[0, m], w_in[0]) + dot_nt(d_in[1, m], w_in[1])
        if m:
            part_out[m - 1] = part.astype(BF16)
            send_part(send_dh, 3, m)
        else:
            total[...] = part

    cores["d", 0].wait_recv()
    cores["d", 1].wait_recv()
    down_grads(c, own_d.at, True)
    his[0].start()
    his[1].start()
    send_joint_part(send_dh, 3)
    for m in range(n_fsdp):
        in_grads(1 - c, m, stage["g"](m), False)
        cores["g", m].start()
    for m in range(n_fsdp):
        cores["g", m].wait_recv()
        in_grads(c, m, own_g.at[m], True)
        his[2 + m].start()

    dkv_copies = [
        remote(dkv_send.at[reach - o], dkv_came.at[o - 1], dkv_ssem.at[o - 1], dkv_rsem.at[o - 1],
               (lax.rem(s + n_seq - o, n_seq), z))
        for o in range(1, reach + 1)
    ]
    gain_copies = [
        remote(dgains, gain_in.at[k], gain_send.at[k], gain_recv.at[k], at.plane(k))
        for k in range(1, n_seq)
    ]
    gain_lines = [
        remote(gain_line.at[0], gain_line.at[m], gain_send.at[n_seq + m], gain_recv.at[n_seq + m],
               at.line(m))
        for m in range(1, n_fsdp)
    ]

    def to_middle():
        take_parts(send_dh)
        dh = total[...]
        for m in range(1, n_fsdp):
            dh = dh + part_in[1, m - 1].astype(F32)
        mid = mid_s[...]
        d_mid, d_gain = norm_back(mid, gain(FFN_IN), norm_scale(mid), dh)
        d_mid = d_mid + cot_ref[...].astype(F32)
        mid_s[...] = d_mid
        dgains[FFN_IN : FFN_IN + 1, :] = d_gain
        o_raw = o_s[...]
        d_o, d_gain = norm_back(o_raw, gain(ATT_OUT), norm_scale(o_raw), d_mid)
        dgains[ATT_OUT : ATT_OUT + 1, :] = d_gain
        do_s[...] = d_o.astype(BF16)
        for h in range(head_count):
            here = pl.ds(h * head_width, head_width)
            datt_s[h] = dot_nt(do_s[...], wo_s[here, :]).astype(BF16)

    def unturn(rows_in):
        return turn(rows_in, turns[0], -turns[1])

    def through_head(h):
        probs = p_s[h].astype(F32)
        d_att = datt_s[h]
        d_probs = dot_nt(d_att, values())
        d_scores = probs * (d_probs - jnp.sum(probs * d_probs, axis=-1, keepdims=True))
        ds_low = d_scores.astype(BF16)
        scale = head_width**-0.5
        ds_s[h] = ds_low
        cols = slice(h * head_width, (h + 1) * head_width)
        q_raw = raw_s[:, cols]
        d_q, d_gain = norm_back(
            q_raw, gain(QUERY), norm_scale(q_raw), unturn(dot_nn(ds_low, keys()) * scale)
        )
        dqkv_s[:, cols] = d_q.astype(BF16)
        dgains[QUERY : QUERY + 1, :head_width] += d_gain

    def return_keys():
        for side, left, right, scale in (
            (0, ds_s, q_s, head_width**-0.5),
            (1, p_s, datt_s, 1.0),
        ):
            cols = slice(side * head_width, (side + 1) * head_width)
            d_side = scale * inner_rows(
                left[...].reshape(head_count * rows, (reach + 1) * rows),
                right[...].reshape(head_count * rows, head_width),
            )
            for b in range(reach):
                dkv_send[b, :, cols] = d_side[b * rows : (b + 1) * rows].astype(BF16)
            dkv_s[:, cols] = d_side[reach * rows :]
        for copy in dkv_copies:
            copy.start()

    def grad_tiles(left_at, turned, right, n_cols, dst, adds):
        tile = n_cols // 3
        for k in range(3):
            grads = dot_nn(turned[left_at, :], right[:, k * tile : (k + 1) * tile])
            if adds:
                grads = grads + dst[:, k * tile : (k + 1) * tile].astype(F32)
            dst[:, k * tile : (k + 1) * tile] = grads.astype(BF16)

    def core_grads(kind, turned, right, span, n_cols):
        for m in range(n_fsdp):
            start = flip(z, m, 2) * span + (1 - c) * (span // 2)
            grad_tiles(many(start, span // 2), turned, right, n_cols, stage[kind](m), False)
            cores[kind, m].start()
        for m in list(range(1, n_fsdp)) + [0]:
            start = flip(z, m, 2) * span + c * (span // 2)
            cores[kind, m].wait_recv()
            grad_tiles(many(start, span // 2), turned, right, n_cols, mine_of(kind, m), True)
            if m and kind == "o":
                line_sums[kind, m].start()
        if kind == "q":
            his[-1].start()

    def output_grads():
        h_turn[pl.ds(0, query_width), pl.ds(0, rows)] = att_s[...].T
        core_grads("o", h_turn.at[:, pl.ds(0, rows)], do_s, rows_o, width)

    def key_grads():
        h_turn[:, pl.ds(rows, rows)] = h1_s[...].T
        d_kv = dkv_s[...]
        for o in range(reach):
            dkv_copies[o].wait_recv()
            d_kv = d_kv + dkv_came[o].astype(F32)
        k_raw = raw_s[:, query_width : query_width + head_width]
        d_k, d_gain = norm_back(
            k_raw, gain(KEY), norm_scale(k_raw), unturn(d_kv[:, :head_width])
        )
        dqkv_s[:, query_width : query_width + head_width] = d_k.astype(BF16)
        dqkv_s[:, query_width + head_width :] = d_kv[:, head_width:].astype(BF16)
        dgains[KEY : KEY + 1, :head_width] = d_gain
        core_grads("q", h_turn.at[:, pl.ds(rows, rows)], dqkv_s, depth, heads_width)

    def sum_line(j):
        kind = chunks[j][0]
        where = lo_part(kind, at.x, at.y) if kind == "q" else whole
        for m in range(1, n_fsdp):
            line_sums[kind, m].wait_recv()
            add(mine_of(kind, 0), where, {"o": line_o, "q": line_q}[kind].at[m - 1])
        (puts if kind == "q" else his)[j].start()

    def to_input():
        x = x_ref[...].astype(F32)
        d_h = dot_nt(dqkv_s[...], qkv_s[...])
        d_x, d_gain = norm_back(x, gain(ATT_IN), norm_scale(x), d_h)
        small_out[pl.ds(0, rows), :] = mid_s[...] + d_x
        dgains[ATT_IN : ATT_IN + 1, :] = d_gain
        for copy in gain_copies:
            copy.start()

    def sum_gains():
        sums = dgains[...]
        for k, copy in enumerate(gain_copies):
            copy.wait_recv()
            sums = sums + gain_in[k + 1]
        gain_line[0] = sums
        for copy in gain_lines:
            copy.start()

    take_hi(0)
    take_hi(1)
    to_middle()
    through_head(0)
    through_head(1)
    take_hi(2)
    take_hi(3)
    take_lo(0)
    take_lo(1)
    begin_hand(0)
    begin_hand(1)
    through_head(2)
    through_head(3)
    return_keys()
    output_grads()
    take_hi(4)
    take_hi(5)
    take_lo(2)
    take_lo(3)
    key_grads()
    begin_hand(2)
    hand_on(0, 1)
    hand_on(1, 1)
    take_lo(4)
    take_lo(5)
    begin_hand(3)
    to_input()
    hand_on(0, 2)
    hand_on(1, 2)
    sum_line(6)
    hand_on(2, 1)
    begin_hand(4)
    begin_hand(5)
    take_hi(7)
    hand_on(3, 1)
    hand_on(2, 2)
    sum_gains()
    take_hi(6)
    take_lo(7)
    hand_on(4, 1)
    hand_on(5, 1)
    hand_on(3, 2)
    take_lo(6)
    begin_hand(6)
    sum_line(7)
    begin_hand(7)
    hand_on(6, 1)
    hand_on(4, 2)
    hand_on(5, 2)
    hand_on(7, 1)
    hand_on(6, 2)
    hand_on(7, 2)
    sums = gain_line[0]
    for m, copy in enumerate(gain_lines):
        copy.wait_recv()
        sums = sums + gain_line[m + 1]
    for row in range(6):
        size = depth if row < QUERY else head_width // n_fsdp
        for block in range(n_fsdp):

            @pl.when(z == block)
            def _():
                small_out[2 * rows + row : 2 * rows + row + 1, :size] = sums[
                    row : row + 1, block * size : (block + 1) * size
                ]


    for j in range(len(chunks)):
        hands[j][2].wait_recv()
        for k in range(3):
            hands[j][k].wait_send()
        his[j].wait_send()
        los[j].wait_send()
        if lines[j] is not None:
            lines[j].wait_send()
    for copy in list(cores.values()) + list(line_sums.values()):
        copy.wait_send()
    for copy in gain_copies + gain_lines + dkv_copies + kv_copies + packs + seg_copies:
        copy.wait_send()
    for i in range(n_att):
        weight_sent(i)
    rows_sent(send_df, 2)
    parts_sent(send_dh, 3)


def layer(n_seq, n_fsdp, share, hidden, reach, head_count, x, cot, rates, segs, gains,
          w_gate, w_up, w_query, w_key, w_value, w_output, w_down):
    rows, width = x.shape
    depth = width // n_fsdp
    head_width = w_key.shape[1]
    query_width = w_query.shape[1]
    heads_width = query_width + 2 * head_width
    rows_o = w_output.shape[0]
    n_items = 4 * (n_fsdp - 1)
    anywhere = pl.BlockSpec(memory_space=pl.ANY)
    in_vmem = pl.BlockSpec(memory_space=pltpu.VMEM)
    shape = jax.ShapeDtypeStruct
    sems = pltpu.SemaphoreType.DMA

    def low(*size):
        return pltpu.VMEM(size, BF16)

    def full(*size):
        return pltpu.VMEM(size, F32)

    return pl.pallas_call(
        functools.partial(layer_kernel, n_seq, n_fsdp, share, reach, head_count),
        out_shape=[
            shape((2 * rows + 8, width), F32),
            shape((2 * n_fsdp + 1, depth, hidden), BF16),
            shape((hidden // 128 + 2, 128, width), BF16),
        ],
        in_specs=[in_vmem] * 10 + [anywhere] * 7,
        out_specs=[in_vmem] + [anywhere] * 2,
        scratch_shapes=[
            low(width, heads_width),
            low(n_fsdp * rows_o, width),
            low(2, width, hidden),
            low(hidden, width),
            full(n_fsdp, 8, -(-sum(g.shape[0] for g in gains) // 128) * 128),
            pltpu.VMEM((n_seq, 8, rows), jnp.int32),
            full(8, width),
            low(rows, (reach + 1) * rows),
            full(2, rows, head_width // 2),
            low(rows, width),
            full(rows, heads_width),
            low(head_count, rows, head_width),
            low(rows, 2 * head_width),
            low(reach + 1, rows, 2 * head_width),
            low(head_count, rows, (reach + 1) * rows),
            low(rows, query_width),
            full(rows, width),
            full(rows, width),
            low(n_fsdp, rows, width),
            low(n_fsdp, rows, width),
            low(max(width, 2 * n_fsdp * rows), hidden),
            low(n_fsdp, rows, hidden),
            low(2, n_fsdp, rows, hidden),
            low(width, n_fsdp * rows),
            low(n_fsdp - 1, rows, width),
            low(2, n_fsdp - 1, rows, width),
            low(2, rows, width),
            full(rows, width),
            low(hidden // 256, 128, width),
            low(n_fsdp, depth, hidden),
            low(n_fsdp, rows_o // 2, width),
            low(n_fsdp, depth // 2, heads_width),
            low(hidden // 256, 64, width),
            low(n_fsdp, depth // 2, hidden),
            low(1, rows_o // 4, width),
            low(n_fsdp, depth // 2, heads_width // 2),
            low(hidden // 256, 32, width),
            low(n_fsdp, depth // 2, hidden // 2),
            low(1, rows_o // 8, width),
            low(n_fsdp, depth // 2, heads_width // 4),
            low(n_fsdp - 1, rows_o // 2, width),
            low(n_fsdp - 1, depth // 2, heads_width // 4),
            low(rows, width),
            low(head_count, rows, head_width),
            low(head_count, rows, (reach + 1) * rows),
            full(rows, 2 * head_width),
            low(reach, rows, 2 * head_width),
            low(reach, rows, 2 * head_width),
            low(rows, heads_width),
            full(8, width),
            full(n_seq, 8, width),
            full(n_fsdp, 8, width),
            sems((n_items, 5)),
            sems((n_items, 5)),
            sems((7,)),
            sems((n_fsdp,)),
            sems((n_fsdp,)),
            sems((n_seq,)),
            sems((n_seq,)),
            sems((reach,)),
            sems((reach,)),
            sems((4, n_fsdp)),
            sems((4, n_fsdp)),
            sems((7,)),
            sems((reach,)),
            sems((reach,)),
            sems((2 + 3 * n_fsdp,)),
            sems((2 + 3 * n_fsdp,)),
            sems((4 + n_fsdp,)),
            sems((4 + n_fsdp,)),
            sems((4 + n_fsdp,)),
            sems((4 + n_fsdp,)),
            sems((4 + n_fsdp,)),
            sems((4 + n_fsdp,)),
            sems((2, n_fsdp)),
            sems((2, n_fsdp)),
            sems((4 + n_fsdp,)),
            sems((4 + n_fsdp, 3)),
            sems((4 + n_fsdp, 3)),
            sems((n_seq + n_fsdp,)),
            sems((n_seq + n_fsdp,)),
        ],
        compiler_params=pltpu.CompilerParams(
            collective_id=0, has_side_effects=True, vmem_limit_bytes=63 << 20
        ),
        name="decoder_layer",
    )(x, cot, rates, segs, *gains, w_gate, w_up, w_query, w_key, w_value, w_output, w_down)


def finish_kernel(
    share, skip_ref, wins_ref, d0_ref, d1_ref, d2_ref, qkv_ref, wo_ref, small_ref,
    gate_ref, up_ref, down_ref, wq_ref, wk_ref, wv_ref, wo_out, out_ref, dx_ref, *gain_outs,
):
    n_win, hidden = wins_ref.shape[0] // 2, wins_ref.shape[2]
    starts = [window_start(i, share) for i in range(n_win)]
    for i, ref in enumerate((gate_ref, up_ref)):
        for w in range(n_win):
            at = i * n_win + w
            first = starts[w]
            last = starts[w + 1] if w + 1 < n_win else first + hidden
            shared = starts[w - 1] + hidden - first if w else 0
            if shared:
                ref[:, first : first + shared] = wins_ref[at, :, :shared].astype(F32) + wins_ref[
                    at - 1, :, hidden - shared :
                ].astype(F32)
            ref[:, first + shared : last] = wins_ref[at, :, shared : last - first].astype(F32)
    for k, ref in enumerate((d0_ref, d1_ref, d2_ref)):
        down_ref[pl.ds(k * ref.shape[0], ref.shape[0]), :] = ref[...].astype(F32)
    start = 0
    for ref in (wq_ref, wk_ref, wv_ref):
        size = ref.shape[1]
        ref[...] = qkv_ref[0, :, start : start + size].astype(F32)
        start += size
    wo_out[...] = wo_ref[...].astype(F32)

    @pl.when(pl.program_id(0) == 0)
    def _():
        rows_here = dx_ref.shape[0]
        dx_ref[...] = small_ref[:rows_here]
        out_ref[...] = small_ref[rows_here : 2 * rows_here].astype(BF16)
        for row, ref in enumerate(gain_outs):
            ref[...] = small_ref[2 * rows_here + row, : ref.shape[0]]


def finish(share, skipped, gain_sizes, query_width, head_width, rows_o, windows, tiles, small):
    n_win, rows, hidden = windows.shape
    n_win = n_win // 2
    width = tiles.shape[2]
    rows_here = small.shape[0] // 2 - 4
    slab = 32
    steps = rows // slab
    down_slab = share // steps // 3
    heads_width = query_width + 2 * head_width
    down = tiles.reshape(-1, width)
    start_o = (down.shape[0] - rows_o) // slab
    shape = jax.ShapeDtypeStruct

    def slabs(n_rows, n_cols, n_slabs):
        return pl.BlockSpec(
            (n_rows, n_cols), lambda i, skip: (jnp.minimum(i, n_slabs - 1), 0)
        )

    def down_part(k):
        return pl.BlockSpec((down_slab, width), lambda i, skip: (3 * i + k + skip[0], 0))

    def whole(array_shape):
        return pl.BlockSpec(array_shape, lambda i, skip: (0,) * len(array_shape))

    return pl.pallas_call(
        functools.partial(finish_kernel, share),
        grid_spec=pltpu.PrefetchScalarGridSpec(
            num_scalar_prefetch=1,
            grid=(steps,),
            in_specs=[
                pl.BlockSpec((2 * n_win, slab, hidden), lambda i, skip: (0, i, 0)),
                down_part(0),
                down_part(1),
                down_part(2),
                pl.BlockSpec((1, slab, heads_width), lambda i, skip: (2 * n_win, i, 0)),
                pl.BlockSpec(
                    (slab, width),
                    lambda i, skip: (start_o + jnp.minimum(i, rows_o // slab - 1), 0),
                ),
                whole(small.shape),
            ],
            out_specs=[
                slabs(slab, n_win * share, steps),
                slabs(slab, n_win * share, steps),
                slabs(3 * down_slab, width, steps),
                slabs(slab, query_width, steps),
                slabs(slab, head_width, steps),
                slabs(slab, head_width, steps),
                slabs(slab, width, rows_o // slab),
                whole((rows_here, width)),
                whole((rows_here, width)),
            ]
            + [whole((size,)) for size in gain_sizes],
        ),
        out_shape=[
            shape((rows, n_win * share), F32),
            shape((rows, n_win * share), F32),
            shape((share, width), F32),
            shape((rows, query_width), F32),
            shape((rows, head_width), F32),
            shape((rows, head_width), F32),
            shape((rows_o, width), F32),
            shape((rows_here, width), BF16),
            shape((rows_here, width), F32),
        ]
        + [shape((size,), F32) for size in gain_sizes],
        compiler_params=pltpu.CompilerParams(vmem_limit_bytes=48 << 20),
        name="finish",
    )((skipped // down_slab).reshape(1), windows, down, down, down, windows, down, small)


def shards(n_seq, n_fsdp, *args):
    w_query, w_key, w_output, w_gate = args[4], args[5], args[9], args[12]
    depth, ffn_width = w_gate.shape
    rows_here = args[0].shape[1]
    share = ffn_width // n_fsdp
    reach = (WINDOW - 2 + rows_here) // rows_here
    fits = (
        n_seq == 8
        and n_fsdp == 4
        and args[0].shape[0] == 1
        and reach < n_seq
        and rows_here == 128
        and window_width(share, n_fsdp) == 256 * (2 * n_fsdp - 1)
        and depth % 32 == 0
        and w_output.shape[0] == 256
        and w_key.shape[1] % 256 == 0
        and w_query.shape[1] % 512 == 0
        and w_output.shape[1] % 384 == 0
        and ffn_width % n_fsdp == 0
        and share % 16 == 0
        and rows_here // 2 * (share // 64) * 2 == rows_here * (depth // 32) * 3
        and (share - window_start(1, share)) % 64 == 0
        and window_start(n_fsdp - 1, share) + window_width(share, n_fsdp) == ffn_width
    )
    if fits:
        return shards_fused(n_seq, n_fsdp, *args)
    return shards_plain(*args)


def shards_fused(
    n_seq,
    n_fsdp,
    inputs,
    segments,
    cotangent,
    gain_attn_in,
    w_query,
    w_key,
    w_value,
    gain_query,
    gain_key,
    w_output,
    gain_attn_out,
    gain_ffn_in,
    w_gate,
    w_up,
    w_down,
    gain_ffn_out,
):
    rows_here, width = inputs.shape[1:]
    head_width = w_key.shape[1]
    query_width = w_query.shape[1]
    head_count = query_width // head_width
    share = w_gate.shape[1] // n_fsdp
    hidden = window_width(share, n_fsdp)
    reach = (WINDOW - 2 + rows_here) // rows_here
    line = lax.axis_index("fsdp")
    gains = (gain_attn_in, gain_attn_out, gain_ffn_in, gain_ffn_out, gain_query, gain_key)
    rates = 10000.0 ** (-(np.arange(head_width // 2, dtype=np.float32) * 2.0) / head_width)
    small, fin_gu, fin_d = layer(
        n_seq, n_fsdp, share, hidden, reach, head_count,
        inputs[0], cotangent[0], jnp.asarray(rates, F32)[None], segments, gains,
        w_gate, w_up, w_query, w_key, w_value, w_output, w_down,
    )
    (
        grad_gate, grad_up, grad_down, grad_q, grad_k, grad_v, grad_o, outputs, d_inputs,
        g_attn_in, g_attn_out, g_ffn_in, g_ffn_out, g_query, g_key,
    ) = finish(
        share, line * share - window_start(line, share), [g.shape[0] for g in gains],
        query_width, head_width, w_output.shape[0], fin_gu, fin_d, small,
    )
    return (
        outputs[None],
        d_inputs[None],
        g_attn_in,
        grad_q,
        grad_k,
        grad_v,
        g_query,
        g_key,
        grad_o,
        g_attn_out,
        g_ffn_in,
        grad_gate,
        grad_up,
        grad_down,
        g_ffn_out,
    )


def solution(mesh):
    placed = (
        P("fsdp", "seq", None),
        P("fsdp", "seq"),
        P("fsdp", "seq", None),
        P("fsdp"),
        P("fsdp", None),
        P("fsdp", None),
        P("fsdp", None),
        P("fsdp"),
        P("fsdp"),
        P("fsdp", None),
        P("fsdp"),
        P("fsdp"),
        P("fsdp", None),
        P("fsdp", None),
        P("fsdp", None),
        P("fsdp"),
    )
    return jax.shard_map(
        functools.partial(shards, mesh.shape["seq"], mesh.shape["fsdp"]),
        mesh=mesh,
        in_specs=placed,
        out_specs=(
            P("fsdp", "seq", None),
            P("fsdp", "seq", None),
            P("fsdp"),
            P("fsdp", None),
            P("fsdp", None),
            P("fsdp", None),
            P("fsdp"),
            P("fsdp"),
            P("fsdp", None),
            P("fsdp"),
            P("fsdp"),
            P("fsdp", None),
            P("fsdp", None),
            P("fsdp", None),
            P("fsdp"),
        ),
        check_vma=False,
    )
```

```python
import functools

import jax
import jax.numpy as jnp
import numpy as np
from jax import lax
from jax.experimental import pallas as pl
from jax.experimental.pallas import tpu as pltpu
from jax.sharding import PartitionSpec as P

WINDOW = 512


epsilon = 1e-06
masked_value = -1e30


def from_behind(block, axis, distance):
    devices = range(lax.axis_size(axis))
    route = [(i - distance, i) for i in devices if i - distance in devices]
    return lax.ppermute(block, axis, route)


def norm_rows(rows_in, gain_vec):
    return (
        rows_in
        * lax.rsqrt(jnp.mean(rows_in * rows_in, axis=-1, keepdims=True) + epsilon)
        * gain_vec
    )


def angles(positions, head_width):
    inv_rates = 10000.0 ** (-(jnp.arange(head_width // 2, dtype=jnp.float32) * 2.0) / head_width)
    return positions.astype(jnp.float32)[:, None] * inv_rates[None, :]


def rotate(rows_in, angles_at):
    half_width = rows_in.shape[-1] // 2
    lower_half = rows_in[..., :half_width]
    upper_half = rows_in[..., half_width:]
    cosine = jnp.cos(angles_at)
    sine_part = jnp.sin(angles_at)
    return jnp.concatenate(
        [
            lower_half * cosine - upper_half * sine_part,
            upper_half * cosine + lower_half * sine_part,
        ],
        axis=-1,
    )


def geglu_act(gate_proj, up_proj):
    return jax.nn.gelu(gate_proj, approximate=True) * up_proj


def inner_rows(left, right):
    return lax.dot_general(
        left, right, (((0,), (0,)), ((), ())), preferred_element_type=jnp.float32
    )


def outer_cols(left, right):
    return lax.dot_general(
        left, right, (((1,), (1,)), ((), ())), preferred_element_type=jnp.float32
    )


def shards_plain(
    inputs,
    segments,
    cotangent,
    gain_attn_in,
    w_query,
    w_key,
    w_value,
    gain_query,
    gain_key,
    w_output,
    gain_attn_out,
    gain_ffn_in,
    w_gate,
    w_up,
    w_down,
    gain_ffn_out,
):
    rows_here = inputs.shape[1]
    head_width = w_key.shape[1]
    head_count = w_query.shape[1] // head_width
    reach_devs = (WINDOW - 2 + rows_here) // rows_here
    score_scale = head_width ** (-0.5)
    first_row = lax.axis_index("seq") * rows_here
    tokens = inputs[0].astype(jnp.float32)
    seg_here = segments[0]
    positions = first_row + jnp.arange(rows_here, dtype=jnp.int32)
    angles_at = angles(positions - seg_here, head_width)
    wq_all, wk_all, wv_all, wo_all, g_attn_in, g_query, g_key, g_attn_out, g_ffn_in, g_ffn_out = (
        lax.all_gather(w_query, "fsdp", axis=0, tiled=True),
        lax.all_gather(w_key, "fsdp", axis=0, tiled=True),
        lax.all_gather(w_value, "fsdp", axis=0, tiled=True),
        lax.all_gather(w_output, "fsdp", axis=0, tiled=True),
        lax.all_gather(gain_attn_in, "fsdp", axis=0, tiled=True),
        lax.all_gather(gain_query, "fsdp", axis=0, tiled=True),
        lax.all_gather(gain_key, "fsdp", axis=0, tiled=True),
        lax.all_gather(gain_attn_out, "fsdp", axis=0, tiled=True),
        lax.all_gather(gain_ffn_in, "fsdp", axis=0, tiled=True),
        lax.all_gather(gain_ffn_out, "fsdp", axis=0, tiled=True),
    )
    g_attn_in = g_attn_in.astype(jnp.float32)
    g_query = g_query.astype(jnp.float32)
    g_key = g_key.astype(jnp.float32)
    g_attn_out = g_attn_out.astype(jnp.float32)
    g_ffn_in = g_ffn_in.astype(jnp.float32)
    g_ffn_out = g_ffn_out.astype(jnp.float32)
    normed_one, pull_one = jax.vjp(norm_rows, tokens, g_attn_in)
    h_one = normed_one.astype(jnp.bfloat16)
    q_raw = jnp.dot(h_one, wq_all, preferred_element_type=jnp.float32)
    k_raw = jnp.dot(h_one, wk_all, preferred_element_type=jnp.float32)
    v_raw = jnp.dot(h_one, wv_all, preferred_element_type=jnp.float32)

    def prepare(q_in, k_in, gq_in, gk_in):
        q_rows = q_in.reshape(q_in.shape[0], head_count, head_width)
        q_fin = rotate(norm_rows(q_rows, gq_in), angles_at[:, None, :])
        k_fin = rotate(norm_rows(k_in, gk_in), angles_at)
        return (q_fin, k_fin)

    (q_fin, k_fin), pull_prep = jax.vjp(prepare, q_raw, k_raw, g_query, g_key)
    q_low = q_fin.astype(jnp.bfloat16).reshape(rows_here * head_count, head_width)
    k_low = k_fin.astype(jnp.bfloat16)
    v_low = v_raw.astype(jnp.bfloat16)
    key_parts = []
    value_parts = []
    seg_parts = []
    for offset in range(reach_devs, 0, -1):
        k_came, v_came, s_came = from_behind((k_low, v_low, seg_here), "seq", offset)
        key_parts.append(k_came)
        value_parts.append(v_came)
        seg_parts.append(s_came)
    key_rows = jnp.concatenate(key_parts + [k_low], axis=0)
    value_rows = jnp.concatenate(value_parts + [v_low], axis=0)
    key_segs = jnp.concatenate(seg_parts + [seg_here], axis=0)
    key_place = (
        first_row
        - reach_devs * rows_here
        + jnp.arange((reach_devs + 1) * rows_here, dtype=jnp.int32)
    )
    distance = positions[:, None] - key_place[None, :]
    allowed = (
        (distance >= 0)
        & (distance < WINDOW)
        & (key_place[None, :] >= 0)
        & (seg_here[:, None] == key_segs[None, :])
    )
    scores = (outer_cols(q_low, key_rows) * score_scale).reshape(rows_here, head_count, -1)
    masked = jnp.where(allowed[:, None, :], scores, masked_value)
    attn_probs = jax.nn.softmax(masked, axis=-1).reshape(rows_here * head_count, -1)
    probs_low = attn_probs.astype(jnp.bfloat16)
    attended = jnp.dot(probs_low, value_rows, preferred_element_type=jnp.float32)
    att_low = attended.reshape(rows_here, head_count * head_width).astype(jnp.bfloat16)
    o_raw = jnp.dot(att_low, wo_all, preferred_element_type=jnp.float32)
    branch_att, pull_att = jax.vjp(norm_rows, o_raw, g_attn_out)
    middle = tokens + branch_att
    normed_two, pull_mid = jax.vjp(norm_rows, middle, g_ffn_in)
    h_two = normed_two.astype(jnp.bfloat16)
    gate_all, up_all, down_all = (
        lax.all_gather(w_gate, "fsdp", axis=0, tiled=True),
        lax.all_gather(w_up, "fsdp", axis=0, tiled=True),
        lax.all_gather(w_down, "fsdp", axis=0, tiled=True),
    )
    gate_proj = jnp.dot(h_two, gate_all, preferred_element_type=jnp.float32)
    up_proj = jnp.dot(h_two, up_all, preferred_element_type=jnp.float32)
    act_full, pull_act = jax.vjp(geglu_act, gate_proj, up_proj)
    act_low = act_full.astype(jnp.bfloat16)
    f_raw = jnp.dot(act_low, down_all, preferred_element_type=jnp.float32)
    branch_ffn, pull_out = jax.vjp(norm_rows, f_raw, g_ffn_out)
    outputs = (middle + branch_ffn).astype(jnp.bfloat16)
    upstream = cotangent[0].astype(jnp.float32)
    d_fraw, d_gffn_out = pull_out(upstream)
    d_flow = d_fraw.astype(jnp.bfloat16)
    gate_shard, up_shard, down_shard, d_flow = lax.optimization_barrier(
        (w_gate, w_up, w_down, d_flow)
    )
    gate_back, up_back, down_back = (
        lax.all_gather(gate_shard, "fsdp", axis=0, tiled=True),
        lax.all_gather(up_shard, "fsdp", axis=0, tiled=True),
        lax.all_gather(down_shard, "fsdp", axis=0, tiled=True),
    )
    d_act = outer_cols(d_flow, down_back)
    d_gate, d_up = pull_act(d_act)
    dg_low = d_gate.astype(jnp.bfloat16)
    du_low = d_up.astype(jnp.bfloat16)
    d_htwo = outer_cols(dg_low, gate_back) + outer_cols(du_low, up_back)
    grad_down_part = lax.psum_scatter(
        inner_rows(act_low, d_flow).astype(jnp.bfloat16), "fsdp", scatter_dimension=0, tiled=True
    )
    grad_in_part = lax.psum_scatter(
        jnp.concatenate([inner_rows(h_two, dg_low), inner_rows(h_two, du_low)], axis=1).astype(
            jnp.bfloat16
        ),
        "fsdp",
        scatter_dimension=0,
        tiled=True,
    ).astype(jnp.float32)
    hidden_width = w_gate.shape[1]
    grad_gate_part = grad_in_part[:, :hidden_width]
    grad_up_part = grad_in_part[:, hidden_width:]
    d_mid_norm, d_gffn_in = pull_mid(d_htwo)
    d_middle = upstream + d_mid_norm
    d_oraw, d_gattn_out = pull_att(d_middle)
    d_olow = d_oraw.astype(jnp.bfloat16)
    grad_wo = inner_rows(att_low, d_olow)
    d_att_low = (
        outer_cols(d_olow, wo_all).astype(jnp.bfloat16).reshape(rows_here * head_count, head_width)
    )
    d_probs = outer_cols(d_att_low, value_rows)
    d_scores = attn_probs * (d_probs - jnp.sum(attn_probs * d_probs, axis=-1, keepdims=True))
    ds_low = d_scores.astype(jnp.bfloat16)
    d_qfin = jnp.dot(ds_low, key_rows, preferred_element_type=jnp.float32) * score_scale
    d_keys = inner_rows(ds_low, q_low) * score_scale
    d_values = inner_rows(probs_low, d_att_low)
    d_kfin = d_keys[reach_devs * rows_here :]
    d_vsum = d_values[reach_devs * rows_here :]
    for offset in range(1, reach_devs + 1):
        slot_index = reach_devs - offset
        k_back, v_back = (
            from_behind(
                d_keys[slot_index * rows_here : (slot_index + 1) * rows_here].astype(jnp.bfloat16),
                "seq",
                -offset,
            ).astype(jnp.float32),
            from_behind(
                d_values[slot_index * rows_here : (slot_index + 1) * rows_here].astype(
                    jnp.bfloat16
                ),
                "seq",
                -offset,
            ).astype(jnp.float32),
        )
        d_kfin = d_kfin + k_back
        d_vsum = d_vsum + v_back
    d_qraw, d_kraw, d_gquery, d_gkey = pull_prep(
        (d_qfin.reshape(rows_here, head_count, head_width), d_kfin)
    )
    dq_low = d_qraw.astype(jnp.bfloat16)
    dk_low = d_kraw.astype(jnp.bfloat16)
    dv_low = d_vsum.astype(jnp.bfloat16)
    d_hone = outer_cols(dq_low, wq_all) + outer_cols(dk_low, wk_all) + outer_cols(dv_low, wv_all)
    grad_wq = inner_rows(h_one, dq_low)
    grad_wk = inner_rows(h_one, dk_low)
    grad_wv = inner_rows(h_one, dv_low)
    d_tok_norm, d_gattn_in = pull_one(d_hone)
    d_inputs = d_middle + d_tok_norm
    part_wq, part_wk, part_wv, part_wo, part_gai, part_gq, part_gk, part_gao, part_gfi, part_gfo = (
        lax.psum_scatter(
            grad_wq.astype(jnp.bfloat16), "fsdp", scatter_dimension=0, tiled=True
        ).astype(jnp.float32),
        lax.psum_scatter(
            grad_wk.astype(jnp.bfloat16), "fsdp", scatter_dimension=0, tiled=True
        ).astype(jnp.float32),
        lax.psum_scatter(
            grad_wv.astype(jnp.bfloat16), "fsdp", scatter_dimension=0, tiled=True
        ).astype(jnp.float32),
        lax.psum_scatter(
            grad_wo.astype(jnp.bfloat16), "fsdp", scatter_dimension=0, tiled=True
        ).astype(jnp.float32),
        lax.psum_scatter(
            d_gattn_in.astype(jnp.bfloat16), "fsdp", scatter_dimension=0, tiled=True
        ).astype(jnp.float32),
        lax.psum_scatter(
            d_gquery.astype(jnp.bfloat16), "fsdp", scatter_dimension=0, tiled=True
        ).astype(jnp.float32),
        lax.psum_scatter(
            d_gkey.astype(jnp.bfloat16), "fsdp", scatter_dimension=0, tiled=True
        ).astype(jnp.float32),
        lax.psum_scatter(
            d_gattn_out.astype(jnp.bfloat16), "fsdp", scatter_dimension=0, tiled=True
        ).astype(jnp.float32),
        lax.psum_scatter(
            d_gffn_in.astype(jnp.bfloat16), "fsdp", scatter_dimension=0, tiled=True
        ).astype(jnp.float32),
        lax.psum_scatter(
            d_gffn_out.astype(jnp.bfloat16), "fsdp", scatter_dimension=0, tiled=True
        ).astype(jnp.float32),
    )
    cols_wq, cols_wk, cols_wv, cols_wo, cols_gate, cols_up, cols_down = (
        lax.psum_scatter(
            part_wq.astype(jnp.bfloat16), "seq", scatter_dimension=1, tiled=True
        ).astype(jnp.float32),
        lax.psum_scatter(
            part_wk.astype(jnp.bfloat16), "seq", scatter_dimension=1, tiled=True
        ).astype(jnp.float32),
        lax.psum_scatter(
            part_wv.astype(jnp.bfloat16), "seq", scatter_dimension=1, tiled=True
        ).astype(jnp.float32),
        lax.psum_scatter(
            part_wo.astype(jnp.bfloat16), "seq", scatter_dimension=1, tiled=True
        ).astype(jnp.float32),
        lax.psum_scatter(
            grad_gate_part.astype(jnp.bfloat16), "seq", scatter_dimension=1, tiled=True
        ).astype(jnp.float32),
        lax.psum_scatter(
            grad_up_part.astype(jnp.bfloat16), "seq", scatter_dimension=1, tiled=True
        ).astype(jnp.float32),
        lax.psum_scatter(grad_down_part, "seq", scatter_dimension=1, tiled=True).astype(
            jnp.float32
        ),
    )
    sum_wq, sum_wk, sum_wv, sum_wo, sum_gate, sum_up, sum_down = (
        lax.all_gather(cols_wq.astype(jnp.bfloat16), "seq", axis=1, tiled=True).astype(
            cols_wq.dtype
        ),
        lax.all_gather(cols_wk.astype(jnp.bfloat16), "seq", axis=1, tiled=True).astype(
            cols_wk.dtype
        ),
        lax.all_gather(cols_wv.astype(jnp.bfloat16), "seq", axis=1, tiled=True).astype(
            cols_wv.dtype
        ),
        lax.all_gather(cols_wo.astype(jnp.bfloat16), "seq", axis=1, tiled=True).astype(
            cols_wo.dtype
        ),
        lax.all_gather(cols_gate.astype(jnp.bfloat16), "seq", axis=1, tiled=True).astype(
            cols_gate.dtype
        ),
        lax.all_gather(cols_up.astype(jnp.bfloat16), "seq", axis=1, tiled=True).astype(
            cols_up.dtype
        ),
        lax.all_gather(cols_down.astype(jnp.bfloat16), "seq", axis=1, tiled=True).astype(
            cols_down.dtype
        ),
    )
    sum_gai, sum_gq, sum_gk, sum_gao, sum_gfi, sum_gfo = lax.psum(
        (part_gai, part_gq, part_gk, part_gao, part_gfi, part_gfo), "seq"
    )
    return (
        outputs[None],
        d_inputs[None],
        sum_gai,
        sum_wq,
        sum_wk,
        sum_wv,
        sum_gq,
        sum_gk,
        sum_wo,
        sum_gao,
        sum_gfi,
        sum_gate,
        sum_up,
        sum_down,
        sum_gfo,
    )


MESH = pl.DeviceIdType.MESH
BF16 = jnp.bfloat16
F32 = jnp.float32
GELU_RATE = 0.7978845608028654
GELU_CUBE = 0.044715
HID_TILE = 256
ATT_IN, ATT_OUT, FFN_IN, FFN_OUT, QUERY, KEY = range(6)


def bit_of(value, mask):
    return lax.rem(lax.div(value, mask), 2)


def flip(value, masks, bits):
    for b in range(bits):
        if (masks >> b) & 1:
            value = value + (1 << b) * (1 - 2 * bit_of(value, 1 << b))
    return value


def greet(devices):
    barrier = pltpu.get_barrier_semaphore()
    for device in devices:
        pl.semaphore_signal(barrier, inc=1, device_id=device, device_id_type=MESH)
    pl.semaphore_wait(barrier, len(devices))


def remote(src, dst, send, recv, device):
    return pltpu.make_async_remote_copy(
        src_ref=src, dst_ref=dst, send_sem=send, recv_sem=recv,
        device_id=device, device_id_type=MESH,
    )


def many(offset, size):
    return pl.ds(pl.multiple_of(offset, size if size % 128 == 0 else 16), size)


def lanes(offset, size):
    return pl.ds(pl.multiple_of(offset, 128), size)


def window_start(z, share):
    if isinstance(z, int):
        return z * share // 128 * 128
    return lax.div(z * share, 128) * 128


def window_width(share, n_fsdp):
    widest = max((z + 1) * share - window_start(z, share) for z in range(n_fsdp))
    return -(-widest // HID_TILE) * HID_TILE


def dot_nt(left, right):
    return lax.dot_general(left, right, (((1,), (1,)), ((), ())), preferred_element_type=F32)


def dot_nn(left, right):
    return jnp.dot(left, right, preferred_element_type=F32)


def norm_scale(rows_in):
    return lax.rsqrt(jnp.mean(rows_in * rows_in, axis=-1, keepdims=True) + epsilon)


def norm_back(rows_in, gain, scale, upstream):
    pulled = upstream * gain
    inner = jnp.mean(pulled * rows_in, axis=-1, keepdims=True)
    d_rows = scale * pulled - rows_in * (scale * scale * scale * inner)
    return d_rows, jnp.sum(upstream * rows_in * scale, axis=0, keepdims=True)


def turn(rows_in, cosine, sine_part):
    half = rows_in.shape[-1] // 2
    lower, upper = rows_in[:, :half], rows_in[:, half:]
    return jnp.concatenate(
        [lower * cosine - upper * sine_part, upper * cosine + lower * sine_part], axis=-1
    )


class Place:
    def __init__(self):
        self.s = lax.axis_index("seq")
        self.z = lax.axis_index("fsdp")
        self.c = bit_of(self.s, 1)
        self.x = bit_of(self.s, 2)
        self.y = bit_of(self.s, 4)

    def plane(self, masks):
        return (flip(self.s, masks, 3), self.z)

    def line(self, masks):
        return (self.s, flip(self.z, masks, 2))

    def halves(self, first_x):
        if first_x:
            return self.x, self.y, 2, 4
        return self.y, self.x, 4, 2


def layer_kernel(
    n_seq, n_fsdp, share, reach, head_count,
    x_ref, cot_ref, rates_ref, seg_ref,
    gain_a, gain_b, gain_c, gain_d, gain_e, gain_f,
    gate_ref, up_ref, wq_ref, wk_ref, wv_ref, wo_ref, wd_ref,
    small_out, fin_gu, fin_d,
    qkv_s, wo_s, w_in, w_down, pack_all, seg_all, gains, allowed, turns,
    h1_s, raw_s, q_s, kv_own, kv_s, p_s, att_s, o_s, mid_s,
    h_all, df_all, bent_s, act, d_in, h_turn, part_out, part_in, relay_in, total,
    own_d, own_g, own_o, own_q, hi_d, hi_g, hi_o, hi_q, lo_d, lo_g, lo_o, lo_q, line_o, line_q,
    do_s, datt_s, ds_s, dkv_s, dkv_send, dkv_came, dqkv_s, dgains, gain_in, gain_line,
    w_send, w_recv, own_sem, pack_send, pack_recv, seg_send, seg_recv, kv_send, kv_recv,
    ex_send, ex_recv, relay_sem, dkv_ssem, dkv_rsem,
    c_send, c_recv, hi_send, hi_recv, lo_send, lo_recv, z_send, z_recv, oq_send, oq_recv,
    put_sem, ag_send, ag_recv, gain_send, gain_recv,
):
    at = Place()
    s, z, c = at.s, at.z, at.c
    rows, width = x_ref.shape
    depth = width // n_fsdp
    hidden = w_in.shape[2]
    head_width = wk_ref.shape[1]
    query_width = head_count * head_width
    heads_width = query_width + 2 * head_width
    rows_o = wo_ref.shape[0]
    n_hid = hidden // HID_TILE
    third = width // 3
    middle_z = (z > 0) & (z < n_fsdp - 1)
    tokens = n_fsdp * rows

    def hid(n):
        return lanes(n * HID_TILE, HID_TILE)

    def outs(n):
        return lanes(n * third, third)

    skipped = z * share - window_start(z, share)
    spare = hidden - share
    if spare:
        w_down[pl.ds(0, spare)] = jnp.zeros((spare, width), BF16)
        w_down[pl.ds(share, spare)] = jnp.zeros((spare, width), BF16)
    here_z = many(z * depth, depth)
    own_copies = [
        pltpu.make_async_copy(src, dst, own_sem.at[i])
        for i, (src, dst) in enumerate((
            (wq_ref, qkv_s.at[here_z, pl.ds(0, query_width)]),
            (wk_ref, qkv_s.at[here_z, pl.ds(query_width, head_width)]),
            (wv_ref, qkv_s.at[here_z, pl.ds(query_width + head_width, head_width)]),
            (wo_ref, wo_s.at[many(z * rows_o, rows_o)]),
            (wd_ref, w_down.at[many(skipped, share)]),
            (gate_ref.at[:, lanes(window_start(z, share), hidden)], w_in.at[0, here_z]),
            (up_ref.at[:, lanes(window_start(z, share), hidden)], w_in.at[1, here_z]),
        ))
    ]
    seg_all[s] = jnp.broadcast_to(seg_ref[...], seg_all.shape[1:])
    start = 0
    for ref in (gain_a, gain_b, gain_c, gain_d, gain_e, gain_f):
        size = ref.shape[0]
        pack_all[z, 0:1, start : start + size] = ref[...].astype(F32).reshape(1, size)
        start += size
    greet([at.plane(k) for k in range(1, n_seq)] + [at.line(m) for m in range(1, n_fsdp)])

    packs = [
        remote(pack_all.at[z], pack_all.at[z], pack_send.at[m], pack_recv.at[m], at.line(m))
        for m in range(1, n_fsdp)
    ]
    seg_copies = [
        remote(seg_all.at[s], seg_all.at[s], seg_send.at[k], seg_recv.at[k], at.plane(k))
        for k in range(1, n_seq)
    ]
    kv_copies = [
        remote(kv_own, kv_s.at[reach - o], kv_send.at[o - 1], kv_recv.at[o - 1],
               (lax.rem(s + o, n_seq), z))
        for o in range(1, reach + 1)
    ]

    def w_region(kind, sub, whose, hi, lo, level):
        base = whose * depth
        if kind == "q":
            cols = (
                lanes(hi * (query_width // 2) + lo * (query_width // 4), query_width // 4),
                lanes(hi * (query_width // 2), query_width // 2),
                pl.ds(0, query_width),
            )[level]
            return qkv_s.at[many(base + c * (depth // 2), depth // 2), cols]
        if kind == "kv":
            start = query_width + c * head_width
            if level == 0:
                start = start + lo * (head_width // 2)
            cols = lanes(start, head_width if level else head_width // 2)
            if level == 2:
                return qkv_s.at[many(base, depth), cols]
            return qkv_s.at[many(base + hi * (depth // 2), depth // 2), cols]
        if kind == "wo":
            start = whose * rows_o + c * (rows_o // 2)
            if level < 2:
                start = start + hi * (rows_o // 4)
            if level < 1:
                start = start + lo * (rows_o // 8)
            return wo_s.at[many(start, rows_o // (8, 4, 2)[level])]
        skip, size = sub
        if level == 2:
            return [
                w_in.at[c, many(base + half * (depth // 2) + skip, size)] for half in range(2)
            ]
        here = many(base + hi * (depth // 2) + skip, size)
        if level == 1:
            return w_in.at[c, here]
        return w_in.at[c, here, lanes(lo * (hidden // 2), hidden // 2)]

    def w_sources(kind, sub, to, hi, lo):
        if kind == "q":
            cols = lanes(hi * (query_width // 2) + lo * (query_width // 4), query_width // 4)
            return [wq_ref.at[many(c * (depth // 2), depth // 2), cols]]
        if kind == "wo":
            start = c * (rows_o // 2) + hi * (rows_o // 4) + lo * (rows_o // 8)
            return [wo_ref.at[many(start, rows_o // 8)]]
        if kind == "kv":
            here = many(hi * (depth // 2), depth // 2)
            cols = lanes(lo * (head_width // 2), head_width // 2)
            return [ref.at[here, cols] for ref in (wk_ref, wv_ref)]
        skip, size = sub
        here = many(hi * (depth // 2) + skip, size)
        cols = lanes(window_start(to, share) + lo * (hidden // 2), hidden // 2)
        return [ref.at[here, cols] for ref in (gate_ref, up_ref)]

    items = []
    for kinds in (("q", "kv"), ("wo",)):
        for m in range(1, n_fsdp):
            for kind in kinds:
                items.append((kind, m, (m % 2 == 1) == (kind in ("kv", "wo")), None))
    n_att = len(items)
    for m in range(1, n_fsdp):
        items.append(("gu", m, m % 2 == 1, (0, depth // 2)))
    steps, starts = [], []
    for i, (kind, m, first_x, sub) in enumerate(items):
        hi, lo, mask_hi, mask_lo = at.halves(first_x)
        there = flip(z, m, 2)
        firsts = [
            remote(src, w_region(kind, sub, z, hi, lo, 0), w_send.at[i, 0], w_recv.at[i, 0],
                   at.line(m))
            for src in w_sources(kind, sub, there, hi, lo)
        ]
        starts.append(firsts)
        stages = [firsts[:1]]
        for k, mask in enumerate((mask_lo, mask_hi, 1)):
            parts = w_region(kind, sub, there, hi, lo, k)
            stages.append([
                remote(part, part, w_send.at[i, k + 1 + n], w_recv.at[i, k + 1 + n], at.plane(mask))
                for n, part in enumerate(parts if isinstance(parts, list) else [parts])
            ])
        steps.append(stages)

    def begin_weight(i):
        if len(starts[i]) == 1:
            starts[i][0].start()
        else:
            for core, first in enumerate(starts[i]):
                pl.when(c == core)(first.start)

    def weight_here(i, stage):
        for copy in steps[i][stage]:
            copy.wait_recv()

    def move_weight(i, stage):
        weight_here(i, stage - 1)
        for copy in steps[i][stage]:
            copy.start()

    def weight_sent(i):
        for copies in steps[i]:
            for copy in copies:
                copy.wait_send()

    n_items = len(items)
    n_qkv = 2 * (n_fsdp - 1)
    ahead, lag = 6, 3
    for copy in packs + seg_copies:
        copy.start()
    for i in range(ahead):
        begin_weight(i)
    for copy in own_copies:
        copy.start()

    def weight_steps(t):
        for stage in (3, 2, 1):
            i = t - lag * (stage - 1)
            if 0 <= i < n_att:
                move_weight(i, stage)
                if stage == 1 and i + ahead < n_items:
                    begin_weight(i + ahead)

    weight_steps(0)
    weight_steps(1)
    for copy in seg_copies:
        copy.wait_recv()
    across = lax.broadcasted_iota(jnp.int32, (rows, rows), 0)
    along = lax.broadcasted_iota(jnp.int32, (rows, rows), 1)
    seg_here = jnp.broadcast_to(seg_ref[...].astype(F32), (rows, rows)).T
    for o in range(reach, -1, -1):
        key_seg = seg_all[lax.rem(s + n_seq - o, n_seq), 0:1, :].astype(F32)
        apart = across - along + o * rows
        fine = (apart >= 0) & (apart < WINDOW) & (seg_here == key_seg) & (s >= o)
        allowed[:, pl.ds((reach - o) * rows, rows)] = jnp.where(fine, 1.0, 0.0).astype(BF16)
    angle = ((s * rows + across).astype(F32) - seg_here) * rates_ref[...]
    turns[0] = jnp.cos(angle)
    turns[1] = jnp.sin(angle)
    for copy in packs:
        copy.wait_recv()
    gains[...] = jnp.zeros(gains.shape, F32)
    start = 0
    for row in range(6):
        size = (depth if row < QUERY else head_width // n_fsdp)
        for block in range(n_fsdp):
            gains[row : row + 1, block * size : (block + 1) * size] = pack_all[
                block, 0:1, start : start + size
            ]
        start += size

    def gain(row):
        return gains[row : row + 1, : (width if row < QUERY else head_width)]

    x = x_ref[...].astype(F32)
    h1_s[...] = (x * norm_scale(x) * gain(ATT_IN)).astype(BF16)

    for t in range(2, n_att + 2 * lag):
        weight_steps(t)
    for i in range(n_qkv):
        weight_here(i, 3)
    for copy in own_copies[:3]:
        copy.wait()

    def move_gu(*moves):
        for k, stage in moves:
            move_weight(n_att + k - 1, stage)

    move_gu((1, 1))
    tile = heads_width // 3

    @pl.loop(0, 3)
    def _(n):
        cols = lanes(n * tile, tile)
        raw_s[:, cols] = dot_nn(h1_s[...], qkv_s[:, cols])

    k_raw = raw_s[:, query_width : query_width + head_width]
    kv_own[:, :head_width] = turn(
        k_raw * norm_scale(k_raw) * gain(KEY), turns[0], turns[1]
    ).astype(BF16)
    kv_own[:, head_width:] = raw_s[:, query_width + head_width :].astype(BF16)
    for copy in kv_copies:
        copy.start()
    kv_s[reach] = kv_own[...]
    for h in range(head_count):
        q_raw = raw_s[:, h * head_width : (h + 1) * head_width]
        q_fin = q_raw * norm_scale(q_raw) * gain(QUERY)
        q_s[h] = turn(q_fin, turns[0], turns[1]).astype(BF16)
    for i in range(n_qkv, n_att):
        weight_here(i, 3)
    own_copies[3].wait()
    move_gu((1, 2))
    move_gu((2, 1))
    for copy in kv_copies:
        copy.wait_recv()

    def keys():
        return kv_s[:, :, :head_width].reshape((reach + 1) * rows, head_width)

    def values():
        return kv_s[:, :, head_width:].reshape((reach + 1) * rows, head_width)

    for h in range(head_count):
        scores = dot_nt(q_s[h], keys()) * (head_width**-0.5)
        masked = jnp.where(allowed[...].astype(F32) > 0.5, scores, masked_value)
        grown = jnp.exp(masked - jnp.max(masked, axis=-1, keepdims=True))
        probs = grown / jnp.sum(grown, axis=-1, keepdims=True)
        p_s[h] = probs.astype(BF16)
        att_s[:, h * head_width : (h + 1) * head_width] = dot_nn(p_s[h], values()).astype(BF16)

    move_gu((3, 1))
    @pl.loop(0, 3)
    def _(n):
        o_s[:, outs(n)] = dot_nn(att_s[...], wo_s[:, outs(n)])

    o_raw = o_s[...]
    middle = x_ref[...].astype(F32) + o_raw * norm_scale(o_raw) * gain(ATT_OUT)
    mid_s[...] = middle
    h_all[0] = (middle * norm_scale(middle) * gain(FFN_IN)).astype(BF16)

    def exchange(phase, src, dst):
        return {
            m: remote(src(m), dst(m), ex_send.at[phase, m], ex_recv.at[phase, m], at.line(m))
            for m in range(1, n_fsdp)
        }

    last = n_fsdp - 1
    send_h = exchange(0, lambda m: h_all.at[0], lambda m: h_all.at[m])
    send_f = exchange(1, lambda m: part_out.at[m - 1], lambda m: part_in.at[0, m - 1])
    send_df = exchange(2, lambda m: df_all.at[0], lambda m: df_all.at[m])
    send_dh = exchange(3, lambda m: part_out.at[m - 1], lambda m: part_in.at[1, m - 1])
    onward = {
        phase: remote(rows_all.at[2], rows_all.at[last],
                      relay_sem.at[phase], ex_recv.at[phase, last], at.line(1))
        for phase, rows_all in ((0, h_all), (2, df_all))
    }
    by_way = {
        phase: remote(part_out.at[last - 1], relay_in.at[phase // 2],
                      relay_sem.at[phase], relay_sem.at[phase + 3], at.line(1))
        for phase in (1, 3)
    }

    def send_rows(copies):
        copies[2].start()
        pl.when(middle_z)(copies[last].start)
        copies[1].start()

    def relay_rows(copies, phase):
        @pl.when(middle_z)
        def _():
            copies[2].wait_recv()
            onward[phase].start()

    def take_rows(copies, m):
        if m == 2:
            pl.when(~middle_z)(copies[2].wait_recv)
        elif m:
            copies[m].wait_recv()

    def send_part(copies, phase, m):
        if m == 1:
            copies[1].start()
        elif m == 2:
            pl.when(~middle_z)(copies[2].start)
        else:
            pl.when(~middle_z)(by_way[phase].start)
            pl.when(middle_z)(copies[last].start)

    def send_joint_part(copies, phase):
        @pl.when(middle_z)
        def _():
            by_way[phase].wait_recv()
            part_out[1] = (
                part_out[1].astype(F32) + relay_in[phase // 2].astype(F32)
            ).astype(BF16)
            copies[2].start()

    def take_parts(copies):
        copies[1].wait_recv()
        copies[2].wait_recv()
        pl.when(middle_z)(copies[last].wait_recv)

    def rows_sent(copies, phase):
        copies[1].wait_send()
        copies[2].wait_send()

        @pl.when(middle_z)
        def _():
            copies[last].wait_send()
            onward[phase].wait_send()

    def parts_sent(copies, phase):
        copies[1].wait_send()
        copies[2].wait_send()
        pl.when(middle_z)(copies[last].wait_send)
        pl.when(~middle_z)(by_way[phase].wait_send)

    send_rows(send_h)

    @pl.when(~middle_z)
    def _():
        part_in[0, last - 1] = jnp.zeros((rows, width), BF16)
        part_in[1, last - 1] = jnp.zeros((rows, width), BF16)

    move_gu((2, 2))
    move_gu((1, 3))
    move_gu((3, 2))
    relay_rows(send_h, 0)
    move_gu((2, 3))
    move_gu((3, 3))
    for i in range(n_att, n_items):
        weight_here(i, 3)
    for copy in own_copies[4:]:
        copy.wait()
    half_h = hidden // 2

    for m in range(n_fsdp - 1, -1, -1):
        take_rows(send_h, m)
        for n in range(2):
            cols = slice(n * half_h, (n + 1) * half_h)
            gate = dot_nn(h_all[m], w_in[0, :, cols])
            up = dot_nn(h_all[m], w_in[1, :, cols])
            squared = gate * gate
            bent = jnp.tanh(GELU_RATE * (gate + GELU_CUBE * squared * gate))
            gelu = 0.5 * gate * (1.0 + bent)
            slope = 0.5 * (1.0 + bent) + 0.5 * gate * (1.0 - bent * bent) * (
                GELU_RATE * (1.0 + 3.0 * GELU_CUBE * squared)
            )
            bent_s[pl.ds(m * rows, rows), cols] = gelu.astype(BF16)
            bent_s[pl.ds(tokens + m * rows, rows), cols] = (slope * up).astype(BF16)
            act[m, :, cols] = (gelu * up).astype(BF16)
        part = dot_nn(act[m], w_down[...])
        if m:
            part_out[m - 1] = part.astype(BF16)
            send_part(send_f, 1, m)
        else:
            total[...] = part

    send_joint_part(send_f, 1)
    for m in range(n_fsdp):
        h_turn[:, pl.ds(m * rows, rows)] = h_all[m].T
    for i in range(n_att, n_items):
        weight_sent(i)

    take_parts(send_f)
    f_raw = total[...]
    for m in range(1, n_fsdp):
        f_raw = f_raw + part_in[0, m - 1].astype(F32)
    cot = cot_ref[...].astype(F32)
    scale = norm_scale(f_raw)
    d_f, d_gain = norm_back(f_raw, gain(FFN_OUT), scale, cot)
    df_all[0] = d_f.astype(BF16)
    send_rows(send_df)
    small_out[pl.ds(rows, rows), :] = mid_s[...] + f_raw * scale * gain(FFN_OUT)
    dgains[...] = jnp.zeros(dgains.shape, F32)
    dgains[FFN_OUT : FFN_OUT + 1, :] = d_gain
    parts_sent(send_f, 1)

    chunks = [("d", 0, False), ("d", 1, True)]
    chunks += [("g", m, m % 2 == 0) for m in range(n_fsdp)]
    chunks += [("o", 0, False), ("q", 0, True)]
    tiles_d = hidden // 256
    spans_d = (pl.ds(0, n_fsdp), pl.ds(n_fsdp, tiles_d - n_fsdp))

    def mine_of(kind, i):
        if kind == "d":
            return own_d.at[spans_d[i]]
        return {"g": own_g, "o": own_o, "q": own_q}[kind].at[i]

    def hi_part(kind, hi):
        if kind == "d":
            return slice(None), many(hi * 64, 64), slice(None)
        if kind == "g":
            return many(hi * (depth // 2), depth // 2), slice(None)
        if kind == "q":
            return slice(None), lanes(hi * (heads_width // 2), heads_width // 2)
        return many(hi * (rows_o // 4), rows_o // 4), slice(None)

    def lo_part(kind, hi, lo):
        if kind == "d":
            return slice(None), many(hi * 64 + lo * 32, 32), slice(None)
        if kind == "g":
            return (
                many(hi * (depth // 2), depth // 2),
                lanes(lo * (hidden // 2), hidden // 2),
            )
        if kind == "q":
            start = hi * (heads_width // 2) + lo * (heads_width // 4)
            return slice(None), lanes(start, heads_width // 4)
        return many(hi * (rows_o // 4) + lo * (rows_o // 8), rows_o // 8), slice(None)

    def fin_part(kind, i, where, core):
        if kind == "d":
            span = spans_d[i]
            tiles = pl.ds(core * tiles_d + span.start, span.size)
            return fin_d.at[tiles, where[-2], :]
        rows_at, cols_at = where
        if kind == "g":
            return fin_gu.at[core * n_fsdp + i, rows_at, cols_at]
        if kind == "o":
            return fin_d.at[2 * tiles_d + core, rows_at, :]
        base = core * (depth // 2)
        if isinstance(cols_at, slice):
            cols_at = pl.ds(0, heads_width)
        return fin_gu.at[2 * n_fsdp, many(base, depth // 2), cols_at]
    def add(ref, where, other):
        rows_at, cols_at = where
        start = 0 if isinstance(rows_at, slice) else rows_at.start
        slab = 16

        @pl.loop(0, other.shape[0] // slab)
        def _(n):
            here = pl.ds(pl.multiple_of(start + n * slab, slab), slab)
            there = pl.ds(pl.multiple_of(n * slab, slab), slab)
            ref[here, cols_at] = (
                ref[here, cols_at].astype(F32) + other[there, :].astype(F32)
            ).astype(BF16)

    whole = (slice(None), slice(None))
    from_hi = {"d": hi_d, "g": hi_g, "o": hi_o, "q": hi_q}
    from_lo = {"d": lo_d, "g": lo_g, "o": lo_o, "q": lo_q}
    his, los, lines = [], [], []
    for j, (kind, i, first_x) in enumerate(chunks):
        hi, lo, mask_hi, mask_lo = at.halves(first_x)
        mine = mine_of(kind, i)
        if kind == "q":
            parts = (
                own_q.at[:, :, hi_part(kind, 1 - hi)[1]], hi_q,
                own_q.at[:, :, lo_part(kind, hi, 1 - lo)[1]], lo_q,
            )
        else:
            slot = spans_d[i] if kind == "d" else i
            parts = (
                mine.at[hi_part(kind, 1 - hi)], from_hi[kind].at[slot],
                mine.at[lo_part(kind, hi, 1 - lo)], from_lo[kind].at[slot],
            )
        his.append(
            remote(parts[0], parts[1], hi_send.at[j], hi_recv.at[j], at.plane(mask_hi))
        )
        los.append(
            remote(parts[2], parts[3], lo_send.at[j], lo_recv.at[j], at.plane(mask_lo))
        )
        line = None
        if kind == "g" and i:
            line = remote(mine.at[lo_part(kind, hi, lo)],
                          fin_part(kind, z, lo_part(kind, hi, lo), c),
                          z_send.at[j], z_recv.at[j], at.line(i))
        lines.append(line)
    stage = {
        "d": lambda i: part_in.at[0] if i else h_all,
        "g": lambda i: bent_s.at[pl.ds(i * depth, depth)],
        "q": lambda i: w_in.at[0, pl.ds(i * (depth // 2), depth // 2), pl.ds(0, heads_width)],
        "o": lambda i: w_in.at[1, pl.ds(i * (rows_o // 2), rows_o // 2), pl.ds(0, width)],
    }
    to_core = [("d", 0), ("d", 1)]
    to_core += [(kind, m) for kind in "goq" for m in range(n_fsdp)]
    cores = {
        key: remote(stage[key[0]](key[1]), mine_of(*key), c_send.at[k], c_recv.at[k], at.plane(1))
        for k, key in enumerate(to_core)
    }
    line_sums = {}
    for k, (kind, ref) in enumerate((("o", line_o), ("q", line_q))):
        for m in range(1, n_fsdp):
            part = mine_of(kind, m)
            if kind == "q":
                part = part.at[lo_part(kind, at.x, at.y)]
            line_sums[kind, m] = remote(
                part, ref.at[m - 1], oq_send.at[k, m], oq_recv.at[k, m], at.line(m)
            )

    puts, hands = [], []
    for j, (kind, i, first_x) in enumerate(chunks):
        hi, lo, mask_hi, mask_lo = at.halves(first_x)
        which = flip(z, i, 2) if kind == "g" else i
        piece = fin_part(kind, which, lo_part(kind, hi, lo), c)
        half = fin_part(kind, which, hi_part(kind, hi), c)
        full = fin_part(kind, which, whole, c)
        put = None
        if lines[j] is None:
            put = pltpu.make_async_copy(
                mine_of(kind, i).at[lo_part(kind, hi, lo)], piece, put_sem.at[j]
            )
        puts.append(put)
        hands.append([
            remote(part, part, ag_send.at[j, k], ag_recv.at[j, k], at.plane(mask))
            for k, (part, mask) in enumerate(((piece, mask_lo), (half, mask_hi), (full, 1)))
        ])

    def add_all(kind, i, where, came):
        if kind == "d":
            for n in range(spans_d[i].start, spans_d[i].start + spans_d[i].size):
                add(own_d.at[n], where[1:], came.at[n])
        elif kind == "q":
            for m in range(n_fsdp):
                add(own_q.at[m], where, came.at[m])
        else:
            add(mine_of(kind, i), where, came.at[i])

    def take_hi(j):
        kind, i, first_x = chunks[j]
        hi, lo, _, _ = at.halves(first_x)
        his[j].wait_recv()
        add_all(kind, i, hi_part(kind, hi), from_hi[kind])
        los[j].start()

    def take_lo(j):
        kind, i, first_x = chunks[j]
        hi, lo, _, _ = at.halves(first_x)
        los[j].wait_recv()
        add_all(kind, i, lo_part(kind, hi, lo), from_lo[kind])
        if lines[j] is not None:
            lines[j].start()
        elif kind == "q":
            for m in range(1, n_fsdp):
                line_sums[kind, m].start()
        else:
            puts[j].start()

    def begin_hand(j):
        if lines[j] is not None:
            lines[j].wait_recv()
        else:
            puts[j].wait()
        hands[j][0].start()

    def hand_on(j, k):
        hands[j][k - 1].wait_recv()
        hands[j][k].start()

    def down_stage(n):
        return h_all.at[n] if n < n_fsdp else part_in.at[0, n - n_fsdp]

    def down_grads(core, dst_of, adds):
        right = df_all[...].reshape(tokens, width)
        for n in range(tiles_d):
            left = act[:, :, lanes(core * (hidden // 2) + n * 128, 128)].reshape(tokens, 128).T
            grads = dot_nn(left, right)
            dst = dst_of[n] if adds else dst_of(n)
            if adds:
                grads = grads + dst[...].astype(F32)
            dst[...] = grads.astype(BF16)

    def in_grads(core, m, dst, adds):
        left_at = many(flip(z, m, 2) * depth, depth)

        for n in range(2):
            cols = slice(n * half_h, (n + 1) * half_h)
            grads = dot_nn(h_turn[left_at, :], d_in[core, :, :, cols].reshape(tokens, half_h))
            if adds:
                grads = grads + dst[:, cols].astype(F32)
            dst[:, cols] = grads.astype(BF16)

    rows_sent(send_h, 0)
    for m in range(n_fsdp):
        if m == 1:
            relay_rows(send_df, 2)
        take_rows(send_df, m)
        if m == last:
            down_grads(1 - c, down_stage, False)
            cores["d", 0].start()
            cores["d", 1].start()
        for n in range(2):
            cols = slice(n * half_h, (n + 1) * half_h)
            d_act = dot_nt(df_all[m], w_down[cols, :])
            slope = bent_s[pl.ds(tokens + m * rows, rows), cols].astype(F32)
            d_in[0, m, :, cols] = (d_act * slope).astype(BF16)
            gelu = bent_s[pl.ds(m * rows, rows), cols].astype(F32)
            d_in[1, m, :, cols] = (d_act * gelu).astype(BF16)
        part = dot_nt(d_in[0, m], w_in[0]) + dot_nt(d_in[1, m], w_in[1])
        if m:
            part_out[m - 1] = part.astype(BF16)
            send_part(send_dh, 3, m)
        else:
            total[...] = part

    cores["d", 0].wait_recv()
    cores["d", 1].wait_recv()
    down_grads(c, own_d.at, True)
    his[0].start()
    his[1].start()
    send_joint_part(send_dh, 3)
    for m in range(n_fsdp):
        in_grads(1 - c, m, stage["g"](m), False)
        cores["g", m].start()
    for m in range(n_fsdp):
        cores["g", m].wait_recv()
        in_grads(c, m, own_g.at[m], True)
        his[2 + m].start()

    dkv_copies = [
        remote(dkv_send.at[reach - o], dkv_came.at[o - 1], dkv_ssem.at[o - 1], dkv_rsem.at[o - 1],
               (lax.rem(s + n_seq - o, n_seq), z))
        for o in range(1, reach + 1)
    ]
    gain_copies = [
        remote(dgains, gain_in.at[k], gain_send.at[k], gain_recv.at[k], at.plane(k))
        for k in range(1, n_seq)
    ]
    gain_lines = [
        remote(gain_line.at[0], gain_line.at[m], gain_send.at[n_seq + m], gain_recv.at[n_seq + m],
               at.line(m))
        for m in range(1, n_fsdp)
    ]

    def to_middle():
        take_parts(send_dh)
        dh = total[...]
        for m in range(1, n_fsdp):
            dh = dh + part_in[1, m - 1].astype(F32)
        mid = mid_s[...]
        d_mid, d_gain = norm_back(mid, gain(FFN_IN), norm_scale(mid), dh)
        d_mid = d_mid + cot_ref[...].astype(F32)
        mid_s[...] = d_mid
        dgains[FFN_IN : FFN_IN + 1, :] = d_gain
        o_raw = o_s[...]
        d_o, d_gain = norm_back(o_raw, gain(ATT_OUT), norm_scale(o_raw), d_mid)
        dgains[ATT_OUT : ATT_OUT + 1, :] = d_gain
        do_s[...] = d_o.astype(BF16)
        for h in range(head_count):
            here = pl.ds(h * head_width, head_width)
            datt_s[h] = dot_nt(do_s[...], wo_s[here, :]).astype(BF16)

    def unturn(rows_in):
        return turn(rows_in, turns[0], -turns[1])

    def through_head(h):
        probs = p_s[h].astype(F32)
        d_att = datt_s[h]
        d_probs = dot_nt(d_att, values())
        d_scores = probs * (d_probs - jnp.sum(probs * d_probs, axis=-1, keepdims=True))
        ds_low = d_scores.astype(BF16)
        scale = head_width**-0.5
        ds_s[h] = ds_low
        cols = slice(h * head_width, (h + 1) * head_width)
        q_raw = raw_s[:, cols]
        d_q, d_gain = norm_back(
            q_raw, gain(QUERY), norm_scale(q_raw), unturn(dot_nn(ds_low, keys()) * scale)
        )
        dqkv_s[:, cols] = d_q.astype(BF16)
        dgains[QUERY : QUERY + 1, :head_width] += d_gain

    def return_keys():
        for side, left, right, scale in (
            (0, ds_s, q_s, head_width**-0.5),
            (1, p_s, datt_s, 1.0),
        ):
            cols = slice(side * head_width, (side + 1) * head_width)
            d_side = scale * inner_rows(
                left[...].reshape(head_count * rows, (reach + 1) * rows),
                right[...].reshape(head_count * rows, head_width),
            )
            for b in range(reach):
                dkv_send[b, :, cols] = d_side[b * rows : (b + 1) * rows].astype(BF16)
            dkv_s[:, cols] = d_side[reach * rows :]
        for copy in dkv_copies:
            copy.start()

    def grad_tiles(left_at, turned, right, n_cols, dst, adds):
        tile = n_cols // 3
        for k in range(3):
            grads = dot_nn(turned[left_at, :], right[:, k * tile : (k + 1) * tile])
            if adds:
                grads = grads + dst[:, k * tile : (k + 1) * tile].astype(F32)
            dst[:, k * tile : (k + 1) * tile] = grads.astype(BF16)

    def core_grads(kind, turned, right, span, n_cols):
        for m in range(n_fsdp):
            start = flip(z, m, 2) * span + (1 - c) * (span // 2)
            grad_tiles(many(start, span // 2), turned, right, n_cols, stage[kind](m), False)
            cores[kind, m].start()
        for m in list(range(1, n_fsdp)) + [0]:
            start = flip(z, m, 2) * span + c * (span // 2)
            cores[kind, m].wait_recv()
            grad_tiles(many(start, span // 2), turned, right, n_cols, mine_of(kind, m), True)
            if m and kind == "o":
                line_sums[kind, m].start()
        if kind == "q":
            his[-1].start()

    def output_grads():
        h_turn[pl.ds(0, query_width), pl.ds(0, rows)] = att_s[...].T
        core_grads("o", h_turn.at[:, pl.ds(0, rows)], do_s, rows_o, width)

    def key_grads():
        h_turn[:, pl.ds(rows, rows)] = h1_s[...].T
        d_kv = dkv_s[...]
        for o in range(reach):
            dkv_copies[o].wait_recv()
            d_kv = d_kv + dkv_came[o].astype(F32)
        k_raw = raw_s[:, query_width : query_width + head_width]
        d_k, d_gain = norm_back(
            k_raw, gain(KEY), norm_scale(k_raw), unturn(d_kv[:, :head_width])
        )
        dqkv_s[:, query_width : query_width + head_width] = d_k.astype(BF16)
        dqkv_s[:, query_width + head_width :] = d_kv[:, head_width:].astype(BF16)
        dgains[KEY : KEY + 1, :head_width] = d_gain
        core_grads("q", h_turn.at[:, pl.ds(rows, rows)], dqkv_s, depth, heads_width)

    def sum_line(j):
        kind = chunks[j][0]
        where = lo_part(kind, at.x, at.y) if kind == "q" else whole
        for m in range(1, n_fsdp):
            line_sums[kind, m].wait_recv()
            add(mine_of(kind, 0), where, {"o": line_o, "q": line_q}[kind].at[m - 1])
        (puts if kind == "q" else his)[j].start()

    def to_input():
        x = x_ref[...].astype(F32)
        d_h = dot_nt(dqkv_s[...], qkv_s[...])
        d_x, d_gain = norm_back(x, gain(ATT_IN), norm_scale(x), d_h)
        small_out[pl.ds(0, rows), :] = mid_s[...] + d_x
        dgains[ATT_IN : ATT_IN + 1, :] = d_gain
        for copy in gain_copies:
            copy.start()

    def sum_gains():
        sums = dgains[...]
        for k, copy in enumerate(gain_copies):
            copy.wait_recv()
            sums = sums + gain_in[k + 1]
        gain_line[0] = sums
        for copy in gain_lines:
            copy.start()

    take_hi(0)
    take_hi(1)
    to_middle()
    through_head(0)
    through_head(1)
    take_hi(2)
    take_hi(3)
    take_lo(0)
    take_lo(1)
    begin_hand(0)
    begin_hand(1)
    through_head(2)
    through_head(3)
    return_keys()
    output_grads()
    take_hi(4)
    take_hi(5)
    take_lo(2)
    take_lo(3)
    key_grads()
    begin_hand(2)
    hand_on(0, 1)
    hand_on(1, 1)
    take_lo(4)
    take_lo(5)
    begin_hand(3)
    to_input()
    hand_on(0, 2)
    hand_on(1, 2)
    sum_line(6)
    hand_on(2, 1)
    begin_hand(4)
    begin_hand(5)
    take_hi(7)
    hand_on(3, 1)
    hand_on(2, 2)
    sum_gains()
    take_hi(6)
    take_lo(7)
    hand_on(4, 1)
    hand_on(5, 1)
    hand_on(3, 2)
    take_lo(6)
    begin_hand(6)
    sum_line(7)
    begin_hand(7)
    hand_on(6, 1)
    hand_on(4, 2)
    hand_on(5, 2)
    hand_on(7, 1)
    hand_on(6, 2)
    hand_on(7, 2)
    sums = gain_line[0]
    for m, copy in enumerate(gain_lines):
        copy.wait_recv()
        sums = sums + gain_line[m + 1]
    for row in range(6):
        size = depth if row < QUERY else head_width // n_fsdp
        for block in range(n_fsdp):

            @pl.when(z == block)
            def _():
                small_out[2 * rows + row : 2 * rows + row + 1, :size] = sums[
                    row : row + 1, block * size : (block + 1) * size
                ]


    for j in range(len(chunks)):
        hands[j][2].wait_recv()
        for k in range(3):
            hands[j][k].wait_send()
        his[j].wait_send()
        los[j].wait_send()
        if lines[j] is not None:
            lines[j].wait_send()
    for copy in list(cores.values()) + list(line_sums.values()):
        copy.wait_send()
    for copy in gain_copies + gain_lines + dkv_copies + kv_copies + packs + seg_copies:
        copy.wait_send()
    for i in range(n_att):
        weight_sent(i)
    rows_sent(send_df, 2)
    parts_sent(send_dh, 3)


def layer(n_seq, n_fsdp, share, hidden, reach, head_count, x, cot, rates, segs, gains,
          w_gate, w_up, w_query, w_key, w_value, w_output, w_down):
    rows, width = x.shape
    depth = width // n_fsdp
    head_width = w_key.shape[1]
    query_width = w_query.shape[1]
    heads_width = query_width + 2 * head_width
    rows_o = w_output.shape[0]
    n_items = 4 * (n_fsdp - 1)
    anywhere = pl.BlockSpec(memory_space=pl.ANY)
    in_vmem = pl.BlockSpec(memory_space=pltpu.VMEM)
    shape = jax.ShapeDtypeStruct
    sems = pltpu.SemaphoreType.DMA

    def low(*size):
        return pltpu.VMEM(size, BF16)

    def full(*size):
        return pltpu.VMEM(size, F32)

    return pl.pallas_call(
        functools.partial(layer_kernel, n_seq, n_fsdp, share, reach, head_count),
        out_shape=[
            shape((2 * rows + 8, width), F32),
            shape((2 * n_fsdp + 1, depth, hidden), BF16),
            shape((hidden // 128 + 2, 128, width), BF16),
        ],
        in_specs=[in_vmem] * 10 + [anywhere] * 7,
        out_specs=[in_vmem] + [anywhere] * 2,
        scratch_shapes=[
            low(width, heads_width),
            low(n_fsdp * rows_o, width),
            low(2, width, hidden),
            low(hidden, width),
            full(n_fsdp, 8, -(-sum(g.shape[0] for g in gains) // 128) * 128),
            pltpu.VMEM((n_seq, 8, rows), jnp.int32),
            full(8, width),
            low(rows, (reach + 1) * rows),
            full(2, rows, head_width // 2),
            low(rows, width),
            full(rows, heads_width),
            low(head_count, rows, head_width),
            low(rows, 2 * head_width),
            low(reach + 1, rows, 2 * head_width),
            low(head_count, rows, (reach + 1) * rows),
            low(rows, query_width),
            full(rows, width),
            full(rows, width),
            low(n_fsdp, rows, width),
            low(n_fsdp, rows, width),
            low(max(width, 2 * n_fsdp * rows), hidden),
            low(n_fsdp, rows, hidden),
            low(2, n_fsdp, rows, hidden),
            low(width, n_fsdp * rows),
            low(n_fsdp - 1, rows, width),
            low(2, n_fsdp - 1, rows, width),
            low(2, rows, width),
            full(rows, width),
            low(hidden // 256, 128, width),
            low(n_fsdp, depth, hidden),
            low(n_fsdp, rows_o // 2, width),
            low(n_fsdp, depth // 2, heads_width),
            low(hidden // 256, 64, width),
            low(n_fsdp, depth // 2, hidden),
            low(1, rows_o // 4, width),
            low(n_fsdp, depth // 2, heads_width // 2),
            low(hidden // 256, 32, width),
            low(n_fsdp, depth // 2, hidden // 2),
            low(1, rows_o // 8, width),
            low(n_fsdp, depth // 2, heads_width // 4),
            low(n_fsdp - 1, rows_o // 2, width),
            low(n_fsdp - 1, depth // 2, heads_width // 4),
            low(rows, width),
            low(head_count, rows, head_width),
            low(head_count, rows, (reach + 1) * rows),
            full(rows, 2 * head_width),
            low(reach, rows, 2 * head_width),
            low(reach, rows, 2 * head_width),
            low(rows, heads_width),
            full(8, width),
            full(n_seq, 8, width),
            full(n_fsdp, 8, width),
            sems((n_items, 5)),
            sems((n_items, 5)),
            sems((7,)),
            sems((n_fsdp,)),
            sems((n_fsdp,)),
            sems((n_seq,)),
            sems((n_seq,)),
            sems((reach,)),
            sems((reach,)),
            sems((4, n_fsdp)),
            sems((4, n_fsdp)),
            sems((7,)),
            sems((reach,)),
            sems((reach,)),
            sems((2 + 3 * n_fsdp,)),
            sems((2 + 3 * n_fsdp,)),
            sems((4 + n_fsdp,)),
            sems((4 + n_fsdp,)),
            sems((4 + n_fsdp,)),
            sems((4 + n_fsdp,)),
            sems((4 + n_fsdp,)),
            sems((4 + n_fsdp,)),
            sems((2, n_fsdp)),
            sems((2, n_fsdp)),
            sems((4 + n_fsdp,)),
            sems((4 + n_fsdp, 3)),
            sems((4 + n_fsdp, 3)),
            sems((n_seq + n_fsdp,)),
            sems((n_seq + n_fsdp,)),
        ],
        compiler_params=pltpu.CompilerParams(
            collective_id=0, has_side_effects=True, vmem_limit_bytes=63 << 20
        ),
        name="decoder_layer",
    )(x, cot, rates, segs, *gains, w_gate, w_up, w_query, w_key, w_value, w_output, w_down)


def finish_kernel(
    share, skip_ref, wins_ref, d0_ref, d1_ref, d2_ref, qkv_ref, wo_ref, small_ref,
    gate_ref, up_ref, down_ref, wq_ref, wk_ref, wv_ref, wo_out, out_ref, dx_ref, *gain_outs,
):
    n_win, hidden = wins_ref.shape[0] // 2, wins_ref.shape[2]
    starts = [window_start(i, share) for i in range(n_win)]
    for i, ref in enumerate((gate_ref, up_ref)):
        for w in range(n_win):
            at = i * n_win + w
            first = starts[w]
            last = starts[w + 1] if w + 1 < n_win else first + hidden
            shared = starts[w - 1] + hidden - first if w else 0
            if shared:
                ref[:, first : first + shared] = wins_ref[at, :, :shared].astype(F32) + wins_ref[
                    at - 1, :, hidden - shared :
                ].astype(F32)
            ref[:, first + shared : last] = wins_ref[at, :, shared : last - first].astype(F32)
    for k, ref in enumerate((d0_ref, d1_ref, d2_ref)):
        down_ref[pl.ds(k * ref.shape[0], ref.shape[0]), :] = ref[...].astype(F32)
    start = 0
    for ref in (wq_ref, wk_ref, wv_ref):
        size = ref.shape[1]
        ref[...] = qkv_ref[0, :, start : start + size].astype(F32)
        start += size
    wo_out[...] = wo_ref[...].astype(F32)

    @pl.when(pl.program_id(0) == 0)
    def _():
        rows_here = dx_ref.shape[0]
        dx_ref[...] = small_ref[:rows_here]
        out_ref[...] = small_ref[rows_here : 2 * rows_here].astype(BF16)
        for row, ref in enumerate(gain_outs):
            ref[...] = small_ref[2 * rows_here + row, : ref.shape[0]]


def finish(share, skipped, gain_sizes, query_width, head_width, rows_o, windows, tiles, small):
    n_win, rows, hidden = windows.shape
    n_win = n_win // 2
    width = tiles.shape[2]
    rows_here = small.shape[0] // 2 - 4
    slab = 32
    steps = rows // slab
    down_slab = share // steps // 3
    heads_width = query_width + 2 * head_width
    down = tiles.reshape(-1, width)
    start_o = (down.shape[0] - rows_o) // slab
    shape = jax.ShapeDtypeStruct

    def slabs(n_rows, n_cols, n_slabs):
        return pl.BlockSpec(
            (n_rows, n_cols), lambda i, skip: (jnp.minimum(i, n_slabs - 1), 0)
        )

    def down_part(k):
        return pl.BlockSpec((down_slab, width), lambda i, skip: (3 * i + k + skip[0], 0))

    def whole(array_shape):
        return pl.BlockSpec(array_shape, lambda i, skip: (0,) * len(array_shape))

    return pl.pallas_call(
        functools.partial(finish_kernel, share),
        grid_spec=pltpu.PrefetchScalarGridSpec(
            num_scalar_prefetch=1,
            grid=(steps,),
            in_specs=[
                pl.BlockSpec((2 * n_win, slab, hidden), lambda i, skip: (0, i, 0)),
                down_part(0),
                down_part(1),
                down_part(2),
                pl.BlockSpec((1, slab, heads_width), lambda i, skip: (2 * n_win, i, 0)),
                pl.BlockSpec(
                    (slab, width),
                    lambda i, skip: (start_o + jnp.minimum(i, rows_o // slab - 1), 0),
                ),
                whole(small.shape),
            ],
            out_specs=[
                slabs(slab, n_win * share, steps),
                slabs(slab, n_win * share, steps),
                slabs(3 * down_slab, width, steps),
                slabs(slab, query_width, steps),
                slabs(slab, head_width, steps),
                slabs(slab, head_width, steps),
                slabs(slab, width, rows_o // slab),
                whole((rows_here, width)),
                whole((rows_here, width)),
            ]
            + [whole((size,)) for size in gain_sizes],
        ),
        out_shape=[
            shape((rows, n_win * share), F32),
            shape((rows, n_win * share), F32),
            shape((share, width), F32),
            shape((rows, query_width), F32),
            shape((rows, head_width), F32),
            shape((rows, head_width), F32),
            shape((rows_o, width), F32),
            shape((rows_here, width), BF16),
            shape((rows_here, width), F32),
        ]
        + [shape((size,), F32) for size in gain_sizes],
        compiler_params=pltpu.CompilerParams(vmem_limit_bytes=63 << 20),
        name="finish",
    )((skipped // down_slab).reshape(1), windows, down, down, down, windows, down, small)


def shards(n_seq, n_fsdp, *args):
    w_query, w_key, w_output, w_gate = args[4], args[5], args[9], args[12]
    depth, ffn_width = w_gate.shape
    rows_here = args[0].shape[1]
    share = ffn_width // n_fsdp
    reach = (WINDOW - 2 + rows_here) // rows_here
    fits = (
        n_seq == 8
        and n_fsdp == 4
        and args[0].shape[0] == 1
        and reach < n_seq
        and rows_here == 128
        and window_width(share, n_fsdp) == 256 * (2 * n_fsdp - 1)
        and depth % 32 == 0
        and w_output.shape[0] == 256
        and w_key.shape[1] % 256 == 0
        and w_query.shape[1] % 512 == 0
        and w_output.shape[1] % 384 == 0
        and ffn_width % n_fsdp == 0
        and share % 16 == 0
        and rows_here // 2 * (share // 64) * 2 == rows_here * (depth // 32) * 3
        and (share - window_start(1, share)) % 64 == 0
        and window_start(n_fsdp - 1, share) + window_width(share, n_fsdp) == ffn_width
    )
    if fits:
        return shards_fused(n_seq, n_fsdp, *args)
    return shards_plain(*args)


def shards_fused(
    n_seq,
    n_fsdp,
    inputs,
    segments,
    cotangent,
    gain_attn_in,
    w_query,
    w_key,
    w_value,
    gain_query,
    gain_key,
    w_output,
    gain_attn_out,
    gain_ffn_in,
    w_gate,
    w_up,
    w_down,
    gain_ffn_out,
):
    rows_here, width = inputs.shape[1:]
    head_width = w_key.shape[1]
    query_width = w_query.shape[1]
    head_count = query_width // head_width
    share = w_gate.shape[1] // n_fsdp
    hidden = window_width(share, n_fsdp)
    reach = (WINDOW - 2 + rows_here) // rows_here
    line = lax.axis_index("fsdp")
    gains = (gain_attn_in, gain_attn_out, gain_ffn_in, gain_ffn_out, gain_query, gain_key)
    rates = 10000.0 ** (-(np.arange(head_width // 2, dtype=np.float32) * 2.0) / head_width)
    small, fin_gu, fin_d = layer(
        n_seq, n_fsdp, share, hidden, reach, head_count,
        inputs[0], cotangent[0], jnp.asarray(rates, F32)[None], segments, gains,
        w_gate, w_up, w_query, w_key, w_value, w_output, w_down,
    )
    (
        grad_gate, grad_up, grad_down, grad_q, grad_k, grad_v, grad_o, outputs, d_inputs,
        g_attn_in, g_attn_out, g_ffn_in, g_ffn_out, g_query, g_key,
    ) = finish(
        share, line * share - window_start(line, share), [g.shape[0] for g in gains],
        query_width, head_width, w_output.shape[0], fin_gu, fin_d, small,
    )
    return (
        outputs[None],
        d_inputs[None],
        g_attn_in,
        grad_q,
        grad_k,
        grad_v,
        g_query,
        g_key,
        grad_o,
        g_attn_out,
        g_ffn_in,
        grad_gate,
        grad_up,
        grad_down,
        g_ffn_out,
    )


def solution(mesh):
    placed = (
        P("fsdp", "seq", None),
        P("fsdp", "seq"),
        P("fsdp", "seq", None),
        P("fsdp"),
        P("fsdp", None),
        P("fsdp", None),
        P("fsdp", None),
        P("fsdp"),
        P("fsdp"),
        P("fsdp", None),
        P("fsdp"),
        P("fsdp"),
        P("fsdp", None),
        P("fsdp", None),
        P("fsdp", None),
        P("fsdp"),
    )
    return jax.shard_map(
        functools.partial(shards, mesh.shape["seq"], mesh.shape["fsdp"]),
        mesh=mesh,
        in_specs=placed,
        out_specs=(
            P("fsdp", "seq", None),
            P("fsdp", "seq", None),
            P("fsdp"),
            P("fsdp", None),
            P("fsdp", None),
            P("fsdp", None),
            P("fsdp"),
            P("fsdp"),
            P("fsdp", None),
            P("fsdp"),
            P("fsdp"),
            P("fsdp", None),
            P("fsdp", None),
            P("fsdp", None),
            P("fsdp"),
        ),
        check_vma=False,
    )
```

```python
import functools

import jax
import jax.numpy as jnp
import numpy as np
from jax import lax
from jax.experimental import pallas as pl
from jax.experimental.pallas import tpu as pltpu
from jax.sharding import PartitionSpec as P

WINDOW = 512


epsilon = 1e-06
masked_value = -1e30


def from_behind(block, axis, distance):
    devices = range(lax.axis_size(axis))
    route = [(i - distance, i) for i in devices if i - distance in devices]
    return lax.ppermute(block, axis, route)


def norm_rows(rows_in, gain_vec):
    return (
        rows_in
        * lax.rsqrt(jnp.mean(rows_in * rows_in, axis=-1, keepdims=True) + epsilon)
        * gain_vec
    )


def angles(positions, head_width):
    inv_rates = 10000.0 ** (-(jnp.arange(head_width // 2, dtype=jnp.float32) * 2.0) / head_width)
    return positions.astype(jnp.float32)[:, None] * inv_rates[None, :]


def rotate(rows_in, angles_at):
    half_width = rows_in.shape[-1] // 2
    lower_half = rows_in[..., :half_width]
    upper_half = rows_in[..., half_width:]
    cosine = jnp.cos(angles_at)
    sine_part = jnp.sin(angles_at)
    return jnp.concatenate(
        [
            lower_half * cosine - upper_half * sine_part,
            upper_half * cosine + lower_half * sine_part,
        ],
        axis=-1,
    )


def geglu_act(gate_proj, up_proj):
    return jax.nn.gelu(gate_proj, approximate=True) * up_proj


def inner_rows(left, right):
    return lax.dot_general(
        left, right, (((0,), (0,)), ((), ())), preferred_element_type=jnp.float32
    )


def outer_cols(left, right):
    return lax.dot_general(
        left, right, (((1,), (1,)), ((), ())), preferred_element_type=jnp.float32
    )


def shards_plain(
    inputs,
    segments,
    cotangent,
    gain_attn_in,
    w_query,
    w_key,
    w_value,
    gain_query,
    gain_key,
    w_output,
    gain_attn_out,
    gain_ffn_in,
    w_gate,
    w_up,
    w_down,
    gain_ffn_out,
):
    rows_here = inputs.shape[1]
    head_width = w_key.shape[1]
    head_count = w_query.shape[1] // head_width
    reach_devs = (WINDOW - 2 + rows_here) // rows_here
    score_scale = head_width ** (-0.5)
    first_row = lax.axis_index("seq") * rows_here
    tokens = inputs[0].astype(jnp.float32)
    seg_here = segments[0]
    positions = first_row + jnp.arange(rows_here, dtype=jnp.int32)
    angles_at = angles(positions - seg_here, head_width)
    wq_all, wk_all, wv_all, wo_all, g_attn_in, g_query, g_key, g_attn_out, g_ffn_in, g_ffn_out = (
        lax.all_gather(w_query, "fsdp", axis=0, tiled=True),
        lax.all_gather(w_key, "fsdp", axis=0, tiled=True),
        lax.all_gather(w_value, "fsdp", axis=0, tiled=True),
        lax.all_gather(w_output, "fsdp", axis=0, tiled=True),
        lax.all_gather(gain_attn_in, "fsdp", axis=0, tiled=True),
        lax.all_gather(gain_query, "fsdp", axis=0, tiled=True),
        lax.all_gather(gain_key, "fsdp", axis=0, tiled=True),
        lax.all_gather(gain_attn_out, "fsdp", axis=0, tiled=True),
        lax.all_gather(gain_ffn_in, "fsdp", axis=0, tiled=True),
        lax.all_gather(gain_ffn_out, "fsdp", axis=0, tiled=True),
    )
    g_attn_in = g_attn_in.astype(jnp.float32)
    g_query = g_query.astype(jnp.float32)
    g_key = g_key.astype(jnp.float32)
    g_attn_out = g_attn_out.astype(jnp.float32)
    g_ffn_in = g_ffn_in.astype(jnp.float32)
    g_ffn_out = g_ffn_out.astype(jnp.float32)
    normed_one, pull_one = jax.vjp(norm_rows, tokens, g_attn_in)
    h_one = normed_one.astype(jnp.bfloat16)
    q_raw = jnp.dot(h_one, wq_all, preferred_element_type=jnp.float32)
    k_raw = jnp.dot(h_one, wk_all, preferred_element_type=jnp.float32)
    v_raw = jnp.dot(h_one, wv_all, preferred_element_type=jnp.float32)

    def prepare(q_in, k_in, gq_in, gk_in):
        q_rows = q_in.reshape(q_in.shape[0], head_count, head_width)
        q_fin = rotate(norm_rows(q_rows, gq_in), angles_at[:, None, :])
        k_fin = rotate(norm_rows(k_in, gk_in), angles_at)
        return (q_fin, k_fin)

    (q_fin, k_fin), pull_prep = jax.vjp(prepare, q_raw, k_raw, g_query, g_key)
    q_low = q_fin.astype(jnp.bfloat16).reshape(rows_here * head_count, head_width)
    k_low = k_fin.astype(jnp.bfloat16)
    v_low = v_raw.astype(jnp.bfloat16)
    key_parts = []
    value_parts = []
    seg_parts = []
    for offset in range(reach_devs, 0, -1):
        k_came, v_came, s_came = from_behind((k_low, v_low, seg_here), "seq", offset)
        key_parts.append(k_came)
        value_parts.append(v_came)
        seg_parts.append(s_came)
    key_rows = jnp.concatenate(key_parts + [k_low], axis=0)
    value_rows = jnp.concatenate(value_parts + [v_low], axis=0)
    key_segs = jnp.concatenate(seg_parts + [seg_here], axis=0)
    key_place = (
        first_row
        - reach_devs * rows_here
        + jnp.arange((reach_devs + 1) * rows_here, dtype=jnp.int32)
    )
    distance = positions[:, None] - key_place[None, :]
    allowed = (
        (distance >= 0)
        & (distance < WINDOW)
        & (key_place[None, :] >= 0)
        & (seg_here[:, None] == key_segs[None, :])
    )
    scores = (outer_cols(q_low, key_rows) * score_scale).reshape(rows_here, head_count, -1)
    masked = jnp.where(allowed[:, None, :], scores, masked_value)
    attn_probs = jax.nn.softmax(masked, axis=-1).reshape(rows_here * head_count, -1)
    probs_low = attn_probs.astype(jnp.bfloat16)
    attended = jnp.dot(probs_low, value_rows, preferred_element_type=jnp.float32)
    att_low = attended.reshape(rows_here, head_count * head_width).astype(jnp.bfloat16)
    o_raw = jnp.dot(att_low, wo_all, preferred_element_type=jnp.float32)
    branch_att, pull_att = jax.vjp(norm_rows, o_raw, g_attn_out)
    middle = tokens + branch_att
    normed_two, pull_mid = jax.vjp(norm_rows, middle, g_ffn_in)
    h_two = normed_two.astype(jnp.bfloat16)
    gate_all, up_all, down_all = (
        lax.all_gather(w_gate, "fsdp", axis=0, tiled=True),
        lax.all_gather(w_up, "fsdp", axis=0, tiled=True),
        lax.all_gather(w_down, "fsdp", axis=0, tiled=True),
    )
    gate_proj = jnp.dot(h_two, gate_all, preferred_element_type=jnp.float32)
    up_proj = jnp.dot(h_two, up_all, preferred_element_type=jnp.float32)
    act_full, pull_act = jax.vjp(geglu_act, gate_proj, up_proj)
    act_low = act_full.astype(jnp.bfloat16)
    f_raw = jnp.dot(act_low, down_all, preferred_element_type=jnp.float32)
    branch_ffn, pull_out = jax.vjp(norm_rows, f_raw, g_ffn_out)
    outputs = (middle + branch_ffn).astype(jnp.bfloat16)
    upstream = cotangent[0].astype(jnp.float32)
    d_fraw, d_gffn_out = pull_out(upstream)
    d_flow = d_fraw.astype(jnp.bfloat16)
    gate_shard, up_shard, down_shard, d_flow = lax.optimization_barrier(
        (w_gate, w_up, w_down, d_flow)
    )
    gate_back, up_back, down_back = (
        lax.all_gather(gate_shard, "fsdp", axis=0, tiled=True),
        lax.all_gather(up_shard, "fsdp", axis=0, tiled=True),
        lax.all_gather(down_shard, "fsdp", axis=0, tiled=True),
    )
    d_act = outer_cols(d_flow, down_back)
    d_gate, d_up = pull_act(d_act)
    dg_low = d_gate.astype(jnp.bfloat16)
    du_low = d_up.astype(jnp.bfloat16)
    d_htwo = outer_cols(dg_low, gate_back) + outer_cols(du_low, up_back)
    grad_down_part = lax.psum_scatter(
        inner_rows(act_low, d_flow).astype(jnp.bfloat16), "fsdp", scatter_dimension=0, tiled=True
    )
    grad_in_part = lax.psum_scatter(
        jnp.concatenate([inner_rows(h_two, dg_low), inner_rows(h_two, du_low)], axis=1).astype(
            jnp.bfloat16
        ),
        "fsdp",
        scatter_dimension=0,
        tiled=True,
    ).astype(jnp.float32)
    hidden_width = w_gate.shape[1]
    grad_gate_part = grad_in_part[:, :hidden_width]
    grad_up_part = grad_in_part[:, hidden_width:]
    d_mid_norm, d_gffn_in = pull_mid(d_htwo)
    d_middle = upstream + d_mid_norm
    d_oraw, d_gattn_out = pull_att(d_middle)
    d_olow = d_oraw.astype(jnp.bfloat16)
    grad_wo = inner_rows(att_low, d_olow)
    d_att_low = (
        outer_cols(d_olow, wo_all).astype(jnp.bfloat16).reshape(rows_here * head_count, head_width)
    )
    d_probs = outer_cols(d_att_low, value_rows)
    d_scores = attn_probs * (d_probs - jnp.sum(attn_probs * d_probs, axis=-1, keepdims=True))
    ds_low = d_scores.astype(jnp.bfloat16)
    d_qfin = jnp.dot(ds_low, key_rows, preferred_element_type=jnp.float32) * score_scale
    d_keys = inner_rows(ds_low, q_low) * score_scale
    d_values = inner_rows(probs_low, d_att_low)
    d_kfin = d_keys[reach_devs * rows_here :]
    d_vsum = d_values[reach_devs * rows_here :]
    for offset in range(1, reach_devs + 1):
        slot_index = reach_devs - offset
        k_back, v_back = (
            from_behind(
                d_keys[slot_index * rows_here : (slot_index + 1) * rows_here].astype(jnp.bfloat16),
                "seq",
                -offset,
            ).astype(jnp.float32),
            from_behind(
                d_values[slot_index * rows_here : (slot_index + 1) * rows_here].astype(
                    jnp.bfloat16
                ),
                "seq",
                -offset,
            ).astype(jnp.float32),
        )
        d_kfin = d_kfin + k_back
        d_vsum = d_vsum + v_back
    d_qraw, d_kraw, d_gquery, d_gkey = pull_prep(
        (d_qfin.reshape(rows_here, head_count, head_width), d_kfin)
    )
    dq_low = d_qraw.astype(jnp.bfloat16)
    dk_low = d_kraw.astype(jnp.bfloat16)
    dv_low = d_vsum.astype(jnp.bfloat16)
    d_hone = outer_cols(dq_low, wq_all) + outer_cols(dk_low, wk_all) + outer_cols(dv_low, wv_all)
    grad_wq = inner_rows(h_one, dq_low)
    grad_wk = inner_rows(h_one, dk_low)
    grad_wv = inner_rows(h_one, dv_low)
    d_tok_norm, d_gattn_in = pull_one(d_hone)
    d_inputs = d_middle + d_tok_norm
    part_wq, part_wk, part_wv, part_wo, part_gai, part_gq, part_gk, part_gao, part_gfi, part_gfo = (
        lax.psum_scatter(
            grad_wq.astype(jnp.bfloat16), "fsdp", scatter_dimension=0, tiled=True
        ).astype(jnp.float32),
        lax.psum_scatter(
            grad_wk.astype(jnp.bfloat16), "fsdp", scatter_dimension=0, tiled=True
        ).astype(jnp.float32),
        lax.psum_scatter(
            grad_wv.astype(jnp.bfloat16), "fsdp", scatter_dimension=0, tiled=True
        ).astype(jnp.float32),
        lax.psum_scatter(
            grad_wo.astype(jnp.bfloat16), "fsdp", scatter_dimension=0, tiled=True
        ).astype(jnp.float32),
        lax.psum_scatter(
            d_gattn_in.astype(jnp.bfloat16), "fsdp", scatter_dimension=0, tiled=True
        ).astype(jnp.float32),
        lax.psum_scatter(
            d_gquery.astype(jnp.bfloat16), "fsdp", scatter_dimension=0, tiled=True
        ).astype(jnp.float32),
        lax.psum_scatter(
            d_gkey.astype(jnp.bfloat16), "fsdp", scatter_dimension=0, tiled=True
        ).astype(jnp.float32),
        lax.psum_scatter(
            d_gattn_out.astype(jnp.bfloat16), "fsdp", scatter_dimension=0, tiled=True
        ).astype(jnp.float32),
        lax.psum_scatter(
            d_gffn_in.astype(jnp.bfloat16), "fsdp", scatter_dimension=0, tiled=True
        ).astype(jnp.float32),
        lax.psum_scatter(
            d_gffn_out.astype(jnp.bfloat16), "fsdp", scatter_dimension=0, tiled=True
        ).astype(jnp.float32),
    )
    cols_wq, cols_wk, cols_wv, cols_wo, cols_gate, cols_up, cols_down = (
        lax.psum_scatter(
            part_wq.astype(jnp.bfloat16), "seq", scatter_dimension=1, tiled=True
        ).astype(jnp.float32),
        lax.psum_scatter(
            part_wk.astype(jnp.bfloat16), "seq", scatter_dimension=1, tiled=True
        ).astype(jnp.float32),
        lax.psum_scatter(
            part_wv.astype(jnp.bfloat16), "seq", scatter_dimension=1, tiled=True
        ).astype(jnp.float32),
        lax.psum_scatter(
            part_wo.astype(jnp.bfloat16), "seq", scatter_dimension=1, tiled=True
        ).astype(jnp.float32),
        lax.psum_scatter(
            grad_gate_part.astype(jnp.bfloat16), "seq", scatter_dimension=1, tiled=True
        ).astype(jnp.float32),
        lax.psum_scatter(
            grad_up_part.astype(jnp.bfloat16), "seq", scatter_dimension=1, tiled=True
        ).astype(jnp.float32),
        lax.psum_scatter(grad_down_part, "seq", scatter_dimension=1, tiled=True).astype(
            jnp.float32
        ),
    )
    sum_wq, sum_wk, sum_wv, sum_wo, sum_gate, sum_up, sum_down = (
        lax.all_gather(cols_wq.astype(jnp.bfloat16), "seq", axis=1, tiled=True).astype(
            cols_wq.dtype
        ),
        lax.all_gather(cols_wk.astype(jnp.bfloat16), "seq", axis=1, tiled=True).astype(
            cols_wk.dtype
        ),
        lax.all_gather(cols_wv.astype(jnp.bfloat16), "seq", axis=1, tiled=True).astype(
            cols_wv.dtype
        ),
        lax.all_gather(cols_wo.astype(jnp.bfloat16), "seq", axis=1, tiled=True).astype(
            cols_wo.dtype
        ),
        lax.all_gather(cols_gate.astype(jnp.bfloat16), "seq", axis=1, tiled=True).astype(
            cols_gate.dtype
        ),
        lax.all_gather(cols_up.astype(jnp.bfloat16), "seq", axis=1, tiled=True).astype(
            cols_up.dtype
        ),
        lax.all_gather(cols_down.astype(jnp.bfloat16), "seq", axis=1, tiled=True).astype(
            cols_down.dtype
        ),
    )
    sum_gai, sum_gq, sum_gk, sum_gao, sum_gfi, sum_gfo = lax.psum(
        (part_gai, part_gq, part_gk, part_gao, part_gfi, part_gfo), "seq"
    )
    return (
        outputs[None],
        d_inputs[None],
        sum_gai,
        sum_wq,
        sum_wk,
        sum_wv,
        sum_gq,
        sum_gk,
        sum_wo,
        sum_gao,
        sum_gfi,
        sum_gate,
        sum_up,
        sum_down,
        sum_gfo,
    )


MESH = pl.DeviceIdType.MESH
BF16 = jnp.bfloat16
F32 = jnp.float32
GELU_RATE = 0.7978845608028654
GELU_CUBE = 0.044715
HID_TILE = 256
ATT_IN, ATT_OUT, FFN_IN, FFN_OUT, QUERY, KEY = range(6)


def bit_of(value, mask):
    return lax.rem(lax.div(value, mask), 2)


def flip(value, masks, bits):
    for b in range(bits):
        if (masks >> b) & 1:
            value = value + (1 << b) * (1 - 2 * bit_of(value, 1 << b))
    return value


def greet(devices):
    barrier = pltpu.get_barrier_semaphore()
    for device in devices:
        pl.semaphore_signal(barrier, inc=1, device_id=device, device_id_type=MESH)
    pl.semaphore_wait(barrier, len(devices))


def remote(src, dst, send, recv, device):
    return pltpu.make_async_remote_copy(
        src_ref=src, dst_ref=dst, send_sem=send, recv_sem=recv,
        device_id=device, device_id_type=MESH,
    )


def many(offset, size):
    return pl.ds(pl.multiple_of(offset, size if size % 128 == 0 else 16), size)


def lanes(offset, size):
    return pl.ds(pl.multiple_of(offset, 128), size)


def window_start(z, share):
    if isinstance(z, int):
        return z * share // 128 * 128
    return lax.div(z * share, 128) * 128


def window_width(share, n_fsdp):
    widest = max((z + 1) * share - window_start(z, share) for z in range(n_fsdp))
    return -(-widest // HID_TILE) * HID_TILE


def dot_nt(left, right):
    return lax.dot_general(left, right, (((1,), (1,)), ((), ())), preferred_element_type=F32)


def dot_nn(left, right):
    return jnp.dot(left, right, preferred_element_type=F32)


def norm_scale(rows_in):
    return lax.rsqrt(jnp.mean(rows_in * rows_in, axis=-1, keepdims=True) + epsilon)


def norm_back(rows_in, gain, scale, upstream):
    pulled = upstream * gain
    inner = jnp.mean(pulled * rows_in, axis=-1, keepdims=True)
    d_rows = scale * pulled - rows_in * (scale * scale * scale * inner)
    return d_rows, jnp.sum(upstream * rows_in * scale, axis=0, keepdims=True)


def turn(rows_in, cosine, sine_part):
    half = rows_in.shape[-1] // 2
    lower, upper = rows_in[:, :half], rows_in[:, half:]
    return jnp.concatenate(
        [lower * cosine - upper * sine_part, upper * cosine + lower * sine_part], axis=-1
    )


class Place:
    def __init__(self):
        self.s = lax.axis_index("seq")
        self.z = lax.axis_index("fsdp")
        self.c = bit_of(self.s, 1)
        self.x = bit_of(self.s, 2)
        self.y = bit_of(self.s, 4)

    def plane(self, masks):
        return (flip(self.s, masks, 3), self.z)

    def line(self, masks):
        return (self.s, flip(self.z, masks, 2))

    def halves(self, first_x):
        if first_x:
            return self.x, self.y, 2, 4
        return self.y, self.x, 4, 2


def layer_kernel(
    n_seq, n_fsdp, share, reach, head_count,
    x_ref, cot_ref, rates_ref, seg_ref,
    gain_a, gain_b, gain_c, gain_d, gain_e, gain_f,
    gate_ref, up_ref, wq_ref, wk_ref, wv_ref, wo_ref, wd_ref,
    small_out, fin_gu, fin_d,
    qkv_s, wo_s, w_in, w_down, pack_all, seg_all, gains, allowed, turns,
    h1_s, raw_s, q_s, kv_own, kv_s, p_s, att_s, o_s, mid_s,
    h_all, df_all, bent_s, act, d_in, h_turn, part_out, part_in, relay_in, total,
    own_d, own_g, own_o, own_q, hi_d, hi_g, hi_o, hi_q, lo_d, lo_g, lo_o, lo_q, line_o, line_q,
    do_s, datt_s, ds_s, dkv_s, dkv_send, dkv_came, dqkv_s, dgains, gain_in, gain_line,
    w_send, w_recv, own_sem, pack_send, pack_recv, seg_send, seg_recv, kv_send, kv_recv,
    ex_send, ex_recv, relay_sem, dkv_ssem, dkv_rsem,
    c_send, c_recv, hi_send, hi_recv, lo_send, lo_recv, z_send, z_recv, oq_send, oq_recv,
    put_sem, ag_send, ag_recv, gain_send, gain_recv,
):
    at = Place()
    s, z, c = at.s, at.z, at.c
    rows, width = x_ref.shape
    depth = width // n_fsdp
    hidden = w_in.shape[2]
    head_width = wk_ref.shape[1]
    query_width = head_count * head_width
    heads_width = query_width + 2 * head_width
    rows_o = wo_ref.shape[0]
    n_hid = hidden // HID_TILE
    third = width // 3
    middle_z = (z > 0) & (z < n_fsdp - 1)
    tokens = n_fsdp * rows

    def hid(n):
        return lanes(n * HID_TILE, HID_TILE)

    def outs(n):
        return lanes(n * third, third)

    skipped = z * share - window_start(z, share)
    spare = hidden - share
    if spare:
        w_down[pl.ds(0, spare)] = jnp.zeros((spare, width), BF16)
        w_down[pl.ds(share, spare)] = jnp.zeros((spare, width), BF16)
    here_z = many(z * depth, depth)
    own_copies = [
        pltpu.make_async_copy(src, dst, own_sem.at[i])
        for i, (src, dst) in enumerate((
            (wq_ref, qkv_s.at[here_z, pl.ds(0, query_width)]),
            (wk_ref, qkv_s.at[here_z, pl.ds(query_width, head_width)]),
            (wv_ref, qkv_s.at[here_z, pl.ds(query_width + head_width, head_width)]),
            (wo_ref, wo_s.at[many(z * rows_o, rows_o)]),
            (wd_ref, w_down.at[many(skipped, share)]),
            (gate_ref.at[:, lanes(window_start(z, share), hidden)], w_in.at[0, here_z]),
            (up_ref.at[:, lanes(window_start(z, share), hidden)], w_in.at[1, here_z]),
        ))
    ]
    seg_all[s] = jnp.broadcast_to(seg_ref[...], seg_all.shape[1:])
    start = 0
    for ref in (gain_a, gain_b, gain_c, gain_d, gain_e, gain_f):
        size = ref.shape[0]
        pack_all[z, 0:1, start : start + size] = ref[...].astype(F32).reshape(1, size)
        start += size
    greet([at.plane(k) for k in range(1, n_seq)] + [at.line(m) for m in range(1, n_fsdp)])

    packs = [
        remote(pack_all.at[z], pack_all.at[z], pack_send.at[m], pack_recv.at[m], at.line(m))
        for m in range(1, n_fsdp)
    ]
    seg_copies = [
        remote(seg_all.at[s], seg_all.at[s], seg_send.at[k], seg_recv.at[k], at.plane(k))
        for k in range(1, n_seq)
    ]
    kv_copies = [
        remote(kv_own, kv_s.at[reach - o], kv_send.at[o - 1], kv_recv.at[o - 1],
               (lax.rem(s + o, n_seq), z))
        for o in range(1, reach + 1)
    ]

    def w_region(kind, sub, whose, hi, lo, level):
        base = whose * depth
        if kind == "q":
            cols = (
                lanes(hi * (query_width // 2) + lo * (query_width // 4), query_width // 4),
                lanes(hi * (query_width // 2), query_width // 2),
                pl.ds(0, query_width),
            )[level]
            return qkv_s.at[many(base + c * (depth // 2), depth // 2), cols]
        if kind == "kv":
            start = query_width + c * head_width
            if level == 0:
                start = start + lo * (head_width // 2)
            cols = lanes(start, head_width if level else head_width // 2)
            if level == 2:
                return qkv_s.at[many(base, depth), cols]
            return qkv_s.at[many(base + hi * (depth // 2), depth // 2), cols]
        if kind == "wo":
            start = whose * rows_o + c * (rows_o // 2)
            if level < 2:
                start = start + hi * (rows_o // 4)
            if level < 1:
                start = start + lo * (rows_o // 8)
            return wo_s.at[many(start, rows_o // (8, 4, 2)[level])]
        skip, size = sub
        if level == 2:
            return [
                w_in.at[c, many(base + half * (depth // 2) + skip, size)] for half in range(2)
            ]
        here = many(base + hi * (depth // 2) + skip, size)
        if level == 1:
            return w_in.at[c, here]
        return w_in.at[c, here, lanes(lo * (hidden // 2), hidden // 2)]

    def w_sources(kind, sub, to, hi, lo):
        if kind == "q":
            cols = lanes(hi * (query_width // 2) + lo * (query_width // 4), query_width // 4)
            return [wq_ref.at[many(c * (depth // 2), depth // 2), cols]]
        if kind == "wo":
            start = c * (rows_o // 2) + hi * (rows_o // 4) + lo * (rows_o // 8)
            return [wo_ref.at[many(start, rows_o // 8)]]
        if kind == "kv":
            here = many(hi * (depth // 2), depth // 2)
            cols = lanes(lo * (head_width // 2), head_width // 2)
            return [ref.at[here, cols] for ref in (wk_ref, wv_ref)]
        skip, size = sub
        here = many(hi * (depth // 2) + skip, size)
        cols = lanes(window_start(to, share) + lo * (hidden // 2), hidden // 2)
        return [ref.at[here, cols] for ref in (gate_ref, up_ref)]

    items = []
    for kinds in (("q", "kv"), ("wo",)):
        for m in range(1, n_fsdp):
            for kind in kinds:
                items.append((kind, m, (m % 2 == 1) == (kind in ("kv", "wo")), None))
    n_att = len(items)
    for m in range(1, n_fsdp):
        items.append(("gu", m, m % 2 == 1, (0, depth // 2)))
    steps, starts = [], []
    for i, (kind, m, first_x, sub) in enumerate(items):
        hi, lo, mask_hi, mask_lo = at.halves(first_x)
        there = flip(z, m, 2)
        firsts = [
            remote(src, w_region(kind, sub, z, hi, lo, 0), w_send.at[i, 0], w_recv.at[i, 0],
                   at.line(m))
            for src in w_sources(kind, sub, there, hi, lo)
        ]
        starts.append(firsts)
        stages = [firsts[:1]]
        for k, mask in enumerate((mask_lo, mask_hi, 1)):
            parts = w_region(kind, sub, there, hi, lo, k)
            stages.append([
                remote(part, part, w_send.at[i, k + 1 + n], w_recv.at[i, k + 1 + n], at.plane(mask))
                for n, part in enumerate(parts if isinstance(parts, list) else [parts])
            ])
        steps.append(stages)

    def begin_weight(i):
        if len(starts[i]) == 1:
            starts[i][0].start()
        else:
            for core, first in enumerate(starts[i]):
                pl.when(c == core)(first.start)

    def weight_here(i, stage):
        for copy in steps[i][stage]:
            copy.wait_recv()

    def move_weight(i, stage):
        weight_here(i, stage - 1)
        for copy in steps[i][stage]:
            copy.start()

    def weight_sent(i):
        for copies in steps[i]:
            for copy in copies:
                copy.wait_send()

    n_items = len(items)
    n_qkv = 2 * (n_fsdp - 1)
    ahead, lag = 6, 3
    for copy in packs + seg_copies:
        copy.start()
    for i in range(ahead):
        begin_weight(i)
    for copy in own_copies:
        copy.start()

    def weight_steps(t):
        for stage in (3, 2, 1):
            i = t - lag * (stage - 1)
            if 0 <= i < n_att:
                move_weight(i, stage)
                if stage == 1 and i + ahead < n_items:
                    begin_weight(i + ahead)

    weight_steps(0)
    weight_steps(1)
    for copy in seg_copies:
        copy.wait_recv()
    across = lax.broadcasted_iota(jnp.int32, (rows, rows), 0)
    along = lax.broadcasted_iota(jnp.int32, (rows, rows), 1)
    seg_here = jnp.broadcast_to(seg_ref[...].astype(F32), (rows, rows)).T
    for o in range(reach, -1, -1):
        key_seg = seg_all[lax.rem(s + n_seq - o, n_seq), 0:1, :].astype(F32)
        apart = across - along + o * rows
        fine = (apart >= 0) & (apart < WINDOW) & (seg_here == key_seg) & (s >= o)
        allowed[:, pl.ds((reach - o) * rows, rows)] = jnp.where(fine, 1.0, 0.0).astype(BF16)
    angle = ((s * rows + across).astype(F32) - seg_here) * rates_ref[...]
    turns[0] = jnp.cos(angle)
    turns[1] = jnp.sin(angle)
    for copy in packs:
        copy.wait_recv()
    gains[...] = jnp.zeros(gains.shape, F32)
    start = 0
    for row in range(6):
        size = (depth if row < QUERY else head_width // n_fsdp)
        for block in range(n_fsdp):
            gains[row : row + 1, block * size : (block + 1) * size] = pack_all[
                block, 0:1, start : start + size
            ]
        start += size

    def gain(row):
        return gains[row : row + 1, : (width if row < QUERY else head_width)]

    x = x_ref[...].astype(F32)
    h1_s[...] = (x * norm_scale(x) * gain(ATT_IN)).astype(BF16)

    for t in range(2, n_att + 2 * lag):
        weight_steps(t)
    for i in range(n_qkv):
        weight_here(i, 3)
    for copy in own_copies[:3]:
        copy.wait()

    def move_gu(*moves):
        for k, stage in moves:
            move_weight(n_att + k - 1, stage)

    move_gu((1, 1))
    tile = heads_width // 3

    @pl.loop(0, 3)
    def _(n):
        cols = lanes(n * tile, tile)
        raw_s[:, cols] = dot_nn(h1_s[...], qkv_s[:, cols])

    k_raw = raw_s[:, query_width : query_width + head_width]
    kv_own[:, :head_width] = turn(
        k_raw * norm_scale(k_raw) * gain(KEY), turns[0], turns[1]
    ).astype(BF16)
    kv_own[:, head_width:] = raw_s[:, query_width + head_width :].astype(BF16)
    for copy in kv_copies:
        copy.start()
    kv_s[reach] = kv_own[...]
    for h in range(head_count):
        q_raw = raw_s[:, h * head_width : (h + 1) * head_width]
        q_fin = q_raw * norm_scale(q_raw) * gain(QUERY)
        q_s[h] = turn(q_fin, turns[0], turns[1]).astype(BF16)
    for i in range(n_qkv, n_att):
        weight_here(i, 3)
    own_copies[3].wait()
    move_gu((1, 2))
    move_gu((2, 1))
    for copy in kv_copies:
        copy.wait_recv()

    def keys():
        return kv_s[:, :, :head_width].reshape((reach + 1) * rows, head_width)

    def values():
        return kv_s[:, :, head_width:].reshape((reach + 1) * rows, head_width)

    for h in range(head_count):
        scores = dot_nt(q_s[h], keys()) * (head_width**-0.5)
        masked = jnp.where(allowed[...].astype(F32) > 0.5, scores, masked_value)
        grown = jnp.exp(masked - jnp.max(masked, axis=-1, keepdims=True))
        probs = grown / jnp.sum(grown, axis=-1, keepdims=True)
        p_s[h] = probs.astype(BF16)
        att_s[:, h * head_width : (h + 1) * head_width] = dot_nn(p_s[h], values()).astype(BF16)

    move_gu((3, 1))
    @pl.loop(0, 3)
    def _(n):
        o_s[:, outs(n)] = dot_nn(att_s[...], wo_s[:, outs(n)])

    o_raw = o_s[...]
    middle = x_ref[...].astype(F32) + o_raw * norm_scale(o_raw) * gain(ATT_OUT)
    mid_s[...] = middle
    h_all[0] = (middle * norm_scale(middle) * gain(FFN_IN)).astype(BF16)

    def exchange(phase, src, dst):
        return {
            m: remote(src(m), dst(m), ex_send.at[phase, m], ex_recv.at[phase, m], at.line(m))
            for m in range(1, n_fsdp)
        }

    last = n_fsdp - 1
    send_h = exchange(0, lambda m: h_all.at[0], lambda m: h_all.at[m])
    send_f = exchange(1, lambda m: part_out.at[m - 1], lambda m: part_in.at[0, m - 1])
    send_df = exchange(2, lambda m: df_all.at[0], lambda m: df_all.at[m])
    send_dh = exchange(3, lambda m: part_out.at[m - 1], lambda m: part_in.at[1, m - 1])
    onward = {
        phase: remote(rows_all.at[2], rows_all.at[last],
                      relay_sem.at[phase], ex_recv.at[phase, last], at.line(1))
        for phase, rows_all in ((0, h_all), (2, df_all))
    }
    by_way = {
        phase: remote(part_out.at[last - 1], relay_in.at[phase // 2],
                      relay_sem.at[phase], relay_sem.at[phase + 3], at.line(1))
        for phase in (1, 3)
    }

    def send_rows(copies):
        copies[2].start()
        pl.when(middle_z)(copies[last].start)
        copies[1].start()

    def relay_rows(copies, phase):
        @pl.when(middle_z)
        def _():
            copies[2].wait_recv()
            onward[phase].start()

    def take_rows(copies, m):
        if m == 2:
            pl.when(~middle_z)(copies[2].wait_recv)
        elif m:
            copies[m].wait_recv()

    def send_part(copies, phase, m):
        if m == 1:
            copies[1].start()
        elif m == 2:
            pl.when(~middle_z)(copies[2].start)
        else:
            pl.when(~middle_z)(by_way[phase].start)
            pl.when(middle_z)(copies[last].start)

    def send_joint_part(copies, phase):
        @pl.when(middle_z)
        def _():
            by_way[phase].wait_recv()
            part_out[1] = (
                part_out[1].astype(F32) + relay_in[phase // 2].astype(F32)
            ).astype(BF16)
            copies[2].start()

    def take_parts(copies):
        copies[1].wait_recv()
        copies[2].wait_recv()
        pl.when(middle_z)(copies[last].wait_recv)

    def rows_sent(copies, phase):
        copies[1].wait_send()
        copies[2].wait_send()

        @pl.when(middle_z)
        def _():
            copies[last].wait_send()
            onward[phase].wait_send()

    def parts_sent(copies, phase):
        copies[1].wait_send()
        copies[2].wait_send()
        pl.when(middle_z)(copies[last].wait_send)
        pl.when(~middle_z)(by_way[phase].wait_send)

    send_rows(send_h)

    @pl.when(~middle_z)
    def _():
        part_in[0, last - 1] = jnp.zeros((rows, width), BF16)
        part_in[1, last - 1] = jnp.zeros((rows, width), BF16)

    move_gu((2, 2))
    move_gu((1, 3))
    move_gu((3, 2))
    relay_rows(send_h, 0)
    move_gu((2, 3))
    move_gu((3, 3))
    for i in range(n_att, n_items):
        weight_here(i, 3)
    for copy in own_copies[4:]:
        copy.wait()
    half_h = hidden // 2

    for m in range(n_fsdp - 1, -1, -1):
        take_rows(send_h, m)
        for n in range(2):
            cols = slice(n * half_h, (n + 1) * half_h)
            gate = dot_nn(h_all[m], w_in[0, :, cols])
            up = dot_nn(h_all[m], w_in[1, :, cols])
            squared = gate * gate
            bent = jnp.tanh(GELU_RATE * (gate + GELU_CUBE * squared * gate))
            gelu = 0.5 * gate * (1.0 + bent)
            slope = 0.5 * (1.0 + bent) + 0.5 * gate * (1.0 - bent * bent) * (
                GELU_RATE * (1.0 + 3.0 * GELU_CUBE * squared)
            )
            bent_s[pl.ds(m * rows, rows), cols] = gelu.astype(BF16)
            bent_s[pl.ds(tokens + m * rows, rows), cols] = (slope * up).astype(BF16)
            act[m, :, cols] = (gelu * up).astype(BF16)
        part = dot_nn(act[m], w_down[...])
        if m:
            part_out[m - 1] = part.astype(BF16)
            send_part(send_f, 1, m)
        else:
            total[...] = part

    send_joint_part(send_f, 1)
    for m in range(n_fsdp):
        h_turn[:, pl.ds(m * rows, rows)] = h_all[m].T
    for i in range(n_att, n_items):
        weight_sent(i)

    take_parts(send_f)
    f_raw = total[...]
    for m in range(1, n_fsdp):
        f_raw = f_raw + part_in[0, m - 1].astype(F32)
    cot = cot_ref[...].astype(F32)
    scale = norm_scale(f_raw)
    d_f, d_gain = norm_back(f_raw, gain(FFN_OUT), scale, cot)
    df_all[0] = d_f.astype(BF16)
    send_rows(send_df)
    small_out[pl.ds(rows, rows), :] = mid_s[...] + f_raw * scale * gain(FFN_OUT)
    dgains[...] = jnp.zeros(dgains.shape, F32)
    dgains[FFN_OUT : FFN_OUT + 1, :] = d_gain
    parts_sent(send_f, 1)

    chunks = [("d", 0, False), ("d", 1, True)]
    chunks += [("g", m, m % 2 == 0) for m in range(n_fsdp)]
    chunks += [("o", 0, False), ("q", 0, True)]
    tiles_d = hidden // 256
    spans_d = (pl.ds(0, n_fsdp), pl.ds(n_fsdp, tiles_d - n_fsdp))

    def mine_of(kind, i):
        if kind == "d":
            return own_d.at[spans_d[i]]
        return {"g": own_g, "o": own_o, "q": own_q}[kind].at[i]

    def hi_part(kind, hi):
        if kind == "d":
            return slice(None), many(hi * 64, 64), slice(None)
        if kind == "g":
            return many(hi * (depth // 2), depth // 2), slice(None)
        if kind == "q":
            return slice(None), lanes(hi * (heads_width // 2), heads_width // 2)
        return many(hi * (rows_o // 4), rows_o // 4), slice(None)

    def lo_part(kind, hi, lo):
        if kind == "d":
            return slice(None), many(hi * 64 + lo * 32, 32), slice(None)
        if kind == "g":
            return (
                many(hi * (depth // 2), depth // 2),
                lanes(lo * (hidden // 2), hidden // 2),
            )
        if kind == "q":
            start = hi * (heads_width // 2) + lo * (heads_width // 4)
            return slice(None), lanes(start, heads_width // 4)
        return many(hi * (rows_o // 4) + lo * (rows_o // 8), rows_o // 8), slice(None)

    def fin_part(kind, i, where, core):
        if kind == "d":
            span = spans_d[i]
            tiles = pl.ds(core * tiles_d + span.start, span.size)
            return fin_d.at[tiles, where[-2], :]
        rows_at, cols_at = where
        if kind == "g":
            return fin_gu.at[core * n_fsdp + i, rows_at, cols_at]
        if kind == "o":
            return fin_d.at[2 * tiles_d + core, rows_at, :]
        base = core * (depth // 2)
        if isinstance(cols_at, slice):
            cols_at = pl.ds(0, heads_width)
        return fin_gu.at[2 * n_fsdp, many(base, depth // 2), cols_at]
    def add(ref, where, other):
        rows_at, cols_at = where
        start = 0 if isinstance(rows_at, slice) else rows_at.start
        slab = 16

        @pl.loop(0, other.shape[0] // slab)
        def _(n):
            here = pl.ds(pl.multiple_of(start + n * slab, slab), slab)
            there = pl.ds(pl.multiple_of(n * slab, slab), slab)
            ref[here, cols_at] = (
                ref[here, cols_at].astype(F32) + other[there, :].astype(F32)
            ).astype(BF16)

    whole = (slice(None), slice(None))
    from_hi = {"d": hi_d, "g": hi_g, "o": hi_o, "q": hi_q}
    from_lo = {"d": lo_d, "g": lo_g, "o": lo_o, "q": lo_q}
    his, los, lines = [], [], []
    for j, (kind, i, first_x) in enumerate(chunks):
        hi, lo, mask_hi, mask_lo = at.halves(first_x)
        mine = mine_of(kind, i)
        if kind == "q":
            parts = (
                own_q.at[:, :, hi_part(kind, 1 - hi)[1]], hi_q,
                own_q.at[:, :, lo_part(kind, hi, 1 - lo)[1]], lo_q,
            )
        else:
            slot = spans_d[i] if kind == "d" else i
            parts = (
                mine.at[hi_part(kind, 1 - hi)], from_hi[kind].at[slot],
                mine.at[lo_part(kind, hi, 1 - lo)], from_lo[kind].at[slot],
            )
        his.append(
            remote(parts[0], parts[1], hi_send.at[j], hi_recv.at[j], at.plane(mask_hi))
        )
        los.append(
            remote(parts[2], parts[3], lo_send.at[j], lo_recv.at[j], at.plane(mask_lo))
        )
        line = None
        if kind == "g" and i:
            line = remote(mine.at[lo_part(kind, hi, lo)],
                          fin_part(kind, z, lo_part(kind, hi, lo), c),
                          z_send.at[j], z_recv.at[j], at.line(i))
        lines.append(line)
    stage = {
        "d": lambda i: part_in.at[0] if i else h_all,
        "g": lambda i: bent_s.at[pl.ds(i * depth, depth)],
        "q": lambda i: w_in.at[0, pl.ds(i * (depth // 2), depth // 2), pl.ds(0, heads_width)],
        "o": lambda i: w_in.at[1, pl.ds(i * (rows_o // 2), rows_o // 2), pl.ds(0, width)],
    }
    to_core = [("d", 0), ("d", 1)]
    to_core += [(kind, m) for kind in "goq" for m in range(n_fsdp)]
    cores = {
        key: remote(stage[key[0]](key[1]), mine_of(*key), c_send.at[k], c_recv.at[k], at.plane(1))
        for k, key in enumerate(to_core)
    }
    line_sums = {}
    for k, (kind, ref) in enumerate((("o", line_o), ("q", line_q))):
        for m in range(1, n_fsdp):
            part = mine_of(kind, m)
            if kind == "q":
                part = part.at[lo_part(kind, at.x, at.y)]
            line_sums[kind, m] = remote(
                part, ref.at[m - 1], oq_send.at[k, m], oq_recv.at[k, m], at.line(m)
            )

    puts, hands = [], []
    for j, (kind, i, first_x) in enumerate(chunks):
        hi, lo, mask_hi, mask_lo = at.halves(first_x)
        which = flip(z, i, 2) if kind == "g" else i
        piece = fin_part(kind, which, lo_part(kind, hi, lo), c)
        half = fin_part(kind, which, hi_part(kind, hi), c)
        full = fin_part(kind, which, whole, c)
        put = None
        if lines[j] is None:
            put = pltpu.make_async_copy(
                mine_of(kind, i).at[lo_part(kind, hi, lo)], piece, put_sem.at[j]
            )
        puts.append(put)
        hands.append([
            remote(part, part, ag_send.at[j, k], ag_recv.at[j, k], at.plane(mask))
            for k, (part, mask) in enumerate(((piece, mask_lo), (half, mask_hi), (full, 1)))
        ])

    def add_all(kind, i, where, came):
        if kind == "d":
            for n in range(spans_d[i].start, spans_d[i].start + spans_d[i].size):
                add(own_d.at[n], where[1:], came.at[n])
        elif kind == "q":
            for m in range(n_fsdp):
                add(own_q.at[m], where, came.at[m])
        else:
            add(mine_of(kind, i), where, came.at[i])

    def take_hi(j):
        kind, i, first_x = chunks[j]
        hi, lo, _, _ = at.halves(first_x)
        his[j].wait_recv()
        add_all(kind, i, hi_part(kind, hi), from_hi[kind])
        los[j].start()

    def take_lo(j):
        kind, i, first_x = chunks[j]
        hi, lo, _, _ = at.halves(first_x)
        los[j].wait_recv()
        add_all(kind, i, lo_part(kind, hi, lo), from_lo[kind])
        if lines[j] is not None:
            lines[j].start()
        elif kind == "q":
            for m in range(1, n_fsdp):
                line_sums[kind, m].start()
        else:
            puts[j].start()

    def begin_hand(j):
        if lines[j] is not None:
            lines[j].wait_recv()
        else:
            puts[j].wait()
        hands[j][0].start()

    def hand_on(j, k):
        hands[j][k - 1].wait_recv()
        hands[j][k].start()

    def down_stage(n):
        return h_all.at[n] if n < n_fsdp else part_in.at[0, n - n_fsdp]

    def down_grads(core, dst_of, adds):
        right = df_all[...].reshape(tokens, width)
        for n in range(tiles_d):
            left = act[:, :, lanes(core * (hidden // 2) + n * 128, 128)].reshape(tokens, 128).T
            grads = dot_nn(left, right)
            dst = dst_of[n] if adds else dst_of(n)
            if adds:
                grads = grads + dst[...].astype(F32)
            dst[...] = grads.astype(BF16)

    def in_grads(core, m, dst, adds):
        left_at = many(flip(z, m, 2) * depth, depth)

        for n in range(2):
            cols = slice(n * half_h, (n + 1) * half_h)
            grads = dot_nn(h_turn[left_at, :], d_in[core, :, :, cols].reshape(tokens, half_h))
            if adds:
                grads = grads + dst[:, cols].astype(F32)
            dst[:, cols] = grads.astype(BF16)

    rows_sent(send_h, 0)
    for m in range(n_fsdp):
        if m == 1:
            relay_rows(send_df, 2)
        take_rows(send_df, m)
        if m == last:
            down_grads(1 - c, down_stage, False)
            cores["d", 0].start()
            cores["d", 1].start()
        for n in range(2):
            cols = slice(n * half_h, (n + 1) * half_h)
            d_act = dot_nt(df_all[m], w_down[cols, :])
            slope = bent_s[pl.ds(tokens + m * rows, rows), cols].astype(F32)
            d_in[0, m, :, cols] = (d_act * slope).astype(BF16)
            gelu = bent_s[pl.ds(m * rows, rows), cols].astype(F32)
            d_in[1, m, :, cols] = (d_act * gelu).astype(BF16)
        part = dot_nt(d_in[0, m], w_in[0]) + dot_nt(d_in[1, m], w_in[1])
        if m:
            part_out[m - 1] = part.astype(BF16)
            send_part(send_dh, 3, m)
        else:
            total[...] = part

    cores["d", 0].wait_recv()
    cores["d", 1].wait_recv()
    down_grads(c, own_d.at, True)
    his[0].start()
    his[1].start()
    send_joint_part(send_dh, 3)
    for m in range(n_fsdp):
        in_grads(1 - c, m, stage["g"](m), False)
        cores["g", m].start()
    for m in range(n_fsdp):
        cores["g", m].wait_recv()
        in_grads(c, m, own_g.at[m], True)
        his[2 + m].start()

    dkv_copies = [
        remote(dkv_send.at[reach - o], dkv_came.at[o - 1], dkv_ssem.at[o - 1], dkv_rsem.at[o - 1],
               (lax.rem(s + n_seq - o, n_seq), z))
        for o in range(1, reach + 1)
    ]
    gain_copies = [
        remote(dgains, gain_in.at[k], gain_send.at[k], gain_recv.at[k], at.plane(k))
        for k in range(1, n_seq)
    ]
    gain_lines = [
        remote(gain_line.at[0], gain_line.at[m], gain_send.at[n_seq + m], gain_recv.at[n_seq + m],
               at.line(m))
        for m in range(1, n_fsdp)
    ]

    def to_middle():
        take_parts(send_dh)
        dh = total[...]
        for m in range(1, n_fsdp):
            dh = dh + part_in[1, m - 1].astype(F32)
        mid = mid_s[...]
        d_mid, d_gain = norm_back(mid, gain(FFN_IN), norm_scale(mid), dh)
        d_mid = d_mid + cot_ref[...].astype(F32)
        mid_s[...] = d_mid
        dgains[FFN_IN : FFN_IN + 1, :] = d_gain
        o_raw = o_s[...]
        d_o, d_gain = norm_back(o_raw, gain(ATT_OUT), norm_scale(o_raw), d_mid)
        dgains[ATT_OUT : ATT_OUT + 1, :] = d_gain
        do_s[...] = d_o.astype(BF16)
        for h in range(head_count):
            here = pl.ds(h * head_width, head_width)
            datt_s[h] = dot_nt(do_s[...], wo_s[here, :]).astype(BF16)

    def unturn(rows_in):
        return turn(rows_in, turns[0], -turns[1])

    def through_head(h):
        probs = p_s[h].astype(F32)
        d_att = datt_s[h]
        d_probs = dot_nt(d_att, values())
        d_scores = probs * (d_probs - jnp.sum(probs * d_probs, axis=-1, keepdims=True))
        ds_low = d_scores.astype(BF16)
        scale = head_width**-0.5
        ds_s[h] = ds_low
        cols = slice(h * head_width, (h + 1) * head_width)
        q_raw = raw_s[:, cols]
        d_q, d_gain = norm_back(
            q_raw, gain(QUERY), norm_scale(q_raw), unturn(dot_nn(ds_low, keys()) * scale)
        )
        dqkv_s[:, cols] = d_q.astype(BF16)
        dgains[QUERY : QUERY + 1, :head_width] += d_gain

    def return_keys():
        for side, left, right, scale in (
            (0, ds_s, q_s, head_width**-0.5),
            (1, p_s, datt_s, 1.0),
        ):
            cols = slice(side * head_width, (side + 1) * head_width)
            d_side = scale * inner_rows(
                left[...].reshape(head_count * rows, (reach + 1) * rows),
                right[...].reshape(head_count * rows, head_width),
            )
            for b in range(reach):
                dkv_send[b, :, cols] = d_side[b * rows : (b + 1) * rows].astype(BF16)
            dkv_s[:, cols] = d_side[reach * rows :]
        for copy in dkv_copies:
            copy.start()

    def grad_tiles(left_at, turned, right, n_cols, dst, adds):
        tile = n_cols // 3
        for k in range(3):
            grads = dot_nn(turned[left_at, :], right[:, k * tile : (k + 1) * tile])
            if adds:
                grads = grads + dst[:, k * tile : (k + 1) * tile].astype(F32)
            dst[:, k * tile : (k + 1) * tile] = grads.astype(BF16)

    def core_grads(kind, turned, right, span, n_cols):
        for m in range(n_fsdp):
            start = flip(z, m, 2) * span + (1 - c) * (span // 2)
            grad_tiles(many(start, span // 2), turned, right, n_cols, stage[kind](m), False)
            cores[kind, m].start()
        for m in list(range(1, n_fsdp)) + [0]:
            start = flip(z, m, 2) * span + c * (span // 2)
            cores[kind, m].wait_recv()
            grad_tiles(many(start, span // 2), turned, right, n_cols, mine_of(kind, m), True)
            if m and kind == "o":
                line_sums[kind, m].start()
        if kind == "q":
            his[-1].start()

    def output_grads():
        h_turn[pl.ds(0, query_width), pl.ds(0, rows)] = att_s[...].T
        core_grads("o", h_turn.at[:, pl.ds(0, rows)], do_s, rows_o, width)

    def key_grads():
        h_turn[:, pl.ds(rows, rows)] = h1_s[...].T
        d_kv = dkv_s[...]
        for o in range(reach):
            dkv_copies[o].wait_recv()
            d_kv = d_kv + dkv_came[o].astype(F32)
        k_raw = raw_s[:, query_width : query_width + head_width]
        d_k, d_gain = norm_back(
            k_raw, gain(KEY), norm_scale(k_raw), unturn(d_kv[:, :head_width])
        )
        dqkv_s[:, query_width : query_width + head_width] = d_k.astype(BF16)
        dqkv_s[:, query_width + head_width :] = d_kv[:, head_width:].astype(BF16)
        dgains[KEY : KEY + 1, :head_width] = d_gain
        core_grads("q", h_turn.at[:, pl.ds(rows, rows)], dqkv_s, depth, heads_width)

    def sum_line(j):
        kind = chunks[j][0]
        where = lo_part(kind, at.x, at.y) if kind == "q" else whole
        for m in range(1, n_fsdp):
            line_sums[kind, m].wait_recv()
            add(mine_of(kind, 0), where, {"o": line_o, "q": line_q}[kind].at[m - 1])
        (puts if kind == "q" else his)[j].start()

    def to_input():
        x = x_ref[...].astype(F32)
        d_h = dot_nt(dqkv_s[...], qkv_s[...])
        d_x, d_gain = norm_back(x, gain(ATT_IN), norm_scale(x), d_h)
        small_out[pl.ds(0, rows), :] = mid_s[...] + d_x
        dgains[ATT_IN : ATT_IN + 1, :] = d_gain
        for copy in gain_copies:
            copy.start()

    def sum_gains():
        sums = dgains[...]
        for k, copy in enumerate(gain_copies):
            copy.wait_recv()
            sums = sums + gain_in[k + 1]
        gain_line[0] = sums
        for copy in gain_lines:
            copy.start()

    take_hi(0)
    take_hi(1)
    to_middle()
    through_head(0)
    through_head(1)
    through_head(2)
    through_head(3)
    return_keys()
    output_grads()
    take_hi(2)
    take_hi(3)
    take_lo(0)
    take_lo(1)
    begin_hand(0)
    begin_hand(1)
    key_grads()
    take_hi(4)
    take_hi(5)
    take_lo(2)
    take_lo(3)
    begin_hand(2)
    sum_line(6)
    hand_on(0, 1)
    hand_on(1, 1)
    take_lo(4)
    take_lo(5)
    to_input()
    begin_hand(3)
    hand_on(0, 2)
    hand_on(1, 2)
    take_hi(7)
    hand_on(2, 1)
    begin_hand(4)
    begin_hand(5)
    take_hi(6)
    hand_on(3, 1)
    take_lo(7)
    hand_on(2, 2)
    sum_gains()
    take_lo(6)
    begin_hand(6)
    hand_on(4, 1)
    hand_on(5, 1)
    sum_line(7)
    begin_hand(7)
    hand_on(3, 2)
    hand_on(6, 1)
    hand_on(7, 1)
    hand_on(4, 2)
    hand_on(5, 2)
    hand_on(6, 2)
    hand_on(7, 2)
    sums = gain_line[0]
    for m, copy in enumerate(gain_lines):
        copy.wait_recv()
        sums = sums + gain_line[m + 1]
    for row in range(6):
        size = depth if row < QUERY else head_width // n_fsdp
        for block in range(n_fsdp):

            @pl.when(z == block)
            def _():
                small_out[2 * rows + row : 2 * rows + row + 1, :size] = sums[
                    row : row + 1, block * size : (block + 1) * size
                ]


    for j in range(len(chunks)):
        hands[j][2].wait_recv()
        for k in range(3):
            hands[j][k].wait_send()
        his[j].wait_send()
        los[j].wait_send()
        if lines[j] is not None:
            lines[j].wait_send()
    for copy in list(cores.values()) + list(line_sums.values()):
        copy.wait_send()
    for copy in gain_copies + gain_lines + dkv_copies + kv_copies + packs + seg_copies:
        copy.wait_send()
    for i in range(n_att):
        weight_sent(i)
    rows_sent(send_df, 2)
    parts_sent(send_dh, 3)


def layer(n_seq, n_fsdp, share, hidden, reach, head_count, x, cot, rates, segs, gains,
          w_gate, w_up, w_query, w_key, w_value, w_output, w_down):
    rows, width = x.shape
    depth = width // n_fsdp
    head_width = w_key.shape[1]
    query_width = w_query.shape[1]
    heads_width = query_width + 2 * head_width
    rows_o = w_output.shape[0]
    n_items = 4 * (n_fsdp - 1)
    anywhere = pl.BlockSpec(memory_space=pl.ANY)
    in_vmem = pl.BlockSpec(memory_space=pltpu.VMEM)
    shape = jax.ShapeDtypeStruct
    sems = pltpu.SemaphoreType.DMA

    def low(*size):
        return pltpu.VMEM(size, BF16)

    def full(*size):
        return pltpu.VMEM(size, F32)

    return pl.pallas_call(
        functools.partial(layer_kernel, n_seq, n_fsdp, share, reach, head_count),
        out_shape=[
            shape((2 * rows + 8, width), F32),
            shape((2 * n_fsdp + 1, depth, hidden), BF16),
            shape((hidden // 128 + 2, 128, width), BF16),
        ],
        in_specs=[in_vmem] * 10 + [anywhere] * 7,
        out_specs=[in_vmem] + [anywhere] * 2,
        scratch_shapes=[
            low(width, heads_width),
            low(n_fsdp * rows_o, width),
            low(2, width, hidden),
            low(hidden, width),
            full(n_fsdp, 8, -(-sum(g.shape[0] for g in gains) // 128) * 128),
            pltpu.VMEM((n_seq, 8, rows), jnp.int32),
            full(8, width),
            low(rows, (reach + 1) * rows),
            full(2, rows, head_width // 2),
            low(rows, width),
            full(rows, heads_width),
            low(head_count, rows, head_width),
            low(rows, 2 * head_width),
            low(reach + 1, rows, 2 * head_width),
            low(head_count, rows, (reach + 1) * rows),
            low(rows, query_width),
            full(rows, width),
            full(rows, width),
            low(n_fsdp, rows, width),
            low(n_fsdp, rows, width),
            low(max(width, 2 * n_fsdp * rows), hidden),
            low(n_fsdp, rows, hidden),
            low(2, n_fsdp, rows, hidden),
            low(width, n_fsdp * rows),
            low(n_fsdp - 1, rows, width),
            low(2, n_fsdp - 1, rows, width),
            low(2, rows, width),
            full(rows, width),
            low(hidden // 256, 128, width),
            low(n_fsdp, depth, hidden),
            low(n_fsdp, rows_o // 2, width),
            low(n_fsdp, depth // 2, heads_width),
            low(hidden // 256, 64, width),
            low(n_fsdp, depth // 2, hidden),
            low(1, rows_o // 4, width),
            low(n_fsdp, depth // 2, heads_width // 2),
            low(hidden // 256, 32, width),
            low(n_fsdp, depth // 2, hidden // 2),
            low(1, rows_o // 8, width),
            low(n_fsdp, depth // 2, heads_width // 4),
            low(n_fsdp - 1, rows_o // 2, width),
            low(n_fsdp - 1, depth // 2, heads_width // 4),
            low(rows, width),
            low(head_count, rows, head_width),
            low(head_count, rows, (reach + 1) * rows),
            full(rows, 2 * head_width),
            low(reach, rows, 2 * head_width),
            low(reach, rows, 2 * head_width),
            low(rows, heads_width),
            full(8, width),
            full(n_seq, 8, width),
            full(n_fsdp, 8, width),
            sems((n_items, 5)),
            sems((n_items, 5)),
            sems((7,)),
            sems((n_fsdp,)),
            sems((n_fsdp,)),
            sems((n_seq,)),
            sems((n_seq,)),
            sems((reach,)),
            sems((reach,)),
            sems((4, n_fsdp)),
            sems((4, n_fsdp)),
            sems((7,)),
            sems((reach,)),
            sems((reach,)),
            sems((2 + 3 * n_fsdp,)),
            sems((2 + 3 * n_fsdp,)),
            sems((4 + n_fsdp,)),
            sems((4 + n_fsdp,)),
            sems((4 + n_fsdp,)),
            sems((4 + n_fsdp,)),
            sems((4 + n_fsdp,)),
            sems((4 + n_fsdp,)),
            sems((2, n_fsdp)),
            sems((2, n_fsdp)),
            sems((4 + n_fsdp,)),
            sems((4 + n_fsdp, 3)),
            sems((4 + n_fsdp, 3)),
            sems((n_seq + n_fsdp,)),
            sems((n_seq + n_fsdp,)),
        ],
        compiler_params=pltpu.CompilerParams(
            collective_id=0, has_side_effects=True, vmem_limit_bytes=63 << 20
        ),
        name="decoder_layer",
    )(x, cot, rates, segs, *gains, w_gate, w_up, w_query, w_key, w_value, w_output, w_down)


def finish_kernel(
    share, skip_ref, wins_ref, d0_ref, d1_ref, d2_ref, qkv_ref, wo_ref, small_ref,
    gate_ref, up_ref, down_ref, wq_ref, wk_ref, wv_ref, wo_out, out_ref, dx_ref, *gain_outs,
):
    n_win, hidden = wins_ref.shape[0] // 2, wins_ref.shape[2]
    starts = [window_start(i, share) for i in range(n_win)]
    for i, ref in enumerate((gate_ref, up_ref)):
        for w in range(n_win):
            at = i * n_win + w
            first = starts[w]
            last = starts[w + 1] if w + 1 < n_win else first + hidden
            shared = starts[w - 1] + hidden - first if w else 0
            if shared:
                ref[:, first : first + shared] = wins_ref[at, :, :shared].astype(F32) + wins_ref[
                    at - 1, :, hidden - shared :
                ].astype(F32)
            ref[:, first + shared : last] = wins_ref[at, :, shared : last - first].astype(F32)
    for k, ref in enumerate((d0_ref, d1_ref, d2_ref)):
        down_ref[pl.ds(k * ref.shape[0], ref.shape[0]), :] = ref[...].astype(F32)
    start = 0
    for ref in (wq_ref, wk_ref, wv_ref):
        size = ref.shape[1]
        ref[...] = qkv_ref[0, :, start : start + size].astype(F32)
        start += size
    wo_out[...] = wo_ref[...].astype(F32)

    @pl.when(pl.program_id(0) == 0)
    def _():
        rows_here = dx_ref.shape[0]
        dx_ref[...] = small_ref[:rows_here]
        out_ref[...] = small_ref[rows_here : 2 * rows_here].astype(BF16)
        for row, ref in enumerate(gain_outs):
            ref[...] = small_ref[2 * rows_here + row, : ref.shape[0]]


def finish(share, skipped, gain_sizes, query_width, head_width, rows_o, windows, tiles, small):
    n_win, rows, hidden = windows.shape
    n_win = n_win // 2
    width = tiles.shape[2]
    rows_here = small.shape[0] // 2 - 4
    slab = 32
    steps = rows // slab
    down_slab = share // steps // 3
    heads_width = query_width + 2 * head_width
    down = tiles.reshape(-1, width)
    start_o = (down.shape[0] - rows_o) // slab
    shape = jax.ShapeDtypeStruct

    def slabs(n_rows, n_cols, n_slabs):
        return pl.BlockSpec(
            (n_rows, n_cols), lambda i, skip: (jnp.minimum(i, n_slabs - 1), 0)
        )

    def down_part(k):
        return pl.BlockSpec((down_slab, width), lambda i, skip: (3 * i + k + skip[0], 0))

    def whole(array_shape):
        return pl.BlockSpec(array_shape, lambda i, skip: (0,) * len(array_shape))

    return pl.pallas_call(
        functools.partial(finish_kernel, share),
        grid_spec=pltpu.PrefetchScalarGridSpec(
            num_scalar_prefetch=1,
            grid=(steps,),
            in_specs=[
                pl.BlockSpec((2 * n_win, slab, hidden), lambda i, skip: (0, i, 0)),
                down_part(0),
                down_part(1),
                down_part(2),
                pl.BlockSpec((1, slab, heads_width), lambda i, skip: (2 * n_win, i, 0)),
                pl.BlockSpec(
                    (slab, width),
                    lambda i, skip: (start_o + jnp.minimum(i, rows_o // slab - 1), 0),
                ),
                whole(small.shape),
            ],
            out_specs=[
                slabs(slab, n_win * share, steps),
                slabs(slab, n_win * share, steps),
                slabs(3 * down_slab, width, steps),
                slabs(slab, query_width, steps),
                slabs(slab, head_width, steps),
                slabs(slab, head_width, steps),
                slabs(slab, width, rows_o // slab),
                whole((rows_here, width)),
                whole((rows_here, width)),
            ]
            + [whole((size,)) for size in gain_sizes],
        ),
        out_shape=[
            shape((rows, n_win * share), F32),
            shape((rows, n_win * share), F32),
            shape((share, width), F32),
            shape((rows, query_width), F32),
            shape((rows, head_width), F32),
            shape((rows, head_width), F32),
            shape((rows_o, width), F32),
            shape((rows_here, width), BF16),
            shape((rows_here, width), F32),
        ]
        + [shape((size,), F32) for size in gain_sizes],
        compiler_params=pltpu.CompilerParams(vmem_limit_bytes=63 << 20),
        name="finish",
    )((skipped // down_slab).reshape(1), windows, down, down, down, windows, down, small)


def shards(n_seq, n_fsdp, *args):
    w_query, w_key, w_output, w_gate = args[4], args[5], args[9], args[12]
    depth, ffn_width = w_gate.shape
    rows_here = args[0].shape[1]
    share = ffn_width // n_fsdp
    reach = (WINDOW - 2 + rows_here) // rows_here
    fits = (
        n_seq == 8
        and n_fsdp == 4
        and args[0].shape[0] == 1
        and reach < n_seq
        and rows_here == 128
        and window_width(share, n_fsdp) == 256 * (2 * n_fsdp - 1)
        and depth % 32 == 0
        and w_output.shape[0] == 256
        and w_key.shape[1] % 256 == 0
        and w_query.shape[1] % 512 == 0
        and w_output.shape[1] % 384 == 0
        and ffn_width % n_fsdp == 0
        and share % 16 == 0
        and rows_here // 2 * (share // 64) * 2 == rows_here * (depth // 32) * 3
        and (share - window_start(1, share)) % 64 == 0
        and window_start(n_fsdp - 1, share) + window_width(share, n_fsdp) == ffn_width
    )
    if fits:
        return shards_fused(n_seq, n_fsdp, *args)
    return shards_plain(*args)


def shards_fused(
    n_seq,
    n_fsdp,
    inputs,
    segments,
    cotangent,
    gain_attn_in,
    w_query,
    w_key,
    w_value,
    gain_query,
    gain_key,
    w_output,
    gain_attn_out,
    gain_ffn_in,
    w_gate,
    w_up,
    w_down,
    gain_ffn_out,
):
    rows_here, width = inputs.shape[1:]
    head_width = w_key.shape[1]
    query_width = w_query.shape[1]
    head_count = query_width // head_width
    share = w_gate.shape[1] // n_fsdp
    hidden = window_width(share, n_fsdp)
    reach = (WINDOW - 2 + rows_here) // rows_here
    line = lax.axis_index("fsdp")
    gains = (gain_attn_in, gain_attn_out, gain_ffn_in, gain_ffn_out, gain_query, gain_key)
    rates = 10000.0 ** (-(np.arange(head_width // 2, dtype=np.float32) * 2.0) / head_width)
    small, fin_gu, fin_d = layer(
        n_seq, n_fsdp, share, hidden, reach, head_count,
        inputs[0], cotangent[0], jnp.asarray(rates, F32)[None], segments, gains,
        w_gate, w_up, w_query, w_key, w_value, w_output, w_down,
    )
    (
        grad_gate, grad_up, grad_down, grad_q, grad_k, grad_v, grad_o, outputs, d_inputs,
        g_attn_in, g_attn_out, g_ffn_in, g_ffn_out, g_query, g_key,
    ) = finish(
        share, line * share - window_start(line, share), [g.shape[0] for g in gains],
        query_width, head_width, w_output.shape[0], fin_gu, fin_d, small,
    )
    return (
        outputs[None],
        d_inputs[None],
        g_attn_in,
        grad_q,
        grad_k,
        grad_v,
        g_query,
        g_key,
        grad_o,
        g_attn_out,
        g_ffn_in,
        grad_gate,
        grad_up,
        grad_down,
        g_ffn_out,
    )


def solution(mesh):
    placed = (
        P("fsdp", "seq", None),
        P("fsdp", "seq"),
        P("fsdp", "seq", None),
        P("fsdp"),
        P("fsdp", None),
        P("fsdp", None),
        P("fsdp", None),
        P("fsdp"),
        P("fsdp"),
        P("fsdp", None),
        P("fsdp"),
        P("fsdp"),
        P("fsdp", None),
        P("fsdp", None),
        P("fsdp", None),
        P("fsdp"),
    )
    return jax.shard_map(
        functools.partial(shards, mesh.shape["seq"], mesh.shape["fsdp"]),
        mesh=mesh,
        in_specs=placed,
        out_specs=(
            P("fsdp", "seq", None),
            P("fsdp", "seq", None),
            P("fsdp"),
            P("fsdp", None),
            P("fsdp", None),
            P("fsdp", None),
            P("fsdp"),
            P("fsdp"),
            P("fsdp", None),
            P("fsdp"),
            P("fsdp"),
            P("fsdp", None),
            P("fsdp", None),
            P("fsdp", None),
            P("fsdp"),
        ),
        check_vma=False,
    )
```

```python
import functools

import jax
import jax.numpy as jnp
import numpy as np
from jax import lax
from jax.experimental import pallas as pl
from jax.experimental.pallas import tpu as pltpu
from jax.sharding import PartitionSpec as P

WINDOW = 512


epsilon = 1e-06
masked_value = -1e30


def from_behind(block, axis, distance):
    devices = range(lax.axis_size(axis))
    route = [(i - distance, i) for i in devices if i - distance in devices]
    return lax.ppermute(block, axis, route)


def norm_rows(rows_in, gain_vec):
    return (
        rows_in
        * lax.rsqrt(jnp.mean(rows_in * rows_in, axis=-1, keepdims=True) + epsilon)
        * gain_vec
    )


def angles(positions, head_width):
    inv_rates = 10000.0 ** (-(jnp.arange(head_width // 2, dtype=jnp.float32) * 2.0) / head_width)
    return positions.astype(jnp.float32)[:, None] * inv_rates[None, :]


def rotate(rows_in, angles_at):
    half_width = rows_in.shape[-1] // 2
    lower_half = rows_in[..., :half_width]
    upper_half = rows_in[..., half_width:]
    cosine = jnp.cos(angles_at)
    sine_part = jnp.sin(angles_at)
    return jnp.concatenate(
        [
            lower_half * cosine - upper_half * sine_part,
            upper_half * cosine + lower_half * sine_part,
        ],
        axis=-1,
    )


def geglu_act(gate_proj, up_proj):
    return jax.nn.gelu(gate_proj, approximate=True) * up_proj


def inner_rows(left, right):
    return lax.dot_general(
        left, right, (((0,), (0,)), ((), ())), preferred_element_type=jnp.float32
    )


def outer_cols(left, right):
    return lax.dot_general(
        left, right, (((1,), (1,)), ((), ())), preferred_element_type=jnp.float32
    )


def shards_plain(
    inputs,
    segments,
    cotangent,
    gain_attn_in,
    w_query,
    w_key,
    w_value,
    gain_query,
    gain_key,
    w_output,
    gain_attn_out,
    gain_ffn_in,
    w_gate,
    w_up,
    w_down,
    gain_ffn_out,
):
    rows_here = inputs.shape[1]
    head_width = w_key.shape[1]
    head_count = w_query.shape[1] // head_width
    reach_devs = (WINDOW - 2 + rows_here) // rows_here
    score_scale = head_width ** (-0.5)
    first_row = lax.axis_index("seq") * rows_here
    tokens = inputs[0].astype(jnp.float32)
    seg_here = segments[0]
    positions = first_row + jnp.arange(rows_here, dtype=jnp.int32)
    angles_at = angles(positions - seg_here, head_width)
    wq_all, wk_all, wv_all, wo_all, g_attn_in, g_query, g_key, g_attn_out, g_ffn_in, g_ffn_out = (
        lax.all_gather(w_query, "fsdp", axis=0, tiled=True),
        lax.all_gather(w_key, "fsdp", axis=0, tiled=True),
        lax.all_gather(w_value, "fsdp", axis=0, tiled=True),
        lax.all_gather(w_output, "fsdp", axis=0, tiled=True),
        lax.all_gather(gain_attn_in, "fsdp", axis=0, tiled=True),
        lax.all_gather(gain_query, "fsdp", axis=0, tiled=True),
        lax.all_gather(gain_key, "fsdp", axis=0, tiled=True),
        lax.all_gather(gain_attn_out, "fsdp", axis=0, tiled=True),
        lax.all_gather(gain_ffn_in, "fsdp", axis=0, tiled=True),
        lax.all_gather(gain_ffn_out, "fsdp", axis=0, tiled=True),
    )
    g_attn_in = g_attn_in.astype(jnp.float32)
    g_query = g_query.astype(jnp.float32)
    g_key = g_key.astype(jnp.float32)
    g_attn_out = g_attn_out.astype(jnp.float32)
    g_ffn_in = g_ffn_in.astype(jnp.float32)
    g_ffn_out = g_ffn_out.astype(jnp.float32)
    normed_one, pull_one = jax.vjp(norm_rows, tokens, g_attn_in)
    h_one = normed_one.astype(jnp.bfloat16)
    q_raw = jnp.dot(h_one, wq_all, preferred_element_type=jnp.float32)
    k_raw = jnp.dot(h_one, wk_all, preferred_element_type=jnp.float32)
    v_raw = jnp.dot(h_one, wv_all, preferred_element_type=jnp.float32)

    def prepare(q_in, k_in, gq_in, gk_in):
        q_rows = q_in.reshape(q_in.shape[0], head_count, head_width)
        q_fin = rotate(norm_rows(q_rows, gq_in), angles_at[:, None, :])
        k_fin = rotate(norm_rows(k_in, gk_in), angles_at)
        return (q_fin, k_fin)

    (q_fin, k_fin), pull_prep = jax.vjp(prepare, q_raw, k_raw, g_query, g_key)
    q_low = q_fin.astype(jnp.bfloat16).reshape(rows_here * head_count, head_width)
    k_low = k_fin.astype(jnp.bfloat16)
    v_low = v_raw.astype(jnp.bfloat16)
    key_parts = []
    value_parts = []
    seg_parts = []
    for offset in range(reach_devs, 0, -1):
        k_came, v_came, s_came = from_behind((k_low, v_low, seg_here), "seq", offset)
        key_parts.append(k_came)
        value_parts.append(v_came)
        seg_parts.append(s_came)
    key_rows = jnp.concatenate(key_parts + [k_low], axis=0)
    value_rows = jnp.concatenate(value_parts + [v_low], axis=0)
    key_segs = jnp.concatenate(seg_parts + [seg_here], axis=0)
    key_place = (
        first_row
        - reach_devs * rows_here
        + jnp.arange((reach_devs + 1) * rows_here, dtype=jnp.int32)
    )
    distance = positions[:, None] - key_place[None, :]
    allowed = (
        (distance >= 0)
        & (distance < WINDOW)
        & (key_place[None, :] >= 0)
        & (seg_here[:, None] == key_segs[None, :])
    )
    scores = (outer_cols(q_low, key_rows) * score_scale).reshape(rows_here, head_count, -1)
    masked = jnp.where(allowed[:, None, :], scores, masked_value)
    attn_probs = jax.nn.softmax(masked, axis=-1).reshape(rows_here * head_count, -1)
    probs_low = attn_probs.astype(jnp.bfloat16)
    attended = jnp.dot(probs_low, value_rows, preferred_element_type=jnp.float32)
    att_low = attended.reshape(rows_here, head_count * head_width).astype(jnp.bfloat16)
    o_raw = jnp.dot(att_low, wo_all, preferred_element_type=jnp.float32)
    branch_att, pull_att = jax.vjp(norm_rows, o_raw, g_attn_out)
    middle = tokens + branch_att
    normed_two, pull_mid = jax.vjp(norm_rows, middle, g_ffn_in)
    h_two = normed_two.astype(jnp.bfloat16)
    gate_all, up_all, down_all = (
        lax.all_gather(w_gate, "fsdp", axis=0, tiled=True),
        lax.all_gather(w_up, "fsdp", axis=0, tiled=True),
        lax.all_gather(w_down, "fsdp", axis=0, tiled=True),
    )
    gate_proj = jnp.dot(h_two, gate_all, preferred_element_type=jnp.float32)
    up_proj = jnp.dot(h_two, up_all, preferred_element_type=jnp.float32)
    act_full, pull_act = jax.vjp(geglu_act, gate_proj, up_proj)
    act_low = act_full.astype(jnp.bfloat16)
    f_raw = jnp.dot(act_low, down_all, preferred_element_type=jnp.float32)
    branch_ffn, pull_out = jax.vjp(norm_rows, f_raw, g_ffn_out)
    outputs = (middle + branch_ffn).astype(jnp.bfloat16)
    upstream = cotangent[0].astype(jnp.float32)
    d_fraw, d_gffn_out = pull_out(upstream)
    d_flow = d_fraw.astype(jnp.bfloat16)
    gate_shard, up_shard, down_shard, d_flow = lax.optimization_barrier(
        (w_gate, w_up, w_down, d_flow)
    )
    gate_back, up_back, down_back = (
        lax.all_gather(gate_shard, "fsdp", axis=0, tiled=True),
        lax.all_gather(up_shard, "fsdp", axis=0, tiled=True),
        lax.all_gather(down_shard, "fsdp", axis=0, tiled=True),
    )
    d_act = outer_cols(d_flow, down_back)
    d_gate, d_up = pull_act(d_act)
    dg_low = d_gate.astype(jnp.bfloat16)
    du_low = d_up.astype(jnp.bfloat16)
    d_htwo = outer_cols(dg_low, gate_back) + outer_cols(du_low, up_back)
    grad_down_part = lax.psum_scatter(
        inner_rows(act_low, d_flow).astype(jnp.bfloat16), "fsdp", scatter_dimension=0, tiled=True
    )
    grad_in_part = lax.psum_scatter(
        jnp.concatenate([inner_rows(h_two, dg_low), inner_rows(h_two, du_low)], axis=1).astype(
            jnp.bfloat16
        ),
        "fsdp",
        scatter_dimension=0,
        tiled=True,
    ).astype(jnp.float32)
    hidden_width = w_gate.shape[1]
    grad_gate_part = grad_in_part[:, :hidden_width]
    grad_up_part = grad_in_part[:, hidden_width:]
    d_mid_norm, d_gffn_in = pull_mid(d_htwo)
    d_middle = upstream + d_mid_norm
    d_oraw, d_gattn_out = pull_att(d_middle)
    d_olow = d_oraw.astype(jnp.bfloat16)
    grad_wo = inner_rows(att_low, d_olow)
    d_att_low = (
        outer_cols(d_olow, wo_all).astype(jnp.bfloat16).reshape(rows_here * head_count, head_width)
    )
    d_probs = outer_cols(d_att_low, value_rows)
    d_scores = attn_probs * (d_probs - jnp.sum(attn_probs * d_probs, axis=-1, keepdims=True))
    ds_low = d_scores.astype(jnp.bfloat16)
    d_qfin = jnp.dot(ds_low, key_rows, preferred_element_type=jnp.float32) * score_scale
    d_keys = inner_rows(ds_low, q_low) * score_scale
    d_values = inner_rows(probs_low, d_att_low)
    d_kfin = d_keys[reach_devs * rows_here :]
    d_vsum = d_values[reach_devs * rows_here :]
    for offset in range(1, reach_devs + 1):
        slot_index = reach_devs - offset
        k_back, v_back = (
            from_behind(
                d_keys[slot_index * rows_here : (slot_index + 1) * rows_here].astype(jnp.bfloat16),
                "seq",
                -offset,
            ).astype(jnp.float32),
            from_behind(
                d_values[slot_index * rows_here : (slot_index + 1) * rows_here].astype(
                    jnp.bfloat16
                ),
                "seq",
                -offset,
            ).astype(jnp.float32),
        )
        d_kfin = d_kfin + k_back
        d_vsum = d_vsum + v_back
    d_qraw, d_kraw, d_gquery, d_gkey = pull_prep(
        (d_qfin.reshape(rows_here, head_count, head_width), d_kfin)
    )
    dq_low = d_qraw.astype(jnp.bfloat16)
    dk_low = d_kraw.astype(jnp.bfloat16)
    dv_low = d_vsum.astype(jnp.bfloat16)
    d_hone = outer_cols(dq_low, wq_all) + outer_cols(dk_low, wk_all) + outer_cols(dv_low, wv_all)
    grad_wq = inner_rows(h_one, dq_low)
    grad_wk = inner_rows(h_one, dk_low)
    grad_wv = inner_rows(h_one, dv_low)
    d_tok_norm, d_gattn_in = pull_one(d_hone)
    d_inputs = d_middle + d_tok_norm
    part_wq, part_wk, part_wv, part_wo, part_gai, part_gq, part_gk, part_gao, part_gfi, part_gfo = (
        lax.psum_scatter(
            grad_wq.astype(jnp.bfloat16), "fsdp", scatter_dimension=0, tiled=True
        ).astype(jnp.float32),
        lax.psum_scatter(
            grad_wk.astype(jnp.bfloat16), "fsdp", scatter_dimension=0, tiled=True
        ).astype(jnp.float32),
        lax.psum_scatter(
            grad_wv.astype(jnp.bfloat16), "fsdp", scatter_dimension=0, tiled=True
        ).astype(jnp.float32),
        lax.psum_scatter(
            grad_wo.astype(jnp.bfloat16), "fsdp", scatter_dimension=0, tiled=True
        ).astype(jnp.float32),
        lax.psum_scatter(
            d_gattn_in.astype(jnp.bfloat16), "fsdp", scatter_dimension=0, tiled=True
        ).astype(jnp.float32),
        lax.psum_scatter(
            d_gquery.astype(jnp.bfloat16), "fsdp", scatter_dimension=0, tiled=True
        ).astype(jnp.float32),
        lax.psum_scatter(
            d_gkey.astype(jnp.bfloat16), "fsdp", scatter_dimension=0, tiled=True
        ).astype(jnp.float32),
        lax.psum_scatter(
            d_gattn_out.astype(jnp.bfloat16), "fsdp", scatter_dimension=0, tiled=True
        ).astype(jnp.float32),
        lax.psum_scatter(
            d_gffn_in.astype(jnp.bfloat16), "fsdp", scatter_dimension=0, tiled=True
        ).astype(jnp.float32),
        lax.psum_scatter(
            d_gffn_out.astype(jnp.bfloat16), "fsdp", scatter_dimension=0, tiled=True
        ).astype(jnp.float32),
    )
    cols_wq, cols_wk, cols_wv, cols_wo, cols_gate, cols_up, cols_down = (
        lax.psum_scatter(
            part_wq.astype(jnp.bfloat16), "seq", scatter_dimension=1, tiled=True
        ).astype(jnp.float32),
        lax.psum_scatter(
            part_wk.astype(jnp.bfloat16), "seq", scatter_dimension=1, tiled=True
        ).astype(jnp.float32),
        lax.psum_scatter(
            part_wv.astype(jnp.bfloat16), "seq", scatter_dimension=1, tiled=True
        ).astype(jnp.float32),
        lax.psum_scatter(
            part_wo.astype(jnp.bfloat16), "seq", scatter_dimension=1, tiled=True
        ).astype(jnp.float32),
        lax.psum_scatter(
            grad_gate_part.astype(jnp.bfloat16), "seq", scatter_dimension=1, tiled=True
        ).astype(jnp.float32),
        lax.psum_scatter(
            grad_up_part.astype(jnp.bfloat16), "seq", scatter_dimension=1, tiled=True
        ).astype(jnp.float32),
        lax.psum_scatter(grad_down_part, "seq", scatter_dimension=1, tiled=True).astype(
            jnp.float32
        ),
    )
    sum_wq, sum_wk, sum_wv, sum_wo, sum_gate, sum_up, sum_down = (
        lax.all_gather(cols_wq.astype(jnp.bfloat16), "seq", axis=1, tiled=True).astype(
            cols_wq.dtype
        ),
        lax.all_gather(cols_wk.astype(jnp.bfloat16), "seq", axis=1, tiled=True).astype(
            cols_wk.dtype
        ),
        lax.all_gather(cols_wv.astype(jnp.bfloat16), "seq", axis=1, tiled=True).astype(
            cols_wv.dtype
        ),
        lax.all_gather(cols_wo.astype(jnp.bfloat16), "seq", axis=1, tiled=True).astype(
            cols_wo.dtype
        ),
        lax.all_gather(cols_gate.astype(jnp.bfloat16), "seq", axis=1, tiled=True).astype(
            cols_gate.dtype
        ),
        lax.all_gather(cols_up.astype(jnp.bfloat16), "seq", axis=1, tiled=True).astype(
            cols_up.dtype
        ),
        lax.all_gather(cols_down.astype(jnp.bfloat16), "seq", axis=1, tiled=True).astype(
            cols_down.dtype
        ),
    )
    sum_gai, sum_gq, sum_gk, sum_gao, sum_gfi, sum_gfo = lax.psum(
        (part_gai, part_gq, part_gk, part_gao, part_gfi, part_gfo), "seq"
    )
    return (
        outputs[None],
        d_inputs[None],
        sum_gai,
        sum_wq,
        sum_wk,
        sum_wv,
        sum_gq,
        sum_gk,
        sum_wo,
        sum_gao,
        sum_gfi,
        sum_gate,
        sum_up,
        sum_down,
        sum_gfo,
    )


MESH = pl.DeviceIdType.MESH
BF16 = jnp.bfloat16
F32 = jnp.float32
GELU_RATE = 0.7978845608028654
GELU_CUBE = 0.044715
HID_TILE = 256
ATT_IN, ATT_OUT, FFN_IN, FFN_OUT, QUERY, KEY = range(6)


def bit_of(value, mask):
    return lax.rem(lax.div(value, mask), 2)


def flip(value, masks, bits):
    for b in range(bits):
        if (masks >> b) & 1:
            value = value + (1 << b) * (1 - 2 * bit_of(value, 1 << b))
    return value


def greet(devices):
    barrier = pltpu.get_barrier_semaphore()
    for device in devices:
        pl.semaphore_signal(barrier, inc=1, device_id=device, device_id_type=MESH)
    pl.semaphore_wait(barrier, len(devices))


def remote(src, dst, send, recv, device):
    return pltpu.make_async_remote_copy(
        src_ref=src, dst_ref=dst, send_sem=send, recv_sem=recv,
        device_id=device, device_id_type=MESH,
    )


def many(offset, size):
    return pl.ds(pl.multiple_of(offset, size if size % 128 == 0 else 16), size)


def lanes(offset, size):
    return pl.ds(pl.multiple_of(offset, 128), size)


def window_start(z, share):
    if isinstance(z, int):
        return z * share // 128 * 128
    return lax.div(z * share, 128) * 128


def window_width(share, n_fsdp):
    widest = max((z + 1) * share - window_start(z, share) for z in range(n_fsdp))
    return -(-widest // HID_TILE) * HID_TILE


def dot_nt(left, right):
    return lax.dot_general(left, right, (((1,), (1,)), ((), ())), preferred_element_type=F32)


def dot_nn(left, right):
    return jnp.dot(left, right, preferred_element_type=F32)


def norm_scale(rows_in):
    return lax.rsqrt(jnp.mean(rows_in * rows_in, axis=-1, keepdims=True) + epsilon)


def norm_back(rows_in, gain, scale, upstream):
    pulled = upstream * gain
    inner = jnp.mean(pulled * rows_in, axis=-1, keepdims=True)
    d_rows = scale * pulled - rows_in * (scale * scale * scale * inner)
    return d_rows, jnp.sum(upstream * rows_in * scale, axis=0, keepdims=True)


def turn(rows_in, cosine, sine_part):
    half = rows_in.shape[-1] // 2
    lower, upper = rows_in[:, :half], rows_in[:, half:]
    return jnp.concatenate(
        [lower * cosine - upper * sine_part, upper * cosine + lower * sine_part], axis=-1
    )


class Place:
    def __init__(self):
        self.s = lax.axis_index("seq")
        self.z = lax.axis_index("fsdp")
        self.c = bit_of(self.s, 1)
        self.x = bit_of(self.s, 2)
        self.y = bit_of(self.s, 4)

    def plane(self, masks):
        return (flip(self.s, masks, 3), self.z)

    def line(self, masks):
        return (self.s, flip(self.z, masks, 2))

    def halves(self, first_x):
        if first_x:
            return self.x, self.y, 2, 4
        return self.y, self.x, 4, 2


def layer_kernel(
    n_seq, n_fsdp, share, reach, head_count,
    x_ref, cot_ref, rates_ref, seg_ref,
    gain_a, gain_b, gain_c, gain_d, gain_e, gain_f,
    gate_ref, up_ref, wq_ref, wk_ref, wv_ref, wo_ref, wd_ref,
    small_out, fin_gu, fin_d,
    qkv_s, wo_s, w_in, w_down, pack_all, seg_all, gains, allowed, turns,
    h1_s, raw_s, q_s, kv_own, kv_s, p_s, att_s, o_s, mid_s,
    h_all, df_all, bent_s, act, d_in, h_turn, part_out, part_in, relay_in, total,
    own_d, own_g, own_o, own_q, hi_d, hi_g, hi_o, hi_q, lo_d, lo_g, lo_o, lo_q, line_o, line_q,
    do_s, datt_s, ds_s, dkv_s, dkv_send, dkv_came, dqkv_s, dgains, gain_in, gain_line,
    w_send, w_recv, own_sem, pack_send, pack_recv, seg_send, seg_recv, kv_send, kv_recv,
    ex_send, ex_recv, relay_sem, dkv_ssem, dkv_rsem,
    c_send, c_recv, hi_send, hi_recv, lo_send, lo_recv, z_send, z_recv, oq_send, oq_recv,
    put_sem, ag_send, ag_recv, gain_send, gain_recv,
):
    at = Place()
    s, z, c = at.s, at.z, at.c
    rows, width = x_ref.shape
    depth = width // n_fsdp
    hidden = w_in.shape[2]
    head_width = wk_ref.shape[1]
    query_width = head_count * head_width
    heads_width = query_width + 2 * head_width
    rows_o = wo_ref.shape[0]
    n_hid = hidden // HID_TILE
    third = width // 3
    middle_z = (z > 0) & (z < n_fsdp - 1)
    tokens = n_fsdp * rows

    def hid(n):
        return lanes(n * HID_TILE, HID_TILE)

    def outs(n):
        return lanes(n * third, third)

    skipped = z * share - window_start(z, share)
    spare = hidden - share
    if spare:
        w_down[pl.ds(0, spare)] = jnp.zeros((spare, width), BF16)
        w_down[pl.ds(share, spare)] = jnp.zeros((spare, width), BF16)
    here_z = many(z * depth, depth)
    own_copies = [
        pltpu.make_async_copy(src, dst, own_sem.at[i])
        for i, (src, dst) in enumerate((
            (wq_ref, qkv_s.at[here_z, pl.ds(0, query_width)]),
            (wk_ref, qkv_s.at[here_z, pl.ds(query_width, head_width)]),
            (wv_ref, qkv_s.at[here_z, pl.ds(query_width + head_width, head_width)]),
            (wo_ref, wo_s.at[many(z * rows_o, rows_o)]),
            (wd_ref, w_down.at[many(skipped, share)]),
            (gate_ref.at[:, lanes(window_start(z, share), hidden)], w_in.at[0, here_z]),
            (up_ref.at[:, lanes(window_start(z, share), hidden)], w_in.at[1, here_z]),
        ))
    ]
    seg_all[s] = jnp.broadcast_to(seg_ref[...], seg_all.shape[1:])
    start = 0
    for ref in (gain_a, gain_b, gain_c, gain_d, gain_e, gain_f):
        size = ref.shape[0]
        pack_all[z, 0:1, start : start + size] = ref[...].astype(F32).reshape(1, size)
        start += size
    greet([at.plane(k) for k in range(1, n_seq)] + [at.line(m) for m in range(1, n_fsdp)])

    packs = [
        remote(pack_all.at[z], pack_all.at[z], pack_send.at[m], pack_recv.at[m], at.line(m))
        for m in range(1, n_fsdp)
    ]
    seg_copies = [
        remote(seg_all.at[s], seg_all.at[s], seg_send.at[k], seg_recv.at[k], at.plane(k))
        for k in range(1, n_seq)
    ]
    kv_copies = [
        remote(kv_own, kv_s.at[reach - o], kv_send.at[o - 1], kv_recv.at[o - 1],
               (lax.rem(s + o, n_seq), z))
        for o in range(1, reach + 1)
    ]

    def w_region(kind, sub, whose, hi, lo, level):
        base = whose * depth
        if kind == "q":
            cols = (
                lanes(hi * (query_width // 2) + lo * (query_width // 4), query_width // 4),
                lanes(hi * (query_width // 2), query_width // 2),
                pl.ds(0, query_width),
            )[level]
            return qkv_s.at[many(base + c * (depth // 2), depth // 2), cols]
        if kind == "kv":
            start = query_width + c * head_width
            if level == 0:
                start = start + lo * (head_width // 2)
            cols = lanes(start, head_width if level else head_width // 2)
            if level == 2:
                return qkv_s.at[many(base, depth), cols]
            return qkv_s.at[many(base + hi * (depth // 2), depth // 2), cols]
        if kind == "wo":
            start = whose * rows_o + c * (rows_o // 2)
            if level < 2:
                start = start + hi * (rows_o // 4)
            if level < 1:
                start = start + lo * (rows_o // 8)
            return wo_s.at[many(start, rows_o // (8, 4, 2)[level])]
        skip, size = sub
        if level == 2:
            return [
                w_in.at[c, many(base + half * (depth // 2) + skip, size)] for half in range(2)
            ]
        here = many(base + hi * (depth // 2) + skip, size)
        if level == 1:
            return w_in.at[c, here]
        return w_in.at[c, here, lanes(lo * (hidden // 2), hidden // 2)]

    def w_sources(kind, sub, to, hi, lo):
        if kind == "q":
            cols = lanes(hi * (query_width // 2) + lo * (query_width // 4), query_width // 4)
            return [wq_ref.at[many(c * (depth // 2), depth // 2), cols]]
        if kind == "wo":
            start = c * (rows_o // 2) + hi * (rows_o // 4) + lo * (rows_o // 8)
            return [wo_ref.at[many(start, rows_o // 8)]]
        if kind == "kv":
            here = many(hi * (depth // 2), depth // 2)
            cols = lanes(lo * (head_width // 2), head_width // 2)
            return [ref.at[here, cols] for ref in (wk_ref, wv_ref)]
        skip, size = sub
        here = many(hi * (depth // 2) + skip, size)
        cols = lanes(window_start(to, share) + lo * (hidden // 2), hidden // 2)
        return [ref.at[here, cols] for ref in (gate_ref, up_ref)]

    items = []
    for kinds in (("q", "kv"), ("wo",)):
        for m in range(1, n_fsdp):
            for kind in kinds:
                items.append((kind, m, (m % 2 == 1) == (kind in ("kv", "wo")), None))
    n_att = len(items)
    for m in range(1, n_fsdp):
        items.append(("gu", m, m % 2 == 1, (0, depth // 2)))
    steps, starts = [], []
    for i, (kind, m, first_x, sub) in enumerate(items):
        hi, lo, mask_hi, mask_lo = at.halves(first_x)
        there = flip(z, m, 2)
        firsts = [
            remote(src, w_region(kind, sub, z, hi, lo, 0), w_send.at[i, 0], w_recv.at[i, 0],
                   at.line(m))
            for src in w_sources(kind, sub, there, hi, lo)
        ]
        starts.append(firsts)
        stages = [firsts[:1]]
        for k, mask in enumerate((mask_lo, mask_hi, 1)):
            parts = w_region(kind, sub, there, hi, lo, k)
            stages.append([
                remote(part, part, w_send.at[i, k + 1 + n], w_recv.at[i, k + 1 + n], at.plane(mask))
                for n, part in enumerate(parts if isinstance(parts, list) else [parts])
            ])
        steps.append(stages)

    def begin_weight(i):
        if len(starts[i]) == 1:
            starts[i][0].start()
        else:
            for core, first in enumerate(starts[i]):
                pl.when(c == core)(first.start)

    def weight_here(i, stage):
        for copy in steps[i][stage]:
            copy.wait_recv()

    def move_weight(i, stage):
        weight_here(i, stage - 1)
        for copy in steps[i][stage]:
            copy.start()

    def weight_sent(i):
        for copies in steps[i]:
            for copy in copies:
                copy.wait_send()

    n_items = len(items)
    n_qkv = 2 * (n_fsdp - 1)
    ahead, lag = 6, 3
    for copy in packs + seg_copies:
        copy.start()
    for i in range(ahead):
        begin_weight(i)
    for copy in own_copies:
        copy.start()

    def weight_steps(t):
        for stage in (3, 2, 1):
            i = t - lag * (stage - 1)
            if 0 <= i < n_att:
                move_weight(i, stage)
                if stage == 1 and i + ahead < n_items:
                    begin_weight(i + ahead)

    weight_steps(0)
    weight_steps(1)
    for copy in seg_copies:
        copy.wait_recv()
    across = lax.broadcasted_iota(jnp.int32, (rows, rows), 0)
    along = lax.broadcasted_iota(jnp.int32, (rows, rows), 1)
    seg_here = jnp.broadcast_to(seg_ref[...].astype(F32), (rows, rows)).T
    for o in range(reach, -1, -1):
        key_seg = seg_all[lax.rem(s + n_seq - o, n_seq), 0:1, :].astype(F32)
        apart = across - along + o * rows
        fine = (apart >= 0) & (apart < WINDOW) & (seg_here == key_seg) & (s >= o)
        allowed[:, pl.ds((reach - o) * rows, rows)] = jnp.where(fine, 1.0, 0.0).astype(BF16)
    angle = ((s * rows + across).astype(F32) - seg_here) * rates_ref[...]
    turns[0] = jnp.cos(angle)
    turns[1] = jnp.sin(angle)
    for copy in packs:
        copy.wait_recv()
    gains[...] = jnp.zeros(gains.shape, F32)
    start = 0
    for row in range(6):
        size = (depth if row < QUERY else head_width // n_fsdp)
        for block in range(n_fsdp):
            gains[row : row + 1, block * size : (block + 1) * size] = pack_all[
                block, 0:1, start : start + size
            ]
        start += size

    def gain(row):
        return gains[row : row + 1, : (width if row < QUERY else head_width)]

    x = x_ref[...].astype(F32)
    h1_s[...] = (x * norm_scale(x) * gain(ATT_IN)).astype(BF16)

    for t in range(2, n_att + 2 * lag):
        weight_steps(t)
    for i in range(n_qkv):
        weight_here(i, 3)
    for copy in own_copies[:3]:
        copy.wait()

    def move_gu(*moves):
        for k, stage in moves:
            move_weight(n_att + k - 1, stage)

    move_gu((1, 1))
    raw_s[...] = dot_nn(h1_s[...], qkv_s[...])

    k_raw = raw_s[:, query_width : query_width + head_width]
    kv_own[:, :head_width] = turn(
        k_raw * norm_scale(k_raw) * gain(KEY), turns[0], turns[1]
    ).astype(BF16)
    kv_own[:, head_width:] = raw_s[:, query_width + head_width :].astype(BF16)
    for copy in kv_copies:
        copy.start()
    kv_s[reach] = kv_own[...]
    for h in range(head_count):
        q_raw = raw_s[:, h * head_width : (h + 1) * head_width]
        q_fin = q_raw * norm_scale(q_raw) * gain(QUERY)
        q_s[h] = turn(q_fin, turns[0], turns[1]).astype(BF16)
    for i in range(n_qkv, n_att):
        weight_here(i, 3)
    own_copies[3].wait()
    move_gu((1, 2))
    move_gu((2, 1))
    for copy in kv_copies:
        copy.wait_recv()

    def keys():
        return kv_s[:, :, :head_width].reshape((reach + 1) * rows, head_width)

    def values():
        return kv_s[:, :, head_width:].reshape((reach + 1) * rows, head_width)

    for h in range(head_count):
        scores = dot_nt(q_s[h], keys()) * (head_width**-0.5)
        masked = jnp.where(allowed[...].astype(F32) > 0.5, scores, masked_value)
        grown = jnp.exp(masked - jnp.max(masked, axis=-1, keepdims=True))
        probs = grown / jnp.sum(grown, axis=-1, keepdims=True)
        p_s[h] = probs.astype(BF16)
        att_s[:, h * head_width : (h + 1) * head_width] = dot_nn(p_s[h], values()).astype(BF16)

    move_gu((3, 1))
    o_raw = dot_nn(att_s[...], wo_s[...])
    o_s[...] = o_raw
    middle = x_ref[...].astype(F32) + o_raw * norm_scale(o_raw) * gain(ATT_OUT)
    mid_s[...] = middle
    h_all[0] = (middle * norm_scale(middle) * gain(FFN_IN)).astype(BF16)

    def exchange(phase, src, dst):
        return {
            m: remote(src(m), dst(m), ex_send.at[phase, m], ex_recv.at[phase, m], at.line(m))
            for m in range(1, n_fsdp)
        }

    last = n_fsdp - 1
    send_h = exchange(0, lambda m: h_all.at[0], lambda m: h_all.at[m])
    send_f = exchange(1, lambda m: part_out.at[m - 1], lambda m: part_in.at[0, m - 1])
    send_df = exchange(2, lambda m: df_all.at[0], lambda m: df_all.at[m])
    send_dh = exchange(3, lambda m: part_out.at[m - 1], lambda m: part_in.at[1, m - 1])
    onward = {
        phase: remote(rows_all.at[2], rows_all.at[last],
                      relay_sem.at[phase], ex_recv.at[phase, last], at.line(1))
        for phase, rows_all in ((0, h_all), (2, df_all))
    }
    by_way = {
        phase: remote(part_out.at[last - 1], relay_in.at[phase // 2],
                      relay_sem.at[phase], relay_sem.at[phase + 3], at.line(1))
        for phase in (1, 3)
    }

    def send_rows(copies):
        copies[2].start()
        pl.when(middle_z)(copies[last].start)
        copies[1].start()

    def relay_rows(copies, phase):
        @pl.when(middle_z)
        def _():
            copies[2].wait_recv()
            onward[phase].start()

    def take_rows(copies, m):
        if m == 2:
            pl.when(~middle_z)(copies[2].wait_recv)
        elif m:
            copies[m].wait_recv()

    def send_part(copies, phase, m):
        if m == 1:
            copies[1].start()
        elif m == 2:
            pl.when(~middle_z)(copies[2].start)
        else:
            pl.when(~middle_z)(by_way[phase].start)
            pl.when(middle_z)(copies[last].start)

    def send_joint_part(copies, phase):
        @pl.when(middle_z)
        def _():
            by_way[phase].wait_recv()
            part_out[1] = (
                part_out[1].astype(F32) + relay_in[phase // 2].astype(F32)
            ).astype(BF16)
            copies[2].start()

    def take_parts(copies):
        copies[1].wait_recv()
        copies[2].wait_recv()
        pl.when(middle_z)(copies[last].wait_recv)

    def rows_sent(copies, phase):
        copies[1].wait_send()
        copies[2].wait_send()

        @pl.when(middle_z)
        def _():
            copies[last].wait_send()
            onward[phase].wait_send()

    def parts_sent(copies, phase):
        copies[1].wait_send()
        copies[2].wait_send()
        pl.when(middle_z)(copies[last].wait_send)
        pl.when(~middle_z)(by_way[phase].wait_send)

    send_rows(send_h)

    @pl.when(~middle_z)
    def _():
        part_in[0, last - 1] = jnp.zeros((rows, width), BF16)
        part_in[1, last - 1] = jnp.zeros((rows, width), BF16)

    move_gu((2, 2))
    move_gu((1, 3))
    move_gu((3, 2))
    relay_rows(send_h, 0)
    move_gu((2, 3))
    move_gu((3, 3))
    for i in range(n_att, n_items):
        weight_here(i, 3)
    for copy in own_copies[4:]:
        copy.wait()
    half_h = hidden // 2

    for m in range(n_fsdp - 1, -1, -1):
        take_rows(send_h, m)
        for n in range(2):
            cols = slice(n * half_h, (n + 1) * half_h)
            gate = dot_nn(h_all[m], w_in[0, :, cols])
            up = dot_nn(h_all[m], w_in[1, :, cols])
            squared = gate * gate
            bent = jnp.tanh(GELU_RATE * (gate + GELU_CUBE * squared * gate))
            gelu = 0.5 * gate * (1.0 + bent)
            slope = 0.5 * (1.0 + bent) + 0.5 * gate * (1.0 - bent * bent) * (
                GELU_RATE * (1.0 + 3.0 * GELU_CUBE * squared)
            )
            bent_s[pl.ds(m * rows, rows), cols] = gelu.astype(BF16)
            bent_s[pl.ds(tokens + m * rows, rows), cols] = (slope * up).astype(BF16)
            act[m, :, cols] = (gelu * up).astype(BF16)
        part = dot_nn(act[m], w_down[...])
        if m:
            part_out[m - 1] = part.astype(BF16)
            send_part(send_f, 1, m)
        else:
            total[...] = part

    send_joint_part(send_f, 1)
    for m in range(n_fsdp):
        h_turn[:, pl.ds(m * rows, rows)] = h_all[m].T
    for i in range(n_att, n_items):
        weight_sent(i)

    take_parts(send_f)
    f_raw = total[...]
    for m in range(1, n_fsdp):
        f_raw = f_raw + part_in[0, m - 1].astype(F32)
    cot = cot_ref[...].astype(F32)
    scale = norm_scale(f_raw)
    d_f, d_gain = norm_back(f_raw, gain(FFN_OUT), scale, cot)
    df_all[0] = d_f.astype(BF16)
    send_rows(send_df)
    small_out[pl.ds(rows, rows), :] = mid_s[...] + f_raw * scale * gain(FFN_OUT)
    dgains[...] = jnp.zeros(dgains.shape, F32)
    dgains[FFN_OUT : FFN_OUT + 1, :] = d_gain
    parts_sent(send_f, 1)

    chunks = [("d", 0, False), ("d", 1, True)]
    chunks += [("g", m, m % 2 == 0) for m in range(n_fsdp)]
    chunks += [("o", 0, False), ("q", 0, True)]
    tiles_d = hidden // 256
    spans_d = (pl.ds(0, n_fsdp), pl.ds(n_fsdp, tiles_d - n_fsdp))

    def mine_of(kind, i):
        if kind == "d":
            return own_d.at[spans_d[i]]
        return {"g": own_g, "o": own_o, "q": own_q}[kind].at[i]

    def hi_part(kind, hi):
        if kind == "d":
            return slice(None), many(hi * 64, 64), slice(None)
        if kind == "g":
            return many(hi * (depth // 2), depth // 2), slice(None)
        if kind == "q":
            return slice(None), lanes(hi * (heads_width // 2), heads_width // 2)
        return many(hi * (rows_o // 4), rows_o // 4), slice(None)

    def lo_part(kind, hi, lo):
        if kind == "d":
            return slice(None), many(hi * 64 + lo * 32, 32), slice(None)
        if kind == "g":
            return (
                many(hi * (depth // 2), depth // 2),
                lanes(lo * (hidden // 2), hidden // 2),
            )
        if kind == "q":
            start = hi * (heads_width // 2) + lo * (heads_width // 4)
            return slice(None), lanes(start, heads_width // 4)
        return many(hi * (rows_o // 4) + lo * (rows_o // 8), rows_o // 8), slice(None)

    def fin_part(kind, i, where, core):
        if kind == "d":
            span = spans_d[i]
            tiles = pl.ds(core * tiles_d + span.start, span.size)
            return fin_d.at[tiles, where[-2], :]
        rows_at, cols_at = where
        if kind == "g":
            return fin_gu.at[core * n_fsdp + i, rows_at, cols_at]
        if kind == "o":
            return fin_d.at[2 * tiles_d + core, rows_at, :]
        base = core * (depth // 2)
        if isinstance(cols_at, slice):
            cols_at = pl.ds(0, heads_width)
        return fin_gu.at[2 * n_fsdp, many(base, depth // 2), cols_at]
    def add(ref, where, other):
        rows_at, cols_at = where
        start = 0 if isinstance(rows_at, slice) else rows_at.start
        slab = 16

        @pl.loop(0, other.shape[0] // slab)
        def _(n):
            here = pl.ds(pl.multiple_of(start + n * slab, slab), slab)
            there = pl.ds(pl.multiple_of(n * slab, slab), slab)
            ref[here, cols_at] = (
                ref[here, cols_at].astype(F32) + other[there, :].astype(F32)
            ).astype(BF16)

    whole = (slice(None), slice(None))
    from_hi = {"d": hi_d, "g": hi_g, "o": hi_o, "q": hi_q}
    from_lo = {"d": lo_d, "g": lo_g, "o": lo_o, "q": lo_q}
    his, los, lines = [], [], []
    for j, (kind, i, first_x) in enumerate(chunks):
        hi, lo, mask_hi, mask_lo = at.halves(first_x)
        mine = mine_of(kind, i)
        if kind == "q":
            parts = (
                own_q.at[:, :, hi_part(kind, 1 - hi)[1]], hi_q,
                own_q.at[:, :, lo_part(kind, hi, 1 - lo)[1]], lo_q,
            )
        else:
            slot = spans_d[i] if kind == "d" else i
            parts = (
                mine.at[hi_part(kind, 1 - hi)], from_hi[kind].at[slot],
                mine.at[lo_part(kind, hi, 1 - lo)], from_lo[kind].at[slot],
            )
        his.append(
            remote(parts[0], parts[1], hi_send.at[j], hi_recv.at[j], at.plane(mask_hi))
        )
        los.append(
            remote(parts[2], parts[3], lo_send.at[j], lo_recv.at[j], at.plane(mask_lo))
        )
        line = None
        if kind == "g" and i:
            line = remote(mine.at[lo_part(kind, hi, lo)],
                          fin_part(kind, z, lo_part(kind, hi, lo), c),
                          z_send.at[j], z_recv.at[j], at.line(i))
        lines.append(line)
    stage = {
        "d": lambda i: part_in.at[0] if i else h_all,
        "g": lambda i: bent_s.at[pl.ds(i * depth, depth)],
        "q": lambda i: w_in.at[0, pl.ds(i * (depth // 2), depth // 2), pl.ds(0, heads_width)],
        "o": lambda i: w_in.at[1, pl.ds(i * (rows_o // 2), rows_o // 2), pl.ds(0, width)],
    }
    to_core = [("d", 0), ("d", 1)]
    to_core += [(kind, m) for kind in "goq" for m in range(n_fsdp)]
    cores = {
        key: remote(stage[key[0]](key[1]), mine_of(*key), c_send.at[k], c_recv.at[k], at.plane(1))
        for k, key in enumerate(to_core)
    }
    line_sums = {}
    for k, (kind, ref) in enumerate((("o", line_o), ("q", line_q))):
        for m in range(1, n_fsdp):
            part = mine_of(kind, m)
            if kind == "q":
                part = part.at[lo_part(kind, at.x, at.y)]
            line_sums[kind, m] = remote(
                part, ref.at[m - 1], oq_send.at[k, m], oq_recv.at[k, m], at.line(m)
            )

    puts, hands = [], []
    for j, (kind, i, first_x) in enumerate(chunks):
        hi, lo, mask_hi, mask_lo = at.halves(first_x)
        which = flip(z, i, 2) if kind == "g" else i
        piece = fin_part(kind, which, lo_part(kind, hi, lo), c)
        half = fin_part(kind, which, hi_part(kind, hi), c)
        full = fin_part(kind, which, whole, c)
        put = None
        if lines[j] is None:
            put = pltpu.make_async_copy(
                mine_of(kind, i).at[lo_part(kind, hi, lo)], piece, put_sem.at[j]
            )
        puts.append(put)
        hands.append([
            remote(part, part, ag_send.at[j, k], ag_recv.at[j, k], at.plane(mask))
            for k, (part, mask) in enumerate(((piece, mask_lo), (half, mask_hi), (full, 1)))
        ])

    def add_all(kind, i, where, came):
        if kind == "d":
            for n in range(spans_d[i].start, spans_d[i].start + spans_d[i].size):
                add(own_d.at[n], where[1:], came.at[n])
        elif kind == "q":
            for m in range(n_fsdp):
                add(own_q.at[m], where, came.at[m])
        else:
            add(mine_of(kind, i), where, came.at[i])

    def take_hi(j):
        kind, i, first_x = chunks[j]
        hi, lo, _, _ = at.halves(first_x)
        his[j].wait_recv()
        add_all(kind, i, hi_part(kind, hi), from_hi[kind])
        los[j].start()

    def take_lo(j):
        kind, i, first_x = chunks[j]
        hi, lo, _, _ = at.halves(first_x)
        los[j].wait_recv()
        add_all(kind, i, lo_part(kind, hi, lo), from_lo[kind])
        if lines[j] is not None:
            lines[j].start()
        elif kind == "q":
            for m in range(1, n_fsdp):
                line_sums[kind, m].start()
        else:
            puts[j].start()

    def begin_hand(j):
        if lines[j] is not None:
            lines[j].wait_recv()
        else:
            puts[j].wait()
        hands[j][0].start()

    def hand_on(j, k):
        hands[j][k - 1].wait_recv()
        hands[j][k].start()

    def down_stage(n):
        return h_all.at[n] if n < n_fsdp else part_in.at[0, n - n_fsdp]

    def down_grads(core, dst_of, adds):
        right = df_all[...].reshape(tokens, width)
        for n in range(tiles_d):
            left = act[:, :, lanes(core * (hidden // 2) + n * 128, 128)].reshape(tokens, 128).T
            grads = dot_nn(left, right)
            dst = dst_of[n] if adds else dst_of(n)
            if adds:
                grads = grads + dst[...].astype(F32)
            dst[...] = grads.astype(BF16)

    def in_grads(core, m, dst, adds):
        left_at = many(flip(z, m, 2) * depth, depth)

        for n in range(2):
            cols = slice(n * half_h, (n + 1) * half_h)
            grads = dot_nn(h_turn[left_at, :], d_in[core, :, :, cols].reshape(tokens, half_h))
            if adds:
                grads = grads + dst[:, cols].astype(F32)
            dst[:, cols] = grads.astype(BF16)

    rows_sent(send_h, 0)
    for m in range(n_fsdp):
        if m == 1:
            relay_rows(send_df, 2)
        take_rows(send_df, m)
        if m == last:
            down_grads(1 - c, down_stage, False)
            cores["d", 0].start()
            cores["d", 1].start()
        for n in range(2):
            cols = slice(n * half_h, (n + 1) * half_h)
            d_act = dot_nt(df_all[m], w_down[cols, :])
            slope = bent_s[pl.ds(tokens + m * rows, rows), cols].astype(F32)
            d_in[0, m, :, cols] = (d_act * slope).astype(BF16)
            gelu = bent_s[pl.ds(m * rows, rows), cols].astype(F32)
            d_in[1, m, :, cols] = (d_act * gelu).astype(BF16)
        part = dot_nt(d_in[0, m], w_in[0]) + dot_nt(d_in[1, m], w_in[1])
        if m:
            part_out[m - 1] = part.astype(BF16)
            send_part(send_dh, 3, m)
        else:
            total[...] = part

    cores["d", 0].wait_recv()
    cores["d", 1].wait_recv()
    down_grads(c, own_d.at, True)
    his[0].start()
    his[1].start()
    send_joint_part(send_dh, 3)
    for m in range(n_fsdp):
        in_grads(1 - c, m, stage["g"](m), False)
        cores["g", m].start()
    for m in range(n_fsdp):
        cores["g", m].wait_recv()
        in_grads(c, m, own_g.at[m], True)
        his[2 + m].start()

    dkv_copies = [
        remote(dkv_send.at[reach - o], dkv_came.at[o - 1], dkv_ssem.at[o - 1], dkv_rsem.at[o - 1],
               (lax.rem(s + n_seq - o, n_seq), z))
        for o in range(1, reach + 1)
    ]
    gain_copies = [
        remote(dgains, gain_in.at[k], gain_send.at[k], gain_recv.at[k], at.plane(k))
        for k in range(1, n_seq)
    ]
    gain_lines = [
        remote(gain_line.at[0], gain_line.at[m], gain_send.at[n_seq + m], gain_recv.at[n_seq + m],
               at.line(m))
        for m in range(1, n_fsdp)
    ]

    def to_middle():
        take_parts(send_dh)
        dh = total[...]
        for m in range(1, n_fsdp):
            dh = dh + part_in[1, m - 1].astype(F32)
        mid = mid_s[...]
        d_mid, d_gain = norm_back(mid, gain(FFN_IN), norm_scale(mid), dh)
        d_mid = d_mid + cot_ref[...].astype(F32)
        mid_s[...] = d_mid
        dgains[FFN_IN : FFN_IN + 1, :] = d_gain
        o_raw = o_s[...]
        d_o, d_gain = norm_back(o_raw, gain(ATT_OUT), norm_scale(o_raw), d_mid)
        dgains[ATT_OUT : ATT_OUT + 1, :] = d_gain
        do_s[...] = d_o.astype(BF16)
        for h in range(head_count):
            here = pl.ds(h * head_width, head_width)
            datt_s[h] = dot_nt(do_s[...], wo_s[here, :]).astype(BF16)

    def unturn(rows_in):
        return turn(rows_in, turns[0], -turns[1])

    def through_head(h):
        probs = p_s[h].astype(F32)
        d_att = datt_s[h]
        d_probs = dot_nt(d_att, values())
        d_scores = probs * (d_probs - jnp.sum(probs * d_probs, axis=-1, keepdims=True))
        ds_low = d_scores.astype(BF16)
        scale = head_width**-0.5
        ds_s[h] = ds_low
        cols = slice(h * head_width, (h + 1) * head_width)
        q_raw = raw_s[:, cols]
        d_q, d_gain = norm_back(
            q_raw, gain(QUERY), norm_scale(q_raw), unturn(dot_nn(ds_low, keys()) * scale)
        )
        dqkv_s[:, cols] = d_q.astype(BF16)
        dgains[QUERY : QUERY + 1, :head_width] += d_gain

    def return_keys():
        for side, left, right, scale in (
            (0, ds_s, q_s, head_width**-0.5),
            (1, p_s, datt_s, 1.0),
        ):
            cols = slice(side * head_width, (side + 1) * head_width)
            d_side = scale * inner_rows(
                left[...].reshape(head_count * rows, (reach + 1) * rows),
                right[...].reshape(head_count * rows, head_width),
            )
            for b in range(reach):
                dkv_send[b, :, cols] = d_side[b * rows : (b + 1) * rows].astype(BF16)
            dkv_s[:, cols] = d_side[reach * rows :]
        for copy in dkv_copies:
            copy.start()

    def grad_tiles(left_at, turned, right, n_cols, dst, adds):
        tile = n_cols // 3
        for k in range(3):
            grads = dot_nn(turned[left_at, :], right[:, k * tile : (k + 1) * tile])
            if adds:
                grads = grads + dst[:, k * tile : (k + 1) * tile].astype(F32)
            dst[:, k * tile : (k + 1) * tile] = grads.astype(BF16)

    def core_grads(kind, turned, right, span, n_cols):
        for m in range(n_fsdp):
            start = flip(z, m, 2) * span + (1 - c) * (span // 2)
            grad_tiles(many(start, span // 2), turned, right, n_cols, stage[kind](m), False)
            cores[kind, m].start()
        for m in list(range(1, n_fsdp)) + [0]:
            start = flip(z, m, 2) * span + c * (span // 2)
            cores[kind, m].wait_recv()
            grad_tiles(many(start, span // 2), turned, right, n_cols, mine_of(kind, m), True)
            if m and kind == "o":
                line_sums[kind, m].start()
        if kind == "q":
            his[-1].start()

    def output_grads():
        h_turn[pl.ds(0, query_width), pl.ds(0, rows)] = att_s[...].T
        core_grads("o", h_turn.at[:, pl.ds(0, rows)], do_s, rows_o, width)

    def key_grads():
        h_turn[:, pl.ds(rows, rows)] = h1_s[...].T
        d_kv = dkv_s[...]
        for o in range(reach):
            dkv_copies[o].wait_recv()
            d_kv = d_kv + dkv_came[o].astype(F32)
        k_raw = raw_s[:, query_width : query_width + head_width]
        d_k, d_gain = norm_back(
            k_raw, gain(KEY), norm_scale(k_raw), unturn(d_kv[:, :head_width])
        )
        dqkv_s[:, query_width : query_width + head_width] = d_k.astype(BF16)
        dqkv_s[:, query_width + head_width :] = d_kv[:, head_width:].astype(BF16)
        dgains[KEY : KEY + 1, :head_width] = d_gain
        core_grads("q", h_turn.at[:, pl.ds(rows, rows)], dqkv_s, depth, heads_width)

    def sum_line(j):
        kind = chunks[j][0]
        where = lo_part(kind, at.x, at.y) if kind == "q" else whole
        for m in range(1, n_fsdp):
            line_sums[kind, m].wait_recv()
            add(mine_of(kind, 0), where, {"o": line_o, "q": line_q}[kind].at[m - 1])
        (puts if kind == "q" else his)[j].start()

    def to_input():
        x = x_ref[...].astype(F32)
        d_h = dot_nt(dqkv_s[...], qkv_s[...])
        d_x, d_gain = norm_back(x, gain(ATT_IN), norm_scale(x), d_h)
        small_out[pl.ds(0, rows), :] = mid_s[...] + d_x
        dgains[ATT_IN : ATT_IN + 1, :] = d_gain
        for copy in gain_copies:
            copy.start()

    def sum_gains():
        sums = dgains[...]
        for k, copy in enumerate(gain_copies):
            copy.wait_recv()
            sums = sums + gain_in[k + 1]
        gain_line[0] = sums
        for copy in gain_lines:
            copy.start()

    take_hi(0)
    take_hi(1)
    to_middle()
    through_head(0)
    through_head(1)
    through_head(2)
    through_head(3)
    return_keys()
    output_grads()
    take_hi(2)
    take_hi(3)
    take_lo(0)
    take_lo(1)
    begin_hand(0)
    begin_hand(1)
    key_grads()
    take_hi(4)
    take_hi(5)
    take_lo(2)
    take_lo(3)
    begin_hand(2)
    sum_line(6)
    hand_on(0, 1)
    hand_on(1, 1)
    take_lo(4)
    take_lo(5)
    to_input()
    begin_hand(3)
    hand_on(0, 2)
    hand_on(1, 2)
    take_hi(7)
    hand_on(2, 1)
    begin_hand(4)
    begin_hand(5)
    take_hi(6)
    hand_on(3, 1)
    take_lo(7)
    hand_on(2, 2)
    sum_gains()
    take_lo(6)
    begin_hand(6)
    hand_on(4, 1)
    hand_on(5, 1)
    sum_line(7)
    begin_hand(7)
    hand_on(3, 2)
    hand_on(6, 1)
    hand_on(7, 1)
    hand_on(4, 2)
    hand_on(5, 2)
    hand_on(6, 2)
    hand_on(7, 2)
    sums = gain_line[0]
    for m, copy in enumerate(gain_lines):
        copy.wait_recv()
        sums = sums + gain_line[m + 1]
    for row in range(6):
        size = depth if row < QUERY else head_width // n_fsdp
        for block in range(n_fsdp):

            @pl.when(z == block)
            def _():
                small_out[2 * rows + row : 2 * rows + row + 1, :size] = sums[
                    row : row + 1, block * size : (block + 1) * size
                ]


    for j in range(len(chunks)):
        hands[j][2].wait_recv()
        for k in range(3):
            hands[j][k].wait_send()
        his[j].wait_send()
        los[j].wait_send()
        if lines[j] is not None:
            lines[j].wait_send()
    for copy in list(cores.values()) + list(line_sums.values()):
        copy.wait_send()
    for copy in gain_copies + gain_lines + dkv_copies + kv_copies + packs + seg_copies:
        copy.wait_send()
    for i in range(n_att):
        weight_sent(i)
    rows_sent(send_df, 2)
    parts_sent(send_dh, 3)


def layer(n_seq, n_fsdp, share, hidden, reach, head_count, x, cot, rates, segs, gains,
          w_gate, w_up, w_query, w_key, w_value, w_output, w_down):
    rows, width = x.shape
    depth = width // n_fsdp
    head_width = w_key.shape[1]
    query_width = w_query.shape[1]
    heads_width = query_width + 2 * head_width
    rows_o = w_output.shape[0]
    n_items = 4 * (n_fsdp - 1)
    anywhere = pl.BlockSpec(memory_space=pl.ANY)
    in_vmem = pl.BlockSpec(memory_space=pltpu.VMEM)
    shape = jax.ShapeDtypeStruct
    sems = pltpu.SemaphoreType.DMA

    def low(*size):
        return pltpu.VMEM(size, BF16)

    def full(*size):
        return pltpu.VMEM(size, F32)

    return pl.pallas_call(
        functools.partial(layer_kernel, n_seq, n_fsdp, share, reach, head_count),
        out_shape=[
            shape((2 * rows + 8, width), F32),
            shape((2 * n_fsdp + 1, depth, hidden), BF16),
            shape((hidden // 128 + 2, 128, width), BF16),
        ],
        in_specs=[in_vmem] * 10 + [anywhere] * 7,
        out_specs=[in_vmem] + [anywhere] * 2,
        scratch_shapes=[
            low(width, heads_width),
            low(n_fsdp * rows_o, width),
            low(2, width, hidden),
            low(hidden, width),
            full(n_fsdp, 8, -(-sum(g.shape[0] for g in gains) // 128) * 128),
            pltpu.VMEM((n_seq, 8, rows), jnp.int32),
            full(8, width),
            low(rows, (reach + 1) * rows),
            full(2, rows, head_width // 2),
            low(rows, width),
            full(rows, heads_width),
            low(head_count, rows, head_width),
            low(rows, 2 * head_width),
            low(reach + 1, rows, 2 * head_width),
            low(head_count, rows, (reach + 1) * rows),
            low(rows, query_width),
            full(rows, width),
            full(rows, width),
            low(n_fsdp, rows, width),
            low(n_fsdp, rows, width),
            low(max(width, 2 * n_fsdp * rows), hidden),
            low(n_fsdp, rows, hidden),
            low(2, n_fsdp, rows, hidden),
            low(width, n_fsdp * rows),
            low(n_fsdp - 1, rows, width),
            low(2, n_fsdp - 1, rows, width),
            low(2, rows, width),
            full(rows, width),
            low(hidden // 256, 128, width),
            low(n_fsdp, depth, hidden),
            low(n_fsdp, rows_o // 2, width),
            low(n_fsdp, depth // 2, heads_width),
            low(hidden // 256, 64, width),
            low(n_fsdp, depth // 2, hidden),
            low(1, rows_o // 4, width),
            low(n_fsdp, depth // 2, heads_width // 2),
            low(hidden // 256, 32, width),
            low(n_fsdp, depth // 2, hidden // 2),
            low(1, rows_o // 8, width),
            low(n_fsdp, depth // 2, heads_width // 4),
            low(n_fsdp - 1, rows_o // 2, width),
            low(n_fsdp - 1, depth // 2, heads_width // 4),
            low(rows, width),
            low(head_count, rows, head_width),
            low(head_count, rows, (reach + 1) * rows),
            full(rows, 2 * head_width),
            low(reach, rows, 2 * head_width),
            low(reach, rows, 2 * head_width),
            low(rows, heads_width),
            full(8, width),
            full(n_seq, 8, width),
            full(n_fsdp, 8, width),
            sems((n_items, 5)),
            sems((n_items, 5)),
            sems((7,)),
            sems((n_fsdp,)),
            sems((n_fsdp,)),
            sems((n_seq,)),
            sems((n_seq,)),
            sems((reach,)),
            sems((reach,)),
            sems((4, n_fsdp)),
            sems((4, n_fsdp)),
            sems((7,)),
            sems((reach,)),
            sems((reach,)),
            sems((2 + 3 * n_fsdp,)),
            sems((2 + 3 * n_fsdp,)),
            sems((4 + n_fsdp,)),
            sems((4 + n_fsdp,)),
            sems((4 + n_fsdp,)),
            sems((4 + n_fsdp,)),
            sems((4 + n_fsdp,)),
            sems((4 + n_fsdp,)),
            sems((2, n_fsdp)),
            sems((2, n_fsdp)),
            sems((4 + n_fsdp,)),
            sems((4 + n_fsdp, 3)),
            sems((4 + n_fsdp, 3)),
            sems((n_seq + n_fsdp,)),
            sems((n_seq + n_fsdp,)),
        ],
        compiler_params=pltpu.CompilerParams(
            collective_id=0, has_side_effects=True, vmem_limit_bytes=63 << 20
        ),
        name="decoder_layer",
    )(x, cot, rates, segs, *gains, w_gate, w_up, w_query, w_key, w_value, w_output, w_down)


def finish_kernel(
    share, skip_ref, wins_ref, d0_ref, d1_ref, d2_ref, qkv_ref, wo_ref, small_ref,
    gate_ref, up_ref, down_ref, wq_ref, wk_ref, wv_ref, wo_out, out_ref, dx_ref, *gain_outs,
):
    n_win, hidden = wins_ref.shape[0] // 2, wins_ref.shape[2]
    starts = [window_start(i, share) for i in range(n_win)]
    for i, ref in enumerate((gate_ref, up_ref)):
        for w in range(n_win):
            at = i * n_win + w
            first = starts[w]
            last = starts[w + 1] if w + 1 < n_win else first + hidden
            shared = starts[w - 1] + hidden - first if w else 0
            if shared:
                ref[:, first : first + shared] = wins_ref[at, :, :shared].astype(F32) + wins_ref[
                    at - 1, :, hidden - shared :
                ].astype(F32)
            ref[:, first + shared : last] = wins_ref[at, :, shared : last - first].astype(F32)
    for k, ref in enumerate((d0_ref, d1_ref, d2_ref)):
        down_ref[pl.ds(k * ref.shape[0], ref.shape[0]), :] = ref[...].astype(F32)
    start = 0
    for ref in (wq_ref, wk_ref, wv_ref):
        size = ref.shape[1]
        ref[...] = qkv_ref[0, :, start : start + size].astype(F32)
        start += size
    wo_out[...] = wo_ref[...].astype(F32)

    @pl.when(pl.program_id(0) == 0)
    def _():
        rows_here = dx_ref.shape[0]
        dx_ref[...] = small_ref[:rows_here]
        out_ref[...] = small_ref[rows_here : 2 * rows_here].astype(BF16)
        for row, ref in enumerate(gain_outs):
            ref[...] = small_ref[2 * rows_here + row, : ref.shape[0]]


def finish(share, skipped, gain_sizes, query_width, head_width, rows_o, windows, tiles, small):
    n_win, rows, hidden = windows.shape
    n_win = n_win // 2
    width = tiles.shape[2]
    rows_here = small.shape[0] // 2 - 4
    slab = 32
    steps = rows // slab
    down_slab = share // steps // 3
    heads_width = query_width + 2 * head_width
    down = tiles.reshape(-1, width)
    start_o = (down.shape[0] - rows_o) // slab
    shape = jax.ShapeDtypeStruct

    def slabs(n_rows, n_cols, n_slabs):
        return pl.BlockSpec(
            (n_rows, n_cols), lambda i, skip: (jnp.minimum(i, n_slabs - 1), 0)
        )

    def down_part(k):
        return pl.BlockSpec((down_slab, width), lambda i, skip: (3 * i + k + skip[0], 0))

    def whole(array_shape):
        return pl.BlockSpec(array_shape, lambda i, skip: (0,) * len(array_shape))

    return pl.pallas_call(
        functools.partial(finish_kernel, share),
        grid_spec=pltpu.PrefetchScalarGridSpec(
            num_scalar_prefetch=1,
            grid=(steps,),
            in_specs=[
                pl.BlockSpec((2 * n_win, slab, hidden), lambda i, skip: (0, i, 0)),
                down_part(0),
                down_part(1),
                down_part(2),
                pl.BlockSpec((1, slab, heads_width), lambda i, skip: (2 * n_win, i, 0)),
                pl.BlockSpec(
                    (slab, width),
                    lambda i, skip: (start_o + jnp.minimum(i, rows_o // slab - 1), 0),
                ),
                whole(small.shape),
            ],
            out_specs=[
                slabs(slab, n_win * share, steps),
                slabs(slab, n_win * share, steps),
                slabs(3 * down_slab, width, steps),
                slabs(slab, query_width, steps),
                slabs(slab, head_width, steps),
                slabs(slab, head_width, steps),
                slabs(slab, width, rows_o // slab),
                whole((rows_here, width)),
                whole((rows_here, width)),
            ]
            + [whole((size,)) for size in gain_sizes],
        ),
        out_shape=[
            shape((rows, n_win * share), F32),
            shape((rows, n_win * share), F32),
            shape((share, width), F32),
            shape((rows, query_width), F32),
            shape((rows, head_width), F32),
            shape((rows, head_width), F32),
            shape((rows_o, width), F32),
            shape((rows_here, width), BF16),
            shape((rows_here, width), F32),
        ]
        + [shape((size,), F32) for size in gain_sizes],
        compiler_params=pltpu.CompilerParams(vmem_limit_bytes=63 << 20),
        name="finish",
    )((skipped // down_slab).reshape(1), windows, down, down, down, windows, down, small)


def shards(n_seq, n_fsdp, *args):
    w_query, w_key, w_output, w_gate = args[4], args[5], args[9], args[12]
    depth, ffn_width = w_gate.shape
    rows_here = args[0].shape[1]
    share = ffn_width // n_fsdp
    reach = (WINDOW - 2 + rows_here) // rows_here
    fits = (
        n_seq == 8
        and n_fsdp == 4
        and args[0].shape[0] == 1
        and reach < n_seq
        and rows_here == 128
        and window_width(share, n_fsdp) == 256 * (2 * n_fsdp - 1)
        and depth % 32 == 0
        and w_output.shape[0] == 256
        and w_key.shape[1] % 256 == 0
        and w_query.shape[1] % 512 == 0
        and w_output.shape[1] % 384 == 0
        and ffn_width % n_fsdp == 0
        and share % 16 == 0
        and rows_here // 2 * (share // 64) * 2 == rows_here * (depth // 32) * 3
        and (share - window_start(1, share)) % 64 == 0
        and window_start(n_fsdp - 1, share) + window_width(share, n_fsdp) == ffn_width
    )
    if fits:
        return shards_fused(n_seq, n_fsdp, *args)
    return shards_plain(*args)


def shards_fused(
    n_seq,
    n_fsdp,
    inputs,
    segments,
    cotangent,
    gain_attn_in,
    w_query,
    w_key,
    w_value,
    gain_query,
    gain_key,
    w_output,
    gain_attn_out,
    gain_ffn_in,
    w_gate,
    w_up,
    w_down,
    gain_ffn_out,
):
    rows_here, width = inputs.shape[1:]
    head_width = w_key.shape[1]
    query_width = w_query.shape[1]
    head_count = query_width // head_width
    share = w_gate.shape[1] // n_fsdp
    hidden = window_width(share, n_fsdp)
    reach = (WINDOW - 2 + rows_here) // rows_here
    line = lax.axis_index("fsdp")
    gains = (gain_attn_in, gain_attn_out, gain_ffn_in, gain_ffn_out, gain_query, gain_key)
    rates = 10000.0 ** (-(np.arange(head_width // 2, dtype=np.float32) * 2.0) / head_width)
    small, fin_gu, fin_d = layer(
        n_seq, n_fsdp, share, hidden, reach, head_count,
        inputs[0], cotangent[0], jnp.asarray(rates, F32)[None], segments, gains,
        w_gate, w_up, w_query, w_key, w_value, w_output, w_down,
    )
    (
        grad_gate, grad_up, grad_down, grad_q, grad_k, grad_v, grad_o, outputs, d_inputs,
        g_attn_in, g_attn_out, g_ffn_in, g_ffn_out, g_query, g_key,
    ) = finish(
        share, line * share - window_start(line, share), [g.shape[0] for g in gains],
        query_width, head_width, w_output.shape[0], fin_gu, fin_d, small,
    )
    return (
        outputs[None],
        d_inputs[None],
        g_attn_in,
        grad_q,
        grad_k,
        grad_v,
        g_query,
        g_key,
        grad_o,
        g_attn_out,
        g_ffn_in,
        grad_gate,
        grad_up,
        grad_down,
        g_ffn_out,
    )


def solution(mesh):
    placed = (
        P("fsdp", "seq", None),
        P("fsdp", "seq"),
        P("fsdp", "seq", None),
        P("fsdp"),
        P("fsdp", None),
        P("fsdp", None),
        P("fsdp", None),
        P("fsdp"),
        P("fsdp"),
        P("fsdp", None),
        P("fsdp"),
        P("fsdp"),
        P("fsdp", None),
        P("fsdp", None),
        P("fsdp", None),
        P("fsdp"),
    )
    return jax.shard_map(
        functools.partial(shards, mesh.shape["seq"], mesh.shape["fsdp"]),
        mesh=mesh,
        in_specs=placed,
        out_specs=(
            P("fsdp", "seq", None),
            P("fsdp", "seq", None),
            P("fsdp"),
            P("fsdp", None),
            P("fsdp", None),
            P("fsdp", None),
            P("fsdp"),
            P("fsdp"),
            P("fsdp", None),
            P("fsdp"),
            P("fsdp"),
            P("fsdp", None),
            P("fsdp", None),
            P("fsdp", None),
            P("fsdp"),
        ),
        check_vma=False,
    )
```
